128 devices in a mesh: dp: 2 (over core), gx: 32 (over z, y, x_hi), gy: 2 (over x_lo).
Axes of the slice: x: 4 (x_hi: 2, x_lo: 2; x = x_hi * 2 + x_lo), y: 4, z: 4, core: 2. Of those that a mesh axis runs over, the one named last changes fastest.
Arguments:
- tokens: bfloat16 [25216, 1536], P(('dp', 'gx'), 'gy')
- image_counts: int32 [2], P('dp'), may hold values from 64 to 128, as said below
- slot_order: int32 [2, 128], P('dp', 'gx'), may hold values from 0 to 127, as said below
- cotangent: bfloat16 [25216, 1536], P(('dp', 'gx'), 'gy'), may hold values from -6 to 6
- attention_weights: float32 [768, 3072], P('gx', 'gy')
- attention_first: float32 [768, 3072], P('gx', 'gy'), may hold values from -48 to 48
- attention_second: float32 [768, 3072], P('gx', 'gy'), may hold values from 2.319872 to 37.11795
- expand_weight: float32 [768, 3072], P('gx', 'gy'), may hold values from -0.21875 to 0.21875
- expand_first: float32 [768, 3072], P('gx', 'gy'), may hold values from -112 to 112
- expand_second: float32 [768, 3072], P('gx', 'gy'), may hold values from 13.61664 to 217.86624
- project_weight: float32 [768, 3072], P('gy', 'gx'), may hold values from -0.3125 to 0.3125
- project_first: float32 [768, 3072], P('gy', 'gx'), may hold values from -80 to 80
- project_second: float32 [768, 3072], P('gy', 'gx'), may hold values from 7.993472 to 127.89555
- vectors: float32 [12, 768], P(None, 'gy')
- vector_first: float32 [12, 768], P(None, 'gy'), may hold values from -96 to 96
- vector_second: float32 [12, 768], P(None, 'gy'), may hold values from 9.32992 to 149.27872
Outputs:
- block_out: float32 [25216, 1536], P(('dp', 'gx'), 'gy')
- input_grad: float32 [25216, 1536], P(('dp', 'gx'), 'gy')
- attention_grad: float32 [768, 3072], P('gx', 'gy')
- attention_second_new: float32 [768, 3072], P('gx', 'gy')
- attention_new: float32 [768, 3072], P('gx', 'gy')
- expand_grad: float32 [768, 3072], P('gx', 'gy')
- expand_second_new: float32 [768, 3072], P('gx', 'gy')
- expand_new: float32 [768, 3072], P('gx', 'gy')
- project_grad: float32 [768, 3072], P('gy', 'gx')
- project_second_new: float32 [768, 3072], P('gy', 'gx')
- project_new: float32 [768, 3072], P('gy', 'gx')
- vector_grad: float32 [12, 768], P(None, 'gy')
- vector_second_new: float32 [12, 768], P(None, 'gy')
- vector_new: float32 [12, 768], P(None, 'gy')
The draws below stay inside these ranges and needn't reach their ends.
Inputs may be any that keep to these rules, and one draw needn't show every extreme that they name: `image_counts`: live images of each data group; some group has all 128 slots live. `slot_order`: each row is a permutation of 0 to 127.
All inputs are finite; a program needn't handle non-finite values.
Results may differ from the reference program's by a relative error of at most 0.012.
Values may be sent and summed in bfloat16 or wider, within the bound.
No kernel may reach another device: no remote copies, remote signals or barrier semaphores. Data moves between devices by JAX's collectives and lax.ppermute only.
A program may use at most 192 MiB of HBM per device.

```python
import math
import jax
import jax.numpy as jnp
from jax import lax

D = 768
HEADS = 12
HD = 64
FF = 3072
SEQ = 197
STEP = 10
SLOTS = 128
TOKENS = 50432
N_DP = 2


def draw_tokens(key, part):
    key = jax.random.fold_in(key, 11)
    position = jnp.arange(D, dtype=jnp.float32) / (D - 1)
    base_draw = jax.random.normal(key, (TOKENS, D), jnp.float32)
    feature_ramp = 1.0 + 2.0 * position
    drawn = base_draw * feature_ramp
    packed = jnp.swapaxes(drawn.reshape(TOKENS // 2, 2, D), 1, 2).reshape(TOKENS // 2, 2 * D)
    return packed.astype(jnp.bfloat16)


def draw_image_counts(key, part):
    key = jax.random.fold_in(key, 12)
    count_key, pick_key = jax.random.split(key)
    counts = jax.random.randint(count_key, (N_DP,), (SLOTS + 1) // 2, SLOTS + 1)
    full_group = jax.random.randint(pick_key, (), 0, N_DP)
    return jnp.where(jnp.arange(N_DP) == full_group, SLOTS, counts).astype(jnp.int32)


def draw_slot_order(key, part):
    key = jax.random.fold_in(key, 13)
    group_keys = jax.random.split(key, N_DP)
    return jax.vmap(lambda single: jax.random.permutation(single, SLOTS))(group_keys).astype(jnp.int32)


def draw_attention_weights(key, part):
    key = jax.random.fold_in(key, 14)
    base_key, column_key = jax.random.split(key)
    base_draw = jax.random.normal(base_key, (D, D, 4), jnp.float32)
    column_draw = 0.5 * jax.random.normal(column_key, (1, D, 4), jnp.float32)
    factors = jnp.array([1.0, 1.0, 1.0, 4.0], jnp.float32) / jnp.sqrt(jnp.float32(D))
    column_factors = jnp.array([1.0, 1.0, 1.0, 0.0], jnp.float32) / jnp.sqrt(jnp.float32(D))
    return (base_draw * factors + column_draw * column_factors).reshape(D, 4 * D)


def draw_vectors(key, part):
    key = jax.random.fold_in(key, 15)
    base_draw = jax.random.normal(key, (12, D), jnp.float32)
    row_index = jnp.arange(12)[:, None]
    gain_rows = (row_index == 0) | (row_index == 5)
    return jnp.where(gain_rows, 1.0 + 0.1 * base_draw, 0.2 * base_draw)


def block_levels(stream_key, extent, cuts, smallest, high):
    gain = 1.0
    for axis_at, shards_of in cuts:
        draws = jax.random.uniform(jax.random.fold_in(jax.random.fold_in(stream_key, 6), axis_at), (shards_of,), jnp.float32, smallest / len(cuts), high / len(cuts))
        gain = gain * jnp.repeat(jnp.exp(draws), extent[axis_at] // shards_of).reshape((-1,) + (1,) * (len(extent) - 1 - axis_at))
    return gain


def centred(own_key, extent, spread, limit, cuts=(), kind=jnp.bfloat16):
    values = spread * jax.random.normal(own_key, extent, jnp.float32)
    if cuts:
        values = values * block_levels(own_key, extent, cuts, -0.22, 0.18)
    return jnp.clip(values, -limit, limit).astype(kind)


def setup_inputs(seed: int = 0) -> dict:
    splits = jax.random.split(jax.random.key(seed), 17)
    tokens = draw_tokens(jax.random.fold_in(splits[16], 71), 0)
    image_counts = draw_image_counts(jax.random.fold_in(splits[16], 71), 0)
    slot_order = draw_slot_order(jax.random.fold_in(splits[16], 71), 0)
    cotangent = centred(splits[3], (TOKENS // 2, 2 * D), 1.0, 6.0, ((0, 64), (1, 2)))
    attention_weights = draw_attention_weights(jax.random.fold_in(splits[16], 71), 0)
    attention_first = centred(splits[5], (D, 4 * D), (0.039 * (0.75 * N_DP * SLOTS * SEQ) ** 0.5), 48.0, ((0, 32), (1, 2)), jnp.float32)
    attention_second = jnp.clip(jnp.exp(math.log(37.11795) - 2.7725887 * jax.random.uniform(splits[6], (D, 4 * D), jnp.float32) ** block_levels(splits[6], (D, 4 * D), ((0, 32), (1, 2)), -0.2, 0.2)), 2.319872, 37.11795)
    expand_weight = centred(splits[7], (D, FF), D ** -0.5, 0.21875, ((0, 32), (1, 2)), jnp.float32)
    expand_first = centred(splits[8], (D, FF), (0.094 * (0.75 * N_DP * SLOTS * SEQ) ** 0.5), 112.0, ((0, 32), (1, 2)), jnp.float32)
    expand_second = jnp.clip(jnp.exp(math.log(217.86624) - 2.7725887 * jax.random.uniform(splits[9], (D, FF), jnp.float32) ** block_levels(splits[9], (D, FF), ((0, 32), (1, 2)), -0.2, 0.2)), 13.61664, 217.86624)
    project_weight = centred(splits[10], (D, FF), (FF // 8) ** -0.5, 0.3125, ((0, 2), (1, 32)), jnp.float32)
    project_first = centred(splits[11], (D, FF), (0.072 * (0.75 * N_DP * SLOTS * SEQ) ** 0.5), 80.0, ((0, 2), (1, 32)), jnp.float32)
    project_second = jnp.clip(jnp.exp(math.log(127.89555) - 2.7725887 * jax.random.uniform(splits[12], (D, FF), jnp.float32) ** block_levels(splits[12], (D, FF), ((0, 2), (1, 32)), -0.2, 0.2)), 7.993472, 127.89555)
    vectors = draw_vectors(jax.random.fold_in(splits[16], 71), 0)
    vector_first = centred(splits[14], (12, D), (0.078 * (0.75 * N_DP * SLOTS * SEQ) ** 0.5), 96.0, ((1, 2),), jnp.float32)
    vector_second = jnp.clip(jnp.exp(math.log(149.27872) - 2.7725887 * jax.random.uniform(splits[15], (12, D), jnp.float32) ** block_levels(splits[15], (12, D), ((1, 2),), -0.2, 0.2)), 9.32992, 149.27872)
    return {"tokens": tokens, "image_counts": image_counts, "slot_order": slot_order, "cotangent": cotangent, "attention_weights": attention_weights, "attention_first": attention_first, "attention_second": attention_second, "expand_weight": expand_weight, "expand_first": expand_first, "expand_second": expand_second, "project_weight": project_weight, "project_first": project_first, "project_second": project_second, "vectors": vectors, "vector_first": vector_first, "vector_second": vector_second}


norm_eps = 1e-06
beta_first = 0.9
beta_second = 0.999
learn_rate = 0.04
vector_rate = 0.25
decay_rate = 0.05
adam_eps = 1e-08

@jax.custom_vjp
def low(v):
    return lax.optimization_barrier(v.astype(jnp.bfloat16)).astype(jnp.float32)

@jax.custom_vjp
def low_back(v):
    return v

def low_keep(v):
    return (low(v), None)

def low_pass(kept, grad):
    return (grad,)

def back_keep(v):
    return (v, None)

def back_low(kept, grad):
    return (low(grad),)
low.defvjp(low_keep, low_pass)
low_back.defvjp(back_keep, back_low)

def matmul(left_side, right_side):
    return jnp.dot(left_side, right_side, precision=lax.Precision.HIGHEST, preferred_element_type=jnp.float32)

def unpack_rows(packed):
    return jnp.swapaxes(packed.reshape(packed.shape[0], -1, 2), 1, 2).reshape(packed.shape[0] * 2, -1)

def pack_rows(plain):
    return jnp.swapaxes(plain.reshape(plain.shape[0] // 2, 2, -1), 1, 2).reshape(plain.shape[0] // 2, -1)

def layer_norm(values, gain_row, shift_row):
    center = lax.optimization_barrier(jnp.mean(values, axis=-1, keepdims=True))
    deviation = values - center
    variance = lax.optimization_barrier(jnp.mean(deviation * deviation, axis=-1, keepdims=True))
    return deviation * lax.rsqrt(variance + norm_eps) * gain_row + shift_row

def attend_image(query_rows, key_rows, value_rows):
    scores = jnp.einsum('sha,tha->hst', query_rows, key_rows, precision=lax.Precision.HIGHEST) / math.sqrt(HD)
    scores = low_back(scores)
    soft_weights = low(jax.nn.softmax(scores, axis=-1))
    return jnp.einsum('hst,tha->sha', soft_weights, value_rows, precision=lax.Precision.HIGHEST)

def attend_block(parts):
    return jax.checkpoint(attend_image)(parts[0], parts[1], parts[2])

def forward(packed_stream, attention_packed, expand, project_stored, vectors):
    stream = unpack_rows(packed_stream)
    attention = jnp.transpose(attention_packed.reshape(D, D, 4), (2, 0, 1))
    project = project_stored.T
    head_shape = (-1, SEQ, HEADS, HD)
    normed = low(layer_norm(stream, vectors[0], vectors[1]))
    weight_query = low(attention[0])
    weight_key = low(attention[1])
    weight_value = low(attention[2])
    weight_out = low(attention[3])
    queries = low(low_back(matmul(normed, weight_query) + vectors[2]))
    key_rows = low(low_back(matmul(normed, weight_key)))
    values = low(low_back(matmul(normed, weight_value) + vectors[3]))
    mixed = lax.map(attend_block, (queries.reshape(head_shape), key_rows.reshape(head_shape), values.reshape(head_shape)))
    mixed = low(low_back(mixed.reshape(-1, D)))
    middle = stream + low_back(matmul(mixed, weight_out) + vectors[4])
    second = low(layer_norm(middle, vectors[5], vectors[6]))
    hidden_bias = vectors[8:].T.reshape(FF)
    inner_sum = low_back(matmul(second, low(expand)) + hidden_bias)
    activated = low(jax.nn.gelu(inner_sum, approximate=False))
    return pack_rows(middle + low_back(matmul(activated, low(project)) + vectors[7]))

def adamw_step(parameter, gradient, first_moment, second_moment, step_rate, decay_factor):
    first_new = beta_first * first_moment + (1.0 - beta_first) * gradient
    second_new = beta_second * second_moment + (1.0 - beta_second) * gradient * gradient
    first_hat = first_new / (1.0 - beta_first ** STEP)
    second_hat = second_new / (1.0 - beta_second ** STEP)
    updated = parameter - step_rate * (first_hat / (jnp.sqrt(second_hat) + adam_eps) + decay_factor * parameter)
    return (second_new, updated)

def reference(tokens, image_counts, slot_order, cotangent, attention_weights, attention_first, attention_second, expand_weight, expand_first, expand_second, project_weight, project_first, project_second, vectors, vector_first, vector_second):
    live_slots = (slot_order < image_counts[:, None]).astype(jnp.float32).reshape(-1)
    live_rows = jnp.repeat(live_slots, SEQ)
    upstream = pack_rows(unpack_rows(cotangent.astype(jnp.float32)) * live_rows[:, None])
    block_out, pullback = jax.vjp(forward, tokens.astype(jnp.float32), attention_weights, expand_weight, project_weight, vectors)
    input_grad, attention_grad, expand_grad, project_grad, vector_grad = pullback(upstream)
    attention_second_new, attention_new = adamw_step(attention_weights, attention_grad, attention_first, attention_second, learn_rate, decay_rate)
    expand_second_new, expand_new = adamw_step(expand_weight, expand_grad, expand_first, expand_second, learn_rate, decay_rate)
    project_second_new, project_new = adamw_step(project_weight, project_grad, project_first, project_second, learn_rate, decay_rate)
    vector_second_new, vector_new = adamw_step(vectors, vector_grad, vector_first, vector_second, vector_rate, 0.0)
    return (block_out, input_grad, attention_grad, attention_second_new, attention_new, expand_grad, expand_second_new, expand_new, project_grad, project_second_new, project_new, vector_grad, vector_second_new, vector_new)
```

```python
import jax
import jax.numpy as jnp
from jax import lax
from jax.experimental import pallas as pl
from jax.experimental.pallas import tpu as pltpu
from jax.sharding import Mesh
from jax.sharding import PartitionSpec as P

D = 768
HD = 64
FF = 3072
SEQ = 197
STEP = 10
PAD = 208
IMAGES = 2
ROWS = PAD * IMAGES
HALF = D // 2

norm_eps = 1e-06
beta_first = 0.9
beta_second = 0.999
learn_rate = 0.04
vector_rate = 0.25
decay_rate = 0.05
adam_eps = 1e-08

f32 = jnp.float32
bf16 = jnp.bfloat16

DP = ("dp",)
Z = ("z",)
Y = ("y",)
X = ("xh", "xl")
CHIPS = ("xl", "z", "y", "xh")
EVERY = ("dp", "z", "y", "xh", "xl")


def dot(a, b):
    return lax.dot_general(a, b, (((1,), (0,)), ((), ())), preferred_element_type=f32)


def dot_rows(a, b):
    return lax.dot_general(a, b, (((0,), (0,)), ((), ())), preferred_element_type=f32)


def dot_lanes(a, b):
    return lax.dot_general(a, b, (((1,), (1,)), ((), ())), preferred_element_type=f32)


def call(body, outs, args, scratch=(), flops=0, nbytes=0, name=None):
    smem = {i for i, a in enumerate(args) if a.dtype == jnp.int32}
    return pl.pallas_call(
        body,
        out_shape=[jax.ShapeDtypeStruct(s, t) for s, t in outs],
        in_specs=[
            pl.BlockSpec(memory_space=pltpu.SMEM if i in smem else pltpu.VMEM)
            for i in range(len(args))
        ],
        out_specs=[pl.BlockSpec(memory_space=pltpu.VMEM) for _ in outs],
        scratch_shapes=list(scratch),
        compiler_params=pltpu.CompilerParams(vmem_limit_bytes=52 * 1024 * 1024),
        cost_estimate=pl.CostEstimate(flops=flops, bytes_accessed=nbytes, transcendentals=0),
        name=name,
    )(*args)


def iota(shape, dim):
    return lax.broadcasted_iota(jnp.int32, shape, dim)


def row_picks():
    r = iota((ROWS, PAD), 0)
    j = iota((ROWS, PAD), 1)
    second = r >= PAD
    s = jnp.where(second, r - PAD, r)
    t = jnp.where(second, s + SEQ, s)
    live = s < SEQ
    even = jnp.where(live & (t == 2 * j), 1.0, 0.0).astype(bf16)
    odd = jnp.where(live & (t == 2 * j + 1), 1.0, 0.0).astype(bf16)
    return even, odd


def row_picks_back():
    r = iota((PAD, ROWS), 1)
    j = iota((PAD, ROWS), 0)
    second = r >= PAD
    s = jnp.where(second, r - PAD, r)
    t = jnp.where(second, s + SEQ, s)
    live = s < SEQ
    even = jnp.where(live & (t == 2 * j), 1.0, 0.0).astype(bf16)
    odd = jnp.where(live & (t == 2 * j + 1), 1.0, 0.0).astype(bf16)
    return even, odd


def lane_split():
    l = iota((256, 256), 0)
    c = iota((256, 256), 1)
    target = jnp.where(c < 128, 2 * c, 2 * (c - 128) + 1)
    return jnp.where(l == target, 1.0, 0.0).astype(bf16)


def lane_join():
    l = iota((256, 256), 1)
    c = iota((256, 256), 0)
    target = jnp.where(c < 128, 2 * c, 2 * (c - 128) + 1)
    return jnp.where(l == target, 1.0, 0.0).astype(bf16)


def unpack(own_ref, got_ref, gy):
    own, got = own_ref[...], got_ref[...]
    first = jnp.where(gy == 0, own.astype(f32), got.astype(f32)).astype(bf16)
    last = jnp.where(gy == 0, got.astype(f32), own.astype(f32)).astype(bf16)
    split = lane_split()
    evens, odds = [], []
    for half in (first, last):
        for b in range(3):
            both = dot(half[:, 256 * b : 256 * b + 256], split).astype(bf16)
            evens.append(both[:, :128])
            odds.append(both[:, 128:])
    even_rows, odd_rows = row_picks()
    return dot(even_rows, jnp.concatenate(evens, axis=1)) + dot(odd_rows, jnp.concatenate(odds, axis=1))


def pack(rows_low, gy, keep_ref, send_ref):
    even_rows, odd_rows = row_picks_back()
    even = dot(even_rows, rows_low).astype(bf16)
    odd = dot(odd_rows, rows_low).astype(bf16)
    join = lane_join()
    for b in range(3):
        blocks = []
        for half in range(2):
            at = HALF * half + 128 * b
            both = jnp.concatenate([even[:, at : at + 128], odd[:, at : at + 128]], axis=1)
            blocks.append(dot(both, join))
        keep_ref[:, 256 * b : 256 * b + 256] = jnp.where(gy == 0, blocks[0], blocks[1]).astype(bf16)
        send_ref[:, 256 * b : 256 * b + 256] = jnp.where(gy == 0, blocks[1], blocks[0]).astype(bf16)


def norm_parts(v):
    center = jnp.mean(v, axis=1, keepdims=True)
    away = v - center
    scale = lax.rsqrt(jnp.mean(away * away, axis=1, keepdims=True) + norm_eps)
    return away * scale, scale


def norm_back(grad, scaled, scale, gain):
    pushed = grad * gain
    first = jnp.mean(pushed, axis=1, keepdims=True)
    cross = jnp.mean(pushed * scaled, axis=1, keepdims=True)
    return (pushed - first - scaled * cross) * scale


def prepare_kernel(me_ref, attn_ref, expand_ref, project_ref, attn_out, ff_out):
    me = me_ref[0]
    l = iota((512, 256), 0)
    c = iota((512, 256), 1)
    kind = 2 * me + jnp.where(c < 128, 0, 1)
    pick = jnp.where(l == 4 * (c & 127) + kind, 1.0, 0.0).astype(bf16)
    for b in range(3):
        both = dot(attn_ref[:, 512 * b : 512 * b + 512].astype(bf16), pick).astype(bf16)
        attn_out[:, 128 * b : 128 * b + 128] = both[:, :128]
        attn_out[:, HALF + 128 * b : HALF + 128 * b + 128] = both[:, 128:]
    ff_out[:, :D] = jnp.where(me == 0, expand_ref[:, :D], expand_ref[:, D:]).astype(bf16)
    turned = project_ref[...].T
    mine = jnp.where(me == 0, turned[:48], turned[48:])
    ff_out[:, D : D + HALF] = mine[:24].astype(bf16)
    ff_out[:, D + HALF :] = mine[24:].astype(bf16)


def attend_kernel(
    me_ref, own_ref, got_ref, vec_ref, w_own, w_got,
    x_out, normed_out, qkv_out, soft_out, mixed_out, w_out,
):
    me, gy = me_ref[0], me_ref[1]
    x_out[...] = unpack(own_ref, got_ref, gy).astype(bf16)
    scaled, _ = norm_parts(x_out[...].astype(f32))
    normed_out[...] = (scaled * vec_ref[0:1, :] + vec_ref[1:2, :]).astype(bf16)
    for ref, place in ((w_own, me), (w_got, 1 - me)):
        for half in range(2):
            for y in range(2):
                w_out[pl.ds(2 * place + half, 1), :, HALF * y : HALF * y + HALF] = ref[
                    y, :, HALF * half : HALF * half + HALF
                ][None]

    def project(i, carry):
        cols = pl.ds(pl.multiple_of(256 * i, 256), 256)
        for kind, row in ((0, 2), (1, None), (2, 3)):
            part = dot(normed_out[...], w_out[kind, :, cols])
            if row is not None:
                part = part + vec_ref[row : row + 1, cols]
            qkv_out[kind, :, cols] = part.astype(bf16)
        return carry

    lax.fori_loop(0, 3, project, 0)
    lane = iota((PAD, 128), 1)
    key_live = iota((PAD, PAD), 0) < SEQ

    def attend(i, carry):
        rows = pl.ds(pl.multiple_of(PAD * (i & 1), 16), PAD)
        cols = pl.ds(pl.multiple_of(128 * (i >> 1), 128), 128)
        q = qkv_out[0, rows, cols] * jnp.asarray(0.125, bf16)
        k = qkv_out[1, rows, cols]
        v = qkv_out[2, rows, cols]
        total = None
        for n in range(2):
            inside = (lane < HD) == (n == 0)
            scores = dot_lanes(k, jnp.where(inside, q, jnp.zeros_like(q)))
            scores = jnp.where(key_live, scores, -1e30)
            terms = jnp.exp(scores - jnp.max(scores, axis=0, keepdims=True))
            soft = (terms / jnp.sum(terms, axis=0, keepdims=True)).astype(bf16)
            soft_out[i, n] = soft
            part = dot_rows(soft, jnp.where(inside, v, jnp.zeros_like(v)))
            total = part if total is None else total + part
        mixed_out[rows, cols] = total.astype(bf16)
        return carry

    lax.fori_loop(0, 6 * IMAGES, attend, 0)


def expand_kernel(
    me_ref, live_ref, own_ref, got_ref, vec_ref, bias_ref, x_ref, mixed_ref, w_ref, w1_ref,
    up_out, middle_out, second_out, act_out, slope_out, mine_out, theirs_out,
    total,
):
    me, gy = me_ref[0], me_ref[1]
    up = unpack(own_ref, got_ref, gy)
    image = jnp.where(iota((ROWS, 1), 0) < PAD, live_ref[0], live_ref[1])
    up_out[...] = jnp.where(image == 1, up, 0.0).astype(bf16)
    middle = x_ref[...].astype(f32) + dot(mixed_ref[...], w_ref[3]) + vec_ref[4:5, :]
    middle_out[...] = middle
    scaled, _ = norm_parts(middle)
    second_out[...] = (scaled * vec_ref[5:6, :] + vec_ref[6:7, :]).astype(bf16)

    def hidden(j, carry):
        cols = pl.ds(pl.multiple_of(256 * j, 256), 256)
        inner = dot(second_out[...], w1_ref[:, cols]) + bias_ref[:, cols]
        below = 0.5 + 0.5 * lax.erf(inner * 0.7071067811865476)
        dense = jnp.exp(-0.5 * inner * inner) * 0.3989422804014327
        act = (inner * below).astype(bf16)
        act_out[:, cols] = act
        slope_out[:, cols] = (below + inner * dense).astype(bf16)
        total[cols, :] = dot_rows(act, up_out[...]).astype(bf16)
        return carry

    lax.fori_loop(0, FF // 256, hidden, 0)

    def hand_out(g, carry):
        mine = total[pl.ds(pl.multiple_of(96 * g + 48 * me, 16), 48), :]
        theirs = total[pl.ds(pl.multiple_of(96 * g + 48 * (1 - me), 16), 48), :]
        for y in range(2):
            mine_out[2 * g + y] = mine[:, HALF * y : HALF * y + HALF]
            theirs_out[2 * g + y] = theirs[:, HALF * y : HALF * y + HALF]
        return carry

    lax.fori_loop(0, 32, hand_out, 0)


def contract_kernel(
    me_ref, vec_ref, up_ref, act_ref, slope_ref, second_ref, middle_ref, w1_ref, w2_ref,
    keep_out, send_out, gm_out, gml_out, sums_out, hidden_out, mine_out, theirs_out,
    inner_grad,
):
    me, gy = me_ref[0], me_ref[1]
    block = middle_ref[...] + dot(act_ref[...], w2_ref[...]) + vec_ref[7:8, :]
    pack(block.astype(bf16), gy, keep_out, send_out)

    def hidden(j, carry):
        cols = pl.ds(pl.multiple_of(256 * j, 256), 256)
        grad = dot_lanes(up_ref[...], w2_ref[cols, :]) * slope_ref[:, cols].astype(f32)
        grad = grad.astype(bf16)
        inner_grad[:, cols] = grad
        hidden_out[:, cols] = jnp.sum(grad.astype(f32), axis=0, keepdims=True)
        return carry

    lax.fori_loop(0, FF // 256, hidden, 0)
    turned = second_ref[...].T

    def outer(j, carry):
        y = j // 3
        to = pl.ds(pl.multiple_of(256 * (j - 3 * y), 256), 256)
        for ref, place in ((mine_out, me), (theirs_out, 1 - me)):
            cols = pl.ds(pl.multiple_of(1536 * y + D * place + 256 * (j - 3 * y), 256), 256)
            ref[y, :, to] = dot(turned, inner_grad[:, cols]).astype(bf16)
        return carry

    lax.fori_loop(0, 6, outer, 0)
    grad_second = dot_lanes(inner_grad[...], w1_ref[...])
    scaled, scale = norm_parts(middle_ref[...])
    up = up_ref[...].astype(f32)
    gm = up + norm_back(grad_second, scaled, scale, vec_ref[5:6, :])
    gm_out[...] = gm
    gml_out[...] = gm.astype(bf16)
    sums_out[0:1, :] = jnp.sum(gml_out[...].astype(f32), axis=0, keepdims=True)
    sums_out[1:2, :] = jnp.sum(grad_second * scaled, axis=0, keepdims=True)
    sums_out[2:3, :] = jnp.sum(grad_second, axis=0, keepdims=True)
    sums_out[3:4, :] = jnp.sum(up, axis=0, keepdims=True)


def attend_back_kernel(
    me_ref, gml_ref, normed_ref, qkv_ref, soft_ref, mixed_ref, w_ref,
    grads_out, sums_out, mine_out, theirs_out,
    grad_mixed,
):
    me = me_ref[0]
    grad_mixed[...] = dot_lanes(gml_ref[...], w_ref[3]).astype(bf16)
    lane = iota((PAD, 128), 1)

    def attend(i, carry):
        rows = pl.ds(pl.multiple_of(PAD * (i & 1), 16), PAD)
        cols = pl.ds(pl.multiple_of(128 * (i >> 1), 128), 128)
        q = qkv_ref[0, rows, cols]
        k = qkv_ref[1, rows, cols]
        v = qkv_ref[2, rows, cols]
        g = grad_mixed[rows, cols]
        dq = dk = dv = jnp.zeros((PAD, 128), f32)
        for n in range(2):
            inside = (lane < HD) == (n == 0)
            zero = jnp.zeros_like(g)
            g_in = jnp.where(inside, g, zero)
            soft_low = soft_ref[i, n]
            soft = soft_low.astype(f32)
            grad_soft = dot_lanes(v, g_in)
            level = jnp.sum(grad_soft * soft, axis=0, keepdims=True)
            scores = (soft * (grad_soft - level)).astype(bf16)
            dv = dv + dot(soft_low, g_in)
            dk = dk + dot(scores, jnp.where(inside, q, zero))
            dq = dq + dot_rows(scores, jnp.where(inside, k, zero))
        grads_out[0, rows, cols] = (dq * 0.125).astype(bf16)
        grads_out[1, rows, cols] = (dk * 0.125).astype(bf16)
        grads_out[2, rows, cols] = dv.astype(bf16)
        return carry

    lax.fori_loop(0, 6 * IMAGES, attend, 0)
    normed_turned = normed_ref[...].T
    mixed_turned = mixed_ref[...].T
    for kind in range(4):
        left = mixed_turned if kind == 3 else normed_turned
        right = gml_ref[...] if kind == 3 else grads_out[kind]
        grad = dot(left, right).astype(bf16)
        half = kind % 2

        def store(ref):
            for y in range(2):
                ref[y, :, HALF * half : HALF * half + HALF] = grad[:, HALF * y : HALF * y + HALF]

        pl.when(me == kind // 2)(lambda: store(mine_out))
        pl.when(me != kind // 2)(lambda: store(theirs_out))
    sums_out[0:1, :] = jnp.sum(grads_out[0].astype(f32), axis=0, keepdims=True)
    sums_out[1:2, :] = jnp.sum(grads_out[2].astype(f32), axis=0, keepdims=True)


def input_back_kernel(me_ref, vec_ref, grads_ref, w_ref, x_ref, gm_ref, keep_out, send_out, sums_out):
    gy = me_ref[1]
    grad = dot_lanes(grads_ref[0], w_ref[0])
    grad = grad + dot_lanes(grads_ref[1], w_ref[1])
    grad = grad + dot_lanes(grads_ref[2], w_ref[2])
    scaled, scale = norm_parts(x_ref[...].astype(f32))
    out = gm_ref[...] + norm_back(grad, scaled, scale, vec_ref[0:1, :])
    pack(out.astype(bf16), gy, keep_out, send_out)
    sums_out[0:1, :] = jnp.sum(grad * scaled, axis=0, keepdims=True)
    sums_out[1:2, :] = jnp.sum(grad, axis=0, keepdims=True)


def adamw_step(parameter, gradient, first_moment, second_moment, step_rate, decay_factor):
    first_new = beta_first * first_moment + (1.0 - beta_first) * gradient
    second_new = beta_second * second_moment + (1.0 - beta_second) * gradient * gradient
    first_hat = first_new / (1.0 - beta_first**STEP)
    second_hat = second_new / (1.0 - beta_second**STEP)
    updated = parameter - step_rate * (
        first_hat / (jnp.sqrt(second_hat) + adam_eps) + decay_factor * parameter
    )
    return second_new, updated


def ordered(me, own, got):
    return jnp.where(me == 0, own, got), jnp.where(me == 0, got, own)


def attention_step_kernel(me_ref, own_ref, got_ref, w_ref, m_ref, v_ref, grad_out, second_out, new_out):
    pieces = ordered(me_ref[0], own_ref[...], got_ref[...])
    l = iota((512, 512), 0)
    c = iota((512, 512), 1)
    pick = jnp.where(c == 4 * (l & 127) + (l >> 7), 1.0, 0.0)
    for b in range(3):
        kinds = [
            pieces[k // 2][:, HALF * (k % 2) + 128 * b : HALF * (k % 2) + 128 * b + 128]
            for k in range(4)
        ]
        grad_out[:, 512 * b : 512 * b + 512] = jnp.dot(
            jnp.concatenate(kinds, axis=1), pick, precision=lax.Precision.HIGHEST,
            preferred_element_type=f32,
        )
    second_out[...], new_out[...] = adamw_step(
        w_ref[...], grad_out[...], m_ref[...], v_ref[...], learn_rate, decay_rate
    )


def expand_step_kernel(me_ref, own_ref, got_ref, w_ref, m_ref, v_ref, grad_out, second_out, new_out):
    first, last = ordered(me_ref[0], own_ref[...], got_ref[...])
    grad_out[:, :D] = first
    grad_out[:, D:] = last
    second_out[...], new_out[...] = adamw_step(
        w_ref[...], grad_out[...], m_ref[...], v_ref[...], learn_rate, decay_rate
    )


def project_step_kernel(me_ref, own_ref, got_ref, w_ref, m_ref, v_ref, grad_out, second_out, new_out):
    first, last = ordered(me_ref[0], own_ref[...], got_ref[...])
    grad_out[...] = jnp.concatenate([first, last], axis=0).T
    second_out[...], new_out[...] = adamw_step(
        w_ref[...], grad_out[...], m_ref[...], v_ref[...], learn_rate, decay_rate
    )


def place(axes):
    at = 0
    for a in axes:
        at = at * lax.axis_size(a) + lax.axis_index(a)
    return at


def swap(x, axis):
    return lax.ppermute(x, axis, [(0, 1), (1, 0)])


def core_sum(mine, theirs):
    return (mine.astype(f32) + swap(theirs, "dp").astype(f32)).astype(bf16)


def ring_sum(blocks, axes, dim):
    me = place(axes)
    total = lax.dynamic_index_in_dim(blocks, me, dim, keepdims=False).astype(f32)
    got = []
    for r in (1, 3, 2):
        piece = lax.dynamic_index_in_dim(blocks, (me + r) % 4, dim, keepdims=False)
        got.append(lax.ppermute(piece, axes, [(i, (i + r) % 4) for i in range(4)]))
    for piece in got:
        total = total + piece.astype(f32)
    return total.astype(bf16)


def spread_sum(blocks, axes):
    tiles = lax.all_to_all(blocks, axes, 0, 0, tiled=True)
    return jnp.sum(tiles.astype(f32), axis=0)


def total_of(vector):
    vector = vector + swap(vector, "dp")
    for axes in (X, Y, Z):
        got = [
            lax.ppermute(vector, axes, [(i, (i + r) % 4) for i in range(4)]) for r in (1, 2, 3)
        ]
        vector = vector + got[0] + got[1] + got[2]
    return vector


def own_images(stored, gy):
    rows = stored.shape[0] // 2
    own = lax.dynamic_slice_in_dim(stored, rows * gy, rows, 0)
    other = lax.dynamic_slice_in_dim(stored, rows * (1 - gy), rows, 0)
    pad = ((0, PAD - rows), (0, 0))
    return jnp.pad(own, pad), jnp.pad(other, pad)


def stored_rows(keep, got, gy):
    first = jnp.where(gy == 0, keep, got)[:SEQ]
    last = jnp.where(gy == 0, got, keep)[:SEQ]
    return jnp.concatenate([first, last], axis=0).astype(f32)


def per_device(
    tokens,
    image_counts,
    slot_order,
    cotangent,
    attention_weights,
    attention_first,
    attention_second,
    expand_weight,
    expand_first,
    expand_second,
    project_weight,
    project_first,
    project_second,
    vectors,
    vector_first,
    vector_second,
):
    dp = lax.axis_index("dp")
    gy = lax.axis_index("xl")
    me = jnp.stack([dp, gy]).astype(jnp.int32)

    attn_piece, ff_piece = call(
        prepare_kernel,
        [((24, D), bf16), ((24, 2 * D), bf16)],
        (me, attention_weights, expand_weight, project_weight),
        name="prepare",
    )
    gathered = lax.all_gather(ff_piece, EVERY)
    copies = jnp.broadcast_to(attn_piece[None], (64, 24, D))
    w_own = lax.all_to_all(copies, CHIPS, 0, 0, tiled=True)
    w_got = swap(w_own, "dp")
    w_own = w_own.reshape(2, D, D)
    w_got = w_got.reshape(2, D, D)

    token_own, token_other = own_images(tokens, gy)
    token_got = swap(token_other, "xl")
    grad_own, grad_other = own_images(cotangent, gy)
    grad_got = swap(grad_other, "xl")
    vec_first, vec_last = ordered(gy, vectors, swap(vectors, "xl"))
    vec = jnp.concatenate([vec_first, vec_last], axis=1)
    bias = vec[8:].T.reshape(1, FF)
    live = (slot_order[0] < image_counts[0]).astype(jnp.int32)
    live = lax.dynamic_slice_in_dim(live, IMAGES * gy, IMAGES)

    x, normed, qkv, soft, mixed, w_attn = call(
        attend_kernel,
        [
            ((ROWS, D), bf16),
            ((ROWS, D), bf16),
            ((3, ROWS, D), bf16),
            ((6 * IMAGES, 2, PAD, PAD), bf16),
            ((ROWS, D), bf16),
            ((4, D, D), bf16),
        ],
        (me, token_own, token_got, vec, w_own, w_got),
        flops=6_000_000_000,
        nbytes=20_000_000,
        name="attend",
    )
    gathered = gathered.reshape(2, 32, 2, 24, 2 * D)
    w1 = jnp.transpose(gathered[..., :D], (1, 3, 2, 0, 4)).reshape(D, FF)
    w2 = jnp.transpose(
        gathered[..., D:].reshape(2, 32, 2, 24, 2, HALF), (1, 0, 4, 3, 2, 5)
    ).reshape(FF, D)

    up, middle, second, act, slope, mine2, theirs2 = call(
        expand_kernel,
        [
            ((ROWS, D), bf16),
            ((ROWS, D), f32),
            ((ROWS, D), bf16),
            ((ROWS, FF), bf16),
            ((ROWS, FF), bf16),
            ((64, 48, HALF), bf16),
            ((64, 48, HALF), bf16),
        ],
        (me, live, grad_own, grad_got, vec, bias, x, mixed, w_attn, w1),
        scratch=[pltpu.VMEM((FF, D), bf16)],
        flops=8_000_000_000,
        nbytes=20_000_000,
        name="expand",
    )
    sum2 = core_sum(mine2, theirs2).reshape(4, 4, 4, 48, HALF)
    sum2 = ring_sum(sum2, X, 2).reshape(16, 48, HALF)
    sum2 = spread_sum(sum2, Z + Y)

    keep_out, send_out, gm, gml, sums_c, hidden_sums, mine1, theirs1 = call(
        contract_kernel,
        [
            ((PAD, D), bf16),
            ((PAD, D), bf16),
            ((ROWS, D), f32),
            ((ROWS, D), bf16),
            ((4, D), f32),
            ((1, FF), f32),
            ((2, D, D), bf16),
            ((2, D, D), bf16),
        ],
        (me, vec, up, act, slope, second, middle, w1, w2),
        scratch=[pltpu.VMEM((ROWS, FF), bf16)],
        flops=9_000_000_000,
        nbytes=20_000_000,
        name="contract",
    )
    sum1 = core_sum(mine1, theirs1).reshape(2, 4, 4, 2, 24, D)
    sum1 = ring_sum(sum1, Y, 2).reshape(16, 24, D)
    sum1 = spread_sum(sum1, ("xl", "z", "xh"))

    grads, sums_d, mine0, theirs0 = call(
        attend_back_kernel,
        [((3, ROWS, D), bf16), ((2, D), f32), ((2, D, D), bf16), ((2, D, D), bf16)],
        (me, gml, normed, qkv, soft, mixed, w_attn),
        scratch=[pltpu.VMEM((ROWS, D), bf16)],
        flops=9_000_000_000,
        nbytes=20_000_000,
        name="attend_back",
    )
    sum0 = spread_sum(core_sum(mine0, theirs0).reshape(64, 24, D), CHIPS)

    keep_in, send_in, sums_e = call(
        input_back_kernel,
        [((PAD, D), bf16), ((PAD, D), bf16), ((2, D), f32)],
        (me, vec, grads, w_attn, x, gm),
        flops=3_000_000_000,
        nbytes=10_000_000,
        name="input_back",
    )
    block_out = stored_rows(keep_out, swap(send_out, "xl"), gy)
    input_grad = stored_rows(keep_in, swap(send_in, "xl"), gy)

    vector_sums = jnp.concatenate([sums_e, sums_d, sums_c, hidden_sums.reshape(D, 4).T], axis=0)
    vector_sums = total_of(vector_sums)
    vector_grad = lax.dynamic_slice_in_dim(vector_sums, HALF * gy, HALF, 1)
    vector_second_new, vector_new = adamw_step(
        vectors, vector_grad, vector_first, vector_second, vector_rate, 0.0
    )

    def step(body, own, shape, parameter, first, second_moment, name):
        return call(
            body,
            [(shape, f32)] * 3,
            (me, own, swap(own, "dp"), parameter, first, second_moment),
            name=name,
        )

    project = step(
        project_step_kernel, sum2, (HALF, 96), project_weight, project_first, project_second, "project_step"
    )
    expand = step(
        expand_step_kernel, sum1, (24, 2 * D), expand_weight, expand_first, expand_second, "expand_step"
    )
    attention = step(
        attention_step_kernel, sum0, (24, 2 * D), attention_weights, attention_first, attention_second, "attention_step"
    )
    return (
        block_out,
        input_grad,
        *attention,
        *expand,
        *project,
        vector_grad,
        vector_second_new,
        vector_new,
    )


def solution(mesh):
    fine = Mesh(mesh.devices.reshape(2, 4, 4, 2, 2), EVERY)
    rows = ("dp", "z", "y", "xh")
    deep = ("z", "y", "xh")
    placed = (
        P(rows, "xl"),
        P("dp"),
        P("dp", deep),
        P(rows, "xl"),
        *(P(deep, "xl"),) * 6,
        *(P("xl", deep),) * 3,
        *(P(None, "xl"),) * 3,
    )
    out = (
        P(rows, "xl"),
        P(rows, "xl"),
        *(P(deep, "xl"),) * 6,
        *(P("xl", deep),) * 3,
        *(P(None, "xl"),) * 3,
    )
    return jax.shard_map(per_device, mesh=fine, in_specs=placed, out_specs=out, check_vma=False)
```

```python
import jax
import jax.numpy as jnp
from jax import lax
from jax.experimental import pallas as pl
from jax.experimental.pallas import tpu as pltpu
from jax.sharding import Mesh
from jax.sharding import PartitionSpec as P

D = 768
HD = 64
FF = 3072
SEQ = 197
STEP = 10
PAD = 208
IMAGES = 2
ROWS = PAD * IMAGES
HALF = D // 2

norm_eps = 1e-06
beta_first = 0.9
beta_second = 0.999
learn_rate = 0.04
vector_rate = 0.25
decay_rate = 0.05
adam_eps = 1e-08

f32 = jnp.float32
bf16 = jnp.bfloat16

DP = ("dp",)
Z = ("z",)
Y = ("y",)
X = ("xh", "xl")
CHIPS = ("xl", "z", "y", "xh")
EVERY = ("dp", "z", "y", "xh", "xl")


def dot(a, b):
    return lax.dot_general(a, b, (((1,), (0,)), ((), ())), preferred_element_type=f32)


def dot_rows(a, b):
    return lax.dot_general(a, b, (((0,), (0,)), ((), ())), preferred_element_type=f32)


def dot_lanes(a, b):
    return lax.dot_general(a, b, (((1,), (1,)), ((), ())), preferred_element_type=f32)


def block(shape, index):
    return pl.BlockSpec(shape, index)


WHOLE = pl.BlockSpec(memory_space=pltpu.VMEM)
SCALARS = pl.BlockSpec(memory_space=pltpu.SMEM)
LEFT = pl.BlockSpec(memory_space=pl.ANY)


def call(body, ins, outs, args, grid=(), scratch=(), after=(), cost=10, name=None):
    count = len(args)

    def run(*refs):
        body(*refs[:count], *refs[count + len(after) :])

    return pl.pallas_call(
        run if after else body,
        out_shape=[jax.ShapeDtypeStruct(s, t) for s, t, _ in outs],
        grid=grid,
        in_specs=[*ins, *(LEFT for _ in after)],
        out_specs=[spec for _, _, spec in outs],
        scratch_shapes=list(scratch),
        compiler_params=pltpu.CompilerParams(vmem_limit_bytes=52 * 1024 * 1024),
        cost_estimate=pl.CostEstimate(flops=cost * 10**9 + 1000, bytes_accessed=0, transcendentals=0),
        name=name,
    )(*args, *after)


def iota(shape, dim):
    return lax.broadcasted_iota(jnp.int32, shape, dim)


def row_picks():
    r = iota((ROWS, PAD), 0)
    j = iota((ROWS, PAD), 1)
    second = r >= PAD
    s = jnp.where(second, r - PAD, r)
    t = jnp.where(second, s + SEQ, s)
    live = s < SEQ
    even = jnp.where(live & (t == 2 * j), 1.0, 0.0).astype(bf16)
    odd = jnp.where(live & (t == 2 * j + 1), 1.0, 0.0).astype(bf16)
    return even, odd


def row_picks_back():
    r = iota((PAD, ROWS), 1)
    j = iota((PAD, ROWS), 0)
    second = r >= PAD
    s = jnp.where(second, r - PAD, r)
    t = jnp.where(second, s + SEQ, s)
    live = s < SEQ
    even = jnp.where(live & (t == 2 * j), 1.0, 0.0).astype(bf16)
    odd = jnp.where(live & (t == 2 * j + 1), 1.0, 0.0).astype(bf16)
    return even, odd


def lane_split():
    l = iota((256, 256), 0)
    c = iota((256, 256), 1)
    target = jnp.where(c < 128, 2 * c, 2 * (c - 128) + 1)
    return jnp.where(l == target, 1.0, 0.0).astype(bf16)


def lane_join():
    l = iota((256, 256), 1)
    c = iota((256, 256), 0)
    target = jnp.where(c < 128, 2 * c, 2 * (c - 128) + 1)
    return jnp.where(l == target, 1.0, 0.0).astype(bf16)


def unpack(own_ref, got_ref, gy):
    own, got = own_ref[...], got_ref[...]
    first = jnp.where(gy == 0, own.astype(f32), got.astype(f32)).astype(bf16)
    last = jnp.where(gy == 0, got.astype(f32), own.astype(f32)).astype(bf16)
    split = lane_split()
    evens, odds = [], []
    for half in (first, last):
        for b in range(3):
            both = dot(half[:, 256 * b : 256 * b + 256], split).astype(bf16)
            evens.append(both[:, :128])
            odds.append(both[:, 128:])
    even_rows, odd_rows = row_picks()
    return dot(even_rows, jnp.concatenate(evens, axis=1)) + dot(odd_rows, jnp.concatenate(odds, axis=1))


def pack(rows_low, gy, keep_ref, send_ref):
    even_rows, odd_rows = row_picks_back()
    even = dot(even_rows, rows_low).astype(bf16)
    odd = dot(odd_rows, rows_low).astype(bf16)
    join = lane_join()
    for b in range(3):
        blocks = []
        for half in range(2):
            at = HALF * half + 128 * b
            both = jnp.concatenate([even[:, at : at + 128], odd[:, at : at + 128]], axis=1)
            blocks.append(dot(both, join))
        keep_ref[:, 256 * b : 256 * b + 256] = jnp.where(gy == 0, blocks[0], blocks[1]).astype(bf16)
        send_ref[:, 256 * b : 256 * b + 256] = jnp.where(gy == 0, blocks[1], blocks[0]).astype(bf16)


def norm_parts(v):
    center = jnp.mean(v, axis=1, keepdims=True)
    away = v - center
    scale = lax.rsqrt(jnp.mean(away * away, axis=1, keepdims=True) + norm_eps)
    return away * scale, scale


def norm_back(grad, scaled, scale, gain):
    pushed = grad * gain
    first = jnp.mean(pushed, axis=1, keepdims=True)
    cross = jnp.mean(pushed * scaled, axis=1, keepdims=True)
    return (pushed - first - scaled * cross) * scale


def prepare_kernel(me_ref, attn_ref, expand_ref, project_ref, attn_out, ff_out):
    me = me_ref[0]
    l = iota((512, 256), 0)
    c = iota((512, 256), 1)
    kind = 2 * me + jnp.where(c < 128, 0, 1)
    pick = jnp.where(l == 4 * (c & 127) + kind, 1.0, 0.0).astype(bf16)
    for b in range(3):
        both = dot(attn_ref[:, 512 * b : 512 * b + 512].astype(bf16), pick).astype(bf16)
        attn_out[:, 128 * b : 128 * b + 128] = both[:, :128]
        attn_out[:, HALF + 128 * b : HALF + 128 * b + 128] = both[:, 128:]
    ff_out[:, :D] = jnp.where(me == 0, expand_ref[:, :D], expand_ref[:, D:]).astype(bf16)
    turned = project_ref[...].T
    mine = jnp.where(me == 0, turned[:48], turned[48:])
    ff_out[:, D : D + HALF] = mine[:24].astype(bf16)
    ff_out[:, D + HALF :] = mine[24:].astype(bf16)


def attend_kernel(
    me_ref, own_ref, got_ref, vec_ref, w_own, w_got,
    soft_out, mixed_out, x_out, normed_out, qkv_out, w_out, wo_out,
    x_ref, normed_ref, qkv_ref, w_ref, sems,
):
    step = pl.program_id(0)
    copies = [
        pltpu.make_async_copy(x_ref, x_out, sems.at[0]),
        pltpu.make_async_copy(normed_ref, normed_out, sems.at[1]),
        pltpu.make_async_copy(qkv_ref, qkv_out, sems.at[2]),
        pltpu.make_async_copy(w_ref.at[pl.ds(0, 3)], w_out, sems.at[3]),
        pltpu.make_async_copy(w_ref.at[3], wo_out, sems.at[4]),
    ]

    @pl.when(step == 0)
    def _():
        me, gy = me_ref[0], me_ref[1]
        for ref, place in ((w_own, me), (w_got, 1 - me)):
            for half in range(2):
                for y in range(2):
                    w_ref[pl.ds(2 * place + half, 1), :, HALF * y : HALF * y + HALF] = ref[
                        y, :, HALF * half : HALF * half + HALF
                    ][None]
        copies[3].start()
        copies[4].start()
        x_ref[...] = unpack(own_ref, got_ref, gy).astype(bf16)
        copies[0].start()
        scaled, _ = norm_parts(x_ref[...].astype(f32))
        normed_ref[...] = (scaled * vec_ref[0:1, :] + vec_ref[1:2, :]).astype(bf16)
        copies[1].start()

        def project(i, carry):
            cols = pl.ds(pl.multiple_of(256 * i, 256), 256)
            for kind, row in ((0, 2), (1, None), (2, 3)):
                part = dot(normed_ref[...], w_ref[kind, :, cols])
                if row is not None:
                    part = part + vec_ref[row : row + 1, cols]
                qkv_ref[kind, :, cols] = part.astype(bf16)
            return carry

        lax.fori_loop(0, 3, project, 0)
        copies[2].start()

    @pl.when(step > 0)
    def _():
        cols = pl.ds(pl.multiple_of(128 * (step - 1), 128), 128)
        lane = iota((PAD, 128), 1)
        key_live = iota((PAD, PAD), 0) < SEQ
        for image in range(IMAGES):
            rows = pl.ds(PAD * image, PAD)
            q = qkv_ref[0, rows, cols] * jnp.asarray(0.125, bf16)
            k = qkv_ref[1, rows, cols]
            v = qkv_ref[2, rows, cols]
            total = None
            for n in range(2):
                inside = (lane < HD) == (n == 0)
                scores = dot_lanes(k, jnp.where(inside, q, jnp.zeros_like(q)))
                scores = jnp.where(key_live, scores, -1e30)
                terms = jnp.exp(scores - jnp.max(scores, axis=0, keepdims=True))
                soft = terms * (1.0 / jnp.sum(terms, axis=0, keepdims=True))
                soft = soft.astype(bf16)
                soft_out[0, 2 * image + n] = soft
                part = dot_rows(soft, jnp.where(inside, v, jnp.zeros_like(v)))
                total = part if total is None else total + part
            mixed_out[rows, :] = total.astype(bf16)

    @pl.when(step == 6)
    def _():
        for copy in copies:
            copy.wait()


def gelu_parts(v):
    e = jnp.exp(-0.5 * v * v)
    t = 1.0 / (1.0 + 0.23164188758 * jnp.abs(v))
    tail = ((((1.061405429 * t - 1.453152027) * t + 1.421413741) * t - 0.284496736) * t + 0.254829592) * t
    tail = 0.5 * tail * e
    below = jnp.where(v < 0.0, tail, 1.0 - tail)
    return v * below, below + v * e * 0.3989422804014327


def gather_rows(first, last):
    return jnp.concatenate([first.astype(f32), last.astype(f32)], axis=0).astype(bf16)


def place_rows(w2, ff_ref):
    for d in range(2):
        for g in range(8):
            for y in range(2):
                piece = ff_ref[d, g, y]
                rows = slice(96 * g + 48 * d, 96 * g + 48 * d + 48)
                w2[rows, HALF * y : HALF * y + HALF] = gather_rows(piece[:, :HALF], piece[:, HALF:])


def expand_kernel(
    me_ref, live_ref, own_ref, got_ref, vec_ref, bias_ref, x_ref, mixed_ref, wo_ref, w1_ref,
    act_out, slope_out, mine_out, theirs_out, w1_out, up_out, middle_out, second_out,
    up_ref, second_ref, total,
):
    step = pl.program_id(0)
    me, gy = me_ref[0], me_ref[1]

    @pl.when(step == 0)
    def _():
        up = unpack(own_ref, got_ref, gy)
        image = jnp.where(iota((ROWS, 1), 0) < PAD, live_ref[0], live_ref[1])
        up_ref[...] = jnp.where(image == 1, up, 0.0).astype(bf16)
        up_out[...] = up_ref[...]
        middle = x_ref[...].astype(f32) + dot(mixed_ref[...], wo_ref[...]) + vec_ref[4:5, :]
        middle_out[...] = middle
        scaled, _ = norm_parts(middle)
        second_ref[...] = (scaled * vec_ref[5:6, :] + vec_ref[6:7, :]).astype(bf16)
        second_out[...] = second_ref[...]

    for pair in range(16):
        w1_out[48 * pair : 48 * pair + 48, :] = gather_rows(
            w1_ref[0, 2 * pair, 0], w1_ref[0, 2 * pair + 1, 0]
        )

    for i in range(3):
        cols = slice(256 * i, 256 * i + 256)
        inner = dot(second_ref[...], w1_out[:, cols]) + bias_ref[:, cols]
        act, slope = gelu_parts(inner)
        act = act.astype(bf16)
        act_out[:, cols] = act
        slope_out[:, cols] = slope.astype(bf16)
        total[cols, :] = dot_rows(act, up_ref[...]).astype(bf16)

    for g in range(8):
        for ref, place in ((mine_out, me), (theirs_out, 1 - me)):
            part = total[pl.ds(pl.multiple_of(96 * g + 48 * place, 16), 48), :]
            for y in range(2):
                ref[y, g] = part[:, HALF * y : HALF * y + HALF]


def contract_kernel(
    me_ref, up_ref, slope_ref, second_ref, ff_ref,
    grad_out, hidden_out, mine_out, theirs_out,
    turned, w2,
):
    step = pl.program_id(0)
    me = me_ref[0]

    @pl.when(step == 0)
    def _():
        turned[...] = second_ref[...].T

    place_rows(w2, ff_ref)
    for i in range(3):
        cols = slice(256 * i, 256 * i + 256)
        grad = dot_lanes(up_ref[...], w2[cols, :]) * slope_ref[:, cols].astype(f32)
        grad = grad.astype(bf16)
        grad_out[:, cols] = grad
        hidden_out[:, cols] = jnp.sum(grad.astype(f32), axis=0, keepdims=True)

    def outer(ref):
        for i in range(3):
            cols = slice(256 * i, 256 * i + 256)
            ref[0, :, cols] = dot(turned[...], grad_out[:, cols]).astype(bf16)

    pl.when((step & 1) == me)(lambda: outer(mine_out))
    pl.when((step & 1) != me)(lambda: outer(theirs_out))


def middle_back_kernel(
    me_ref, vec_ref, up_ref, middle_ref, wo_ref, inner_ref, w1_ref, normed_ref, qkv_ref, soft_ref, mixed_ref,
    mine_out, theirs_out, grads_out, gm_out, sums_out,
    grad_second, gml, grad_mixed, normed_turned, mixed_turned,
):
    step = pl.program_id(0)
    me = me_ref[0]

    @pl.when(step == 0)
    def _():
        grad_second[...] = dot_lanes(inner_ref[...], w1_ref[...])

    @pl.when((step > 0) & (step < 4))
    def _():
        grad_second[...] += dot_lanes(inner_ref[...], w1_ref[...])

    @pl.when(step == 3)
    def _():
        grad = grad_second[...]
        scaled, scale = norm_parts(middle_ref[...])
        up = up_ref[...].astype(f32)
        gm = up + norm_back(grad, scaled, scale, vec_ref[5:6, :])
        gm_out[...] = gm
        gml[...] = gm.astype(bf16)
        sums_out[2:3, :] = jnp.sum(gml[...].astype(f32), axis=0, keepdims=True)
        sums_out[3:4, :] = jnp.sum(grad * scaled, axis=0, keepdims=True)
        sums_out[4:5, :] = jnp.sum(grad, axis=0, keepdims=True)
        sums_out[5:6, :] = jnp.sum(up, axis=0, keepdims=True)
        grad_mixed[...] = dot_lanes(gml[...], wo_ref[...]).astype(bf16)
        normed_turned[...] = normed_ref[...].T
        mixed_turned[...] = mixed_ref[...].T

    @pl.when((step > 3) & (step < 10))
    def _():
        cols = pl.ds(pl.multiple_of(128 * (step - 4), 128), 128)
        lane = iota((PAD, 128), 1)
        for image in range(IMAGES):
            rows = pl.ds(PAD * image, PAD)
            q = qkv_ref[0, rows, cols]
            k = qkv_ref[1, rows, cols]
            v = qkv_ref[2, rows, cols]
            g = grad_mixed[rows, cols]
            dq = dk = dv = jnp.zeros((PAD, 128), f32)
            for n in range(2):
                inside = (lane < HD) == (n == 0)
                zero = jnp.zeros_like(g)
                g_in = jnp.where(inside, g, zero)
                soft_low = soft_ref[0, 2 * image + n]
                soft = soft_low.astype(f32)
                grad_soft = dot_lanes(v, g_in)
                level = jnp.sum(grad_soft * soft, axis=0, keepdims=True)
                scores = (soft * (grad_soft - level)).astype(bf16)
                dv = dv + dot(soft_low, g_in)
                dk = dk + dot(scores, jnp.where(inside, q, zero))
                dq = dq + dot_rows(scores, jnp.where(inside, k, zero))
            grads_out[0, rows, cols] = (dq * 0.125).astype(bf16)
            grads_out[1, rows, cols] = (dk * 0.125).astype(bf16)
            grads_out[2, rows, cols] = dv.astype(bf16)

    @pl.when(step >= 10)
    def _():
        cols = pl.ds(pl.multiple_of(HALF * (step - 10), 128), HALF)
        for kind in range(4):
            left = mixed_turned if kind == 3 else normed_turned
            right = gml[:, cols] if kind == 3 else grads_out[kind, :, cols]
            grad = dot(left[...], right).astype(bf16)
            to = slice(HALF * (kind % 2), HALF * (kind % 2) + HALF)

            def store(ref, grad=grad, to=to):
                ref[0, :, to] = grad

            pl.when(me == kind // 2)(lambda store=store: store(mine_out))
            pl.when(me != kind // 2)(lambda store=store: store(theirs_out))
        sums_out[0:1, cols] = jnp.sum(grads_out[0, :, cols].astype(f32), axis=0, keepdims=True)
        sums_out[1:2, cols] = jnp.sum(grads_out[2, :, cols].astype(f32), axis=0, keepdims=True)


def input_back_kernel(me_ref, vec_ref, grads_ref, w_ref, x_ref, gm_ref, keep_out, send_out, sums_out):
    gy = me_ref[1]
    grad = dot_lanes(grads_ref[0], w_ref[0])
    grad = grad + dot_lanes(grads_ref[1], w_ref[1])
    grad = grad + dot_lanes(grads_ref[2], w_ref[2])
    scaled, scale = norm_parts(x_ref[...].astype(f32))
    out = gm_ref[...] + norm_back(grad, scaled, scale, vec_ref[0:1, :])
    pack(out.astype(bf16), gy, keep_out, send_out)
    sums_out[0:1, :] = jnp.sum(grad * scaled, axis=0, keepdims=True)
    sums_out[1:2, :] = jnp.sum(grad, axis=0, keepdims=True)


def output_kernel(me_ref, vec_ref, middle_ref, act_ref, ff_ref, keep_out, send_out, w2, total):
    step = pl.program_id(0)
    place_rows(w2, ff_ref)
    part = dot(act_ref[...], w2[...])

    @pl.when(step == 0)
    def _():
        total[...] = middle_ref[...] + vec_ref[7:8, :] + part

    @pl.when(step > 0)
    def _():
        total[...] += part

    @pl.when(step == 3)
    def _():
        pack(total[...].astype(bf16), me_ref[1], keep_out, send_out)


def assemble_kernel(at_ref, *refs):
    out = refs[-1]
    step = pl.program_id(0)
    for r in range(4):
        pl.when(step == r)(lambda r=r: out.__setitem__(..., refs[r][...].reshape(out.shape)))


def blocks_sum_kernel(at_ref, *refs):
    ins, outs = refs[:-4], refs[-4:]
    step = pl.program_id(0)
    total = ins[0][...].astype(f32)
    for ref in ins[1:]:
        total = total + ref[...].astype(f32)
    total = total.astype(bf16)
    for r in range(4):
        pl.when(step == r)(lambda r=r: outs[r].__setitem__(..., total.reshape(outs[r].shape)))


def adamw_step(parameter, gradient, first_moment, second_moment, step_rate, decay_factor):
    first_new = beta_first * first_moment + (1.0 - beta_first) * gradient
    second_new = beta_second * second_moment + (1.0 - beta_second) * gradient * gradient
    first_hat = first_new / (1.0 - beta_first**STEP)
    second_hat = second_new / (1.0 - beta_second**STEP)
    updated = parameter - step_rate * (
        first_hat / (jnp.sqrt(second_hat) + adam_eps) + decay_factor * parameter
    )
    return second_new, updated


def ordered(me, own, got):
    return jnp.where(me == 0, own, got), jnp.where(me == 0, got, own)


def attention_step_kernel(me_ref, own_ref, got_ref, w_ref, m_ref, v_ref, grad_out, second_out, new_out):
    pieces = ordered(me_ref[0], own_ref[...], got_ref[...])
    l = iota((512, 512), 0)
    c = iota((512, 512), 1)
    pick = jnp.where(c == 4 * (l & 127) + (l >> 7), 1.0, 0.0)
    for b in range(3):
        kinds = [
            pieces[k // 2][:, HALF * (k % 2) + 128 * b : HALF * (k % 2) + 128 * b + 128]
            for k in range(4)
        ]
        grad_out[:, 512 * b : 512 * b + 512] = jnp.dot(
            jnp.concatenate(kinds, axis=1), pick, precision=lax.Precision.HIGHEST,
            preferred_element_type=f32,
        )
    second_out[...], new_out[...] = adamw_step(
        w_ref[...], grad_out[...], m_ref[...], v_ref[...], learn_rate, decay_rate
    )


def expand_step_kernel(me_ref, own_ref, got_ref, w_ref, m_ref, v_ref, grad_out, second_out, new_out):
    first, last = ordered(me_ref[0], own_ref[...], got_ref[...])
    grad_out[:, :D] = first
    grad_out[:, D:] = last
    second_out[...], new_out[...] = adamw_step(
        w_ref[...], grad_out[...], m_ref[...], v_ref[...], learn_rate, decay_rate
    )


def project_step_kernel(me_ref, own_ref, got_ref, w_ref, m_ref, v_ref, grad_out, second_out, new_out):
    first, last = ordered(me_ref[0], own_ref[...], got_ref[...])
    grad_out[...] = jnp.concatenate([first, last], axis=0).T
    second_out[...], new_out[...] = adamw_step(
        w_ref[...], grad_out[...], m_ref[...], v_ref[...], learn_rate, decay_rate
    )


def place(axes):
    at = 0
    for a in axes:
        at = at * lax.axis_size(a) + lax.axis_index(a)
    return at


def swap(x, axis):
    return lax.ppermute(x, axis, [(0, 1), (1, 0)])


def core_sum(mine, theirs):
    return (mine.astype(f32) + swap(theirs, "dp").astype(f32)).astype(bf16)


def assemble(parts, at, shape, piece, index, after=(), cost=0):
    flat = tuple(n for n in piece if n > 1)
    return pl.pallas_call(
        assemble_kernel,
        out_shape=jax.ShapeDtypeStruct(shape, bf16),
        grid_spec=pltpu.PrefetchScalarGridSpec(
            num_scalar_prefetch=1,
            grid=(4,),
            in_specs=[
                *(pl.BlockSpec(flat, lambda r, at: (0,) * len(flat)) for _ in range(4)),
                *(LEFT for _ in after),
            ],
            out_specs=pl.BlockSpec(piece, lambda r, at: index((at[0] + 3 * r) % 4)),
        ),
        compiler_params=pltpu.CompilerParams(vmem_limit_bytes=32 * 1024 * 1024),
        cost_estimate=pl.CostEstimate(flops=cost * 10**9 + 1000, bytes_accessed=0, transcendentals=0),
        name="assemble",
    )(at.reshape(1).astype(jnp.int32), *(p.reshape(flat) for p in parts), *after)


def ring_blocks(parts, at, shape, piece, index):
    spec = pl.BlockSpec(piece, lambda r, at: index((at[0] + r) % 4))
    flat = tuple(n for n in piece if n > 1)
    return pl.pallas_call(
        blocks_sum_kernel,
        out_shape=[jax.ShapeDtypeStruct(flat, bf16)] * 4,
        grid_spec=pltpu.PrefetchScalarGridSpec(
            num_scalar_prefetch=1,
            grid=(4,),
            in_specs=[spec] * len(parts),
            out_specs=[pl.BlockSpec(flat, lambda r, at: (0,) * len(flat))] * 4,
        ),
        compiler_params=pltpu.CompilerParams(vmem_limit_bytes=32 * 1024 * 1024),
        cost_estimate=pl.CostEstimate(flops=1000, bytes_accessed=0, transcendentals=0),
        name="ring_blocks",
    )(at.reshape(1).astype(jnp.int32), *(p.reshape(shape) for p in parts))


def hop(x, axes, r):
    return lax.ppermute(x, axes, [(i, (i + r) % 4) for i in range(4)])


def ring(blocks, axes):
    return blocks[0], *(hop(blocks[r], axes, r) for r in (1, 3, 2))


def crossed(x, axis, bit):
    return lax.ppermute(x, axis, [(i, i ^ bit) for i in range(lax.axis_size(axis))])


def to_all(x, axes):
    near, back = hop(x, axes, 1), hop(x, axes, 3)
    return x, near, hop(x, axes, 2), back


def sum_of(parts):
    total = parts[0].astype(f32)
    for part in parts[1:]:
        total = total + part.astype(f32)
    return total


def spread_sum(blocks, axes):
    tiles = lax.all_to_all(blocks, axes, 0, 0, tiled=True)
    return jnp.sum(tiles.astype(f32), axis=0)


def own_images(stored, gy):
    rows = stored.shape[0] // 2
    own = lax.dynamic_slice_in_dim(stored, rows * gy, rows, 0)
    other = lax.dynamic_slice_in_dim(stored, rows * (1 - gy), rows, 0)
    pad = ((0, PAD - rows), (0, 0))
    return jnp.pad(own, pad), jnp.pad(other, pad)


def stored_rows(keep, got, gy):
    first = jnp.where(gy == 0, keep, got)[:SEQ]
    last = jnp.where(gy == 0, got, keep)[:SEQ]
    return jnp.concatenate([first, last], axis=0).astype(f32)


def per_device(
    tokens,
    image_counts,
    slot_order,
    cotangent,
    attention_weights,
    attention_first,
    attention_second,
    expand_weight,
    expand_first,
    expand_second,
    project_weight,
    project_first,
    project_second,
    vectors,
    vector_first,
    vector_second,
):
    dp = lax.axis_index("dp")
    gy = lax.axis_index("xl")
    me = jnp.stack([dp, gy]).astype(jnp.int32)

    attn_piece, ff_piece = call(
        prepare_kernel,
        [SCALARS, WHOLE, WHOLE, WHOLE],
        [((24, D), bf16, WHOLE), ((24, 2 * D), bf16, WHOLE)],
        (me, attention_weights, expand_weight, project_weight),
        name="prepare",
    )
    ff = lax.all_gather(ff_piece, EVERY).reshape(2, 32, 2, 24, 2 * D)
    at_x, at_y, at_z = place(X), place(Y), place(Z)

    def across_x(p):
        return p % 2, 0, p // 2, 0, 0

    attn = assemble(to_all(attn_piece, X), at_x, (2, 1, 2, 24, D), (1, 1, 1, 24, D), across_x)
    attn = attn.reshape(2, 48, D)
    attn = assemble(to_all(attn, Y), at_y, (2, 4, 48, D), (2, 1, 48, D), lambda p: (0, p, 0, 0))
    attn = attn.reshape(2, 192, D)
    attn = assemble(to_all(attn, Z), at_z, (2, 4, 192, D), (2, 1, 192, D), lambda p: (0, p, 0, 0))
    w_own, w_got = (w.reshape(2, D, D) for w in (attn, swap(attn, "dp")))

    token_own, token_other = own_images(tokens, gy)
    token_got = swap(token_other, "xl")
    grad_own, grad_other = own_images(cotangent, gy)
    grad_got = swap(grad_other, "xl")
    vec_first, vec_last = ordered(gy, vectors, swap(vectors, "xl"))
    vec = jnp.concatenate([vec_first, vec_last], axis=1)
    bias = vec[8:].T.reshape(1, FF)
    live = (slot_order[0] < image_counts[0]).astype(jnp.int32)
    live = lax.dynamic_slice_in_dim(live, IMAGES * gy, IMAGES)

    tall = block((ROWS, D), lambda j: (0, 0))
    wide = block((ROWS, D), lambda j: (0, j))
    w1_block = block((1, 32, 1, 24, D), lambda j: (j % 2, 0, j // 2, 0, 0))
    w2_block = block((2, 8, 2, 24, D), lambda j: (0, j, 0, 0, 1))
    pieces2 = block((2, 8, 48, HALF), lambda j: (0, j, 0, 0))
    soft_shape = (6, 2 * IMAGES, PAD, PAD)

    soft, mixed, x, normed, qkv, w_qkv, w_o = call(
        attend_kernel,
        [SCALARS, *(WHOLE,) * 5],
        [
            (soft_shape, bf16, block((1, *soft_shape[1:]), lambda p: (jnp.maximum(p - 1, 0), 0, 0, 0))),
            ((ROWS, D), bf16, block((ROWS, 128), lambda p: (0, jnp.maximum(p - 1, 0)))),
            ((ROWS, D), bf16, LEFT),
            ((ROWS, D), bf16, LEFT),
            ((3, ROWS, D), bf16, LEFT),
            ((3, D, D), bf16, LEFT),
            ((D, D), bf16, LEFT),
        ],
        (me, token_own, token_got, vec, w_own, w_got),
        grid=(7,),
        scratch=[
            pltpu.VMEM((ROWS, D), bf16),
            pltpu.VMEM((ROWS, D), bf16),
            pltpu.VMEM((3, ROWS, D), bf16),
            pltpu.VMEM((4, D, D), bf16),
            pltpu.SemaphoreType.DMA((5,)),
        ],
        name="attend",
    )

    act, slope, mine2, theirs2, w1, up, middle, second = call(
        expand_kernel,
        [SCALARS, SCALARS, WHOLE, WHOLE, WHOLE, block((1, D), lambda j: (0, j)), WHOLE, WHOLE, WHOLE, w1_block],
        [
            ((ROWS, FF), bf16, wide),
            ((ROWS, FF), bf16, wide),
            ((2, 32, 48, HALF), bf16, pieces2),
            ((2, 32, 48, HALF), bf16, pieces2),
            ((D, FF), bf16, block((D, D), lambda j: (0, j))),
            ((ROWS, D), bf16, tall),
            ((ROWS, D), f32, tall),
            ((ROWS, D), bf16, tall),
        ],
        (me, live, grad_own, grad_got, vec, bias, x, mixed, w_o, ff),
        grid=(4,),
        scratch=[pltpu.VMEM((ROWS, D), bf16), pltpu.VMEM((ROWS, D), bf16), pltpu.VMEM((D, D), bf16)],
        name="expand",
    )
    inner_grad, hidden_sums, mine1, theirs1 = call(
        contract_kernel,
        [SCALARS, WHOLE, wide, WHOLE, w2_block],
        [
            ((ROWS, FF), bf16, wide),
            ((1, FF), f32, block((1, D), lambda j: (0, j))),
            ((2, D, D), bf16, block((1, D, D), lambda j: (j // 2, 0, 0))),
            ((2, D, D), bf16, block((1, D, D), lambda j: (j // 2, 0, 0))),
        ],
        (me, up, slope, second, ff),
        grid=(4,),
        scratch=[pltpu.VMEM((D, ROWS), bf16), pltpu.VMEM((D, D), bf16)],
        name="contract",
    )
    ring2 = ring_blocks(
        (mine2, swap(theirs2, "dp")),
        place(X),
        (2, 16, 2, 48, HALF),
        (1, 16, 1, 48, HALF),
        lambda p: (p % 2, 0, p // 2, 0, 0),
    )
    got1, _ = lax.optimization_barrier((swap(theirs1, "dp"), ring2[0]))
    ring1 = ring_blocks(
        (mine1, got1), place(Y), (8, 4, 48, D), (8, 1, 48, D), lambda p: (0, p, 0, 0)
    )

    mine0, theirs0, grads, gm, sums_c = call(
        middle_back_kernel,
        [
            SCALARS, WHOLE, WHOLE, WHOLE, WHOLE,
            block((ROWS, D), lambda p: (0, jnp.minimum(p, 3))),
            block((D, D), lambda p: (0, jnp.minimum(p, 3))),
            WHOLE, WHOLE,
            block((1, *soft_shape[1:]), lambda p: (jnp.clip(p - 4, 0, 5), 0, 0, 0)),
            WHOLE,
        ],
        [
            ((2, D, D), bf16, block((1, D, D), lambda p: (jnp.maximum(p - 10, 0), 0, 0))),
            ((2, D, D), bf16, block((1, D, D), lambda p: (jnp.maximum(p - 10, 0), 0, 0))),
            ((3, ROWS, D), bf16, block((3, ROWS, D), lambda p: (0, 0, 0))),
            ((ROWS, D), f32, tall),
            ((6, D), f32, block((6, D), lambda p: (0, 0))),
        ],
        (me, vec, up, middle, w_o, inner_grad, w1, normed, qkv, soft, mixed),
        grid=(12,),
        scratch=[
            pltpu.VMEM((ROWS, D), f32),
            pltpu.VMEM((ROWS, D), bf16),
            pltpu.VMEM((ROWS, D), bf16),
            pltpu.VMEM((D, ROWS), bf16),
            pltpu.VMEM((D, ROWS), bf16),
        ],
        after=(ring2[0], ring1[0]),
        name="middle_back",
    )
    got0 = swap(theirs0, "dp")
    ring2 = ring(ring2, X)
    near1 = hop(ring1[1], Y, 1), hop(ring1[3], Y, 3)
    grads, mine0, ring2, near1, far1 = lax.optimization_barrier((grads, mine0, ring2, near1, ring1[2]))
    far1 = hop(far1, Y, 2)
    part2 = sum_of(ring2).astype(bf16)
    tiles2 = lax.all_to_all(part2, Z + Y, 0, 0, tiled=True)

    keep_in, send_in, sums_e = call(
        input_back_kernel,
        [SCALARS, *(WHOLE,) * 5],
        [((PAD, D), bf16, WHOLE), ((PAD, D), bf16, WHOLE), ((2, D), f32, WHOLE)],
        (me, vec, grads, w_qkv, x, gm),
        cost=100,
        after=(part2,),
        name="input_back",
    )
    mine0, got0, sums_e = lax.optimization_barrier((mine0, got0, sums_e))
    vector = jnp.concatenate([sums_e, sums_c, hidden_sums.reshape(D, 4).T], axis=0)
    vector_got = swap(vector, "dp")
    ring0 = ring_blocks(
        (mine0, got0), place(Z), (2, 4, 192, D), (2, 1, 192, D), lambda p: (0, p, 0, 0)
    )
    tiles2, far1, vector_got, _ = lax.optimization_barrier((tiles2, far1, vector_got, ring0[0]))
    ring0 = ring(ring0, Z)
    part1 = sum_of((ring1[0], *near1, far1)).astype(bf16).reshape(16, 24, D)
    part1, vector, vector_got = lax.optimization_barrier((part1, vector, vector_got))
    tiles1 = lax.all_to_all(part1, ("xl", "z", "xh"), 0, 0, tiled=True)
    vector = vector + vector_got
    vector_got = crossed(vector, "xl", 1)
    sum2 = jnp.sum(tiles2.astype(f32), axis=0)
    got2 = swap(sum2, "dp")
    vector_got, _ = lax.optimization_barrier((vector_got, sum2))
    vector = vector + vector_got
    vector_got = crossed(vector, "xh", 1)
    keep_out, send_out = call(
        output_kernel,
        [SCALARS, WHOLE, WHOLE, wide, w2_block],
        [((PAD, D), bf16, block((PAD, D), lambda j: (0, 0)))] * 2,
        (me, vec, middle, act, ff),
        grid=(4,),
        scratch=[pltpu.VMEM((D, D), bf16), pltpu.VMEM((ROWS, D), f32)],
        after=(vector,),
        cost=0,
        name="output",
    )
    vector_got, _ = lax.optimization_barrier((vector_got, keep_out))
    vector = vector + vector_got
    vector_got = crossed(vector, "y", 1)
    tiles1, vector_got = lax.optimization_barrier((tiles1, vector_got))
    vector = vector + vector_got
    vector_got = crossed(vector, "y", 2)
    ring0, tiles1, vector = lax.optimization_barrier((ring0, tiles1, vector))
    part0 = sum_of(ring0).astype(bf16).reshape(16, 24, D)
    tiles0 = lax.all_to_all(part0, ("xl", "y", "xh"), 0, 0, tiled=True)
    part0, tiles1, vector_got = lax.optimization_barrier((part0, tiles1, vector_got))
    vector = vector + vector_got
    vector_got = crossed(vector, "z", 1)
    sum1 = jnp.sum(tiles1.astype(f32), axis=0)
    got1 = swap(sum1, "dp")
    vector = vector + vector_got
    vector = vector + crossed(vector, "z", 2)
    sum0 = jnp.sum(tiles0.astype(f32), axis=0)
    got0 = swap(sum0, "dp")
    block_out = stored_rows(keep_out, swap(send_out, "xl"), gy)
    input_grad = stored_rows(keep_in, swap(send_in, "xl"), gy)

    vector_grad = lax.dynamic_slice_in_dim(vector, HALF * gy, HALF, 1)
    vector_second_new, vector_new = adamw_step(
        vectors, vector_grad, vector_first, vector_second, vector_rate, 0.0
    )

    def step(body, own, got, shape, parameter, first, second_moment, name):
        return call(
            body,
            [SCALARS, *(WHOLE,) * 5],
            [(shape, f32, WHOLE)] * 3,
            (me, own, got, parameter, first, second_moment),
            cost=0,
            name=name,
        )

    project = step(
        project_step_kernel, sum2, got2, (HALF, 96), project_weight, project_first, project_second, "project_step"
    )
    expand = step(
        expand_step_kernel, sum1, got1, (24, 2 * D), expand_weight, expand_first, expand_second, "expand_step"
    )
    attention = step(
        attention_step_kernel, sum0, got0, (24, 2 * D), attention_weights, attention_first, attention_second, "attention_step"
    )
    return (
        block_out,
        input_grad,
        *attention,
        *expand,
        *project,
        vector_grad,
        vector_second_new,
        vector_new,
    )


def solution(mesh):
    fine = Mesh(mesh.devices.reshape(2, 4, 4, 2, 2), EVERY)
    rows = ("dp", "z", "y", "xh")
    deep = ("z", "y", "xh")
    placed = (
        P(rows, "xl"),
        P("dp"),
        P("dp", deep),
        P(rows, "xl"),
        *(P(deep, "xl"),) * 6,
        *(P("xl", deep),) * 3,
        *(P(None, "xl"),) * 3,
    )
    out = (
        P(rows, "xl"),
        P(rows, "xl"),
        *(P(deep, "xl"),) * 6,
        *(P("xl", deep),) * 3,
        *(P(None, "xl"),) * 3,
    )
    return jax.shard_map(per_device, mesh=fine, in_specs=placed, out_specs=out, check_vma=False)
```

```python
import jax
import jax.numpy as jnp
from jax import lax
from jax.experimental import pallas as pl
from jax.experimental.pallas import tpu as pltpu
from jax.sharding import Mesh
from jax.sharding import PartitionSpec as P

D = 768
HD = 64
FF = 3072
SEQ = 197
STEP = 10
PAD = 208
IMAGES = 2
ROWS = PAD * IMAGES
HALF = D // 2

norm_eps = 1e-06
beta_first = 0.9
beta_second = 0.999
learn_rate = 0.04
vector_rate = 0.25
decay_rate = 0.05
adam_eps = 1e-08

f32 = jnp.float32
bf16 = jnp.bfloat16

DP = ("dp",)
Z = ("z",)
Y = ("y",)
X = ("xh", "xl")
CHIPS = ("xl", "z", "y", "xh")
EVERY = ("dp", "z", "y", "xh", "xl")


def dot(a, b):
    return lax.dot_general(a, b, (((1,), (0,)), ((), ())), preferred_element_type=f32)


def dot_rows(a, b):
    return lax.dot_general(a, b, (((0,), (0,)), ((), ())), preferred_element_type=f32)


def dot_lanes(a, b):
    return lax.dot_general(a, b, (((1,), (1,)), ((), ())), preferred_element_type=f32)


def block(shape, index):
    return pl.BlockSpec(shape, index)


WHOLE = pl.BlockSpec(memory_space=pltpu.VMEM)
SCALARS = pl.BlockSpec(memory_space=pltpu.SMEM)
LEFT = pl.BlockSpec(memory_space=pl.ANY)


def call(body, ins, outs, args, grid=(), scratch=(), after=(), cost=10, name=None):
    count = len(args)

    def run(*refs):
        body(*refs[:count], *refs[count + len(after) :])

    return pl.pallas_call(
        run if after else body,
        out_shape=[jax.ShapeDtypeStruct(s, t) for s, t, _ in outs],
        grid=grid,
        in_specs=[*ins, *(LEFT for _ in after)],
        out_specs=[spec for _, _, spec in outs],
        scratch_shapes=list(scratch),
        compiler_params=pltpu.CompilerParams(vmem_limit_bytes=52 * 1024 * 1024),
        cost_estimate=pl.CostEstimate(flops=cost * 10**9 + 1000, bytes_accessed=0, transcendentals=0),
        name=name,
    )(*args, *after)


def iota(shape, dim):
    return lax.broadcasted_iota(jnp.int32, shape, dim)


def row_picks():
    r = iota((ROWS, PAD), 0)
    j = iota((ROWS, PAD), 1)
    second = r >= PAD
    s = jnp.where(second, r - PAD, r)
    t = jnp.where(second, s + SEQ, s)
    live = s < SEQ
    even = jnp.where(live & (t == 2 * j), 1.0, 0.0).astype(bf16)
    odd = jnp.where(live & (t == 2 * j + 1), 1.0, 0.0).astype(bf16)
    return even, odd


def row_picks_back():
    r = iota((PAD, ROWS), 1)
    j = iota((PAD, ROWS), 0)
    second = r >= PAD
    s = jnp.where(second, r - PAD, r)
    t = jnp.where(second, s + SEQ, s)
    live = s < SEQ
    even = jnp.where(live & (t == 2 * j), 1.0, 0.0).astype(bf16)
    odd = jnp.where(live & (t == 2 * j + 1), 1.0, 0.0).astype(bf16)
    return even, odd


def lane_split():
    l = iota((256, 256), 0)
    c = iota((256, 256), 1)
    target = jnp.where(c < 128, 2 * c, 2 * (c - 128) + 1)
    return jnp.where(l == target, 1.0, 0.0).astype(bf16)


def lane_join():
    l = iota((256, 256), 1)
    c = iota((256, 256), 0)
    target = jnp.where(c < 128, 2 * c, 2 * (c - 128) + 1)
    return jnp.where(l == target, 1.0, 0.0).astype(bf16)


def unpack(own_ref, got_ref, gy):
    own, got = own_ref[...], got_ref[...]
    first = jnp.where(gy == 0, own.astype(f32), got.astype(f32)).astype(bf16)
    last = jnp.where(gy == 0, got.astype(f32), own.astype(f32)).astype(bf16)
    split = lane_split()
    evens, odds = [], []
    for half in (first, last):
        for b in range(3):
            both = dot(half[:, 256 * b : 256 * b + 256], split).astype(bf16)
            evens.append(both[:, :128])
            odds.append(both[:, 128:])
    even_rows, odd_rows = row_picks()
    return dot(even_rows, jnp.concatenate(evens, axis=1)) + dot(odd_rows, jnp.concatenate(odds, axis=1))


def pack(rows_low, gy, keep_ref, send_ref):
    even_rows, odd_rows = row_picks_back()
    even = dot(even_rows, rows_low).astype(bf16)
    odd = dot(odd_rows, rows_low).astype(bf16)
    join = lane_join()
    for b in range(3):
        blocks = []
        for half in range(2):
            at = HALF * half + 128 * b
            both = jnp.concatenate([even[:, at : at + 128], odd[:, at : at + 128]], axis=1)
            blocks.append(dot(both, join))
        keep_ref[:, 256 * b : 256 * b + 256] = jnp.where(gy == 0, blocks[0], blocks[1]).astype(bf16)
        send_ref[:, 256 * b : 256 * b + 256] = jnp.where(gy == 0, blocks[1], blocks[0]).astype(bf16)


def norm_parts(v):
    center = jnp.mean(v, axis=1, keepdims=True)
    away = v - center
    scale = lax.rsqrt(jnp.mean(away * away, axis=1, keepdims=True) + norm_eps)
    return away * scale, scale


def norm_back(grad, scaled, scale, gain):
    pushed = grad * gain
    first = jnp.mean(pushed, axis=1, keepdims=True)
    cross = jnp.mean(pushed * scaled, axis=1, keepdims=True)
    return (pushed - first - scaled * cross) * scale


def prepare_kernel(me_ref, attn_ref, expand_ref, project_ref, attn_out, ff_out):
    me = me_ref[0]
    l = iota((512, 256), 0)
    c = iota((512, 256), 1)
    kind = 2 * me + jnp.where(c < 128, 0, 1)
    pick = jnp.where(l == 4 * (c & 127) + kind, 1.0, 0.0).astype(bf16)
    for b in range(3):
        both = dot(attn_ref[:, 512 * b : 512 * b + 512].astype(bf16), pick).astype(bf16)
        attn_out[:, 128 * b : 128 * b + 128] = both[:, :128]
        attn_out[:, HALF + 128 * b : HALF + 128 * b + 128] = both[:, 128:]
    ff_out[:, :D] = jnp.where(me == 0, expand_ref[:, :D], expand_ref[:, D:]).astype(bf16)
    turned = project_ref[...].T
    mine = jnp.where(me == 0, turned[:48], turned[48:])
    ff_out[:, D : D + HALF] = mine[:24].astype(bf16)
    ff_out[:, D + HALF :] = mine[24:].astype(bf16)


def attend_kernel(
    me_ref, own_ref, got_ref, vec_ref, w_own, w_got,
    soft_out, mixed_out, x_out, normed_out, qkv_out, w_out, wo_out,
    x_ref, normed_ref, qkv_ref, w_ref, sems,
):
    step = pl.program_id(0)
    copies = [
        pltpu.make_async_copy(x_ref, x_out, sems.at[0]),
        pltpu.make_async_copy(normed_ref, normed_out, sems.at[1]),
        pltpu.make_async_copy(qkv_ref, qkv_out, sems.at[2]),
        pltpu.make_async_copy(w_ref.at[pl.ds(0, 3)], w_out, sems.at[3]),
        pltpu.make_async_copy(w_ref.at[3], wo_out, sems.at[4]),
    ]

    @pl.when(step == 0)
    def _():
        me, gy = me_ref[0], me_ref[1]
        for ref, place in ((w_own, me), (w_got, 1 - me)):
            for half in range(2):
                for y in range(2):
                    w_ref[pl.ds(2 * place + half, 1), :, HALF * y : HALF * y + HALF] = ref[
                        y, :, HALF * half : HALF * half + HALF
                    ][None]
        copies[3].start()
        copies[4].start()
        x_ref[...] = unpack(own_ref, got_ref, gy).astype(bf16)
        copies[0].start()
        scaled, _ = norm_parts(x_ref[...].astype(f32))
        normed_ref[...] = (scaled * vec_ref[0:1, :] + vec_ref[1:2, :]).astype(bf16)
        copies[1].start()

        def project(i, carry):
            cols = pl.ds(pl.multiple_of(256 * i, 256), 256)
            for kind, row in ((0, 2), (1, None), (2, 3)):
                part = dot(normed_ref[...], w_ref[kind, :, cols])
                if row is not None:
                    part = part + vec_ref[row : row + 1, cols]
                qkv_ref[kind, :, cols] = part.astype(bf16)
            return carry

        lax.fori_loop(0, 3, project, 0)
        copies[2].start()

    @pl.when(step > 0)
    def _():
        cols = pl.ds(pl.multiple_of(128 * (step - 1), 128), 128)
        lane = iota((PAD, 128), 1)
        key_live = iota((PAD, PAD), 0) < SEQ
        for image in range(IMAGES):
            rows = pl.ds(PAD * image, PAD)
            q = qkv_ref[0, rows, cols] * jnp.asarray(0.125, bf16)
            k = qkv_ref[1, rows, cols]
            v = qkv_ref[2, rows, cols]
            total = None
            for n in range(2):
                inside = (lane < HD) == (n == 0)
                scores = dot_lanes(k, jnp.where(inside, q, jnp.zeros_like(q)))
                scores = jnp.where(key_live, scores, -1e30)
                terms = jnp.exp(scores - jnp.max(scores, axis=0, keepdims=True))
                soft = terms * (1.0 / jnp.sum(terms, axis=0, keepdims=True))
                soft = soft.astype(bf16)
                soft_out[0, 2 * image + n] = soft
                part = dot_rows(soft, jnp.where(inside, v, jnp.zeros_like(v)))
                total = part if total is None else total + part
            mixed_out[rows, :] = total.astype(bf16)

    @pl.when(step == 6)
    def _():
        for copy in copies:
            copy.wait()


def gelu_parts(v):
    below = 0.5 + 0.5 * lax.erf(v * 0.7071067811865476)
    return v * below, below + v * jnp.exp(-0.5 * v * v) * 0.3989422804014327


def gather_rows(first, last):
    return jnp.concatenate([first.astype(f32), last.astype(f32)], axis=0).astype(bf16)


def place_rows(w2, ff_ref):
    for d in range(2):
        for g in range(8):
            for y in range(2):
                piece = ff_ref[d, g, y]
                rows = slice(96 * g + 48 * d, 96 * g + 48 * d + 48)
                w2[rows, HALF * y : HALF * y + HALF] = gather_rows(piece[:, :HALF], piece[:, HALF:])


def second_kernel(
    me_ref, live_ref, own_ref, got_ref, vec_ref, x_ref, mixed_ref, wo_ref,
    up_out, middle_out, second_out,
):
    up = unpack(own_ref, got_ref, me_ref[1])
    image = jnp.where(iota((ROWS, 1), 0) < PAD, live_ref[0], live_ref[1])
    up_out[...] = jnp.where(image == 1, up, 0.0).astype(bf16)
    middle = x_ref[...].astype(f32) + dot(mixed_ref[...], wo_ref[...]) + vec_ref[4:5, :]
    middle_out[...] = middle
    scaled, _ = norm_parts(middle)
    second_out[...] = (scaled * vec_ref[5:6, :] + vec_ref[6:7, :]).astype(bf16)


def expand_kernel(
    me_ref, up_ref, second_ref, bias_ref, w1_ref,
    act_out, slope_out, mine_out, theirs_out, w1_out,
    total,
):
    me = me_ref[0]
    for pair in range(16):
        w1_out[48 * pair : 48 * pair + 48, :] = gather_rows(
            w1_ref[0, 2 * pair, 0], w1_ref[0, 2 * pair + 1, 0]
        )

    for i in range(3):
        cols = slice(256 * i, 256 * i + 256)
        inner = dot(second_ref[...], w1_out[:, cols]) + bias_ref[:, cols]
        act, slope = gelu_parts(inner)
        act = act.astype(bf16)
        act_out[:, cols] = act
        slope_out[:, cols] = slope.astype(bf16)
        total[cols, :] = dot_rows(act, up_ref[...]).astype(bf16)

    for g in range(8):
        for ref, place in ((mine_out, me), (theirs_out, 1 - me)):
            part = total[pl.ds(pl.multiple_of(96 * g + 48 * place, 16), 48), :]
            for y in range(2):
                ref[y, g] = part[:, HALF * y : HALF * y + HALF]


def contract_kernel(
    me_ref, up_ref, slope_ref, second_ref, ff_ref,
    grad_out, hidden_out, mine_out, theirs_out,
    turned, w2,
):
    step = pl.program_id(0)
    me = me_ref[0]

    @pl.when(step == 0)
    def _():
        turned[...] = second_ref[...].T

    place_rows(w2, ff_ref)
    for i in range(3):
        cols = slice(256 * i, 256 * i + 256)
        grad = dot_lanes(up_ref[...], w2[cols, :]) * slope_ref[:, cols].astype(f32)
        grad = grad.astype(bf16)
        grad_out[:, cols] = grad
        hidden_out[:, cols] = jnp.sum(grad.astype(f32), axis=0, keepdims=True)

    def outer(ref):
        for i in range(3):
            cols = slice(256 * i, 256 * i + 256)
            ref[0, :, cols] = dot(turned[...], grad_out[:, cols]).astype(bf16)

    pl.when((step & 1) == me)(lambda: outer(mine_out))
    pl.when((step & 1) != me)(lambda: outer(theirs_out))


def middle_back_kernel(
    me_ref, vec_ref, up_ref, middle_ref, wo_ref, inner_ref, w1_ref, normed_ref, qkv_ref, soft_ref, mixed_ref,
    mine_out, theirs_out, grads_out, gm_out, sums_out,
    grad_second, gml, grad_mixed, normed_turned, mixed_turned,
):
    step = pl.program_id(0)
    me = me_ref[0]

    @pl.when(step == 0)
    def _():
        grad_second[...] = dot_lanes(inner_ref[...], w1_ref[...])

    @pl.when((step > 0) & (step < 4))
    def _():
        grad_second[...] += dot_lanes(inner_ref[...], w1_ref[...])

    @pl.when(step == 3)
    def _():
        grad = grad_second[...]
        scaled, scale = norm_parts(middle_ref[...])
        up = up_ref[...].astype(f32)
        gm = up + norm_back(grad, scaled, scale, vec_ref[5:6, :])
        gm_out[...] = gm
        gml[...] = gm.astype(bf16)
        sums_out[2:3, :] = jnp.sum(gml[...].astype(f32), axis=0, keepdims=True)
        sums_out[3:4, :] = jnp.sum(grad * scaled, axis=0, keepdims=True)
        sums_out[4:5, :] = jnp.sum(grad, axis=0, keepdims=True)
        sums_out[5:6, :] = jnp.sum(up, axis=0, keepdims=True)
        grad_mixed[...] = dot_lanes(gml[...], wo_ref[...]).astype(bf16)
        normed_turned[...] = normed_ref[...].T
        mixed_turned[...] = mixed_ref[...].T

    @pl.when((step > 3) & (step < 10))
    def _():
        cols = pl.ds(pl.multiple_of(128 * (step - 4), 128), 128)
        lane = iota((PAD, 128), 1)
        for image in range(IMAGES):
            rows = pl.ds(PAD * image, PAD)
            q = qkv_ref[0, rows, cols]
            k = qkv_ref[1, rows, cols]
            v = qkv_ref[2, rows, cols]
            g = grad_mixed[rows, cols]
            dq = dk = dv = jnp.zeros((PAD, 128), f32)
            for n in range(2):
                inside = (lane < HD) == (n == 0)
                zero = jnp.zeros_like(g)
                g_in = jnp.where(inside, g, zero)
                soft_low = soft_ref[0, 2 * image + n]
                soft = soft_low.astype(f32)
                grad_soft = dot_lanes(v, g_in)
                level = jnp.sum(grad_soft * soft, axis=0, keepdims=True)
                scores = (soft * (grad_soft - level)).astype(bf16)
                dv = dv + dot(soft_low, g_in)
                dk = dk + dot(scores, jnp.where(inside, q, zero))
                dq = dq + dot_rows(scores, jnp.where(inside, k, zero))
            grads_out[0, rows, cols] = (dq * 0.125).astype(bf16)
            grads_out[1, rows, cols] = (dk * 0.125).astype(bf16)
            grads_out[2, rows, cols] = dv.astype(bf16)

    @pl.when(step >= 10)
    def _():
        cols = pl.ds(pl.multiple_of(HALF * (step - 10), 128), HALF)
        for kind in range(4):
            left = mixed_turned if kind == 3 else normed_turned
            right = gml[:, cols] if kind == 3 else grads_out[kind, :, cols]
            grad = dot(left[...], right).astype(bf16)
            to = slice(HALF * (kind % 2), HALF * (kind % 2) + HALF)

            def store(ref, grad=grad, to=to):
                ref[0, :, to] = grad

            pl.when(me == kind // 2)(lambda store=store: store(mine_out))
            pl.when(me != kind // 2)(lambda store=store: store(theirs_out))
        sums_out[0:1, cols] = jnp.sum(grads_out[0, :, cols].astype(f32), axis=0, keepdims=True)
        sums_out[1:2, cols] = jnp.sum(grads_out[2, :, cols].astype(f32), axis=0, keepdims=True)


def input_back_kernel(me_ref, vec_ref, grads_ref, w_ref, x_ref, gm_ref, keep_out, send_out, sums_out):
    gy = me_ref[1]
    grad = dot_lanes(grads_ref[0], w_ref[0])
    grad = grad + dot_lanes(grads_ref[1], w_ref[1])
    grad = grad + dot_lanes(grads_ref[2], w_ref[2])
    scaled, scale = norm_parts(x_ref[...].astype(f32))
    out = gm_ref[...] + norm_back(grad, scaled, scale, vec_ref[0:1, :])
    pack(out.astype(bf16), gy, keep_out, send_out)
    sums_out[0:1, :] = jnp.sum(grad * scaled, axis=0, keepdims=True)
    sums_out[1:2, :] = jnp.sum(grad, axis=0, keepdims=True)


def output_kernel(me_ref, vec_ref, middle_ref, act_ref, ff_ref, keep_out, send_out, w2, total):
    step = pl.program_id(0)
    place_rows(w2, ff_ref)
    part = dot(act_ref[...], w2[...])

    @pl.when(step == 0)
    def _():
        total[...] = middle_ref[...] + vec_ref[7:8, :] + part

    @pl.when(step > 0)
    def _():
        total[...] += part

    @pl.when(step == 3)
    def _():
        pack(total[...].astype(bf16), me_ref[1], keep_out, send_out)


def assemble_kernel(at_ref, *refs):
    out = refs[-1]
    step = pl.program_id(0)
    for r in range(4):
        pl.when(step == r)(lambda r=r: out.__setitem__(..., refs[r][...].reshape(out.shape)))


def blocks_sum_kernel(at_ref, *refs):
    ins, outs = refs[:-4], refs[-4:]
    step = pl.program_id(0)
    total = ins[0][...].astype(f32)
    for ref in ins[1:]:
        total = total + ref[...].astype(f32)
    total = total.astype(bf16)
    for r in range(4):
        pl.when(step == r)(lambda r=r: outs[r].__setitem__(..., total.reshape(outs[r].shape)))


def sum_kernel(a_ref, b_ref, c_ref, d_ref, out_ref):
    total = a_ref[...].astype(f32) + b_ref[...].astype(f32) + c_ref[...].astype(f32) + d_ref[...].astype(f32)
    out_ref[...] = total.astype(bf16)


def last_spread_kernel(a_ref, b_ref, c_ref, d_ref, va_ref, vb_ref, vc_ref, vd_ref, out_ref):
    vector = va_ref[...].astype(f32) + vb_ref[...].astype(f32) + vc_ref[...].astype(f32) + vd_ref[...].astype(f32)
    vector = vector.astype(bf16)
    total = a_ref[...].astype(f32) + b_ref[...].astype(f32) + c_ref[...].astype(f32) + d_ref[...].astype(f32)
    total = total.reshape(2 * 192, D)
    for i in range(16):
        out_ref[i, :16, :] = vector
        out_ref[i, 16:, :] = total[24 * i : 24 * i + 24].astype(bf16)


def adamw_step(parameter, gradient, first_moment, second_moment, step_rate, decay_factor):
    first_new = beta_first * first_moment + (1.0 - beta_first) * gradient
    second_new = beta_second * second_moment + (1.0 - beta_second) * gradient * gradient
    first_hat = first_new / (1.0 - beta_first**STEP)
    second_hat = second_new / (1.0 - beta_second**STEP)
    updated = parameter - step_rate * (
        first_hat / (jnp.sqrt(second_hat) + adam_eps) + decay_factor * parameter
    )
    return second_new, updated


def ordered(me, own, got):
    return jnp.where(me == 0, own, got), jnp.where(me == 0, got, own)


def attention_step_kernel(
    me_ref, own_ref, got_ref, w_ref, m_ref, v_ref, vec_ref, vec_m_ref, vec_v_ref,
    grad_out, second_out, new_out, vec_grad_out, vec_second_out, vec_new_out,
):
    pieces = ordered(me_ref[0], own_ref[16:, :], got_ref[16:, :])
    l = iota((512, 512), 0)
    c = iota((512, 512), 1)
    pick = jnp.where(c == 4 * (l & 127) + (l >> 7), 1.0, 0.0)
    for b in range(3):
        kinds = [
            pieces[k // 2][:, HALF * (k % 2) + 128 * b : HALF * (k % 2) + 128 * b + 128]
            for k in range(4)
        ]
        grad_out[:, 512 * b : 512 * b + 512] = jnp.dot(
            jnp.concatenate(kinds, axis=1), pick, precision=lax.Precision.HIGHEST,
            preferred_element_type=f32,
        )
    second_out[...], new_out[...] = adamw_step(
        w_ref[...], grad_out[...], m_ref[...], v_ref[...], learn_rate, decay_rate
    )
    vector = own_ref[:12, :] + got_ref[:12, :]
    vec_grad_out[...] = jnp.where(me_ref[1] == 0, vector[:, :HALF], vector[:, HALF:])
    vec_second_out[...], vec_new_out[...] = adamw_step(
        vec_ref[...], vec_grad_out[...], vec_m_ref[...], vec_v_ref[...], vector_rate, 0.0
    )


def expand_step_kernel(me_ref, own_ref, got_ref, w_ref, m_ref, v_ref, grad_out, second_out, new_out):
    first, last = ordered(me_ref[0], own_ref[...], got_ref[...])
    grad_out[:, :D] = first
    grad_out[:, D:] = last
    second_out[...], new_out[...] = adamw_step(
        w_ref[...], grad_out[...], m_ref[...], v_ref[...], learn_rate, decay_rate
    )


def project_step_kernel(me_ref, own_ref, got_ref, w_ref, m_ref, v_ref, grad_out, second_out, new_out):
    first, last = ordered(me_ref[0], own_ref[...], got_ref[...])
    grad_out[...] = jnp.concatenate([first, last], axis=0).T
    second_out[...], new_out[...] = adamw_step(
        w_ref[...], grad_out[...], m_ref[...], v_ref[...], learn_rate, decay_rate
    )


def place(axes):
    at = 0
    for a in axes:
        at = at * lax.axis_size(a) + lax.axis_index(a)
    return at


def swap(x, axis):
    return lax.ppermute(x, axis, [(0, 1), (1, 0)])


def core_sum(mine, theirs):
    return (mine.astype(f32) + swap(theirs, "dp").astype(f32)).astype(bf16)


def assemble(parts, at, shape, piece, index, after=(), cost=0):
    flat = tuple(n for n in piece if n > 1)
    return pl.pallas_call(
        assemble_kernel,
        out_shape=jax.ShapeDtypeStruct(shape, bf16),
        grid_spec=pltpu.PrefetchScalarGridSpec(
            num_scalar_prefetch=1,
            grid=(4,),
            in_specs=[
                *(pl.BlockSpec(flat, lambda r, at: (0,) * len(flat)) for _ in range(4)),
                *(LEFT for _ in after),
            ],
            out_specs=pl.BlockSpec(piece, lambda r, at: index((at[0] + 3 * r) % 4)),
        ),
        compiler_params=pltpu.CompilerParams(vmem_limit_bytes=32 * 1024 * 1024),
        cost_estimate=pl.CostEstimate(flops=cost * 10**9 + 1000, bytes_accessed=0, transcendentals=0),
        name="assemble",
    )(at.reshape(1).astype(jnp.int32), *(p.reshape(flat) for p in parts), *after)


def ring_blocks(parts, at, shape, piece, index):
    spec = pl.BlockSpec(piece, lambda r, at: index((at[0] + r) % 4))
    flat = tuple(n for n in piece if n > 1)
    return pl.pallas_call(
        blocks_sum_kernel,
        out_shape=[jax.ShapeDtypeStruct(flat, bf16)] * 4,
        grid_spec=pltpu.PrefetchScalarGridSpec(
            num_scalar_prefetch=1,
            grid=(4,),
            in_specs=[spec] * len(parts),
            out_specs=[pl.BlockSpec(flat, lambda r, at: (0,) * len(flat))] * 4,
        ),
        compiler_params=pltpu.CompilerParams(vmem_limit_bytes=32 * 1024 * 1024),
        cost_estimate=pl.CostEstimate(flops=1000, bytes_accessed=0, transcendentals=0),
        name="ring_blocks",
    )(at.reshape(1).astype(jnp.int32), *(p.reshape(shape) for p in parts))


def hop(x, axes, r):
    return lax.ppermute(x, axes, [(i, (i + r) % 4) for i in range(4)])


def ring(blocks, axes):
    return blocks[0], *(hop(blocks[r], axes, r) for r in (1, 3, 2))


def crossed(x, axis, bit):
    return lax.ppermute(x, axis, [(i, i ^ bit) for i in range(lax.axis_size(axis))])


def to_all(x, axes):
    near, back = hop(x, axes, 1), hop(x, axes, 3)
    return x, near, hop(x, axes, 2), back


def sum_of(parts):
    total = parts[0].astype(f32)
    for part in parts[1:]:
        total = total + part.astype(f32)
    return total


def spread_sum(blocks, axes):
    tiles = lax.all_to_all(blocks, axes, 0, 0, tiled=True)
    return jnp.sum(tiles.astype(f32), axis=0)


def own_images(stored, gy):
    rows = stored.shape[0] // 2
    own = lax.dynamic_slice_in_dim(stored, rows * gy, rows, 0)
    other = lax.dynamic_slice_in_dim(stored, rows * (1 - gy), rows, 0)
    pad = ((0, PAD - rows), (0, 0))
    return jnp.pad(own, pad), jnp.pad(other, pad)


def stored_rows(keep, got, gy):
    first = jnp.where(gy == 0, keep, got)[:SEQ]
    last = jnp.where(gy == 0, got, keep)[:SEQ]
    return jnp.concatenate([first, last], axis=0).astype(f32)


def per_device(
    tokens,
    image_counts,
    slot_order,
    cotangent,
    attention_weights,
    attention_first,
    attention_second,
    expand_weight,
    expand_first,
    expand_second,
    project_weight,
    project_first,
    project_second,
    vectors,
    vector_first,
    vector_second,
):
    dp = lax.axis_index("dp")
    gy = lax.axis_index("xl")
    me = jnp.stack([dp, gy]).astype(jnp.int32)

    token_own, token_other = own_images(tokens, gy)
    token_got = swap(token_other, "xl")
    grad_own, grad_other = own_images(cotangent, gy)
    grad_got = swap(grad_other, "xl")
    vec_got = swap(vectors, "xl")
    attn_piece, ff_piece = call(
        prepare_kernel,
        [SCALARS, WHOLE, WHOLE, WHOLE],
        [((24, D), bf16, WHOLE), ((24, 2 * D), bf16, WHOLE)],
        (me, attention_weights, expand_weight, project_weight),
        name="prepare",
    )
    ff = lax.all_gather(ff_piece, EVERY).reshape(2, 32, 2, 24, 2 * D)
    at_x, at_y, at_z = place(X), place(Y), place(Z)

    def across_x(p):
        return p % 2, 0, p // 2, 0, 0

    attn = to_all(attn_piece, X)
    attn = assemble(attn, at_x, (2, 1, 2, 24, D), (1, 1, 1, 24, D), across_x)
    attn = to_all(attn.reshape(2, 48, D), Y)
    attn, token_got, vec_got = lax.optimization_barrier((attn, token_got, vec_got))
    attn = assemble(attn, at_y, (2, 4, 48, D), (2, 1, 48, D), lambda p: (0, p, 0, 0))
    vec_first, vec_last = ordered(gy, vectors, vec_got)
    vec = jnp.concatenate([vec_first, vec_last], axis=1)
    bias = vec[8:].T.reshape(1, FF)
    live = (slot_order[0] < image_counts[0]).astype(jnp.int32)
    live = lax.dynamic_slice_in_dim(live, IMAGES * gy, IMAGES)
    attn = to_all(attn.reshape(2, 192, D), Z)
    attn, vec, bias, live, token_own, token_got = lax.optimization_barrier(
        (attn, vec, bias, live, token_own, token_got)
    )
    attn = assemble(attn, at_z, (2, 4, 192, D), (2, 1, 192, D), lambda p: (0, p, 0, 0))
    w_own, w_got = (w.reshape(2, D, D) for w in (attn, swap(attn, "dp")))

    tall = block((ROWS, D), lambda j: (0, 0))
    wide = block((ROWS, D), lambda j: (0, j))
    w1_block = block((1, 32, 1, 24, D), lambda j: (j % 2, 0, j // 2, 0, 0))
    w2_block = block((2, 8, 2, 24, D), lambda j: (0, j, 0, 0, 1))
    pieces2 = block((2, 8, 48, HALF), lambda j: (0, j, 0, 0))
    soft_shape = (6, 2 * IMAGES, PAD, PAD)

    soft, mixed, x, normed, qkv, w_qkv, w_o = call(
        attend_kernel,
        [SCALARS, *(WHOLE,) * 5],
        [
            (soft_shape, bf16, block((1, *soft_shape[1:]), lambda p: (jnp.maximum(p - 1, 0), 0, 0, 0))),
            ((ROWS, D), bf16, block((ROWS, 128), lambda p: (0, jnp.maximum(p - 1, 0)))),
            ((ROWS, D), bf16, LEFT),
            ((ROWS, D), bf16, LEFT),
            ((3, ROWS, D), bf16, LEFT),
            ((3, D, D), bf16, LEFT),
            ((D, D), bf16, LEFT),
        ],
        (me, token_own, token_got, vec, w_own, w_got),
        grid=(7,),
        scratch=[
            pltpu.VMEM((ROWS, D), bf16),
            pltpu.VMEM((ROWS, D), bf16),
            pltpu.VMEM((3, ROWS, D), bf16),
            pltpu.VMEM((4, D, D), bf16),
            pltpu.SemaphoreType.DMA((5,)),
        ],
        name="attend",
    )

    up, middle, second = call(
        second_kernel,
        [SCALARS, SCALARS, *(WHOLE,) * 6],
        [((ROWS, D), bf16, WHOLE), ((ROWS, D), f32, WHOLE), ((ROWS, D), bf16, WHOLE)],
        (me, live, grad_own, grad_got, vec, x, mixed, w_o),
        name="second",
    )
    act, slope, mine2, theirs2, w1 = call(
        expand_kernel,
        [SCALARS, WHOLE, WHOLE, block((1, D), lambda j: (0, j)), w1_block],
        [
            ((ROWS, FF), bf16, wide),
            ((ROWS, FF), bf16, wide),
            ((2, 32, 48, HALF), bf16, pieces2),
            ((2, 32, 48, HALF), bf16, pieces2),
            ((D, FF), bf16, block((D, D), lambda j: (0, j))),
        ],
        (me, up, second, bias, ff),
        grid=(4,),
        scratch=[pltpu.VMEM((D, D), bf16)],
        after=(w_o, soft),
        name="expand",
    )
    inner_grad, hidden_sums, mine1, theirs1 = call(
        contract_kernel,
        [SCALARS, WHOLE, wide, WHOLE, w2_block],
        [
            ((ROWS, FF), bf16, wide),
            ((1, FF), f32, block((1, D), lambda j: (0, j))),
            ((2, D, D), bf16, block((1, D, D), lambda j: (j // 2, 0, 0))),
            ((2, D, D), bf16, block((1, D, D), lambda j: (j // 2, 0, 0))),
        ],
        (me, up, slope, second, ff),
        grid=(4,),
        scratch=[pltpu.VMEM((D, ROWS), bf16), pltpu.VMEM((D, D), bf16)],
        name="contract",
    )
    ring2 = ring_blocks(
        (mine2, swap(theirs2, "dp")),
        place(X),
        (2, 16, 2, 48, HALF),
        (1, 16, 1, 48, HALF),
        lambda p: (p % 2, 0, p // 2, 0, 0),
    )
    got1, _ = lax.optimization_barrier((swap(theirs1, "dp"), ring2[0]))
    ring1 = ring_blocks(
        (mine1, got1), place(Y), (8, 4, 48, D), (8, 1, 48, D), lambda p: (0, p, 0, 0)
    )

    mine0, theirs0, grads, gm, sums_c = call(
        middle_back_kernel,
        [
            SCALARS, WHOLE, WHOLE, WHOLE, WHOLE,
            block((ROWS, D), lambda p: (0, jnp.minimum(p, 3))),
            block((D, D), lambda p: (0, jnp.minimum(p, 3))),
            WHOLE, WHOLE,
            block((1, *soft_shape[1:]), lambda p: (jnp.clip(p - 4, 0, 5), 0, 0, 0)),
            WHOLE,
        ],
        [
            ((2, D, D), bf16, block((1, D, D), lambda p: (jnp.maximum(p - 10, 0), 0, 0))),
            ((2, D, D), bf16, block((1, D, D), lambda p: (jnp.maximum(p - 10, 0), 0, 0))),
            ((3, ROWS, D), bf16, block((3, ROWS, D), lambda p: (0, 0, 0))),
            ((ROWS, D), f32, tall),
            ((6, D), f32, block((6, D), lambda p: (0, 0))),
        ],
        (me, vec, up, middle, w_o, inner_grad, w1, normed, qkv, soft, mixed),
        grid=(12,),
        scratch=[
            pltpu.VMEM((ROWS, D), f32),
            pltpu.VMEM((ROWS, D), bf16),
            pltpu.VMEM((ROWS, D), bf16),
            pltpu.VMEM((D, ROWS), bf16),
            pltpu.VMEM((D, ROWS), bf16),
        ],
        after=(ring2[0], ring1[0]),
        name="middle_back",
    )
    got0 = swap(theirs0, "dp")
    ring2 = ring(ring2, X)
    near1 = hop(ring1[1], Y, 1), hop(ring1[3], Y, 3)
    mine0, ring2, near1, far1 = lax.optimization_barrier((mine0, ring2, near1, ring1[2]))
    far1 = hop(far1, Y, 2)
    part2 = call(
        sum_kernel, [WHOLE] * 4, [((16, 48, HALF), bf16, WHOLE)], ring2, cost=100, name="part"
    )[0]
    tiles2 = lax.all_to_all(part2, Z + Y, 0, 0, tiled=True)
    mine0, got0, _ = lax.optimization_barrier((mine0, got0, part2))
    ring0 = ring_blocks(
        (mine0, got0), place(Z), (2, 4, 192, D), (2, 1, 192, D), lambda p: (0, p, 0, 0)
    )
    tiles2, far1, _ = lax.optimization_barrier((tiles2, far1, ring0[0]))
    own0, near0, back0, far0 = ring(ring0, Z)
    keep_out, send_out = call(
        output_kernel,
        [SCALARS, WHOLE, WHOLE, wide, w2_block],
        [((PAD, D), bf16, block((PAD, D), lambda j: (0, 0)))] * 2,
        (me, vec, middle, act, ff),
        grid=(4,),
        scratch=[pltpu.VMEM((D, D), bf16), pltpu.VMEM((ROWS, D), f32)],
        after=(ring0[0],),
        cost=0,
        name="output",
    )
    part1 = sum_of((ring1[0], *near1, far1)).astype(bf16).reshape(16, 24, D)
    tiles1 = lax.all_to_all(part1, ("xl", "z", "xh"), 0, 0, tiled=True)
    grads, near0, back0 = lax.optimization_barrier((grads, near0, back0))
    keep_in, send_in, sums_e = call(
        input_back_kernel,
        [SCALARS, *(WHOLE,) * 5],
        [((PAD, D), bf16, WHOLE), ((PAD, D), bf16, WHOLE), ((2, D), f32, WHOLE)],
        (me, vec, grads, w_qkv, x, gm),
        cost=100,
        after=(part1,),
        name="input_back",
    )
    sums_e, hidden_sums = lax.optimization_barrier((sums_e, hidden_sums))
    vector = jnp.concatenate(
        [sums_e, sums_c, hidden_sums.reshape(D, 4).T, jnp.zeros((4, D), f32)], axis=0
    ).astype(bf16)
    vectors4 = ring((vector,) * 4, Z)
    got_in, got_out = swap(send_in, "xl"), swap(send_out, "xl")
    tiles2, vectors4, got_in, got_out = lax.optimization_barrier((tiles2, vectors4, got_in, got_out))
    sum2 = jnp.sum(tiles2.astype(f32), axis=0)
    got2 = swap(sum2, "dp")
    part0 = call(
        last_spread_kernel,
        [WHOLE] * 8,
        [((16, 40, D), bf16, WHOLE)],
        (own0, near0, back0, far0, *vectors4),
        cost=0,
        name="last_spread",
    )[0]
    tiles0 = lax.all_to_all(part0, ("xl", "y", "xh"), 0, 0, tiled=True)
    sum1 = jnp.sum(tiles1.astype(f32), axis=0)
    got1 = swap(sum1, "dp")
    block_out = stored_rows(keep_out, got_out, gy)
    input_grad = stored_rows(keep_in, got_in, gy)

    def step(body, own, got, shape, state, outs=(), cost=0, name=None):
        state = (me, own, got, *state)
        outs = [(shape, f32, WHOLE)] * 3 + [(o, f32, WHOLE) for o in outs]
        return call(body, [SCALARS, *(WHOLE,) * (len(state) - 1)], outs, state, cost=cost, name=name)

    project = step(
        project_step_kernel, sum2, got2, (HALF, 96),
        (project_weight, project_first, project_second), name="project_step",
    )
    expand = step(
        expand_step_kernel, sum1, got1, (24, 2 * D),
        (expand_weight, expand_first, expand_second), name="expand_step",
    )
    tiles0, block_out, input_grad, project, expand = lax.optimization_barrier(
        (tiles0, block_out, input_grad, project, expand)
    )
    sum0 = jnp.sum(tiles0.astype(f32), axis=0)
    got0 = swap(sum0, "dp")
    *attention, vector_grad, vector_second_new, vector_new = step(
        attention_step_kernel, sum0, got0, (24, 2 * D),
        (attention_weights, attention_first, attention_second, vectors, vector_first, vector_second),
        [(12, HALF)] * 3, name="attention_step",
    )
    return (
        block_out,
        input_grad,
        *attention,
        *expand,
        *project,
        vector_grad,
        vector_second_new,
        vector_new,
    )


def solution(mesh):
    fine = Mesh(mesh.devices.reshape(2, 4, 4, 2, 2), EVERY)
    rows = ("dp", "z", "y", "xh")
    deep = ("z", "y", "xh")
    placed = (
        P(rows, "xl"),
        P("dp"),
        P("dp", deep),
        P(rows, "xl"),
        *(P(deep, "xl"),) * 6,
        *(P("xl", deep),) * 3,
        *(P(None, "xl"),) * 3,
    )
    out = (
        P(rows, "xl"),
        P(rows, "xl"),
        *(P(deep, "xl"),) * 6,
        *(P("xl", deep),) * 3,
        *(P(None, "xl"),) * 3,
    )
    return jax.shard_map(per_device, mesh=fine, in_specs=placed, out_specs=out, check_vma=False)
```

```python
import jax
import jax.numpy as jnp
from jax import lax
from jax.experimental import pallas as pl
from jax.experimental.pallas import tpu as pltpu
from jax.sharding import Mesh
from jax.sharding import PartitionSpec as P

D = 768
HD = 64
FF = 3072
SEQ = 197
STEP = 10
PAD = 208
IMAGES = 2
ROWS = PAD * IMAGES
HALF = D // 2

norm_eps = 1e-06
beta_first = 0.9
beta_second = 0.999
learn_rate = 0.04
vector_rate = 0.25
decay_rate = 0.05
adam_eps = 1e-08

f32 = jnp.float32
bf16 = jnp.bfloat16

DP = ("dp",)
Z = ("z",)
Y = ("y",)
X = ("xh", "xl")
CHIPS = ("xl", "z", "y", "xh")
EVERY = ("dp", "z", "y", "xh", "xl")


def dot(a, b):
    return lax.dot_general(a, b, (((1,), (0,)), ((), ())), preferred_element_type=f32)


def dot_rows(a, b):
    return lax.dot_general(a, b, (((0,), (0,)), ((), ())), preferred_element_type=f32)


def dot_lanes(a, b):
    return lax.dot_general(a, b, (((1,), (1,)), ((), ())), preferred_element_type=f32)


def block(shape, index):
    return pl.BlockSpec(shape, index)


WHOLE = pl.BlockSpec(memory_space=pltpu.VMEM)
SCALARS = pl.BlockSpec(memory_space=pltpu.SMEM)
LEFT = pl.BlockSpec(memory_space=pl.ANY)


def call(body, ins, outs, args, grid=(), scratch=(), after=(), cost=10, prefetch=0, name=None):
    count = len(args)

    def run(*refs):
        body(*refs[:count], *refs[count + len(after) :])

    return pl.pallas_call(
        run if after else body,
        out_shape=[jax.ShapeDtypeStruct(s, t) for s, t, _ in outs],
        grid_spec=pltpu.PrefetchScalarGridSpec(
            num_scalar_prefetch=prefetch,
            grid=grid,
            in_specs=[*ins, *(LEFT for _ in after)],
            out_specs=[spec for _, _, spec in outs],
            scratch_shapes=list(scratch),
        ),
        compiler_params=pltpu.CompilerParams(vmem_limit_bytes=52 * 1024 * 1024),
        cost_estimate=pl.CostEstimate(flops=cost * 10**9 + 1000, bytes_accessed=0, transcendentals=0),
        name=name,
    )(*args, *after)


def iota(shape, dim):
    return lax.broadcasted_iota(jnp.int32, shape, dim)


def row_picks():
    r = iota((ROWS, PAD), 0)
    j = iota((ROWS, PAD), 1)
    second = r >= PAD
    s = jnp.where(second, r - PAD, r)
    t = jnp.where(second, s + SEQ, s)
    live = s < SEQ
    even = jnp.where(live & (t == 2 * j), 1.0, 0.0).astype(bf16)
    odd = jnp.where(live & (t == 2 * j + 1), 1.0, 0.0).astype(bf16)
    return even, odd


def row_picks_back():
    r = iota((PAD, ROWS), 1)
    j = iota((PAD, ROWS), 0)
    second = r >= PAD
    s = jnp.where(second, r - PAD, r)
    t = jnp.where(second, s + SEQ, s)
    live = s < SEQ
    even = jnp.where(live & (t == 2 * j), 1.0, 0.0).astype(bf16)
    odd = jnp.where(live & (t == 2 * j + 1), 1.0, 0.0).astype(bf16)
    return even, odd


def lane_split():
    l = iota((256, 256), 0)
    c = iota((256, 256), 1)
    target = jnp.where(c < 128, 2 * c, 2 * (c - 128) + 1)
    return jnp.where(l == target, 1.0, 0.0).astype(bf16)


def lane_join():
    l = iota((256, 256), 1)
    c = iota((256, 256), 0)
    target = jnp.where(c < 128, 2 * c, 2 * (c - 128) + 1)
    return jnp.where(l == target, 1.0, 0.0).astype(bf16)


def unpack(own_ref, got_ref, gy):
    own, got = own_ref[...], got_ref[...]
    first = jnp.where(gy == 0, own.astype(f32), got.astype(f32)).astype(bf16)
    last = jnp.where(gy == 0, got.astype(f32), own.astype(f32)).astype(bf16)
    split = lane_split()
    evens, odds = [], []
    for half in (first, last):
        for b in range(3):
            both = dot(half[:, 256 * b : 256 * b + 256], split).astype(bf16)
            evens.append(both[:, :128])
            odds.append(both[:, 128:])
    even_rows, odd_rows = row_picks()
    return dot(even_rows, jnp.concatenate(evens, axis=1)) + dot(odd_rows, jnp.concatenate(odds, axis=1))


def pack(rows_low, gy, keep_ref, send_ref):
    even_rows, odd_rows = row_picks_back()
    even = dot(even_rows, rows_low).astype(bf16)
    odd = dot(odd_rows, rows_low).astype(bf16)
    join = lane_join()
    for b in range(3):
        blocks = []
        for half in range(2):
            at = HALF * half + 128 * b
            both = jnp.concatenate([even[:, at : at + 128], odd[:, at : at + 128]], axis=1)
            blocks.append(dot(both, join))
        keep_ref[:, 256 * b : 256 * b + 256] = jnp.where(gy == 0, blocks[0], blocks[1]).astype(bf16)
        send_ref[:, 256 * b : 256 * b + 256] = jnp.where(gy == 0, blocks[1], blocks[0]).astype(bf16)


def norm_parts(v):
    center = jnp.mean(v, axis=1, keepdims=True)
    away = v - center
    scale = lax.rsqrt(jnp.mean(away * away, axis=1, keepdims=True) + norm_eps)
    return away * scale, scale


def norm_back(grad, scaled, scale, gain):
    pushed = grad * gain
    first = jnp.mean(pushed, axis=1, keepdims=True)
    cross = jnp.mean(pushed * scaled, axis=1, keepdims=True)
    return (pushed - first - scaled * cross) * scale


def prepare_kernel(me_ref, attn_ref, expand_ref, project_ref, attn_out, ff_out):
    me = me_ref[0]
    l = iota((512, 256), 0)
    c = iota((512, 256), 1)
    kind = 2 * me + jnp.where(c < 128, 0, 1)
    pick = jnp.where(l == 4 * (c & 127) + kind, 1.0, 0.0).astype(bf16)
    for b in range(3):
        both = dot(attn_ref[:, 512 * b : 512 * b + 512].astype(bf16), pick).astype(bf16)
        attn_out[:, 128 * b : 128 * b + 128] = both[:, :128]
        attn_out[:, HALF + 128 * b : HALF + 128 * b + 128] = both[:, 128:]
    ff_out[:, :D] = jnp.where(me == 0, expand_ref[:, :D], expand_ref[:, D:]).astype(bf16)
    turned = project_ref[...].T
    mine = jnp.where(me == 0, turned[:48], turned[48:])
    ff_out[:, D : D + HALF] = mine[:24].astype(bf16)
    ff_out[:, D + HALF :] = mine[24:].astype(bf16)


def attend_kernel(
    me_ref, own_ref, got_ref, vec_ref, w_own, w_got,
    soft_out, mixed_out, x_out, normed_out, qkv_out, w_out, wo_out,
    x_ref, normed_ref, qkv_ref, w_ref, sems,
):
    step = pl.program_id(0)
    copies = [
        pltpu.make_async_copy(x_ref, x_out, sems.at[0]),
        pltpu.make_async_copy(normed_ref, normed_out, sems.at[1]),
        pltpu.make_async_copy(qkv_ref, qkv_out, sems.at[2]),
        pltpu.make_async_copy(w_ref.at[pl.ds(0, 3)], w_out, sems.at[3]),
        pltpu.make_async_copy(w_ref.at[3], wo_out, sems.at[4]),
    ]

    @pl.when(step == 0)
    def _():
        me, gy = me_ref[0], me_ref[1]
        for ref, place in ((w_own, me), (w_got, 1 - me)):
            for half in range(2):
                for y in range(2):
                    w_ref[pl.ds(2 * place + half, 1), :, HALF * y : HALF * y + HALF] = ref[
                        y, :, HALF * half : HALF * half + HALF
                    ][None]
        copies[3].start()
        copies[4].start()
        x_ref[...] = unpack(own_ref, got_ref, gy).astype(bf16)
        copies[0].start()
        scaled, _ = norm_parts(x_ref[...].astype(f32))
        normed_ref[...] = (scaled * vec_ref[0:1, :] + vec_ref[1:2, :]).astype(bf16)
        copies[1].start()

        def project(i, carry):
            cols = pl.ds(pl.multiple_of(256 * i, 256), 256)
            for kind, row in ((0, 2), (1, None), (2, 3)):
                part = dot(normed_ref[...], w_ref[kind, :, cols])
                if row is not None:
                    part = part + vec_ref[row : row + 1, cols]
                qkv_ref[kind, :, cols] = part.astype(bf16)
            return carry

        lax.fori_loop(0, 3, project, 0)
        copies[2].start()

    @pl.when(step > 0)
    def _():
        cols = pl.ds(pl.multiple_of(128 * (step - 1), 128), 128)
        lane = iota((PAD, 128), 1)
        key_live = iota((PAD, PAD), 0) < SEQ
        for image in range(IMAGES):
            rows = pl.ds(PAD * image, PAD)
            q = qkv_ref[0, rows, cols] * jnp.asarray(0.125, bf16)
            k = qkv_ref[1, rows, cols]
            v = qkv_ref[2, rows, cols]
            total = None
            for n in range(2):
                inside = (lane < HD) == (n == 0)
                scores = dot_lanes(k, jnp.where(inside, q, jnp.zeros_like(q)))
                scores = jnp.where(key_live, scores, -1e30)
                terms = jnp.exp(scores - jnp.max(scores, axis=0, keepdims=True))
                soft = terms * (1.0 / jnp.sum(terms, axis=0, keepdims=True))
                soft = soft.astype(bf16)
                soft_out[0, 2 * image + n] = soft
                part = dot_rows(soft, jnp.where(inside, v, jnp.zeros_like(v)))
                total = part if total is None else total + part
            mixed_out[rows, :] = total.astype(bf16)

    @pl.when(step == 6)
    def _():
        for copy in copies:
            copy.wait()


def gelu_parts(v):
    below = 0.5 + 0.5 * lax.erf(v * 0.7071067811865476)
    return v * below, below + v * jnp.exp(-0.5 * v * v) * 0.3989422804014327


def gather_rows(first, last):
    return jnp.concatenate([first.astype(f32), last.astype(f32)], axis=0).astype(bf16)


def place_rows(w2, ff_ref):
    for d in range(2):
        for g in range(8):
            for y in range(2):
                piece = ff_ref[d, g, y]
                rows = slice(96 * g + 48 * d, 96 * g + 48 * d + 48)
                w2[rows, HALF * y : HALF * y + HALF] = gather_rows(piece[:, :HALF], piece[:, HALF:])


def second_kernel(
    me_ref, live_ref, own_ref, got_ref, vec_ref, x_ref, mixed_ref, wo_ref,
    up_out, middle_out, second_out,
):
    up = unpack(own_ref, got_ref, me_ref[1])
    image = jnp.where(iota((ROWS, 1), 0) < PAD, live_ref[0], live_ref[1])
    up_out[...] = jnp.where(image == 1, up, 0.0).astype(bf16)
    middle = x_ref[...].astype(f32) + dot(mixed_ref[...], wo_ref[...]) + vec_ref[4:5, :]
    middle_out[...] = middle
    scaled, _ = norm_parts(middle)
    second_out[...] = (scaled * vec_ref[5:6, :] + vec_ref[6:7, :]).astype(bf16)


def expand_kernel(
    me_ref, up_ref, second_ref, bias_ref, w1_ref,
    act_out, slope_out, mine_out, theirs_out, w1_out,
    total,
):
    me = me_ref[0]
    for pair in range(16):
        w1_out[48 * pair : 48 * pair + 48, :] = gather_rows(
            w1_ref[0, 2 * pair, 0], w1_ref[0, 2 * pair + 1, 0]
        )

    for i in range(3):
        cols = slice(256 * i, 256 * i + 256)
        inner = dot(second_ref[...], w1_out[:, cols]) + bias_ref[:, cols]
        act, slope = gelu_parts(inner)
        act = act.astype(bf16)
        act_out[:, cols] = act
        slope_out[:, cols] = slope.astype(bf16)
    total[...] = dot_rows(act_out[...], up_ref[...]).astype(bf16)

    for g in range(8):
        for ref, place in ((mine_out, me), (theirs_out, 1 - me)):
            part = total[pl.ds(pl.multiple_of(96 * g + 48 * place, 16), 48), :]
            for y in range(2):
                ref[y, g] = part[:, HALF * y : HALF * y + HALF]


def contract_kernel(
    me_ref, up_ref, slope_ref, second_ref, ff_ref,
    grad_out, hidden_out, mine_out, theirs_out,
    turned, w2,
):
    step = pl.program_id(0)
    me = me_ref[0]

    @pl.when(step == 0)
    def _():
        turned[...] = second_ref[...].T

    place_rows(w2, ff_ref)
    for i in range(3):
        cols = slice(256 * i, 256 * i + 256)
        grad = dot_lanes(up_ref[...], w2[cols, :]) * slope_ref[:, cols].astype(f32)
        grad = grad.astype(bf16)
        grad_out[:, cols] = grad
        hidden_out[:, cols] = jnp.sum(grad.astype(f32), axis=0, keepdims=True)

    def outer(ref):
        for i in range(3):
            cols = slice(256 * i, 256 * i + 256)
            ref[0, :, cols] = dot(turned[...], grad_out[:, cols]).astype(bf16)

    pl.when((step & 1) == me)(lambda: outer(mine_out))
    pl.when((step & 1) != me)(lambda: outer(theirs_out))


def middle_back_kernel(
    me_ref, vec_ref, inner_hbm, w1_hbm, soft_hbm, up_hbm, middle_hbm, wo_hbm, normed_hbm, mixed_hbm, qkv_hbm,
    mine_hbm, theirs_hbm, sums_out, grads_hbm, gm_hbm,
    inner_ref, w1_ref, soft_ref, up_ref, middle_ref, wo_ref, normed_ref, mixed_ref, qkv_ref,
    grad_second, gml, grad_mixed, normed_turned, mixed_turned, pieces, grads_ref, gm_ref, sems,
):
    me = me_ref[0]
    ahead = []
    for j in range(4):
        cols = pl.ds(D * j, D)
        ahead.append((inner_hbm.at[:, cols], inner_ref.at[j]))
        ahead.append((w1_hbm.at[:, cols], w1_ref.at[j]))
    ahead += [
        (middle_hbm, middle_ref), (up_hbm, up_ref), (wo_hbm, wo_ref),
        (normed_hbm, normed_ref), (mixed_hbm, mixed_ref), (qkv_hbm, qkv_ref),
    ]
    reads = [pltpu.make_async_copy(src, dst, sems.at[i]) for i, (src, dst) in enumerate(ahead)]

    def read_soft(i):
        return pltpu.make_async_copy(soft_hbm.at[i], soft_ref.at[i], sems.at[14 + i])

    grads_write = pltpu.make_async_copy(grads_ref, grads_hbm, sems.at[20])
    gm_write = pltpu.make_async_copy(gm_ref, gm_hbm, sems.at[21])

    def write(kind, act):
        cols = pl.ds(HALF * (kind % 2), HALF)
        for to, place in ((mine_hbm, kind // 2), (theirs_hbm, 1 - kind // 2)):
            copy = pltpu.make_async_copy(pieces.at[kind], to.at[:, :, cols], sems.at[22 + kind])
            pl.when(me == place)(lambda copy=copy: act(copy))

    def outer(kind, left, right):
        grad = dot(left[...], right[...]).astype(bf16)
        for y in range(2):
            pieces[kind, y] = grad[:, HALF * y : HALF * y + HALF]
        write(kind, lambda copy: copy.start())

    for read in reads:
        read.start()
    for i in range(6):
        read_soft(i).start()
    for j in range(4):
        reads[2 * j].wait()
        reads[2 * j + 1].wait()
        part = dot_lanes(inner_ref[j], w1_ref[j])
        if j == 0:
            grad_second[...] = part
        else:
            grad_second[...] += part
    for read in reads[8:]:
        read.wait()
    grad = grad_second[...]
    scaled, scale = norm_parts(middle_ref[...])
    up = up_ref[...].astype(f32)
    gm = up + norm_back(grad, scaled, scale, vec_ref[5:6, :])
    gm_ref[...] = gm
    gm_write.start()
    gml[...] = gm.astype(bf16)
    sums_out[2:3, :] = jnp.sum(gml[...].astype(f32), axis=0, keepdims=True)
    sums_out[3:4, :] = jnp.sum(grad * scaled, axis=0, keepdims=True)
    sums_out[4:5, :] = jnp.sum(grad, axis=0, keepdims=True)
    sums_out[5:6, :] = jnp.sum(up, axis=0, keepdims=True)
    grad_mixed[...] = dot_lanes(gml[...], wo_ref[...]).astype(bf16)
    mixed_turned[...] = mixed_ref[...].T
    outer(3, mixed_turned, gml)
    normed_turned[...] = normed_ref[...].T
    lane = iota((PAD, 128), 1)

    def attend(i, carry):
        cols = pl.ds(pl.multiple_of(128 * i, 128), 128)
        read_soft(i).wait()
        for image in range(IMAGES):
            rows = pl.ds(PAD * image, PAD)
            q = qkv_ref[0, rows, cols]
            k = qkv_ref[1, rows, cols]
            v = qkv_ref[2, rows, cols]
            g = grad_mixed[rows, cols]
            dq = dk = dv = jnp.zeros((PAD, 128), f32)
            for n in range(2):
                inside = (lane < HD) == (n == 0)
                zero = jnp.zeros_like(g)
                g_in = jnp.where(inside, g, zero)
                soft_low = soft_ref[i, 2 * image + n]
                soft = soft_low.astype(f32)
                grad_soft = dot_lanes(v, g_in)
                level = jnp.sum(grad_soft * soft, axis=0, keepdims=True)
                scores = (soft * (grad_soft - level)).astype(bf16)
                dv = dv + dot(soft_low, g_in)
                dk = dk + dot(scores, jnp.where(inside, q, zero))
                dq = dq + dot_rows(scores, jnp.where(inside, k, zero))
            grads_ref[0, rows, cols] = (dq * 0.125).astype(bf16)
            grads_ref[1, rows, cols] = (dk * 0.125).astype(bf16)
            grads_ref[2, rows, cols] = dv.astype(bf16)
        return carry

    lax.fori_loop(0, 6, attend, 0)
    grads_write.start()
    for kind in range(3):
        outer(kind, normed_turned, grads_ref.at[kind])
    sums_out[0:1, :] = jnp.sum(grads_ref[0].astype(f32), axis=0, keepdims=True)
    sums_out[1:2, :] = jnp.sum(grads_ref[2].astype(f32), axis=0, keepdims=True)
    grads_write.wait()
    gm_write.wait()
    for kind in range(4):
        write(kind, lambda copy: copy.wait())


def input_back_kernel(
    me_ref, vec_ref, grads_ref, w_ref, x_ref, gm_ref, keep_out, send_out, sums_out, total
):
    step = pl.program_id(0)
    part = dot_lanes(grads_ref[0], w_ref[0])

    @pl.when(step == 0)
    def _():
        total[...] = part

    @pl.when(step > 0)
    def _():
        total[...] += part

    @pl.when(step == 2)
    def _():
        grad = total[...]
        scaled, scale = norm_parts(x_ref[...].astype(f32))
        out = gm_ref[...] + norm_back(grad, scaled, scale, vec_ref[0:1, :])
        pack(out.astype(bf16), me_ref[1], keep_out, send_out)
        sums_out[0:1, :] = jnp.sum(grad * scaled, axis=0, keepdims=True)
        sums_out[1:2, :] = jnp.sum(grad, axis=0, keepdims=True)


def output_kernel(me_ref, vec_ref, middle_ref, act_ref, ff_ref, keep_out, send_out, w2, total):
    step = pl.program_id(0)
    place_rows(w2, ff_ref)
    part = dot(act_ref[...], w2[...])

    @pl.when(step == 0)
    def _():
        total[...] = middle_ref[...] + vec_ref[7:8, :] + part

    @pl.when(step > 0)
    def _():
        total[...] += part

    @pl.when(step == 3)
    def _():
        pack(total[...].astype(bf16), me_ref[1], keep_out, send_out)


def assemble_kernel(at_ref, *refs):
    out = refs[-1]
    step = pl.program_id(0)
    for r in range(4):
        pl.when(step == r)(lambda r=r: out.__setitem__(..., refs[r][...].reshape(out.shape)))


def blocks_sum_kernel(at_ref, *refs):
    ins, outs = refs[:-4], refs[-4:]
    step = pl.program_id(0)
    total = ins[0][...].astype(f32)
    for ref in ins[1:]:
        total = total + ref[...].astype(f32)
    total = total.astype(bf16)
    for r in range(4):
        pl.when(step == r)(lambda r=r: outs[r].__setitem__(..., total.reshape(outs[r].shape)))


def sum_kernel(a_ref, b_ref, c_ref, d_ref, out_ref):
    total = a_ref[...].astype(f32) + b_ref[...].astype(f32) + c_ref[...].astype(f32) + d_ref[...].astype(f32)
    out_ref[...] = total.astype(bf16)


def last_spread_kernel(a_ref, b_ref, c_ref, d_ref, va_ref, vb_ref, vc_ref, vd_ref, out_ref):
    vector = va_ref[...].astype(f32) + vb_ref[...].astype(f32) + vc_ref[...].astype(f32) + vd_ref[...].astype(f32)
    vector = vector.astype(bf16)
    total = a_ref[...].astype(f32) + b_ref[...].astype(f32) + c_ref[...].astype(f32) + d_ref[...].astype(f32)
    total = total.reshape(2 * 192, D)
    for i in range(16):
        out_ref[i, :16, :] = vector
        out_ref[i, 16:, :] = total[24 * i : 24 * i + 24].astype(bf16)


def adamw_step(parameter, gradient, first_moment, second_moment, step_rate, decay_factor):
    first_new = beta_first * first_moment + (1.0 - beta_first) * gradient
    second_new = beta_second * second_moment + (1.0 - beta_second) * gradient * gradient
    first_hat = first_new / (1.0 - beta_first**STEP)
    second_hat = second_new / (1.0 - beta_second**STEP)
    updated = parameter - step_rate * (
        first_hat / (jnp.sqrt(second_hat) + adam_eps) + decay_factor * parameter
    )
    return second_new, updated


def ordered(me, own, got):
    return jnp.where(me == 0, own, got), jnp.where(me == 0, got, own)


def attention_step_kernel(
    me_ref, own_ref, got_ref, w_ref, m_ref, v_ref, vec_ref, vec_m_ref, vec_v_ref,
    grad_out, second_out, new_out, vec_grad_out, vec_second_out, vec_new_out,
):
    pieces = ordered(me_ref[0], own_ref[16:, :], got_ref[16:, :])
    l = iota((512, 512), 0)
    c = iota((512, 512), 1)
    pick = jnp.where(c == 4 * (l & 127) + (l >> 7), 1.0, 0.0)
    for b in range(3):
        kinds = [
            pieces[k // 2][:, HALF * (k % 2) + 128 * b : HALF * (k % 2) + 128 * b + 128]
            for k in range(4)
        ]
        grad_out[:, 512 * b : 512 * b + 512] = jnp.dot(
            jnp.concatenate(kinds, axis=1), pick, precision=lax.Precision.HIGHEST,
            preferred_element_type=f32,
        )
    second_out[...], new_out[...] = adamw_step(
        w_ref[...], grad_out[...], m_ref[...], v_ref[...], learn_rate, decay_rate
    )
    vector = own_ref[:12, :] + got_ref[:12, :]
    vec_grad_out[...] = jnp.where(me_ref[1] == 0, vector[:, :HALF], vector[:, HALF:])
    vec_second_out[...], vec_new_out[...] = adamw_step(
        vec_ref[...], vec_grad_out[...], vec_m_ref[...], vec_v_ref[...], vector_rate, 0.0
    )


def expand_step_kernel(me_ref, own_ref, got_ref, w_ref, m_ref, v_ref, grad_out, second_out, new_out):
    first, last = ordered(me_ref[0], own_ref[...], got_ref[...])
    grad_out[:, :D] = first
    grad_out[:, D:] = last
    second_out[...], new_out[...] = adamw_step(
        w_ref[...], grad_out[...], m_ref[...], v_ref[...], learn_rate, decay_rate
    )


def project_step_kernel(me_ref, own_ref, got_ref, w_ref, m_ref, v_ref, grad_out, second_out, new_out):
    first, last = ordered(me_ref[0], own_ref[...], got_ref[...])
    grad_out[...] = jnp.concatenate([first, last], axis=0).T
    second_out[...], new_out[...] = adamw_step(
        w_ref[...], grad_out[...], m_ref[...], v_ref[...], learn_rate, decay_rate
    )


def place(axes):
    at = 0
    for a in axes:
        at = at * lax.axis_size(a) + lax.axis_index(a)
    return at


def swap(x, axis):
    return lax.ppermute(x, axis, [(0, 1), (1, 0)])


def core_sum(mine, theirs):
    return (mine.astype(f32) + swap(theirs, "dp").astype(f32)).astype(bf16)


def assemble(parts, at, shape, piece, index, after=(), cost=0):
    flat = tuple(n for n in piece if n > 1)
    return pl.pallas_call(
        assemble_kernel,
        out_shape=jax.ShapeDtypeStruct(shape, bf16),
        grid_spec=pltpu.PrefetchScalarGridSpec(
            num_scalar_prefetch=1,
            grid=(4,),
            in_specs=[
                *(pl.BlockSpec(flat, lambda r, at: (0,) * len(flat)) for _ in range(4)),
                *(LEFT for _ in after),
            ],
            out_specs=pl.BlockSpec(piece, lambda r, at: index((at[0] + 3 * r) % 4)),
        ),
        compiler_params=pltpu.CompilerParams(vmem_limit_bytes=32 * 1024 * 1024),
        cost_estimate=pl.CostEstimate(flops=cost * 10**9 + 1000, bytes_accessed=0, transcendentals=0),
        name="assemble",
    )(at.reshape(1).astype(jnp.int32), *(p.reshape(flat) for p in parts), *after)


def ring_blocks(parts, at, shape, piece, index):
    spec = pl.BlockSpec(piece, lambda r, at: index((at[0] + r) % 4))
    flat = tuple(n for n in piece if n > 1)
    return pl.pallas_call(
        blocks_sum_kernel,
        out_shape=[jax.ShapeDtypeStruct(flat, bf16)] * 4,
        grid_spec=pltpu.PrefetchScalarGridSpec(
            num_scalar_prefetch=1,
            grid=(4,),
            in_specs=[spec] * len(parts),
            out_specs=[pl.BlockSpec(flat, lambda r, at: (0,) * len(flat))] * 4,
        ),
        compiler_params=pltpu.CompilerParams(vmem_limit_bytes=32 * 1024 * 1024),
        cost_estimate=pl.CostEstimate(flops=1000, bytes_accessed=0, transcendentals=0),
        name="ring_blocks",
    )(at.reshape(1).astype(jnp.int32), *(p.reshape(shape) for p in parts))


def hop(x, axes, r):
    return lax.ppermute(x, axes, [(i, (i + r) % 4) for i in range(4)])


def ring(blocks, axes):
    return blocks[0], *(hop(blocks[r], axes, r) for r in (1, 3, 2))


def crossed(x, axis, bit):
    return lax.ppermute(x, axis, [(i, i ^ bit) for i in range(lax.axis_size(axis))])


def to_all(x, axes):
    near, back = hop(x, axes, 1), hop(x, axes, 3)
    return x, near, hop(x, axes, 2), back


def sum_of(parts):
    total = parts[0].astype(f32)
    for part in parts[1:]:
        total = total + part.astype(f32)
    return total


def spread_sum(blocks, axes):
    tiles = lax.all_to_all(blocks, axes, 0, 0, tiled=True)
    return jnp.sum(tiles.astype(f32), axis=0)


def own_images(stored, gy):
    rows = stored.shape[0] // 2
    own = lax.dynamic_slice_in_dim(stored, rows * gy, rows, 0)
    other = lax.dynamic_slice_in_dim(stored, rows * (1 - gy), rows, 0)
    pad = ((0, PAD - rows), (0, 0))
    return jnp.pad(own, pad), jnp.pad(other, pad)


def stored_rows(keep, got, gy):
    first = jnp.where(gy == 0, keep, got)[:SEQ]
    last = jnp.where(gy == 0, got, keep)[:SEQ]
    return jnp.concatenate([first, last], axis=0).astype(f32)


def per_device(
    tokens,
    image_counts,
    slot_order,
    cotangent,
    attention_weights,
    attention_first,
    attention_second,
    expand_weight,
    expand_first,
    expand_second,
    project_weight,
    project_first,
    project_second,
    vectors,
    vector_first,
    vector_second,
):
    dp = lax.axis_index("dp")
    gy = lax.axis_index("xl")
    me = jnp.stack([dp, gy]).astype(jnp.int32)

    token_own, token_other = own_images(tokens, gy)
    token_got = swap(token_other, "xl")
    grad_own, grad_other = own_images(cotangent, gy)
    grad_got = swap(grad_other, "xl")
    vec_got = swap(vectors, "xl")
    attn_piece, ff_piece = call(
        prepare_kernel,
        [SCALARS, WHOLE, WHOLE, WHOLE],
        [((24, D), bf16, WHOLE), ((24, 2 * D), bf16, WHOLE)],
        (me, attention_weights, expand_weight, project_weight),
        name="prepare",
    )
    ff = lax.all_gather(ff_piece, EVERY).reshape(2, 32, 2, 24, 2 * D)
    at_x, at_y, at_z = place(X), place(Y), place(Z)

    def across_x(p):
        return p % 2, 0, p // 2, 0, 0

    attn = to_all(attn_piece, X)
    attn = assemble(attn, at_x, (2, 1, 2, 24, D), (1, 1, 1, 24, D), across_x)
    attn = to_all(attn.reshape(2, 48, D), Y)
    attn, token_got, vec_got = lax.optimization_barrier((attn, token_got, vec_got))
    attn = assemble(attn, at_y, (2, 4, 48, D), (2, 1, 48, D), lambda p: (0, p, 0, 0))
    vec_first, vec_last = ordered(gy, vectors, vec_got)
    vec = jnp.concatenate([vec_first, vec_last], axis=1)
    bias = vec[8:].T.reshape(1, FF)
    live = (slot_order[0] < image_counts[0]).astype(jnp.int32)
    live = lax.dynamic_slice_in_dim(live, IMAGES * gy, IMAGES)
    attn = to_all(attn.reshape(2, 192, D), Z)
    attn, vec, bias, live, token_own, token_got = lax.optimization_barrier(
        (attn, vec, bias, live, token_own, token_got)
    )
    attn = assemble(attn, at_z, (2, 4, 192, D), (2, 1, 192, D), lambda p: (0, p, 0, 0))
    w_own, w_got = (w.reshape(2, D, D) for w in (attn, swap(attn, "dp")))

    tall = block((ROWS, D), lambda j: (0, 0))
    wide = block((ROWS, D), lambda j: (0, j))
    w1_block = block((1, 32, 1, 24, D), lambda j: (j % 2, 0, j // 2, 0, 0))
    w2_block = block((2, 8, 2, 24, D), lambda j: (0, j, 0, 0, 1))
    pieces2 = block((2, 8, 48, HALF), lambda j: (0, j, 0, 0))
    soft_shape = (6, 2 * IMAGES, PAD, PAD)

    soft, mixed, x, normed, qkv, w_qkv, w_o = call(
        attend_kernel,
        [SCALARS, *(WHOLE,) * 5],
        [
            (soft_shape, bf16, block((1, *soft_shape[1:]), lambda p: (jnp.maximum(p - 1, 0), 0, 0, 0))),
            ((ROWS, D), bf16, block((ROWS, 128), lambda p: (0, jnp.maximum(p - 1, 0)))),
            ((ROWS, D), bf16, LEFT),
            ((ROWS, D), bf16, LEFT),
            ((3, ROWS, D), bf16, LEFT),
            ((3, D, D), bf16, LEFT),
            ((D, D), bf16, LEFT),
        ],
        (me, token_own, token_got, vec, w_own, w_got),
        grid=(7,),
        scratch=[
            pltpu.VMEM((ROWS, D), bf16),
            pltpu.VMEM((ROWS, D), bf16),
            pltpu.VMEM((3, ROWS, D), bf16),
            pltpu.VMEM((4, D, D), bf16),
            pltpu.SemaphoreType.DMA((5,)),
        ],
        name="attend",
    )

    up, middle, second = call(
        second_kernel,
        [SCALARS, SCALARS, *(WHOLE,) * 6],
        [((ROWS, D), bf16, WHOLE), ((ROWS, D), f32, WHOLE), ((ROWS, D), bf16, WHOLE)],
        (me, live, grad_own, grad_got, vec, x, mixed, w_o),
        name="second",
    )
    act, slope, mine2, theirs2, w1 = call(
        expand_kernel,
        [SCALARS, WHOLE, WHOLE, block((1, D), lambda j: (0, j)), w1_block],
        [
            ((ROWS, FF), bf16, wide),
            ((ROWS, FF), bf16, wide),
            ((2, 32, 48, HALF), bf16, pieces2),
            ((2, 32, 48, HALF), bf16, pieces2),
            ((D, FF), bf16, block((D, D), lambda j: (0, j))),
        ],
        (me, up, second, bias, ff),
        grid=(4,),
        scratch=[pltpu.VMEM((D, D), bf16)],
        after=(w_o, soft),
        name="expand",
    )
    inner_grad, hidden_sums, mine1, theirs1 = call(
        contract_kernel,
        [SCALARS, WHOLE, wide, WHOLE, w2_block],
        [
            ((ROWS, FF), bf16, wide),
            ((1, FF), f32, block((1, D), lambda j: (0, j))),
            ((2, D, D), bf16, block((1, D, D), lambda j: (j // 2, 0, 0))),
            ((2, D, D), bf16, block((1, D, D), lambda j: (j // 2, 0, 0))),
        ],
        (me, up, slope, second, ff),
        grid=(4,),
        scratch=[pltpu.VMEM((D, ROWS), bf16), pltpu.VMEM((D, D), bf16)],
        name="contract",
    )
    ring2 = ring_blocks(
        (mine2, swap(theirs2, "dp")),
        place(X),
        (2, 16, 2, 48, HALF),
        (1, 16, 1, 48, HALF),
        lambda p: (p % 2, 0, p // 2, 0, 0),
    )
    got1, _ = lax.optimization_barrier((swap(theirs1, "dp"), ring2[0]))
    ring1 = ring_blocks(
        (mine1, got1), place(Y), (8, 4, 48, D), (8, 1, 48, D), lambda p: (0, p, 0, 0)
    )

    mine0, theirs0, sums_c, grads, gm = call(
        middle_back_kernel,
        [SCALARS, WHOLE, *(LEFT,) * 9],
        [
            ((2, D, D), bf16, LEFT),
            ((2, D, D), bf16, LEFT),
            ((6, D), f32, WHOLE),
            ((3, ROWS, D), bf16, LEFT),
            ((ROWS, D), f32, LEFT),
        ],
        (me, vec, inner_grad, w1, soft, up, middle, w_o, normed, mixed, qkv),
        scratch=[
            pltpu.VMEM((4, ROWS, D), bf16),
            pltpu.VMEM((4, D, D), bf16),
            pltpu.VMEM(soft_shape, bf16),
            pltpu.VMEM((ROWS, D), bf16),
            pltpu.VMEM((ROWS, D), f32),
            pltpu.VMEM((D, D), bf16),
            pltpu.VMEM((ROWS, D), bf16),
            pltpu.VMEM((ROWS, D), bf16),
            pltpu.VMEM((3, ROWS, D), bf16),
            pltpu.VMEM((ROWS, D), f32),
            pltpu.VMEM((ROWS, D), bf16),
            pltpu.VMEM((ROWS, D), bf16),
            pltpu.VMEM((D, ROWS), bf16),
            pltpu.VMEM((D, ROWS), bf16),
            pltpu.VMEM((4, 2, D, HALF), bf16),
            pltpu.VMEM((3, ROWS, D), bf16),
            pltpu.VMEM((ROWS, D), f32),
            pltpu.SemaphoreType.DMA((26,)),
        ],
        after=(ring2[0], ring1[0]),
        cost=0,
        name="middle_back",
    )
    got0 = swap(theirs0, "dp")
    ring2 = ring(ring2, X)
    near1 = hop(ring1[1], Y, 1), hop(ring1[3], Y, 3)
    ring2, mine0 = lax.optimization_barrier((ring2, mine0))
    mine0, near1, far1 = lax.optimization_barrier((mine0, near1, ring1[2]))
    far1 = hop(far1, Y, 2)
    part2 = call(
        sum_kernel, [WHOLE] * 4, [((16, 48, HALF), bf16, WHOLE)], ring2, cost=100, after=(near1[0], near1[1]), name="part"
    )[0]
    tiles2 = lax.all_to_all(part2, Z + Y, 0, 0, tiled=True)
    mine0, got0, _ = lax.optimization_barrier((mine0, got0, part2))
    ring0 = ring_blocks(
        (mine0, got0), place(Z), (2, 4, 192, D), (2, 1, 192, D), lambda p: (0, p, 0, 0)
    )
    tiles2, far1, _ = lax.optimization_barrier((tiles2, far1, ring0[0]))
    own0, near0, back0, far0 = ring(ring0, Z)
    keep_out, send_out = call(
        output_kernel,
        [SCALARS, WHOLE, WHOLE, wide, w2_block],
        [((PAD, D), bf16, block((PAD, D), lambda j: (0, 0)))] * 2,
        (me, vec, middle, act, ff),
        grid=(4,),
        scratch=[pltpu.VMEM((D, D), bf16), pltpu.VMEM((ROWS, D), f32)],
        after=(ring0[0],),
        cost=0,
        name="output",
    )
    far1, tiles2, keep_out = lax.optimization_barrier((far1, tiles2, keep_out))
    part1 = sum_of((ring1[0], *near1, far1)).astype(bf16).reshape(16, 24, D)
    tiles1 = lax.all_to_all(part1, ("xl", "z", "xh"), 0, 0, tiled=True)
    grads, near0, back0 = lax.optimization_barrier((grads, near0, back0))
    keep_in, send_in, sums_e = call(
        input_back_kernel,
        [
            SCALARS, WHOLE,
            block((1, ROWS, D), lambda k: (k, 0, 0)), block((1, D, D), lambda k: (k, 0, 0)),
            WHOLE, WHOLE,
        ],
        [
            ((PAD, D), bf16, block((PAD, D), lambda k: (0, 0))),
            ((PAD, D), bf16, block((PAD, D), lambda k: (0, 0))),
            ((2, D), f32, block((2, D), lambda k: (0, 0))),
        ],
        (me, vec, grads, w_qkv, x, gm),
        grid=(3,),
        scratch=[pltpu.VMEM((ROWS, D), f32)],
        cost=100,
        after=(part1,),
        name="input_back",
    )
    sums_e, hidden_sums = lax.optimization_barrier((sums_e, hidden_sums))
    vector = jnp.concatenate(
        [sums_e, sums_c, hidden_sums.reshape(D, 4).T, jnp.zeros((4, D), f32)], axis=0
    ).astype(bf16)
    vectors4 = ring((vector,) * 4, Z)
    got_in, got_out = swap(send_in, "xl"), swap(send_out, "xl")
    tiles2, vectors4, got_in, got_out = lax.optimization_barrier((tiles2, vectors4, got_in, got_out))
    sum2 = jnp.sum(tiles2.astype(f32), axis=0)
    got2 = swap(sum2, "dp")
    part0 = call(
        last_spread_kernel,
        [WHOLE] * 8,
        [((16, 40, D), bf16, WHOLE)],
        (own0, near0, back0, far0, *vectors4),
        cost=0,
        name="last_spread",
    )[0]
    tiles0 = lax.all_to_all(part0, ("xl", "y", "xh"), 0, 0, tiled=True)
    sum1 = jnp.sum(tiles1.astype(f32), axis=0)
    got1 = swap(sum1, "dp")
    block_out = stored_rows(keep_out, got_out, gy)
    input_grad = stored_rows(keep_in, got_in, gy)

    def step(body, own, got, shape, state, outs=(), cost=0, name=None):
        state = (me, own, got, *state)
        outs = [(shape, f32, WHOLE)] * 3 + [(o, f32, WHOLE) for o in outs]
        return call(body, [SCALARS, *(WHOLE,) * (len(state) - 1)], outs, state, cost=cost, name=name)

    project = step(
        project_step_kernel, sum2, got2, (HALF, 96),
        (project_weight, project_first, project_second), name="project_step",
    )
    expand = step(
        expand_step_kernel, sum1, got1, (24, 2 * D),
        (expand_weight, expand_first, expand_second), name="expand_step",
    )
    tiles0, project = lax.optimization_barrier((tiles0, project))
    sum0 = jnp.sum(tiles0.astype(f32), axis=0)
    got0 = swap(sum0, "dp")
    *attention, vector_grad, vector_second_new, vector_new = step(
        attention_step_kernel, sum0, got0, (24, 2 * D),
        (attention_weights, attention_first, attention_second, vectors, vector_first, vector_second),
        [(12, HALF)] * 3, name="attention_step",
    )
    return (
        block_out,
        input_grad,
        *attention,
        *expand,
        *project,
        vector_grad,
        vector_second_new,
        vector_new,
    )


def solution(mesh):
    fine = Mesh(mesh.devices.reshape(2, 4, 4, 2, 2), EVERY)
    rows = ("dp", "z", "y", "xh")
    deep = ("z", "y", "xh")
    placed = (
        P(rows, "xl"),
        P("dp"),
        P("dp", deep),
        P(rows, "xl"),
        *(P(deep, "xl"),) * 6,
        *(P("xl", deep),) * 3,
        *(P(None, "xl"),) * 3,
    )
    out = (
        P(rows, "xl"),
        P(rows, "xl"),
        *(P(deep, "xl"),) * 6,
        *(P("xl", deep),) * 3,
        *(P(None, "xl"),) * 3,
    )
    return jax.shard_map(per_device, mesh=fine, in_specs=placed, out_specs=out, check_vma=False)
```

```python
import jax
import jax.numpy as jnp
from jax import lax
from jax.experimental import pallas as pl
from jax.experimental.pallas import tpu as pltpu
from jax.sharding import Mesh
from jax.sharding import PartitionSpec as P

D = 768
HD = 64
FF = 3072
SEQ = 197
STEP = 10
PAD = 208
IMAGES = 2
ROWS = PAD * IMAGES
HALF = D // 2

norm_eps = 1e-06
beta_first = 0.9
beta_second = 0.999
learn_rate = 0.04
vector_rate = 0.25
decay_rate = 0.05
adam_eps = 1e-08

f32 = jnp.float32
bf16 = jnp.bfloat16

DP = ("dp",)
Z = ("z",)
Y = ("y",)
X = ("xh", "xl")
CHIPS = ("xl", "z", "y", "xh")
EVERY = ("dp", "z", "y", "xh", "xl")


def dot(a, b):
    return lax.dot_general(a, b, (((1,), (0,)), ((), ())), preferred_element_type=f32)


def dot_rows(a, b):
    return lax.dot_general(a, b, (((0,), (0,)), ((), ())), preferred_element_type=f32)


def dot_lanes(a, b):
    return lax.dot_general(a, b, (((1,), (1,)), ((), ())), preferred_element_type=f32)


def block(shape, index):
    return pl.BlockSpec(shape, index)


WHOLE = pl.BlockSpec(memory_space=pltpu.VMEM)
SCALARS = pl.BlockSpec(memory_space=pltpu.SMEM)
LEFT = pl.BlockSpec(memory_space=pl.ANY)


def call(body, ins, outs, args, grid=(), scratch=(), after=(), cost=10, prefetch=0, name=None):
    count = len(args)

    def run(*refs):
        body(*refs[:count], *refs[count + len(after) :])

    return pl.pallas_call(
        run if after else body,
        out_shape=[jax.ShapeDtypeStruct(s, t) for s, t, _ in outs],
        grid_spec=pltpu.PrefetchScalarGridSpec(
            num_scalar_prefetch=prefetch,
            grid=grid,
            in_specs=[*ins, *(LEFT for _ in after)],
            out_specs=[spec for _, _, spec in outs],
            scratch_shapes=list(scratch),
        ),
        compiler_params=pltpu.CompilerParams(vmem_limit_bytes=52 * 1024 * 1024),
        cost_estimate=pl.CostEstimate(flops=cost * 10**9 + 1000, bytes_accessed=0, transcendentals=0),
        name=name,
    )(*args, *after)


def iota(shape, dim):
    return lax.broadcasted_iota(jnp.int32, shape, dim)


def row_picks():
    r = iota((ROWS, PAD), 0)
    j = iota((ROWS, PAD), 1)
    second = r >= PAD
    s = jnp.where(second, r - PAD, r)
    t = jnp.where(second, s + SEQ, s)
    live = s < SEQ
    even = jnp.where(live & (t == 2 * j), 1.0, 0.0).astype(bf16)
    odd = jnp.where(live & (t == 2 * j + 1), 1.0, 0.0).astype(bf16)
    return even, odd


def row_picks_back():
    r = iota((PAD, ROWS), 1)
    j = iota((PAD, ROWS), 0)
    second = r >= PAD
    s = jnp.where(second, r - PAD, r)
    t = jnp.where(second, s + SEQ, s)
    live = s < SEQ
    even = jnp.where(live & (t == 2 * j), 1.0, 0.0).astype(bf16)
    odd = jnp.where(live & (t == 2 * j + 1), 1.0, 0.0).astype(bf16)
    return even, odd


def lane_split():
    l = iota((256, 256), 0)
    c = iota((256, 256), 1)
    target = jnp.where(c < 128, 2 * c, 2 * (c - 128) + 1)
    return jnp.where(l == target, 1.0, 0.0).astype(bf16)


def lane_join():
    l = iota((256, 256), 1)
    c = iota((256, 256), 0)
    target = jnp.where(c < 128, 2 * c, 2 * (c - 128) + 1)
    return jnp.where(l == target, 1.0, 0.0).astype(bf16)


def unpack(own_ref, got_ref, gy):
    own, got = own_ref[...], got_ref[...]
    first = jnp.where(gy == 0, own.astype(f32), got.astype(f32)).astype(bf16)
    last = jnp.where(gy == 0, got.astype(f32), own.astype(f32)).astype(bf16)
    split = lane_split()
    evens, odds = [], []
    for half in (first, last):
        for b in range(3):
            both = dot(half[:, 256 * b : 256 * b + 256], split).astype(bf16)
            evens.append(both[:, :128])
            odds.append(both[:, 128:])
    even_rows, odd_rows = row_picks()
    return dot(even_rows, jnp.concatenate(evens, axis=1)) + dot(odd_rows, jnp.concatenate(odds, axis=1))


def pack(rows_low, gy, keep_ref, send_ref):
    even_rows, odd_rows = row_picks_back()
    even = dot(even_rows, rows_low).astype(bf16)
    odd = dot(odd_rows, rows_low).astype(bf16)
    join = lane_join()
    for b in range(3):
        blocks = []
        for half in range(2):
            at = HALF * half + 128 * b
            both = jnp.concatenate([even[:, at : at + 128], odd[:, at : at + 128]], axis=1)
            blocks.append(dot(both, join))
        keep_ref[:, 256 * b : 256 * b + 256] = jnp.where(gy == 0, blocks[0], blocks[1]).astype(bf16)
        send_ref[:, 256 * b : 256 * b + 256] = jnp.where(gy == 0, blocks[1], blocks[0]).astype(bf16)


def norm_parts(v):
    center = jnp.mean(v, axis=1, keepdims=True)
    away = v - center
    scale = lax.rsqrt(jnp.mean(away * away, axis=1, keepdims=True) + norm_eps)
    return away * scale, scale


def norm_back(grad, scaled, scale, gain):
    pushed = grad * gain
    first = jnp.mean(pushed, axis=1, keepdims=True)
    cross = jnp.mean(pushed * scaled, axis=1, keepdims=True)
    return (pushed - first - scaled * cross) * scale


def prepare_kernel(me_ref, attn_ref, expand_ref, project_ref, attn_out, ff_out):
    me = me_ref[0]
    l = iota((512, 256), 0)
    c = iota((512, 256), 1)
    kind = 2 * me + jnp.where(c < 128, 0, 1)
    pick = jnp.where(l == 4 * (c & 127) + kind, 1.0, 0.0).astype(bf16)
    for b in range(3):
        both = dot(attn_ref[:, 512 * b : 512 * b + 512].astype(bf16), pick).astype(bf16)
        attn_out[:, 128 * b : 128 * b + 128] = both[:, :128]
        attn_out[:, HALF + 128 * b : HALF + 128 * b + 128] = both[:, 128:]
    ff_out[:, :D] = jnp.where(me == 0, expand_ref[:, :D], expand_ref[:, D:]).astype(bf16)
    turned = project_ref[...].T
    mine = jnp.where(me == 0, turned[:48], turned[48:])
    ff_out[:, D : D + HALF] = mine[:24].astype(bf16)
    ff_out[:, D + HALF :] = mine[24:].astype(bf16)


def attend_kernel(
    me_ref, own_ref, got_ref, vec_ref, w_own, w_got,
    soft_out, mixed_out, x_out, normed_out, qkv_out, w_out, wo_out,
    x_ref, normed_ref, qkv_ref, w_ref, sems,
):
    step = pl.program_id(0)
    copies = [
        pltpu.make_async_copy(x_ref, x_out, sems.at[0]),
        pltpu.make_async_copy(normed_ref, normed_out, sems.at[1]),
        pltpu.make_async_copy(qkv_ref, qkv_out, sems.at[2]),
        pltpu.make_async_copy(w_ref.at[pl.ds(0, 3)], w_out, sems.at[3]),
        pltpu.make_async_copy(w_ref.at[3], wo_out, sems.at[4]),
    ]

    @pl.when(step == 0)
    def _():
        me, gy = me_ref[0], me_ref[1]
        for ref, place in ((w_own, me), (w_got, 1 - me)):
            for half in range(2):
                for y in range(2):
                    w_ref[pl.ds(2 * place + half, 1), :, HALF * y : HALF * y + HALF] = ref[
                        y, :, HALF * half : HALF * half + HALF
                    ][None]
        copies[3].start()
        copies[4].start()
        x_ref[...] = unpack(own_ref, got_ref, gy).astype(bf16)
        copies[0].start()
        scaled, _ = norm_parts(x_ref[...].astype(f32))
        normed_ref[...] = (scaled * vec_ref[0:1, :] + vec_ref[1:2, :]).astype(bf16)
        copies[1].start()

        def project(i, carry):
            cols = pl.ds(pl.multiple_of(256 * i, 256), 256)
            for kind, row in ((0, 2), (1, None), (2, 3)):
                part = dot(normed_ref[...], w_ref[kind, :, cols])
                if row is not None:
                    part = part + vec_ref[row : row + 1, cols]
                qkv_ref[kind, :, cols] = part.astype(bf16)
            return carry

        lax.fori_loop(0, 3, project, 0)
        copies[2].start()

    @pl.when(step > 0)
    def _():
        cols = pl.ds(pl.multiple_of(128 * (step - 1), 128), 128)
        lane = iota((PAD, 128), 1)
        key_live = iota((PAD, PAD), 0) < SEQ
        for image in range(IMAGES):
            rows = pl.ds(PAD * image, PAD)
            q = qkv_ref[0, rows, cols] * jnp.asarray(0.125, bf16)
            k = qkv_ref[1, rows, cols]
            v = qkv_ref[2, rows, cols]
            total = None
            for n in range(2):
                inside = (lane < HD) == (n == 0)
                scores = dot_lanes(k, jnp.where(inside, q, jnp.zeros_like(q)))
                scores = jnp.where(key_live, scores, -1e30)
                terms = jnp.exp(scores - jnp.max(scores, axis=0, keepdims=True))
                soft = terms * (1.0 / jnp.sum(terms, axis=0, keepdims=True))
                soft = soft.astype(bf16)
                soft_out[0, 2 * image + n] = soft
                part = dot_rows(soft, jnp.where(inside, v, jnp.zeros_like(v)))
                total = part if total is None else total + part
            mixed_out[rows, :] = total.astype(bf16)

    @pl.when(step == 6)
    def _():
        for copy in copies:
            copy.wait()


def gelu_parts(v):
    below = 0.5 + 0.5 * lax.erf(v * 0.7071067811865476)
    return v * below, below + v * jnp.exp(-0.5 * v * v) * 0.3989422804014327


def gather_rows(first, last):
    return jnp.concatenate([first.astype(f32), last.astype(f32)], axis=0).astype(bf16)


def place_rows(w2, ff_ref):
    for d in range(2):
        for g in range(8):
            for y in range(2):
                piece = ff_ref[d, g, y]
                rows = slice(96 * g + 48 * d, 96 * g + 48 * d + 48)
                w2[rows, HALF * y : HALF * y + HALF] = gather_rows(piece[:, :HALF], piece[:, HALF:])


def second_kernel(
    me_ref, live_ref, own_ref, got_ref, vec_ref, x_ref, mixed_ref, wo_ref,
    up_out, middle_out, second_out,
):
    up = unpack(own_ref, got_ref, me_ref[1])
    image = jnp.where(iota((ROWS, 1), 0) < PAD, live_ref[0], live_ref[1])
    up_out[...] = jnp.where(image == 1, up, 0.0).astype(bf16)
    middle = x_ref[...].astype(f32) + dot(mixed_ref[...], wo_ref[...]) + vec_ref[4:5, :]
    middle_out[...] = middle
    scaled, _ = norm_parts(middle)
    second_out[...] = (scaled * vec_ref[5:6, :] + vec_ref[6:7, :]).astype(bf16)


def expand_kernel(
    me_ref, up_ref, second_ref, bias_ref, w1_ref,
    act_out, slope_out, mine_out, theirs_out, w1_out,
    total,
):
    me = me_ref[0]
    for pair in range(16):
        w1_out[48 * pair : 48 * pair + 48, :] = gather_rows(
            w1_ref[0, 2 * pair, 0], w1_ref[0, 2 * pair + 1, 0]
        )

    for i in range(3):
        cols = slice(256 * i, 256 * i + 256)
        inner = dot(second_ref[...], w1_out[:, cols]) + bias_ref[:, cols]
        act, slope = gelu_parts(inner)
        act = act.astype(bf16)
        act_out[:, cols] = act
        slope_out[:, cols] = slope.astype(bf16)
    total[...] = dot_rows(act_out[...], up_ref[...]).astype(bf16)

    for g in range(8):
        for ref, place in ((mine_out, me), (theirs_out, 1 - me)):
            part = total[pl.ds(pl.multiple_of(96 * g + 48 * place, 16), 48), :]
            for y in range(2):
                ref[y, g] = part[:, HALF * y : HALF * y + HALF]


def contract_kernel(
    me_ref, up_ref, slope_ref, second_ref, ff_ref,
    grad_out, hidden_out, mine_out, theirs_out,
    turned, w2,
):
    step = pl.program_id(0)
    me = me_ref[0]

    @pl.when(step == 0)
    def _():
        turned[...] = second_ref[...].T

    place_rows(w2, ff_ref)
    for i in range(3):
        cols = slice(256 * i, 256 * i + 256)
        grad = dot_lanes(up_ref[...], w2[cols, :]) * slope_ref[:, cols].astype(f32)
        grad = grad.astype(bf16)
        grad_out[:, cols] = grad
        hidden_out[:, cols] = jnp.sum(grad.astype(f32), axis=0, keepdims=True)

    def outer(ref):
        for i in range(3):
            cols = slice(256 * i, 256 * i + 256)
            ref[0, :, cols] = dot(turned[...], grad_out[:, cols]).astype(bf16)

    pl.when((step & 1) == me)(lambda: outer(mine_out))
    pl.when((step & 1) != me)(lambda: outer(theirs_out))


def middle_back_kernel(
    me_ref, vec_ref, inner_hbm, w1_hbm, soft_hbm, up_hbm, middle_hbm, wo_hbm, normed_hbm, mixed_hbm, qkv_hbm,
    mine_hbm, theirs_hbm, sums_out, grads_hbm, gm_hbm,
    inner_ref, w1_ref, soft_ref, up_ref, middle_ref, wo_ref, normed_ref, mixed_ref, qkv_ref,
    grad_second, gml, grad_mixed, normed_turned, mixed_turned, pieces, grads_ref, gm_ref, sems,
):
    me = me_ref[0]
    ahead = []
    for j in range(4):
        cols = pl.ds(D * j, D)
        ahead.append((inner_hbm.at[:, cols], inner_ref.at[j]))
        ahead.append((w1_hbm.at[:, cols], w1_ref.at[j]))
    ahead += [
        (middle_hbm, middle_ref), (up_hbm, up_ref), (wo_hbm, wo_ref),
        (normed_hbm, normed_ref), (mixed_hbm, mixed_ref), (qkv_hbm, qkv_ref),
    ]
    reads = [pltpu.make_async_copy(src, dst, sems.at[i]) for i, (src, dst) in enumerate(ahead)]

    def read_soft(i):
        return pltpu.make_async_copy(soft_hbm.at[i], soft_ref.at[i], sems.at[14 + i])

    grads_write = pltpu.make_async_copy(grads_ref, grads_hbm, sems.at[20])
    gm_write = pltpu.make_async_copy(gm_ref, gm_hbm, sems.at[21])

    def write(kind, act):
        cols = pl.ds(HALF * (kind % 2), HALF)
        for to, place in ((mine_hbm, kind // 2), (theirs_hbm, 1 - kind // 2)):
            copy = pltpu.make_async_copy(pieces.at[kind], to.at[:, :, cols], sems.at[22 + kind])
            pl.when(me == place)(lambda copy=copy: act(copy))

    def outer(kind, left, right):
        grad = dot(left[...], right[...]).astype(bf16)
        for y in range(2):
            pieces[kind, y] = grad[:, HALF * y : HALF * y + HALF]
        write(kind, lambda copy: copy.start())

    for read in reads:
        read.start()
    for i in range(6):
        read_soft(i).start()
    for j in range(4):
        reads[2 * j].wait()
        reads[2 * j + 1].wait()
        part = dot_lanes(inner_ref[j], w1_ref[j])
        if j == 0:
            grad_second[...] = part
        else:
            grad_second[...] += part
    for read in reads[8:]:
        read.wait()
    grad = grad_second[...]
    scaled, scale = norm_parts(middle_ref[...])
    up = up_ref[...].astype(f32)
    gm = up + norm_back(grad, scaled, scale, vec_ref[5:6, :])
    gm_ref[...] = gm
    gm_write.start()
    gml[...] = gm.astype(bf16)
    sums_out[2:3, :] = jnp.sum(gml[...].astype(f32), axis=0, keepdims=True)
    sums_out[3:4, :] = jnp.sum(grad * scaled, axis=0, keepdims=True)
    sums_out[4:5, :] = jnp.sum(grad, axis=0, keepdims=True)
    sums_out[5:6, :] = jnp.sum(up, axis=0, keepdims=True)
    grad_mixed[...] = dot_lanes(gml[...], wo_ref[...]).astype(bf16)
    mixed_turned[...] = mixed_ref[...].T
    outer(3, mixed_turned, gml)
    normed_turned[...] = normed_ref[...].T
    lane = iota((PAD, 128), 1)

    def attend(i, carry):
        cols = pl.ds(pl.multiple_of(128 * i, 128), 128)
        read_soft(i).wait()
        for image in range(IMAGES):
            rows = pl.ds(PAD * image, PAD)
            q = qkv_ref[0, rows, cols]
            k = qkv_ref[1, rows, cols]
            v = qkv_ref[2, rows, cols]
            g = grad_mixed[rows, cols]
            dq = dk = dv = jnp.zeros((PAD, 128), f32)
            for n in range(2):
                inside = (lane < HD) == (n == 0)
                zero = jnp.zeros_like(g)
                g_in = jnp.where(inside, g, zero)
                soft_low = soft_ref[i, 2 * image + n]
                soft = soft_low.astype(f32)
                grad_soft = dot_lanes(v, g_in)
                level = jnp.sum(grad_soft * soft, axis=0, keepdims=True)
                scores = (soft * (grad_soft - level)).astype(bf16)
                dv = dv + dot(soft_low, g_in)
                dk = dk + dot(scores, jnp.where(inside, q, zero))
                dq = dq + dot_rows(scores, jnp.where(inside, k, zero))
            grads_ref[0, rows, cols] = (dq * 0.125).astype(bf16)
            grads_ref[1, rows, cols] = (dk * 0.125).astype(bf16)
            grads_ref[2, rows, cols] = dv.astype(bf16)
        return carry

    lax.fori_loop(0, 6, attend, 0)
    grads_write.start()
    for kind in range(3):
        outer(kind, normed_turned, grads_ref.at[kind])
    sums_out[0:1, :] = jnp.sum(grads_ref[0].astype(f32), axis=0, keepdims=True)
    sums_out[1:2, :] = jnp.sum(grads_ref[2].astype(f32), axis=0, keepdims=True)
    grads_write.wait()
    gm_write.wait()
    for kind in range(4):
        write(kind, lambda copy: copy.wait())


def input_back_kernel(
    me_ref, vec_ref, grads_ref, w_ref, x_ref, gm_ref, keep_out, send_out, sums_out, total
):
    step = pl.program_id(0)
    part = dot_lanes(grads_ref[0], w_ref[0])

    @pl.when(step == 0)
    def _():
        total[...] = part

    @pl.when(step > 0)
    def _():
        total[...] += part

    @pl.when(step == 2)
    def _():
        grad = total[...]
        scaled, scale = norm_parts(x_ref[...].astype(f32))
        out = gm_ref[...] + norm_back(grad, scaled, scale, vec_ref[0:1, :])
        pack(out.astype(bf16), me_ref[1], keep_out, send_out)
        sums_out[0:1, :] = jnp.sum(grad * scaled, axis=0, keepdims=True)
        sums_out[1:2, :] = jnp.sum(grad, axis=0, keepdims=True)


def output_kernel(me_ref, vec_ref, middle_ref, act_ref, ff_ref, keep_out, send_out, w2, total):
    step = pl.program_id(0)
    place_rows(w2, ff_ref)
    part = dot(act_ref[...], w2[...])

    @pl.when(step == 0)
    def _():
        total[...] = middle_ref[...] + vec_ref[7:8, :] + part

    @pl.when(step > 0)
    def _():
        total[...] += part

    @pl.when(step == 3)
    def _():
        pack(total[...].astype(bf16), me_ref[1], keep_out, send_out)


def assemble_kernel(at_ref, *refs):
    out = refs[-1]
    step = pl.program_id(0)
    for r in range(4):
        pl.when(step == r)(lambda r=r: out.__setitem__(..., refs[r][...].reshape(out.shape)))


def blocks_sum_kernel(at_ref, *refs):
    ins, outs = refs[:-4], refs[-4:]
    step = pl.program_id(0)
    total = ins[0][...].astype(f32)
    for ref in ins[1:]:
        total = total + ref[...].astype(f32)
    total = total.astype(bf16)
    for r in range(4):
        pl.when(step == r)(lambda r=r: outs[r].__setitem__(..., total.reshape(outs[r].shape)))


def sum_kernel(a_ref, b_ref, c_ref, d_ref, out_ref):
    total = a_ref[...].astype(f32) + b_ref[...].astype(f32) + c_ref[...].astype(f32) + d_ref[...].astype(f32)
    out_ref[...] = total.astype(bf16)


def last_spread_kernel(a_ref, b_ref, c_ref, d_ref, va_ref, vb_ref, vc_ref, vd_ref, out_ref):
    vector = va_ref[...].astype(f32) + vb_ref[...].astype(f32) + vc_ref[...].astype(f32) + vd_ref[...].astype(f32)
    vector = vector.astype(bf16)
    total = a_ref[...].astype(f32) + b_ref[...].astype(f32) + c_ref[...].astype(f32) + d_ref[...].astype(f32)
    total = total.reshape(2 * 192, D)
    for i in range(16):
        out_ref[i, :16, :] = vector
        out_ref[i, 16:, :] = total[24 * i : 24 * i + 24].astype(bf16)


def adamw_step(parameter, gradient, first_moment, second_moment, step_rate, decay_factor):
    first_new = beta_first * first_moment + (1.0 - beta_first) * gradient
    second_new = beta_second * second_moment + (1.0 - beta_second) * gradient * gradient
    first_hat = first_new / (1.0 - beta_first**STEP)
    second_hat = second_new / (1.0 - beta_second**STEP)
    updated = parameter - step_rate * (
        first_hat / (jnp.sqrt(second_hat) + adam_eps) + decay_factor * parameter
    )
    return second_new, updated


def ordered(me, own, got):
    return jnp.where(me == 0, own, got), jnp.where(me == 0, got, own)


def attention_step_kernel(
    me_ref, own_ref, got_ref, w_ref, m_ref, v_ref, vec_ref, vec_m_ref, vec_v_ref,
    grad_out, second_out, new_out, vec_grad_out, vec_second_out, vec_new_out,
):
    pieces = ordered(me_ref[0], own_ref[16:, :], got_ref[16:, :])
    l = iota((512, 512), 0)
    c = iota((512, 512), 1)
    pick = jnp.where(c == 4 * (l & 127) + (l >> 7), 1.0, 0.0)
    for b in range(3):
        kinds = [
            pieces[k // 2][:, HALF * (k % 2) + 128 * b : HALF * (k % 2) + 128 * b + 128]
            for k in range(4)
        ]
        grad_out[:, 512 * b : 512 * b + 512] = jnp.dot(
            jnp.concatenate(kinds, axis=1), pick, precision=lax.Precision.HIGHEST,
            preferred_element_type=f32,
        )
    second_out[...], new_out[...] = adamw_step(
        w_ref[...], grad_out[...], m_ref[...], v_ref[...], learn_rate, decay_rate
    )
    vector = own_ref[:12, :] + got_ref[:12, :]
    vec_grad_out[...] = jnp.where(me_ref[1] == 0, vector[:, :HALF], vector[:, HALF:])
    vec_second_out[...], vec_new_out[...] = adamw_step(
        vec_ref[...], vec_grad_out[...], vec_m_ref[...], vec_v_ref[...], vector_rate, 0.0
    )


def expand_step_kernel(me_ref, own_ref, got_ref, w_ref, m_ref, v_ref, grad_out, second_out, new_out):
    first, last = ordered(me_ref[0], own_ref[...], got_ref[...])
    grad_out[:, :D] = first
    grad_out[:, D:] = last
    second_out[...], new_out[...] = adamw_step(
        w_ref[...], grad_out[...], m_ref[...], v_ref[...], learn_rate, decay_rate
    )


def project_step_kernel(me_ref, own_ref, got_ref, w_ref, m_ref, v_ref, grad_out, second_out, new_out):
    first, last = ordered(me_ref[0], own_ref[...], got_ref[...])
    grad_out[...] = jnp.concatenate([first, last], axis=0).T
    second_out[...], new_out[...] = adamw_step(
        w_ref[...], grad_out[...], m_ref[...], v_ref[...], learn_rate, decay_rate
    )


def place(axes):
    at = 0
    for a in axes:
        at = at * lax.axis_size(a) + lax.axis_index(a)
    return at


def swap(x, axis):
    return lax.ppermute(x, axis, [(0, 1), (1, 0)])


def core_sum(mine, theirs):
    return (mine.astype(f32) + swap(theirs, "dp").astype(f32)).astype(bf16)


def assemble(parts, at, shape, piece, index, after=(), cost=0):
    flat = tuple(n for n in piece if n > 1)
    return pl.pallas_call(
        assemble_kernel,
        out_shape=jax.ShapeDtypeStruct(shape, bf16),
        grid_spec=pltpu.PrefetchScalarGridSpec(
            num_scalar_prefetch=1,
            grid=(4,),
            in_specs=[
                *(pl.BlockSpec(flat, lambda r, at: (0,) * len(flat)) for _ in range(4)),
                *(LEFT for _ in after),
            ],
            out_specs=pl.BlockSpec(piece, lambda r, at: index((at[0] + 3 * r) % 4)),
        ),
        compiler_params=pltpu.CompilerParams(vmem_limit_bytes=32 * 1024 * 1024),
        cost_estimate=pl.CostEstimate(flops=cost * 10**9 + 1000, bytes_accessed=0, transcendentals=0),
        name="assemble",
    )(at.reshape(1).astype(jnp.int32), *(p.reshape(flat) for p in parts), *after)


def ring_blocks(parts, at, shape, piece, index):
    spec = pl.BlockSpec(piece, lambda r, at: index((at[0] + r) % 4))
    flat = tuple(n for n in piece if n > 1)
    return pl.pallas_call(
        blocks_sum_kernel,
        out_shape=[jax.ShapeDtypeStruct(flat, bf16)] * 4,
        grid_spec=pltpu.PrefetchScalarGridSpec(
            num_scalar_prefetch=1,
            grid=(4,),
            in_specs=[spec] * len(parts),
            out_specs=[pl.BlockSpec(flat, lambda r, at: (0,) * len(flat))] * 4,
        ),
        compiler_params=pltpu.CompilerParams(vmem_limit_bytes=32 * 1024 * 1024),
        cost_estimate=pl.CostEstimate(flops=1000, bytes_accessed=0, transcendentals=0),
        name="ring_blocks",
    )(at.reshape(1).astype(jnp.int32), *(p.reshape(shape) for p in parts))


def hop(x, axes, r):
    return lax.ppermute(x, axes, [(i, (i + r) % 4) for i in range(4)])


def ring(blocks, axes):
    return blocks[0], *(hop(blocks[r], axes, r) for r in (1, 3, 2))


def crossed(x, axis, bit):
    return lax.ppermute(x, axis, [(i, i ^ bit) for i in range(lax.axis_size(axis))])


def to_all(x, axes):
    near, back = hop(x, axes, 1), hop(x, axes, 3)
    return x, near, hop(x, axes, 2), back


def sum_of(parts):
    total = parts[0].astype(f32)
    for part in parts[1:]:
        total = total + part.astype(f32)
    return total


def spread_sum(blocks, axes):
    tiles = lax.all_to_all(blocks, axes, 0, 0, tiled=True)
    return jnp.sum(tiles.astype(f32), axis=0)


def own_images(stored, gy):
    rows = stored.shape[0] // 2
    own = lax.dynamic_slice_in_dim(stored, rows * gy, rows, 0)
    other = lax.dynamic_slice_in_dim(stored, rows * (1 - gy), rows, 0)
    pad = ((0, PAD - rows), (0, 0))
    return jnp.pad(own, pad), jnp.pad(other, pad)


def stored_rows(keep, got, gy):
    first = jnp.where(gy == 0, keep, got)[:SEQ]
    last = jnp.where(gy == 0, got, keep)[:SEQ]
    return jnp.concatenate([first, last], axis=0).astype(f32)


def per_device(
    tokens,
    image_counts,
    slot_order,
    cotangent,
    attention_weights,
    attention_first,
    attention_second,
    expand_weight,
    expand_first,
    expand_second,
    project_weight,
    project_first,
    project_second,
    vectors,
    vector_first,
    vector_second,
):
    dp = lax.axis_index("dp")
    gy = lax.axis_index("xl")
    me = jnp.stack([dp, gy]).astype(jnp.int32)

    token_own, token_other = own_images(tokens, gy)
    token_got = swap(token_other, "xl")
    grad_own, grad_other = own_images(cotangent, gy)
    grad_got = swap(grad_other, "xl")
    vec_got = swap(vectors, "xl")
    attn_piece, ff_piece = call(
        prepare_kernel,
        [SCALARS, WHOLE, WHOLE, WHOLE],
        [((24, D), bf16, WHOLE), ((24, 2 * D), bf16, WHOLE)],
        (me, attention_weights, expand_weight, project_weight),
        name="prepare",
    )
    ff = lax.all_gather(ff_piece, EVERY).reshape(2, 32, 2, 24, 2 * D)
    at_x, at_y, at_z = place(X), place(Y), place(Z)

    def across_x(p):
        return p % 2, 0, p // 2, 0, 0

    attn = to_all(attn_piece, X)
    attn = assemble(attn, at_x, (2, 1, 2, 24, D), (1, 1, 1, 24, D), across_x)
    attn = to_all(attn.reshape(2, 48, D), Y)
    attn, token_got, vec_got = lax.optimization_barrier((attn, token_got, vec_got))
    attn = assemble(attn, at_y, (2, 4, 48, D), (2, 1, 48, D), lambda p: (0, p, 0, 0))
    vec_first, vec_last = ordered(gy, vectors, vec_got)
    vec = jnp.concatenate([vec_first, vec_last], axis=1)
    bias = vec[8:].T.reshape(1, FF)
    live = (slot_order[0] < image_counts[0]).astype(jnp.int32)
    live = lax.dynamic_slice_in_dim(live, IMAGES * gy, IMAGES)
    attn = to_all(attn.reshape(2, 192, D), Z)
    attn, vec, bias, live, token_own, token_got = lax.optimization_barrier(
        (attn, vec, bias, live, token_own, token_got)
    )
    attn = assemble(attn, at_z, (2, 4, 192, D), (2, 1, 192, D), lambda p: (0, p, 0, 0))
    w_own, w_got = (w.reshape(2, D, D) for w in (attn, swap(attn, "dp")))

    tall = block((ROWS, D), lambda j: (0, 0))
    wide = block((ROWS, D), lambda j: (0, j))
    w1_block = block((1, 32, 1, 24, D), lambda j: (j % 2, 0, j // 2, 0, 0))
    w2_block = block((2, 8, 2, 24, D), lambda j: (0, j, 0, 0, 1))
    pieces2 = block((2, 8, 48, HALF), lambda j: (0, j, 0, 0))
    soft_shape = (6, 2 * IMAGES, PAD, PAD)

    soft, mixed, x, normed, qkv, w_qkv, w_o = call(
        attend_kernel,
        [SCALARS, *(WHOLE,) * 5],
        [
            (soft_shape, bf16, block((1, *soft_shape[1:]), lambda p: (jnp.maximum(p - 1, 0), 0, 0, 0))),
            ((ROWS, D), bf16, block((ROWS, 128), lambda p: (0, jnp.maximum(p - 1, 0)))),
            ((ROWS, D), bf16, LEFT),
            ((ROWS, D), bf16, LEFT),
            ((3, ROWS, D), bf16, LEFT),
            ((3, D, D), bf16, LEFT),
            ((D, D), bf16, LEFT),
        ],
        (me, token_own, token_got, vec, w_own, w_got),
        grid=(7,),
        scratch=[
            pltpu.VMEM((ROWS, D), bf16),
            pltpu.VMEM((ROWS, D), bf16),
            pltpu.VMEM((3, ROWS, D), bf16),
            pltpu.VMEM((4, D, D), bf16),
            pltpu.SemaphoreType.DMA((5,)),
        ],
        name="attend",
    )

    up, middle, second = call(
        second_kernel,
        [SCALARS, SCALARS, *(WHOLE,) * 6],
        [((ROWS, D), bf16, WHOLE), ((ROWS, D), f32, WHOLE), ((ROWS, D), bf16, WHOLE)],
        (me, live, grad_own, grad_got, vec, x, mixed, w_o),
        name="second",
    )
    act, slope, mine2, theirs2, w1 = call(
        expand_kernel,
        [SCALARS, WHOLE, WHOLE, block((1, D), lambda j: (0, j)), w1_block],
        [
            ((ROWS, FF), bf16, wide),
            ((ROWS, FF), bf16, wide),
            ((2, 32, 48, HALF), bf16, pieces2),
            ((2, 32, 48, HALF), bf16, pieces2),
            ((D, FF), bf16, block((D, D), lambda j: (0, j))),
        ],
        (me, up, second, bias, ff),
        grid=(4,),
        scratch=[pltpu.VMEM((D, D), bf16)],
        after=(w_o, soft),
        name="expand",
    )
    inner_grad, hidden_sums, mine1, theirs1 = call(
        contract_kernel,
        [SCALARS, WHOLE, wide, WHOLE, w2_block],
        [
            ((ROWS, FF), bf16, wide),
            ((1, FF), f32, block((1, D), lambda j: (0, j))),
            ((2, D, D), bf16, block((1, D, D), lambda j: (j // 2, 0, 0))),
            ((2, D, D), bf16, block((1, D, D), lambda j: (j // 2, 0, 0))),
        ],
        (me, up, slope, second, ff),
        grid=(4,),
        scratch=[pltpu.VMEM((D, ROWS), bf16), pltpu.VMEM((D, D), bf16)],
        name="contract",
    )
    ring2 = ring_blocks(
        (mine2, swap(theirs2, "dp")),
        place(X),
        (2, 16, 2, 48, HALF),
        (1, 16, 1, 48, HALF),
        lambda p: (p % 2, 0, p // 2, 0, 0),
    )
    got1, _ = lax.optimization_barrier((swap(theirs1, "dp"), ring2[0]))
    ring1 = ring_blocks(
        (mine1, got1), place(Y), (8, 4, 48, D), (8, 1, 48, D), lambda p: (0, p, 0, 0)
    )

    mine0, theirs0, sums_c, grads, gm = call(
        middle_back_kernel,
        [SCALARS, WHOLE, *(LEFT,) * 9],
        [
            ((2, D, D), bf16, LEFT),
            ((2, D, D), bf16, LEFT),
            ((6, D), f32, WHOLE),
            ((3, ROWS, D), bf16, LEFT),
            ((ROWS, D), f32, LEFT),
        ],
        (me, vec, inner_grad, w1, soft, up, middle, w_o, normed, mixed, qkv),
        scratch=[
            pltpu.VMEM((4, ROWS, D), bf16),
            pltpu.VMEM((4, D, D), bf16),
            pltpu.VMEM(soft_shape, bf16),
            pltpu.VMEM((ROWS, D), bf16),
            pltpu.VMEM((ROWS, D), f32),
            pltpu.VMEM((D, D), bf16),
            pltpu.VMEM((ROWS, D), bf16),
            pltpu.VMEM((ROWS, D), bf16),
            pltpu.VMEM((3, ROWS, D), bf16),
            pltpu.VMEM((ROWS, D), f32),
            pltpu.VMEM((ROWS, D), bf16),
            pltpu.VMEM((ROWS, D), bf16),
            pltpu.VMEM((D, ROWS), bf16),
            pltpu.VMEM((D, ROWS), bf16),
            pltpu.VMEM((4, 2, D, HALF), bf16),
            pltpu.VMEM((3, ROWS, D), bf16),
            pltpu.VMEM((ROWS, D), f32),
            pltpu.SemaphoreType.DMA((26,)),
        ],
        after=(ring2[0], ring1[0]),
        cost=0,
        name="middle_back",
    )
    got0 = swap(theirs0, "dp")
    ring2 = ring(ring2, X)
    near1 = hop(ring1[1], Y, 1), hop(ring1[3], Y, 3)
    ring2, mine0 = lax.optimization_barrier((ring2, mine0))
    mine0, near1, far1 = lax.optimization_barrier((mine0, near1, ring1[2]))
    far1 = hop(far1, Y, 2)
    part2 = call(
        sum_kernel, [WHOLE] * 4, [((16, 48, HALF), bf16, WHOLE)], ring2, cost=100, after=(near1[0], near1[1]), name="part"
    )[0]
    tiles2 = lax.all_to_all(part2, Z + Y, 0, 0, tiled=True)
    mine0, got0, _ = lax.optimization_barrier((mine0, got0, part2))
    ring0 = ring_blocks(
        (mine0, got0), place(Z), (2, 4, 192, D), (2, 1, 192, D), lambda p: (0, p, 0, 0)
    )
    tiles2, far1, _ = lax.optimization_barrier((tiles2, far1, ring0[0]))
    own0, near0, back0, far0 = ring(ring0, Z)
    keep_in, send_in, sums_e = call(
        input_back_kernel,
        [
            SCALARS, WHOLE,
            block((1, ROWS, D), lambda k: (k, 0, 0)), block((1, D, D), lambda k: (k, 0, 0)),
            WHOLE, WHOLE,
        ],
        [
            ((PAD, D), bf16, block((PAD, D), lambda k: (0, 0))),
            ((PAD, D), bf16, block((PAD, D), lambda k: (0, 0))),
            ((2, D), f32, block((2, D), lambda k: (0, 0))),
        ],
        (me, vec, grads, w_qkv, x, gm),
        grid=(3,),
        scratch=[pltpu.VMEM((ROWS, D), f32)],
        cost=100,
        after=(ring0[0],),
        name="input_back",
    )
    sums_e, hidden_sums = lax.optimization_barrier((sums_e, hidden_sums))
    vector = jnp.concatenate(
        [sums_e, sums_c, hidden_sums.reshape(D, 4).T, jnp.zeros((4, D), f32)], axis=0
    ).astype(bf16)
    vectors4 = ring((vector,) * 4, Z)
    got_in = swap(send_in, "xl")
    keep_out, send_out = call(
        output_kernel,
        [SCALARS, WHOLE, WHOLE, wide, w2_block],
        [((PAD, D), bf16, block((PAD, D), lambda j: (0, 0)))] * 2,
        (me, vec, middle, act, ff),
        grid=(4,),
        scratch=[pltpu.VMEM((D, D), bf16), pltpu.VMEM((ROWS, D), f32)],
        after=(vector,),
        cost=0,
        name="output",
    )
    got_out = swap(send_out, "xl")
    far1, tiles2, near0, back0, vectors4, keep_out = lax.optimization_barrier(
        (far1, tiles2, near0, back0, vectors4, keep_out)
    )
    part1 = sum_of((ring1[0], *near1, far1)).astype(bf16).reshape(16, 24, D)
    tiles1 = lax.all_to_all(part1, ("xl", "z", "xh"), 0, 0, tiled=True)
    sum2 = jnp.sum(tiles2.astype(f32), axis=0)
    got2 = swap(sum2, "dp")
    part0 = call(
        last_spread_kernel,
        [WHOLE] * 8,
        [((16, 40, D), bf16, WHOLE)],
        (own0, near0, back0, far0, *vectors4),
        cost=100,
        name="last_spread",
    )[0]
    tiles0 = lax.all_to_all(part0, ("xl", "y", "xh"), 0, 0, tiled=True)
    sum1 = jnp.sum(tiles1.astype(f32), axis=0)
    got1 = swap(sum1, "dp")
    block_out = stored_rows(keep_out, got_out, gy)
    input_grad = stored_rows(keep_in, got_in, gy)

    def step(body, own, got, shape, state, outs=(), cost=0, name=None):
        state = (me, own, got, *state)
        outs = [(shape, f32, WHOLE)] * 3 + [(o, f32, WHOLE) for o in outs]
        return call(body, [SCALARS, *(WHOLE,) * (len(state) - 1)], outs, state, cost=cost, name=name)

    project = step(
        project_step_kernel, sum2, got2, (HALF, 96),
        (project_weight, project_first, project_second), name="project_step",
    )
    expand = step(
        expand_step_kernel, sum1, got1, (24, 2 * D),
        (expand_weight, expand_first, expand_second), name="expand_step",
    )
    tiles0, project = lax.optimization_barrier((tiles0, project))
    sum0 = jnp.sum(tiles0.astype(f32), axis=0)
    got0 = swap(sum0, "dp")
    *attention, vector_grad, vector_second_new, vector_new = step(
        attention_step_kernel, sum0, got0, (24, 2 * D),
        (attention_weights, attention_first, attention_second, vectors, vector_first, vector_second),
        [(12, HALF)] * 3, name="attention_step",
    )
    return (
        block_out,
        input_grad,
        *attention,
        *expand,
        *project,
        vector_grad,
        vector_second_new,
        vector_new,
    )


def solution(mesh):
    fine = Mesh(mesh.devices.reshape(2, 4, 4, 2, 2), EVERY)
    rows = ("dp", "z", "y", "xh")
    deep = ("z", "y", "xh")
    placed = (
        P(rows, "xl"),
        P("dp"),
        P("dp", deep),
        P(rows, "xl"),
        *(P(deep, "xl"),) * 6,
        *(P("xl", deep),) * 3,
        *(P(None, "xl"),) * 3,
    )
    out = (
        P(rows, "xl"),
        P(rows, "xl"),
        *(P(deep, "xl"),) * 6,
        *(P("xl", deep),) * 3,
        *(P(None, "xl"),) * 3,
    )
    return jax.shard_map(per_device, mesh=fine, in_specs=placed, out_specs=out, check_vma=False)
```

```python
import jax
import jax.numpy as jnp
from jax import lax
from jax.experimental import pallas as pl
from jax.experimental.pallas import tpu as pltpu
from jax.sharding import Mesh
from jax.sharding import PartitionSpec as P

D = 768
HD = 64
FF = 3072
SEQ = 197
STEP = 10
PAD = 208
IMAGES = 2
ROWS = PAD * IMAGES
HALF = D // 2

norm_eps = 1e-06
beta_first = 0.9
beta_second = 0.999
learn_rate = 0.04
vector_rate = 0.25
decay_rate = 0.05
adam_eps = 1e-08

f32 = jnp.float32
bf16 = jnp.bfloat16

DP = ("dp",)
Z = ("z",)
Y = ("y",)
X = ("xh", "xl")
CHIPS = ("xl", "z", "y", "xh")
EVERY = ("dp", "z", "y", "xh", "xl")


def dot(a, b):
    return lax.dot_general(a, b, (((1,), (0,)), ((), ())), preferred_element_type=f32)


def dot_rows(a, b):
    return lax.dot_general(a, b, (((0,), (0,)), ((), ())), preferred_element_type=f32)


def dot_lanes(a, b):
    return lax.dot_general(a, b, (((1,), (1,)), ((), ())), preferred_element_type=f32)


def block(shape, index):
    return pl.BlockSpec(shape, index)


WHOLE = pl.BlockSpec(memory_space=pltpu.VMEM)
SCALARS = pl.BlockSpec(memory_space=pltpu.SMEM)
LEFT = pl.BlockSpec(memory_space=pl.ANY)


def call(body, ins, outs, args, grid=(), scratch=(), after=(), cost=10, prefetch=0, name=None):
    count = len(args)

    def run(*refs):
        body(*refs[:count], *refs[count + len(after) :])

    return pl.pallas_call(
        run if after else body,
        out_shape=[jax.ShapeDtypeStruct(s, t) for s, t, _ in outs],
        grid_spec=pltpu.PrefetchScalarGridSpec(
            num_scalar_prefetch=prefetch,
            grid=grid,
            in_specs=[*ins, *(LEFT for _ in after)],
            out_specs=[spec for _, _, spec in outs],
            scratch_shapes=list(scratch),
        ),
        compiler_params=pltpu.CompilerParams(vmem_limit_bytes=52 * 1024 * 1024),
        cost_estimate=pl.CostEstimate(flops=cost * 10**9 + 1000, bytes_accessed=0, transcendentals=0),
        name=name,
    )(*args, *after)


def iota(shape, dim):
    return lax.broadcasted_iota(jnp.int32, shape, dim)


def row_picks():
    r = iota((ROWS, PAD), 0)
    j = iota((ROWS, PAD), 1)
    second = r >= PAD
    s = jnp.where(second, r - PAD, r)
    t = jnp.where(second, s + SEQ, s)
    live = s < SEQ
    even = jnp.where(live & (t == 2 * j), 1.0, 0.0).astype(bf16)
    odd = jnp.where(live & (t == 2 * j + 1), 1.0, 0.0).astype(bf16)
    return even, odd


def row_picks_back():
    r = iota((PAD, ROWS), 1)
    j = iota((PAD, ROWS), 0)
    second = r >= PAD
    s = jnp.where(second, r - PAD, r)
    t = jnp.where(second, s + SEQ, s)
    live = s < SEQ
    even = jnp.where(live & (t == 2 * j), 1.0, 0.0).astype(bf16)
    odd = jnp.where(live & (t == 2 * j + 1), 1.0, 0.0).astype(bf16)
    return even, odd


def lane_split():
    l = iota((256, 256), 0)
    c = iota((256, 256), 1)
    target = jnp.where(c < 128, 2 * c, 2 * (c - 128) + 1)
    return jnp.where(l == target, 1.0, 0.0).astype(bf16)


def lane_join():
    l = iota((256, 256), 1)
    c = iota((256, 256), 0)
    target = jnp.where(c < 128, 2 * c, 2 * (c - 128) + 1)
    return jnp.where(l == target, 1.0, 0.0).astype(bf16)


def unpack(own_ref, got_ref, gy):
    own, got = own_ref[...], got_ref[...]
    first = jnp.where(gy == 0, own.astype(f32), got.astype(f32)).astype(bf16)
    last = jnp.where(gy == 0, got.astype(f32), own.astype(f32)).astype(bf16)
    split = lane_split()
    evens, odds = [], []
    for half in (first, last):
        for b in range(3):
            both = dot(half[:, 256 * b : 256 * b + 256], split).astype(bf16)
            evens.append(both[:, :128])
            odds.append(both[:, 128:])
    even_rows, odd_rows = row_picks()
    return dot(even_rows, jnp.concatenate(evens, axis=1)) + dot(odd_rows, jnp.concatenate(odds, axis=1))


def pack(rows_low, gy, keep_ref, send_ref):
    even_rows, odd_rows = row_picks_back()
    even = dot(even_rows, rows_low).astype(bf16)
    odd = dot(odd_rows, rows_low).astype(bf16)
    join = lane_join()
    for b in range(3):
        blocks = []
        for half in range(2):
            at = HALF * half + 128 * b
            both = jnp.concatenate([even[:, at : at + 128], odd[:, at : at + 128]], axis=1)
            blocks.append(dot(both, join))
        keep_ref[:, 256 * b : 256 * b + 256] = jnp.where(gy == 0, blocks[0], blocks[1]).astype(bf16)
        send_ref[:, 256 * b : 256 * b + 256] = jnp.where(gy == 0, blocks[1], blocks[0]).astype(bf16)


def norm_parts(v):
    center = jnp.mean(v, axis=1, keepdims=True)
    away = v - center
    scale = lax.rsqrt(jnp.mean(away * away, axis=1, keepdims=True) + norm_eps)
    return away * scale, scale


def norm_back(grad, scaled, scale, gain):
    pushed = grad * gain
    first = jnp.mean(pushed, axis=1, keepdims=True)
    cross = jnp.mean(pushed * scaled, axis=1, keepdims=True)
    return (pushed - first - scaled * cross) * scale


def prepare_kernel(me_ref, attn_ref, expand_ref, project_ref, attn_out, ff_out):
    me = me_ref[0]
    l = iota((512, 256), 0)
    c = iota((512, 256), 1)
    kind = 2 * me + jnp.where(c < 128, 0, 1)
    pick = jnp.where(l == 4 * (c & 127) + kind, 1.0, 0.0).astype(bf16)
    for b in range(3):
        both = dot(attn_ref[:, 512 * b : 512 * b + 512].astype(bf16), pick).astype(bf16)
        attn_out[:, 128 * b : 128 * b + 128] = both[:, :128]
        attn_out[:, HALF + 128 * b : HALF + 128 * b + 128] = both[:, 128:]
    ff_out[:, :D] = jnp.where(me == 0, expand_ref[:, :D], expand_ref[:, D:]).astype(bf16)
    turned = project_ref[...].T
    mine = jnp.where(me == 0, turned[:48], turned[48:])
    ff_out[:, D : D + HALF] = mine[:24].astype(bf16)
    ff_out[:, D + HALF :] = mine[24:].astype(bf16)


def attend_kernel(
    me_ref, own_ref, got_ref, vec_ref, w_own, w_got,
    soft_out, mixed_out, x_out, normed_out, qkv_out, w_out, wo_out,
    x_ref, normed_ref, qkv_ref, w_ref, sems,
):
    step = pl.program_id(0)
    copies = [
        pltpu.make_async_copy(x_ref, x_out, sems.at[0]),
        pltpu.make_async_copy(normed_ref, normed_out, sems.at[1]),
        pltpu.make_async_copy(qkv_ref, qkv_out, sems.at[2]),
        pltpu.make_async_copy(w_ref.at[pl.ds(0, 3)], w_out, sems.at[3]),
        pltpu.make_async_copy(w_ref.at[3], wo_out, sems.at[4]),
    ]

    @pl.when(step == 0)
    def _():
        me, gy = me_ref[0], me_ref[1]
        for ref, place in ((w_own, me), (w_got, 1 - me)):
            for half in range(2):
                for y in range(2):
                    w_ref[pl.ds(2 * place + half, 1), :, HALF * y : HALF * y + HALF] = ref[
                        y, :, HALF * half : HALF * half + HALF
                    ][None]
        copies[3].start()
        copies[4].start()
        x_ref[...] = unpack(own_ref, got_ref, gy).astype(bf16)
        copies[0].start()
        scaled, _ = norm_parts(x_ref[...].astype(f32))
        normed_ref[...] = (scaled * vec_ref[0:1, :] + vec_ref[1:2, :]).astype(bf16)
        copies[1].start()

        def project(i, carry):
            cols = pl.ds(pl.multiple_of(256 * i, 256), 256)
            for kind, row in ((0, 2), (1, None), (2, 3)):
                part = dot(normed_ref[...], w_ref[kind, :, cols])
                if row is not None:
                    part = part + vec_ref[row : row + 1, cols]
                qkv_ref[kind, :, cols] = part.astype(bf16)
            return carry

        lax.fori_loop(0, 3, project, 0)
        copies[2].start()

    @pl.when(step > 0)
    def _():
        cols = pl.ds(pl.multiple_of(128 * (step - 1), 128), 128)
        lane = iota((PAD, 128), 1)
        key_live = iota((PAD, PAD), 0) < SEQ
        for image in range(IMAGES):
            rows = pl.ds(PAD * image, PAD)
            q = qkv_ref[0, rows, cols] * jnp.asarray(0.125, bf16)
            k = qkv_ref[1, rows, cols]
            v = qkv_ref[2, rows, cols]
            total = None
            for n in range(2):
                inside = (lane < HD) == (n == 0)
                scores = dot_lanes(k, jnp.where(inside, q, jnp.zeros_like(q)))
                scores = jnp.where(key_live, scores, -1e30)
                terms = jnp.exp(scores - jnp.max(scores, axis=0, keepdims=True))
                soft = terms * (1.0 / jnp.sum(terms, axis=0, keepdims=True))
                soft = soft.astype(bf16)
                soft_out[0, 2 * image + n] = soft
                part = dot_rows(soft, jnp.where(inside, v, jnp.zeros_like(v)))
                total = part if total is None else total + part
            mixed_out[rows, :] = total.astype(bf16)

    @pl.when(step == 6)
    def _():
        for copy in copies:
            copy.wait()


def gelu_parts(v):
    below = 0.5 + 0.5 * lax.erf(v * 0.7071067811865476)
    return v * below, below + v * jnp.exp(-0.5 * v * v) * 0.3989422804014327


def gather_rows(first, last):
    return jnp.concatenate([first.astype(f32), last.astype(f32)], axis=0).astype(bf16)


def place_rows(w2, ff_ref):
    for d in range(2):
        for g in range(8):
            for y in range(2):
                piece = ff_ref[d, g, y]
                rows = slice(96 * g + 48 * d, 96 * g + 48 * d + 48)
                w2[rows, HALF * y : HALF * y + HALF] = gather_rows(piece[:, :HALF], piece[:, HALF:])


def second_kernel(
    me_ref, live_ref, own_ref, got_ref, vec_ref, x_ref, mixed_ref, wo_ref,
    up_out, middle_out, second_out,
):
    up = unpack(own_ref, got_ref, me_ref[1])
    image = jnp.where(iota((ROWS, 1), 0) < PAD, live_ref[0], live_ref[1])
    up_out[...] = jnp.where(image == 1, up, 0.0).astype(bf16)
    middle = x_ref[...].astype(f32) + dot(mixed_ref[...], wo_ref[...]) + vec_ref[4:5, :]
    middle_out[...] = middle
    scaled, _ = norm_parts(middle)
    second_out[...] = (scaled * vec_ref[5:6, :] + vec_ref[6:7, :]).astype(bf16)


def expand_kernel(
    me_ref, up_ref, second_ref, bias_ref, w1_ref,
    act_out, slope_out, mine_out, theirs_out, w1_out,
    total,
):
    me = me_ref[0]
    for pair in range(16):
        w1_out[48 * pair : 48 * pair + 48, :] = gather_rows(
            w1_ref[0, 2 * pair, 0], w1_ref[0, 2 * pair + 1, 0]
        )

    for i in range(3):
        cols = slice(256 * i, 256 * i + 256)
        inner = dot(second_ref[...], w1_out[:, cols]) + bias_ref[:, cols]
        act, slope = gelu_parts(inner)
        act = act.astype(bf16)
        act_out[:, cols] = act
        slope_out[:, cols] = slope.astype(bf16)
    total[...] = dot_rows(act_out[...], up_ref[...]).astype(bf16)

    for g in range(8):
        for ref, place in ((mine_out, me), (theirs_out, 1 - me)):
            part = total[pl.ds(pl.multiple_of(96 * g + 48 * place, 16), 48), :]
            for y in range(2):
                ref[y, g] = part[:, HALF * y : HALF * y + HALF]


def contract_kernel(
    me_ref, up_ref, slope_ref, second_ref, ff_ref,
    grad_out, hidden_out, mine_out, theirs_out,
    turned, w2,
):
    step = pl.program_id(0)
    me = me_ref[0]

    @pl.when(step == 0)
    def _():
        turned[...] = second_ref[...].T

    place_rows(w2, ff_ref)
    for i in range(3):
        cols = slice(256 * i, 256 * i + 256)
        grad = dot_lanes(up_ref[...], w2[cols, :]) * slope_ref[:, cols].astype(f32)
        grad = grad.astype(bf16)
        grad_out[:, cols] = grad
        hidden_out[:, cols] = jnp.sum(grad.astype(f32), axis=0, keepdims=True)

    def outer(ref):
        for i in range(3):
            cols = slice(256 * i, 256 * i + 256)
            ref[0, :, cols] = dot(turned[...], grad_out[:, cols]).astype(bf16)

    pl.when((step & 1) == me)(lambda: outer(mine_out))
    pl.when((step & 1) != me)(lambda: outer(theirs_out))


def middle_back_kernel(
    me_ref, vec_ref, inner_hbm, w1_hbm, soft_hbm, up_hbm, middle_hbm, wo_hbm, normed_hbm, mixed_hbm, qkv_hbm,
    mine_hbm, theirs_hbm, sums_out, grads_hbm, gm_hbm,
    inner_ref, w1_ref, soft_ref, up_ref, middle_ref, wo_ref, normed_ref, mixed_ref, qkv_ref,
    grad_second, gml, grad_mixed, normed_turned, mixed_turned, pieces, grads_ref, gm_ref, sems,
):
    me = me_ref[0]
    ahead = []
    for j in range(4):
        cols = pl.ds(D * j, D)
        ahead.append((inner_hbm.at[:, cols], inner_ref.at[j]))
        ahead.append((w1_hbm.at[:, cols], w1_ref.at[j]))
    ahead += [
        (middle_hbm, middle_ref), (up_hbm, up_ref), (wo_hbm, wo_ref),
        (normed_hbm, normed_ref), (mixed_hbm, mixed_ref), (qkv_hbm, qkv_ref),
    ]
    reads = [pltpu.make_async_copy(src, dst, sems.at[i]) for i, (src, dst) in enumerate(ahead)]

    def read_soft(i):
        return pltpu.make_async_copy(soft_hbm.at[i], soft_ref.at[i], sems.at[14 + i])

    grads_write = pltpu.make_async_copy(grads_ref, grads_hbm, sems.at[20])
    gm_write = pltpu.make_async_copy(gm_ref, gm_hbm, sems.at[21])

    def write(kind, act):
        cols = pl.ds(HALF * (kind % 2), HALF)
        for to, place in ((mine_hbm, kind // 2), (theirs_hbm, 1 - kind // 2)):
            copy = pltpu.make_async_copy(pieces.at[kind], to.at[:, :, cols], sems.at[22 + kind])
            pl.when(me == place)(lambda copy=copy: act(copy))

    def outer(kind, left, right):
        grad = dot(left[...], right[...]).astype(bf16)
        for y in range(2):
            pieces[kind, y] = grad[:, HALF * y : HALF * y + HALF]
        write(kind, lambda copy: copy.start())

    for read in reads:
        read.start()
    for i in range(6):
        read_soft(i).start()
    for j in range(4):
        reads[2 * j].wait()
        reads[2 * j + 1].wait()
        part = dot_lanes(inner_ref[j], w1_ref[j])
        if j == 0:
            grad_second[...] = part
        else:
            grad_second[...] += part
    for read in reads[8:]:
        read.wait()
    grad = grad_second[...]
    scaled, scale = norm_parts(middle_ref[...])
    up = up_ref[...].astype(f32)
    gm = up + norm_back(grad, scaled, scale, vec_ref[5:6, :])
    gm_ref[...] = gm
    gm_write.start()
    gml[...] = gm.astype(bf16)
    sums_out[2:3, :] = jnp.sum(gml[...].astype(f32), axis=0, keepdims=True)
    sums_out[3:4, :] = jnp.sum(grad * scaled, axis=0, keepdims=True)
    sums_out[4:5, :] = jnp.sum(grad, axis=0, keepdims=True)
    sums_out[5:6, :] = jnp.sum(up, axis=0, keepdims=True)
    grad_mixed[...] = dot_lanes(gml[...], wo_ref[...]).astype(bf16)
    mixed_turned[...] = mixed_ref[...].T
    outer(3, mixed_turned, gml)
    normed_turned[...] = normed_ref[...].T
    lane = iota((PAD, 128), 1)

    def attend(i, carry):
        cols = pl.ds(pl.multiple_of(128 * i, 128), 128)
        read_soft(i).wait()
        for image in range(IMAGES):
            rows = pl.ds(PAD * image, PAD)
            q = qkv_ref[0, rows, cols]
            k = qkv_ref[1, rows, cols]
            v = qkv_ref[2, rows, cols]
            g = grad_mixed[rows, cols]
            dq = dk = dv = jnp.zeros((PAD, 128), f32)
            for n in range(2):
                inside = (lane < HD) == (n == 0)
                zero = jnp.zeros_like(g)
                g_in = jnp.where(inside, g, zero)
                soft_low = soft_ref[i, 2 * image + n]
                soft = soft_low.astype(f32)
                grad_soft = dot_lanes(v, g_in)
                level = jnp.sum(grad_soft * soft, axis=0, keepdims=True)
                scores = (soft * (grad_soft - level)).astype(bf16)
                dv = dv + dot(soft_low, g_in)
                dk = dk + dot(scores, jnp.where(inside, q, zero))
                dq = dq + dot_rows(scores, jnp.where(inside, k, zero))
            grads_ref[0, rows, cols] = (dq * 0.125).astype(bf16)
            grads_ref[1, rows, cols] = (dk * 0.125).astype(bf16)
            grads_ref[2, rows, cols] = dv.astype(bf16)
        return carry

    lax.fori_loop(0, 6, attend, 0)
    grads_write.start()
    for kind in range(3):
        outer(kind, normed_turned, grads_ref.at[kind])
    sums_out[0:1, :] = jnp.sum(grads_ref[0].astype(f32), axis=0, keepdims=True)
    sums_out[1:2, :] = jnp.sum(grads_ref[2].astype(f32), axis=0, keepdims=True)
    grads_write.wait()
    gm_write.wait()
    for kind in range(4):
        write(kind, lambda copy: copy.wait())


def input_back_kernel(
    me_ref, vec_ref, grads_ref, w_ref, x_ref, gm_ref, keep_out, send_out, sums_out, total
):
    step = pl.program_id(0)
    part = dot_lanes(grads_ref[0], w_ref[0])

    @pl.when(step == 0)
    def _():
        total[...] = part

    @pl.when(step > 0)
    def _():
        total[...] += part

    @pl.when(step == 2)
    def _():
        grad = total[...]
        scaled, scale = norm_parts(x_ref[...].astype(f32))
        out = gm_ref[...] + norm_back(grad, scaled, scale, vec_ref[0:1, :])
        pack(out.astype(bf16), me_ref[1], keep_out, send_out)
        sums_out[0:1, :] = jnp.sum(grad * scaled, axis=0, keepdims=True)
        sums_out[1:2, :] = jnp.sum(grad, axis=0, keepdims=True)


def output_kernel(me_ref, vec_ref, middle_ref, act_ref, ff_ref, keep_out, send_out, w2, total):
    step = pl.program_id(0)
    place_rows(w2, ff_ref)
    part = dot(act_ref[...], w2[...])

    @pl.when(step == 0)
    def _():
        total[...] = middle_ref[...] + vec_ref[7:8, :] + part

    @pl.when(step > 0)
    def _():
        total[...] += part

    @pl.when(step == 3)
    def _():
        pack(total[...].astype(bf16), me_ref[1], keep_out, send_out)


def assemble_kernel(at_ref, *refs):
    out = refs[-1]
    step = pl.program_id(0)
    for r in range(4):
        pl.when(step == r)(lambda r=r: out.__setitem__(..., refs[r][...].reshape(out.shape)))


def blocks_sum_kernel(at_ref, *refs):
    ins, outs = refs[:-4], refs[-4:]
    step = pl.program_id(0)
    total = ins[0][...].astype(f32)
    for ref in ins[1:]:
        total = total + ref[...].astype(f32)
    total = total.astype(bf16)
    for r in range(4):
        pl.when(step == r)(lambda r=r: outs[r].__setitem__(..., total.reshape(outs[r].shape)))


def sum_kernel(a_ref, b_ref, c_ref, d_ref, out_ref):
    total = a_ref[...].astype(f32) + b_ref[...].astype(f32) + c_ref[...].astype(f32) + d_ref[...].astype(f32)
    out_ref[...] = total.astype(bf16)


def spread_kernel(a_ref, b_ref, c_ref, d_ref, vector_ref, out_ref):
    total = a_ref[...].astype(f32) + b_ref[...].astype(f32) + c_ref[...].astype(f32) + d_ref[...].astype(f32)
    total = total.reshape(2 * 192, D)
    for i in range(16):
        out_ref[i, :16, :] = vector_ref[...].astype(bf16)
        out_ref[i, 16:, :] = total[24 * i : 24 * i + 24].astype(bf16)


def last_sum_kernel(tiles_ref, out_ref):
    total = tiles_ref[0, 16:, :].astype(f32)
    for i in range(1, 16):
        total = total + tiles_ref[i, 16:, :].astype(f32)
    vector = tiles_ref[0, :16, :].astype(f32)
    for i in (2, 4, 6):
        vector = vector + tiles_ref[i, :16, :].astype(f32)
    out_ref[:16, :] = vector
    out_ref[16:, :] = total


def adamw_step(parameter, gradient, first_moment, second_moment, step_rate, decay_factor):
    first_new = beta_first * first_moment + (1.0 - beta_first) * gradient
    second_new = beta_second * second_moment + (1.0 - beta_second) * gradient * gradient
    first_hat = first_new / (1.0 - beta_first**STEP)
    second_hat = second_new / (1.0 - beta_second**STEP)
    updated = parameter - step_rate * (
        first_hat / (jnp.sqrt(second_hat) + adam_eps) + decay_factor * parameter
    )
    return second_new, updated


def ordered(me, own, got):
    return jnp.where(me == 0, own, got), jnp.where(me == 0, got, own)


def attention_step_kernel(
    me_ref, own_ref, got_ref, w_ref, m_ref, v_ref, vec_ref, vec_m_ref, vec_v_ref,
    grad_out, second_out, new_out, vec_grad_out, vec_second_out, vec_new_out,
):
    pieces = ordered(me_ref[0], own_ref[16:, :], got_ref[16:, :])
    l = iota((512, 512), 0)
    c = iota((512, 512), 1)
    pick = jnp.where(c == 4 * (l & 127) + (l >> 7), 1.0, 0.0)
    for b in range(3):
        kinds = [
            pieces[k // 2][:, HALF * (k % 2) + 128 * b : HALF * (k % 2) + 128 * b + 128]
            for k in range(4)
        ]
        grad_out[:, 512 * b : 512 * b + 512] = jnp.dot(
            jnp.concatenate(kinds, axis=1), pick, precision=lax.Precision.HIGHEST,
            preferred_element_type=f32,
        )
    second_out[...], new_out[...] = adamw_step(
        w_ref[...], grad_out[...], m_ref[...], v_ref[...], learn_rate, decay_rate
    )
    vector = own_ref[:12, :] + got_ref[:12, :]
    vec_grad_out[...] = jnp.where(me_ref[1] == 0, vector[:, :HALF], vector[:, HALF:])
    vec_second_out[...], vec_new_out[...] = adamw_step(
        vec_ref[...], vec_grad_out[...], vec_m_ref[...], vec_v_ref[...], vector_rate, 0.0
    )


def expand_step_kernel(me_ref, own_ref, got_ref, w_ref, m_ref, v_ref, grad_out, second_out, new_out):
    first, last = ordered(me_ref[0], own_ref[...], got_ref[...])
    grad_out[:, :D] = first
    grad_out[:, D:] = last
    second_out[...], new_out[...] = adamw_step(
        w_ref[...], grad_out[...], m_ref[...], v_ref[...], learn_rate, decay_rate
    )


def project_step_kernel(me_ref, own_ref, got_ref, w_ref, m_ref, v_ref, grad_out, second_out, new_out):
    first, last = ordered(me_ref[0], own_ref[...], got_ref[...])
    grad_out[...] = jnp.concatenate([first, last], axis=0).T
    second_out[...], new_out[...] = adamw_step(
        w_ref[...], grad_out[...], m_ref[...], v_ref[...], learn_rate, decay_rate
    )


def place(axes):
    at = 0
    for a in axes:
        at = at * lax.axis_size(a) + lax.axis_index(a)
    return at


def swap(x, axis):
    return lax.ppermute(x, axis, [(0, 1), (1, 0)])


def core_sum(mine, theirs):
    return (mine.astype(f32) + swap(theirs, "dp").astype(f32)).astype(bf16)


def assemble(parts, at, shape, piece, index, after=(), cost=0):
    flat = tuple(n for n in piece if n > 1)
    return pl.pallas_call(
        assemble_kernel,
        out_shape=jax.ShapeDtypeStruct(shape, bf16),
        grid_spec=pltpu.PrefetchScalarGridSpec(
            num_scalar_prefetch=1,
            grid=(4,),
            in_specs=[
                *(pl.BlockSpec(flat, lambda r, at: (0,) * len(flat)) for _ in range(4)),
                *(LEFT for _ in after),
            ],
            out_specs=pl.BlockSpec(piece, lambda r, at: index((at[0] + 3 * r) % 4)),
        ),
        compiler_params=pltpu.CompilerParams(vmem_limit_bytes=32 * 1024 * 1024),
        cost_estimate=pl.CostEstimate(flops=cost * 10**9 + 1000, bytes_accessed=0, transcendentals=0),
        name="assemble",
    )(at.reshape(1).astype(jnp.int32), *(p.reshape(flat) for p in parts), *after)


def ring_blocks(parts, at, shape, piece, index):
    spec = pl.BlockSpec(piece, lambda r, at: index((at[0] + r) % 4))
    flat = tuple(n for n in piece if n > 1)
    return pl.pallas_call(
        blocks_sum_kernel,
        out_shape=[jax.ShapeDtypeStruct(flat, bf16)] * 4,
        grid_spec=pltpu.PrefetchScalarGridSpec(
            num_scalar_prefetch=1,
            grid=(4,),
            in_specs=[spec] * len(parts),
            out_specs=[pl.BlockSpec(flat, lambda r, at: (0,) * len(flat))] * 4,
        ),
        compiler_params=pltpu.CompilerParams(vmem_limit_bytes=32 * 1024 * 1024),
        cost_estimate=pl.CostEstimate(flops=1000, bytes_accessed=0, transcendentals=0),
        name="ring_blocks",
    )(at.reshape(1).astype(jnp.int32), *(p.reshape(shape) for p in parts))


def hop(x, axes, r):
    return lax.ppermute(x, axes, [(i, (i + r) % 4) for i in range(4)])


def ring(blocks, axes):
    return blocks[0], *(hop(blocks[r], axes, r) for r in (1, 3, 2))


def crossed(x, axis, bit):
    return lax.ppermute(x, axis, [(i, i ^ bit) for i in range(lax.axis_size(axis))])


def to_all(x, axes):
    near, back = hop(x, axes, 1), hop(x, axes, 3)
    return x, near, hop(x, axes, 2), back


def sum_of(parts):
    total = parts[0].astype(f32)
    for part in parts[1:]:
        total = total + part.astype(f32)
    return total


def spread_sum(blocks, axes):
    tiles = lax.all_to_all(blocks, axes, 0, 0, tiled=True)
    return jnp.sum(tiles.astype(f32), axis=0)


def own_images(stored, gy):
    rows = stored.shape[0] // 2
    own = lax.dynamic_slice_in_dim(stored, rows * gy, rows, 0)
    other = lax.dynamic_slice_in_dim(stored, rows * (1 - gy), rows, 0)
    pad = ((0, PAD - rows), (0, 0))
    return jnp.pad(own, pad), jnp.pad(other, pad)


def stored_rows(keep, got, gy):
    first = jnp.where(gy == 0, keep, got)[:SEQ]
    last = jnp.where(gy == 0, got, keep)[:SEQ]
    return jnp.concatenate([first, last], axis=0).astype(f32)


def per_device(
    tokens,
    image_counts,
    slot_order,
    cotangent,
    attention_weights,
    attention_first,
    attention_second,
    expand_weight,
    expand_first,
    expand_second,
    project_weight,
    project_first,
    project_second,
    vectors,
    vector_first,
    vector_second,
):
    dp = lax.axis_index("dp")
    gy = lax.axis_index("xl")
    me = jnp.stack([dp, gy]).astype(jnp.int32)

    token_own, token_other = own_images(tokens, gy)
    token_got = swap(token_other, "xl")
    grad_own, grad_other = own_images(cotangent, gy)
    grad_got = swap(grad_other, "xl")
    vec_got = swap(vectors, "xl")
    attn_piece, ff_piece = call(
        prepare_kernel,
        [SCALARS, WHOLE, WHOLE, WHOLE],
        [((24, D), bf16, WHOLE), ((24, 2 * D), bf16, WHOLE)],
        (me, attention_weights, expand_weight, project_weight),
        name="prepare",
    )
    ff = lax.all_gather(ff_piece, EVERY).reshape(2, 32, 2, 24, 2 * D)
    at_x, at_y, at_z = place(X), place(Y), place(Z)

    def across_x(p):
        return p % 2, 0, p // 2, 0, 0

    attn = to_all(attn_piece, X)
    attn = assemble(attn, at_x, (2, 1, 2, 24, D), (1, 1, 1, 24, D), across_x)
    attn = to_all(attn.reshape(2, 48, D), Y)
    attn, token_got, vec_got = lax.optimization_barrier((attn, token_got, vec_got))
    attn = assemble(attn, at_y, (2, 4, 48, D), (2, 1, 48, D), lambda p: (0, p, 0, 0))
    vec_first, vec_last = ordered(gy, vectors, vec_got)
    vec = jnp.concatenate([vec_first, vec_last], axis=1)
    bias = vec[8:].T.reshape(1, FF)
    live = (slot_order[0] < image_counts[0]).astype(jnp.int32)
    live = lax.dynamic_slice_in_dim(live, IMAGES * gy, IMAGES)
    attn = to_all(attn.reshape(2, 192, D), Z)
    attn, vec, bias, live, token_own, token_got = lax.optimization_barrier(
        (attn, vec, bias, live, token_own, token_got)
    )
    attn = assemble(attn, at_z, (2, 4, 192, D), (2, 1, 192, D), lambda p: (0, p, 0, 0))
    w_own, w_got = (w.reshape(2, D, D) for w in (attn, swap(attn, "dp")))

    tall = block((ROWS, D), lambda j: (0, 0))
    wide = block((ROWS, D), lambda j: (0, j))
    w1_block = block((1, 32, 1, 24, D), lambda j: (j % 2, 0, j // 2, 0, 0))
    w2_block = block((2, 8, 2, 24, D), lambda j: (0, j, 0, 0, 1))
    pieces2 = block((2, 8, 48, HALF), lambda j: (0, j, 0, 0))
    soft_shape = (6, 2 * IMAGES, PAD, PAD)

    soft, mixed, x, normed, qkv, w_qkv, w_o = call(
        attend_kernel,
        [SCALARS, *(WHOLE,) * 5],
        [
            (soft_shape, bf16, block((1, *soft_shape[1:]), lambda p: (jnp.maximum(p - 1, 0), 0, 0, 0))),
            ((ROWS, D), bf16, block((ROWS, 128), lambda p: (0, jnp.maximum(p - 1, 0)))),
            ((ROWS, D), bf16, LEFT),
            ((ROWS, D), bf16, LEFT),
            ((3, ROWS, D), bf16, LEFT),
            ((3, D, D), bf16, LEFT),
            ((D, D), bf16, LEFT),
        ],
        (me, token_own, token_got, vec, w_own, w_got),
        grid=(7,),
        scratch=[
            pltpu.VMEM((ROWS, D), bf16),
            pltpu.VMEM((ROWS, D), bf16),
            pltpu.VMEM((3, ROWS, D), bf16),
            pltpu.VMEM((4, D, D), bf16),
            pltpu.SemaphoreType.DMA((5,)),
        ],
        name="attend",
    )

    up, middle, second = call(
        second_kernel,
        [SCALARS, SCALARS, *(WHOLE,) * 6],
        [((ROWS, D), bf16, WHOLE), ((ROWS, D), f32, WHOLE), ((ROWS, D), bf16, WHOLE)],
        (me, live, grad_own, grad_got, vec, x, mixed, w_o),
        name="second",
    )
    act, slope, mine2, theirs2, w1 = call(
        expand_kernel,
        [SCALARS, WHOLE, WHOLE, block((1, D), lambda j: (0, j)), w1_block],
        [
            ((ROWS, FF), bf16, wide),
            ((ROWS, FF), bf16, wide),
            ((2, 32, 48, HALF), bf16, pieces2),
            ((2, 32, 48, HALF), bf16, pieces2),
            ((D, FF), bf16, block((D, D), lambda j: (0, j))),
        ],
        (me, up, second, bias, ff),
        grid=(4,),
        scratch=[pltpu.VMEM((D, D), bf16)],
        after=(w_o, soft),
        name="expand",
    )
    inner_grad, hidden_sums, mine1, theirs1 = call(
        contract_kernel,
        [SCALARS, WHOLE, wide, WHOLE, w2_block],
        [
            ((ROWS, FF), bf16, wide),
            ((1, FF), f32, block((1, D), lambda j: (0, j))),
            ((2, D, D), bf16, block((1, D, D), lambda j: (j // 2, 0, 0))),
            ((2, D, D), bf16, block((1, D, D), lambda j: (j // 2, 0, 0))),
        ],
        (me, up, slope, second, ff),
        grid=(4,),
        scratch=[pltpu.VMEM((D, ROWS), bf16), pltpu.VMEM((D, D), bf16)],
        name="contract",
    )
    ring2 = ring_blocks(
        (mine2, swap(theirs2, "dp")),
        place(X),
        (2, 16, 2, 48, HALF),
        (1, 16, 1, 48, HALF),
        lambda p: (p % 2, 0, p // 2, 0, 0),
    )
    got1, _ = lax.optimization_barrier((swap(theirs1, "dp"), ring2[0]))
    ring1 = ring_blocks(
        (mine1, got1), place(Y), (8, 4, 48, D), (8, 1, 48, D), lambda p: (0, p, 0, 0)
    )

    mine0, theirs0, sums_c, grads, gm = call(
        middle_back_kernel,
        [SCALARS, WHOLE, *(LEFT,) * 9],
        [
            ((2, D, D), bf16, LEFT),
            ((2, D, D), bf16, LEFT),
            ((6, D), f32, WHOLE),
            ((3, ROWS, D), bf16, LEFT),
            ((ROWS, D), f32, LEFT),
        ],
        (me, vec, inner_grad, w1, soft, up, middle, w_o, normed, mixed, qkv),
        scratch=[
            pltpu.VMEM((4, ROWS, D), bf16),
            pltpu.VMEM((4, D, D), bf16),
            pltpu.VMEM(soft_shape, bf16),
            pltpu.VMEM((ROWS, D), bf16),
            pltpu.VMEM((ROWS, D), f32),
            pltpu.VMEM((D, D), bf16),
            pltpu.VMEM((ROWS, D), bf16),
            pltpu.VMEM((ROWS, D), bf16),
            pltpu.VMEM((3, ROWS, D), bf16),
            pltpu.VMEM((ROWS, D), f32),
            pltpu.VMEM((ROWS, D), bf16),
            pltpu.VMEM((ROWS, D), bf16),
            pltpu.VMEM((D, ROWS), bf16),
            pltpu.VMEM((D, ROWS), bf16),
            pltpu.VMEM((4, 2, D, HALF), bf16),
            pltpu.VMEM((3, ROWS, D), bf16),
            pltpu.VMEM((ROWS, D), f32),
            pltpu.SemaphoreType.DMA((26,)),
        ],
        after=(ring2[0], ring1[0]),
        cost=0,
        name="middle_back",
    )
    got0 = swap(theirs0, "dp")
    ring2 = ring(ring2, X)
    near1 = hop(ring1[1], Y, 1), hop(ring1[3], Y, 3)
    ring2, mine0 = lax.optimization_barrier((ring2, mine0))
    mine0, near1, far1 = lax.optimization_barrier((mine0, near1, ring1[2]))
    far1 = hop(far1, Y, 2)
    part2 = call(
        sum_kernel, [WHOLE] * 4, [((16, 48, HALF), bf16, WHOLE)], ring2, cost=100, after=(near1[0], near1[1]), name="part"
    )[0]
    tiles2 = lax.all_to_all(part2, Z + Y, 0, 0, tiled=True)
    mine0, got0, _ = lax.optimization_barrier((mine0, got0, part2))
    ring0 = ring_blocks(
        (mine0, got0), place(Z), (2, 4, 192, D), (2, 1, 192, D), lambda p: (0, p, 0, 0)
    )
    tiles2, far1, _ = lax.optimization_barrier((tiles2, far1, ring0[0]))
    own0, near0, back0, far0 = ring(ring0, Z)
    keep_in, send_in, sums_e = call(
        input_back_kernel,
        [
            SCALARS, WHOLE,
            block((1, ROWS, D), lambda k: (k, 0, 0)), block((1, D, D), lambda k: (k, 0, 0)),
            WHOLE, WHOLE,
        ],
        [
            ((PAD, D), bf16, block((PAD, D), lambda k: (0, 0))),
            ((PAD, D), bf16, block((PAD, D), lambda k: (0, 0))),
            ((2, D), f32, block((2, D), lambda k: (0, 0))),
        ],
        (me, vec, grads, w_qkv, x, gm),
        grid=(3,),
        scratch=[pltpu.VMEM((ROWS, D), f32)],
        cost=100,
        after=(ring0[0],),
        name="input_back",
    )
    sums_e, hidden_sums = lax.optimization_barrier((sums_e, hidden_sums))
    vector = jnp.concatenate(
        [sums_e, sums_c, hidden_sums.reshape(D, 4).T, jnp.zeros((4, D), f32)], axis=0
    ).astype(bf16)

    def spread(parts, vector, cost, name):
        return call(
            spread_kernel, [WHOLE] * 5, [((16, 40, D), bf16, WHOLE)], (*parts, vector), cost=cost, name=name
        )[0]

    far1, tiles2, near0, back0, vector = lax.optimization_barrier((far1, tiles2, near0, back0, vector))
    part1 = spread((ring1[0], *near1, far1), vector, 0, "spread")
    tiles1 = lax.all_to_all(part1, ("xl", "z", "xh"), 0, 0, tiled=True)
    keep_out, send_out = call(
        output_kernel,
        [SCALARS, WHOLE, WHOLE, wide, w2_block],
        [((PAD, D), bf16, block((PAD, D), lambda j: (0, 0)))] * 2,
        (me, vec, middle, act, ff),
        grid=(4,),
        scratch=[pltpu.VMEM((D, D), bf16), pltpu.VMEM((ROWS, D), f32)],
        after=(part1,),
        cost=0,
        name="output",
    )
    got_in, got_out = swap(send_in, "xl"), swap(send_out, "xl")
    tiles1, _ = lax.optimization_barrier((tiles1, keep_out))
    sum1 = jnp.sum(tiles1.astype(f32), axis=0)
    sum1, got_in = lax.optimization_barrier((sum1, got_in))
    part0 = spread((own0, near0, back0, far0), sum1[:16], 100, "last_spread")
    tiles0 = lax.all_to_all(part0, ("xl", "y", "xh"), 0, 0, tiled=True)
    tiles2, _ = lax.optimization_barrier((tiles2, part0))
    sum2 = jnp.sum(tiles2.astype(f32), axis=0)
    got2 = swap(sum2, "dp")
    sum1 = sum1[16:]
    got1 = swap(sum1, "dp")
    block_out = stored_rows(keep_out, got_out, gy)
    input_grad = stored_rows(keep_in, got_in, gy)

    def step(body, own, got, shape, state, outs=(), cost=0, name=None):
        state = (me, own, got, *state)
        outs = [(shape, f32, WHOLE)] * 3 + [(o, f32, WHOLE) for o in outs]
        return call(body, [SCALARS, *(WHOLE,) * (len(state) - 1)], outs, state, cost=cost, name=name)

    project = step(
        project_step_kernel, sum2, got2, (HALF, 96),
        (project_weight, project_first, project_second), name="project_step",
    )
    expand = step(
        expand_step_kernel, sum1, got1, (24, 2 * D),
        (expand_weight, expand_first, expand_second), name="expand_step",
    )
    tiles0, project = lax.optimization_barrier((tiles0, project))
    sum0 = call(last_sum_kernel, [WHOLE], [((40, D), f32, WHOLE)], (tiles0,), cost=0, name="last_sum")[0]
    got0 = swap(sum0, "dp")
    *attention, vector_grad, vector_second_new, vector_new = step(
        attention_step_kernel, sum0, got0, (24, 2 * D),
        (attention_weights, attention_first, attention_second, vectors, vector_first, vector_second),
        [(12, HALF)] * 3, name="attention_step",
    )
    return (
        block_out,
        input_grad,
        *attention,
        *expand,
        *project,
        vector_grad,
        vector_second_new,
        vector_new,
    )


def solution(mesh):
    fine = Mesh(mesh.devices.reshape(2, 4, 4, 2, 2), EVERY)
    rows = ("dp", "z", "y", "xh")
    deep = ("z", "y", "xh")
    placed = (
        P(rows, "xl"),
        P("dp"),
        P("dp", deep),
        P(rows, "xl"),
        *(P(deep, "xl"),) * 6,
        *(P("xl", deep),) * 3,
        *(P(None, "xl"),) * 3,
    )
    out = (
        P(rows, "xl"),
        P(rows, "xl"),
        *(P(deep, "xl"),) * 6,
        *(P("xl", deep),) * 3,
        *(P(None, "xl"),) * 3,
    )
    return jax.shard_map(per_device, mesh=fine, in_specs=placed, out_specs=out, check_vma=False)
```

```python
import jax
import jax.numpy as jnp
from jax import lax
from jax.experimental import pallas as pl
from jax.experimental.pallas import tpu as pltpu
from jax.sharding import Mesh
from jax.sharding import PartitionSpec as P

D = 768
HD = 64
FF = 3072
SEQ = 197
STEP = 10
PAD = 208
IMAGES = 2
ROWS = PAD * IMAGES
HALF = D // 2

norm_eps = 1e-06
beta_first = 0.9
beta_second = 0.999
learn_rate = 0.04
vector_rate = 0.25
decay_rate = 0.05
adam_eps = 1e-08

f32 = jnp.float32
bf16 = jnp.bfloat16

DP = ("dp",)
Z = ("z",)
Y = ("y",)
X = ("xh", "xl")
CHIPS = ("xl", "z", "y", "xh")
EVERY = ("dp", "z", "y", "xh", "xl")


def dot(a, b):
    return lax.dot_general(a, b, (((1,), (0,)), ((), ())), preferred_element_type=f32)


def dot_rows(a, b):
    return lax.dot_general(a, b, (((0,), (0,)), ((), ())), preferred_element_type=f32)


def dot_lanes(a, b):
    return lax.dot_general(a, b, (((1,), (1,)), ((), ())), preferred_element_type=f32)


def block(shape, index):
    return pl.BlockSpec(shape, index)


WHOLE = pl.BlockSpec(memory_space=pltpu.VMEM)
SCALARS = pl.BlockSpec(memory_space=pltpu.SMEM)
LEFT = pl.BlockSpec(memory_space=pl.ANY)


def call(body, ins, outs, args, grid=(), scratch=(), after=(), cost=10, prefetch=0, name=None):
    count = len(args)

    def run(*refs):
        body(*refs[:count], *refs[count + len(after) :])

    return pl.pallas_call(
        run if after else body,
        out_shape=[jax.ShapeDtypeStruct(s, t) for s, t, _ in outs],
        grid_spec=pltpu.PrefetchScalarGridSpec(
            num_scalar_prefetch=prefetch,
            grid=grid,
            in_specs=[*ins, *(LEFT for _ in after)],
            out_specs=[spec for _, _, spec in outs],
            scratch_shapes=list(scratch),
        ),
        compiler_params=pltpu.CompilerParams(vmem_limit_bytes=52 * 1024 * 1024),
        cost_estimate=pl.CostEstimate(flops=cost * 10**9 + 1000, bytes_accessed=0, transcendentals=0),
        name=name,
    )(*args, *after)


def iota(shape, dim):
    return lax.broadcasted_iota(jnp.int32, shape, dim)


def row_picks():
    r = iota((ROWS, PAD), 0)
    j = iota((ROWS, PAD), 1)
    second = r >= PAD
    s = jnp.where(second, r - PAD, r)
    t = jnp.where(second, s + SEQ, s)
    live = s < SEQ
    even = jnp.where(live & (t == 2 * j), 1.0, 0.0).astype(bf16)
    odd = jnp.where(live & (t == 2 * j + 1), 1.0, 0.0).astype(bf16)
    return even, odd


def row_picks_back():
    r = iota((PAD, ROWS), 1)
    j = iota((PAD, ROWS), 0)
    second = r >= PAD
    s = jnp.where(second, r - PAD, r)
    t = jnp.where(second, s + SEQ, s)
    live = s < SEQ
    even = jnp.where(live & (t == 2 * j), 1.0, 0.0).astype(bf16)
    odd = jnp.where(live & (t == 2 * j + 1), 1.0, 0.0).astype(bf16)
    return even, odd


def lane_split():
    l = iota((256, 256), 0)
    c = iota((256, 256), 1)
    target = jnp.where(c < 128, 2 * c, 2 * (c - 128) + 1)
    return jnp.where(l == target, 1.0, 0.0).astype(bf16)


def lane_join():
    l = iota((256, 256), 1)
    c = iota((256, 256), 0)
    target = jnp.where(c < 128, 2 * c, 2 * (c - 128) + 1)
    return jnp.where(l == target, 1.0, 0.0).astype(bf16)


def unpack(own_ref, got_ref, gy):
    own, got = own_ref[...], got_ref[...]
    first = jnp.where(gy == 0, own.astype(f32), got.astype(f32)).astype(bf16)
    last = jnp.where(gy == 0, got.astype(f32), own.astype(f32)).astype(bf16)
    split = lane_split()
    evens, odds = [], []
    for half in (first, last):
        for b in range(3):
            both = dot(half[:, 256 * b : 256 * b + 256], split).astype(bf16)
            evens.append(both[:, :128])
            odds.append(both[:, 128:])
    even_rows, odd_rows = row_picks()
    return dot(even_rows, jnp.concatenate(evens, axis=1)) + dot(odd_rows, jnp.concatenate(odds, axis=1))


def pack(rows_low, gy, keep_ref, send_ref):
    even_rows, odd_rows = row_picks_back()
    even = dot(even_rows, rows_low).astype(bf16)
    odd = dot(odd_rows, rows_low).astype(bf16)
    join = lane_join()
    for b in range(3):
        blocks = []
        for half in range(2):
            at = HALF * half + 128 * b
            both = jnp.concatenate([even[:, at : at + 128], odd[:, at : at + 128]], axis=1)
            blocks.append(dot(both, join))
        keep_ref[:, 256 * b : 256 * b + 256] = jnp.where(gy == 0, blocks[0], blocks[1]).astype(bf16)
        send_ref[:, 256 * b : 256 * b + 256] = jnp.where(gy == 0, blocks[1], blocks[0]).astype(bf16)


def norm_parts(v):
    center = jnp.mean(v, axis=1, keepdims=True)
    away = v - center
    scale = lax.rsqrt(jnp.mean(away * away, axis=1, keepdims=True) + norm_eps)
    return away * scale, scale


def norm_back(grad, scaled, scale, gain):
    pushed = grad * gain
    first = jnp.mean(pushed, axis=1, keepdims=True)
    cross = jnp.mean(pushed * scaled, axis=1, keepdims=True)
    return (pushed - first - scaled * cross) * scale


def prepare_kernel(me_ref, attn_ref, expand_ref, project_ref, attn_out, ff_out):
    me = me_ref[0]
    l = iota((512, 256), 0)
    c = iota((512, 256), 1)
    kind = 2 * me + jnp.where(c < 128, 0, 1)
    pick = jnp.where(l == 4 * (c & 127) + kind, 1.0, 0.0).astype(bf16)
    for b in range(3):
        both = dot(attn_ref[:, 512 * b : 512 * b + 512].astype(bf16), pick).astype(bf16)
        attn_out[:, 128 * b : 128 * b + 128] = both[:, :128]
        attn_out[:, HALF + 128 * b : HALF + 128 * b + 128] = both[:, 128:]
    ff_out[:, :D] = jnp.where(me == 0, expand_ref[:, :D], expand_ref[:, D:]).astype(bf16)
    turned = project_ref[...].T
    mine = jnp.where(me == 0, turned[:48], turned[48:])
    ff_out[:, D : D + HALF] = mine[:24].astype(bf16)
    ff_out[:, D + HALF :] = mine[24:].astype(bf16)


def attend_kernel(
    me_ref, own_ref, got_ref, vec_ref, w_own, w_got,
    soft_out, mixed_out, x_out, normed_out, qkv_out, w_out, wo_out,
    x_ref, normed_ref, qkv_ref, w_ref, sems,
):
    step = pl.program_id(0)
    copies = [
        pltpu.make_async_copy(x_ref, x_out, sems.at[0]),
        pltpu.make_async_copy(normed_ref, normed_out, sems.at[1]),
        pltpu.make_async_copy(qkv_ref, qkv_out, sems.at[2]),
        pltpu.make_async_copy(w_ref.at[pl.ds(0, 3)], w_out, sems.at[3]),
        pltpu.make_async_copy(w_ref.at[3], wo_out, sems.at[4]),
    ]

    @pl.when(step == 0)
    def _():
        me, gy = me_ref[0], me_ref[1]
        for ref, place in ((w_own, me), (w_got, 1 - me)):
            for half in range(2):
                for y in range(2):
                    w_ref[pl.ds(2 * place + half, 1), :, HALF * y : HALF * y + HALF] = ref[
                        y, :, HALF * half : HALF * half + HALF
                    ][None]
        copies[3].start()
        copies[4].start()
        x_ref[...] = unpack(own_ref, got_ref, gy).astype(bf16)
        copies[0].start()
        scaled, _ = norm_parts(x_ref[...].astype(f32))
        normed_ref[...] = (scaled * vec_ref[0:1, :] + vec_ref[1:2, :]).astype(bf16)
        copies[1].start()

        def project(i, carry):
            cols = pl.ds(pl.multiple_of(256 * i, 256), 256)
            for kind, row in ((0, 2), (1, None), (2, 3)):
                part = dot(normed_ref[...], w_ref[kind, :, cols])
                if row is not None:
                    part = part + vec_ref[row : row + 1, cols]
                qkv_ref[kind, :, cols] = part.astype(bf16)
            return carry

        lax.fori_loop(0, 3, project, 0)
        copies[2].start()

    @pl.when(step > 0)
    def _():
        cols = pl.ds(pl.multiple_of(128 * (step - 1), 128), 128)
        lane = iota((PAD, 128), 1)
        key_live = iota((PAD, PAD), 0) < SEQ
        for image in range(IMAGES):
            rows = pl.ds(PAD * image, PAD)
            q = qkv_ref[0, rows, cols] * jnp.asarray(0.125, bf16)
            k = qkv_ref[1, rows, cols]
            v = qkv_ref[2, rows, cols]
            total = None
            for n in range(2):
                inside = (lane < HD) == (n == 0)
                scores = dot_lanes(k, jnp.where(inside, q, jnp.zeros_like(q)))
                scores = jnp.where(key_live, scores, -1e30)
                terms = jnp.exp(scores - jnp.max(scores, axis=0, keepdims=True))
                soft = terms * (1.0 / jnp.sum(terms, axis=0, keepdims=True))
                soft = soft.astype(bf16)
                soft_out[0, 2 * image + n] = soft
                part = dot_rows(soft, jnp.where(inside, v, jnp.zeros_like(v)))
                total = part if total is None else total + part
            mixed_out[rows, :] = total.astype(bf16)

    @pl.when(step == 6)
    def _():
        for copy in copies:
            copy.wait()


def gelu_parts(v):
    below = 0.5 + 0.5 * lax.erf(v * 0.7071067811865476)
    return v * below, below + v * jnp.exp(-0.5 * v * v) * 0.3989422804014327


def gather_rows(first, last):
    return jnp.concatenate([first.astype(f32), last.astype(f32)], axis=0).astype(bf16)


def place_rows(w2, ff_ref):
    for d in range(2):
        for g in range(8):
            for y in range(2):
                piece = ff_ref[d, g, y]
                rows = slice(96 * g + 48 * d, 96 * g + 48 * d + 48)
                w2[rows, HALF * y : HALF * y + HALF] = gather_rows(piece[:, :HALF], piece[:, HALF:])


def second_kernel(
    me_ref, live_ref, own_ref, got_ref, vec_ref, x_ref, mixed_ref, wo_ref,
    up_out, middle_out, second_out,
):
    up = unpack(own_ref, got_ref, me_ref[1])
    image = jnp.where(iota((ROWS, 1), 0) < PAD, live_ref[0], live_ref[1])
    up_out[...] = jnp.where(image == 1, up, 0.0).astype(bf16)
    middle = x_ref[...].astype(f32) + dot(mixed_ref[...], wo_ref[...]) + vec_ref[4:5, :]
    middle_out[...] = middle
    scaled, _ = norm_parts(middle)
    second_out[...] = (scaled * vec_ref[5:6, :] + vec_ref[6:7, :]).astype(bf16)


def expand_kernel(
    me_ref, up_ref, second_ref, bias_ref, w1_ref,
    act_out, slope_out, mine_out, theirs_out, w1_out,
    total,
):
    me = me_ref[0]
    for pair in range(16):
        w1_out[48 * pair : 48 * pair + 48, :] = gather_rows(
            w1_ref[0, 2 * pair, 0], w1_ref[0, 2 * pair + 1, 0]
        )

    for i in range(3):
        cols = slice(256 * i, 256 * i + 256)
        inner = dot(second_ref[...], w1_out[:, cols]) + bias_ref[:, cols]
        act, slope = gelu_parts(inner)
        act = act.astype(bf16)
        act_out[:, cols] = act
        slope_out[:, cols] = slope.astype(bf16)
    total[...] = dot_rows(act_out[...], up_ref[...]).astype(bf16)

    for g in range(8):
        for ref, place in ((mine_out, me), (theirs_out, 1 - me)):
            part = total[pl.ds(pl.multiple_of(96 * g + 48 * place, 16), 48), :]
            for y in range(2):
                ref[y, g] = part[:, HALF * y : HALF * y + HALF]


def contract_kernel(
    me_ref, up_ref, slope_ref, second_ref, ff_ref,
    grad_out, hidden_out, mine_out, theirs_out,
    turned, w2,
):
    step = pl.program_id(0)
    me = me_ref[0]

    @pl.when(step == 0)
    def _():
        turned[...] = second_ref[...].T

    place_rows(w2, ff_ref)
    for i in range(3):
        cols = slice(256 * i, 256 * i + 256)
        grad = dot_lanes(up_ref[...], w2[cols, :]) * slope_ref[:, cols].astype(f32)
        grad = grad.astype(bf16)
        grad_out[:, cols] = grad
        hidden_out[:, cols] = jnp.sum(grad.astype(f32), axis=0, keepdims=True)

    def outer(ref):
        for i in range(3):
            cols = slice(256 * i, 256 * i + 256)
            ref[0, :, cols] = dot(turned[...], grad_out[:, cols]).astype(bf16)

    pl.when((step & 1) == me)(lambda: outer(mine_out))
    pl.when((step & 1) != me)(lambda: outer(theirs_out))


def middle_back_kernel(
    me_ref, vec_ref, inner_hbm, w1_hbm, soft_hbm, up_hbm, middle_hbm, wo_hbm, normed_hbm, mixed_hbm, qkv_hbm,
    mine_hbm, theirs_hbm, sums_out, grads_hbm, gm_hbm,
    inner_ref, w1_ref, soft_ref, up_ref, middle_ref, wo_ref, normed_ref, mixed_ref, qkv_ref,
    grad_second, gml, grad_mixed, normed_turned, mixed_turned, pieces, grads_ref, gm_ref, sems,
):
    me = me_ref[0]
    ahead = []
    for j in range(4):
        cols = pl.ds(D * j, D)
        ahead.append((inner_hbm.at[:, cols], inner_ref.at[j]))
        ahead.append((w1_hbm.at[:, cols], w1_ref.at[j]))
    ahead += [
        (middle_hbm, middle_ref), (up_hbm, up_ref), (wo_hbm, wo_ref),
        (normed_hbm, normed_ref), (mixed_hbm, mixed_ref), (qkv_hbm, qkv_ref),
    ]
    reads = [pltpu.make_async_copy(src, dst, sems.at[i]) for i, (src, dst) in enumerate(ahead)]

    def read_soft(i):
        return pltpu.make_async_copy(soft_hbm.at[i], soft_ref.at[i], sems.at[14 + i])

    grads_write = pltpu.make_async_copy(grads_ref, grads_hbm, sems.at[20])
    gm_write = pltpu.make_async_copy(gm_ref, gm_hbm, sems.at[21])

    def write(kind, act):
        cols = pl.ds(HALF * (kind % 2), HALF)
        for to, place in ((mine_hbm, kind // 2), (theirs_hbm, 1 - kind // 2)):
            copy = pltpu.make_async_copy(pieces.at[kind], to.at[:, :, cols], sems.at[22 + kind])
            pl.when(me == place)(lambda copy=copy: act(copy))

    def outer(kind, left, right):
        grad = dot(left[...], right[...]).astype(bf16)
        for y in range(2):
            pieces[kind, y] = grad[:, HALF * y : HALF * y + HALF]
        write(kind, lambda copy: copy.start())

    for read in reads:
        read.start()
    for i in range(6):
        read_soft(i).start()
    for j in range(4):
        reads[2 * j].wait()
        reads[2 * j + 1].wait()
        part = dot_lanes(inner_ref[j], w1_ref[j])
        if j == 0:
            grad_second[...] = part
        else:
            grad_second[...] += part
    for read in reads[8:]:
        read.wait()
    grad = grad_second[...]
    scaled, scale = norm_parts(middle_ref[...])
    up = up_ref[...].astype(f32)
    gm = up + norm_back(grad, scaled, scale, vec_ref[5:6, :])
    gm_ref[...] = gm
    gm_write.start()
    gml[...] = gm.astype(bf16)
    sums_out[2:3, :] = jnp.sum(gml[...].astype(f32), axis=0, keepdims=True)
    sums_out[3:4, :] = jnp.sum(grad * scaled, axis=0, keepdims=True)
    sums_out[4:5, :] = jnp.sum(grad, axis=0, keepdims=True)
    sums_out[5:6, :] = jnp.sum(up, axis=0, keepdims=True)
    grad_mixed[...] = dot_lanes(gml[...], wo_ref[...]).astype(bf16)
    mixed_turned[...] = mixed_ref[...].T
    outer(3, mixed_turned, gml)
    normed_turned[...] = normed_ref[...].T
    lane = iota((PAD, 128), 1)

    def attend(i, carry):
        cols = pl.ds(pl.multiple_of(128 * i, 128), 128)
        read_soft(i).wait()
        for image in range(IMAGES):
            rows = pl.ds(PAD * image, PAD)
            q = qkv_ref[0, rows, cols]
            k = qkv_ref[1, rows, cols]
            v = qkv_ref[2, rows, cols]
            g = grad_mixed[rows, cols]
            dq = dk = dv = jnp.zeros((PAD, 128), f32)
            for n in range(2):
                inside = (lane < HD) == (n == 0)
                zero = jnp.zeros_like(g)
                g_in = jnp.where(inside, g, zero)
                soft_low = soft_ref[i, 2 * image + n]
                soft = soft_low.astype(f32)
                grad_soft = dot_lanes(v, g_in)
                level = jnp.sum(grad_soft * soft, axis=0, keepdims=True)
                scores = (soft * (grad_soft - level)).astype(bf16)
                dv = dv + dot(soft_low, g_in)
                dk = dk + dot(scores, jnp.where(inside, q, zero))
                dq = dq + dot_rows(scores, jnp.where(inside, k, zero))
            grads_ref[0, rows, cols] = (dq * 0.125).astype(bf16)
            grads_ref[1, rows, cols] = (dk * 0.125).astype(bf16)
            grads_ref[2, rows, cols] = dv.astype(bf16)
        return carry

    lax.fori_loop(0, 6, attend, 0)
    grads_write.start()
    for kind in range(3):
        outer(kind, normed_turned, grads_ref.at[kind])
    sums_out[0:1, :] = jnp.sum(grads_ref[0].astype(f32), axis=0, keepdims=True)
    sums_out[1:2, :] = jnp.sum(grads_ref[2].astype(f32), axis=0, keepdims=True)
    grads_write.wait()
    gm_write.wait()
    for kind in range(4):
        write(kind, lambda copy: copy.wait())


def input_back_kernel(
    me_ref, vec_ref, grads_ref, w_ref, x_ref, gm_ref, keep_out, send_out, sums_out, total
):
    step = pl.program_id(0)
    part = dot_lanes(grads_ref[0], w_ref[0])

    @pl.when(step == 0)
    def _():
        total[...] = part

    @pl.when(step > 0)
    def _():
        total[...] += part

    @pl.when(step == 2)
    def _():
        grad = total[...]
        scaled, scale = norm_parts(x_ref[...].astype(f32))
        out = gm_ref[...] + norm_back(grad, scaled, scale, vec_ref[0:1, :])
        pack(out.astype(bf16), me_ref[1], keep_out, send_out)
        sums_out[0:1, :] = jnp.sum(grad * scaled, axis=0, keepdims=True)
        sums_out[1:2, :] = jnp.sum(grad, axis=0, keepdims=True)


def output_kernel(me_ref, vec_ref, middle_ref, act_ref, ff_ref, keep_out, send_out, w2, total):
    step = pl.program_id(0)
    place_rows(w2, ff_ref)
    part = dot(act_ref[...], w2[...])

    @pl.when(step == 0)
    def _():
        total[...] = middle_ref[...] + vec_ref[7:8, :] + part

    @pl.when(step > 0)
    def _():
        total[...] += part

    @pl.when(step == 3)
    def _():
        pack(total[...].astype(bf16), me_ref[1], keep_out, send_out)


def assemble_kernel(at_ref, *refs):
    out = refs[-1]
    step = pl.program_id(0)
    for r in range(4):
        pl.when(step == r)(lambda r=r: out.__setitem__(..., refs[r][...].reshape(out.shape)))


def blocks_sum_kernel(at_ref, *refs):
    ins, outs = refs[:-4], refs[-4:]
    step = pl.program_id(0)
    total = ins[0][...].astype(f32)
    for ref in ins[1:]:
        total = total + ref[...].astype(f32)
    total = total.astype(bf16)
    for r in range(4):
        pl.when(step == r)(lambda r=r: outs[r].__setitem__(..., total.reshape(outs[r].shape)))


def sum_kernel(a_ref, b_ref, c_ref, d_ref, out_ref):
    total = a_ref[...].astype(f32) + b_ref[...].astype(f32) + c_ref[...].astype(f32) + d_ref[...].astype(f32)
    out_ref[...] = total.astype(bf16)


def spread_kernel(a_ref, b_ref, c_ref, d_ref, vector_ref, out_ref):
    total = a_ref[...].astype(f32) + b_ref[...].astype(f32) + c_ref[...].astype(f32) + d_ref[...].astype(f32)
    total = total.reshape(2 * 192, D)
    for i in range(16):
        out_ref[i, :16, :] = vector_ref[...].astype(bf16)
        out_ref[i, 16:, :] = total[24 * i : 24 * i + 24].astype(bf16)


def last_sum_kernel(tiles_ref, out_ref):
    total = tiles_ref[0, 16:, :].astype(f32)
    for i in range(1, 16):
        total = total + tiles_ref[i, 16:, :].astype(f32)
    vector = tiles_ref[0, :16, :].astype(f32)
    for i in (2, 4, 6):
        vector = vector + tiles_ref[i, :16, :].astype(f32)
    out_ref[:16, :] = vector
    out_ref[16:, :] = total


def adamw_step(parameter, gradient, first_moment, second_moment, step_rate, decay_factor):
    first_new = beta_first * first_moment + (1.0 - beta_first) * gradient
    second_new = beta_second * second_moment + (1.0 - beta_second) * gradient * gradient
    first_hat = first_new / (1.0 - beta_first**STEP)
    second_hat = second_new / (1.0 - beta_second**STEP)
    updated = parameter - step_rate * (
        first_hat / (jnp.sqrt(second_hat) + adam_eps) + decay_factor * parameter
    )
    return second_new, updated


def ordered(me, own, got):
    return jnp.where(me == 0, own, got), jnp.where(me == 0, got, own)


def attention_step_kernel(
    me_ref, own_ref, got_ref, w_ref, m_ref, v_ref, vec_ref, vec_m_ref, vec_v_ref,
    grad_out, second_out, new_out, vec_grad_out, vec_second_out, vec_new_out,
):
    pieces = ordered(me_ref[0], own_ref[16:, :], got_ref[16:, :])
    l = iota((512, 512), 0)
    c = iota((512, 512), 1)
    pick = jnp.where(c == 4 * (l & 127) + (l >> 7), 1.0, 0.0)
    for b in range(3):
        kinds = [
            pieces[k // 2][:, HALF * (k % 2) + 128 * b : HALF * (k % 2) + 128 * b + 128]
            for k in range(4)
        ]
        grad_out[:, 512 * b : 512 * b + 512] = jnp.dot(
            jnp.concatenate(kinds, axis=1), pick, precision=lax.Precision.HIGHEST,
            preferred_element_type=f32,
        )
    second_out[...], new_out[...] = adamw_step(
        w_ref[...], grad_out[...], m_ref[...], v_ref[...], learn_rate, decay_rate
    )
    vector = own_ref[:12, :] + got_ref[:12, :]
    vec_grad_out[...] = jnp.where(me_ref[1] == 0, vector[:, :HALF], vector[:, HALF:])
    vec_second_out[...], vec_new_out[...] = adamw_step(
        vec_ref[...], vec_grad_out[...], vec_m_ref[...], vec_v_ref[...], vector_rate, 0.0
    )


def expand_step_kernel(me_ref, own_ref, got_ref, w_ref, m_ref, v_ref, grad_out, second_out, new_out):
    first, last = ordered(me_ref[0], own_ref[...], got_ref[...])
    grad_out[:, :D] = first
    grad_out[:, D:] = last
    second_out[...], new_out[...] = adamw_step(
        w_ref[...], grad_out[...], m_ref[...], v_ref[...], learn_rate, decay_rate
    )


def project_step_kernel(me_ref, own_ref, got_ref, w_ref, m_ref, v_ref, grad_out, second_out, new_out):
    first, last = ordered(me_ref[0], own_ref[...], got_ref[...])
    grad_out[...] = jnp.concatenate([first, last], axis=0).T
    second_out[...], new_out[...] = adamw_step(
        w_ref[...], grad_out[...], m_ref[...], v_ref[...], learn_rate, decay_rate
    )


def place(axes):
    at = 0
    for a in axes:
        at = at * lax.axis_size(a) + lax.axis_index(a)
    return at


def swap(x, axis):
    return lax.ppermute(x, axis, [(0, 1), (1, 0)])


def core_sum(mine, theirs):
    return (mine.astype(f32) + swap(theirs, "dp").astype(f32)).astype(bf16)


def assemble(parts, at, shape, piece, index, after=(), cost=0):
    flat = tuple(n for n in piece if n > 1)
    return pl.pallas_call(
        assemble_kernel,
        out_shape=jax.ShapeDtypeStruct(shape, bf16),
        grid_spec=pltpu.PrefetchScalarGridSpec(
            num_scalar_prefetch=1,
            grid=(4,),
            in_specs=[
                *(pl.BlockSpec(flat, lambda r, at: (0,) * len(flat)) for _ in range(4)),
                *(LEFT for _ in after),
            ],
            out_specs=pl.BlockSpec(piece, lambda r, at: index((at[0] + 3 * r) % 4)),
        ),
        compiler_params=pltpu.CompilerParams(vmem_limit_bytes=32 * 1024 * 1024),
        cost_estimate=pl.CostEstimate(flops=cost * 10**9 + 1000, bytes_accessed=0, transcendentals=0),
        name="assemble",
    )(at.reshape(1).astype(jnp.int32), *(p.reshape(flat) for p in parts), *after)


def ring_blocks(parts, at, shape, piece, index):
    spec = pl.BlockSpec(piece, lambda r, at: index((at[0] + r) % 4))
    flat = tuple(n for n in piece if n > 1)
    return pl.pallas_call(
        blocks_sum_kernel,
        out_shape=[jax.ShapeDtypeStruct(flat, bf16)] * 4,
        grid_spec=pltpu.PrefetchScalarGridSpec(
            num_scalar_prefetch=1,
            grid=(4,),
            in_specs=[spec] * len(parts),
            out_specs=[pl.BlockSpec(flat, lambda r, at: (0,) * len(flat))] * 4,
        ),
        compiler_params=pltpu.CompilerParams(vmem_limit_bytes=32 * 1024 * 1024),
        cost_estimate=pl.CostEstimate(flops=1000, bytes_accessed=0, transcendentals=0),
        name="ring_blocks",
    )(at.reshape(1).astype(jnp.int32), *(p.reshape(shape) for p in parts))


def hop(x, axes, r):
    return lax.ppermute(x, axes, [(i, (i + r) % 4) for i in range(4)])


def ring(blocks, axes):
    return blocks[0], *(hop(blocks[r], axes, r) for r in (1, 3, 2))


def crossed(x, axis, bit):
    return lax.ppermute(x, axis, [(i, i ^ bit) for i in range(lax.axis_size(axis))])


def to_all(x, axes):
    near, back = hop(x, axes, 1), hop(x, axes, 3)
    return x, near, hop(x, axes, 2), back


def sum_of(parts):
    total = parts[0].astype(f32)
    for part in parts[1:]:
        total = total + part.astype(f32)
    return total


def spread_sum(blocks, axes):
    tiles = lax.all_to_all(blocks, axes, 0, 0, tiled=True)
    return jnp.sum(tiles.astype(f32), axis=0)


def own_images(stored, gy):
    rows = stored.shape[0] // 2
    own = lax.dynamic_slice_in_dim(stored, rows * gy, rows, 0)
    other = lax.dynamic_slice_in_dim(stored, rows * (1 - gy), rows, 0)
    pad = ((0, PAD - rows), (0, 0))
    return jnp.pad(own, pad), jnp.pad(other, pad)


def stored_rows(keep, got, gy):
    first = jnp.where(gy == 0, keep, got)[:SEQ]
    last = jnp.where(gy == 0, got, keep)[:SEQ]
    return jnp.concatenate([first, last], axis=0).astype(f32)


def per_device(
    tokens,
    image_counts,
    slot_order,
    cotangent,
    attention_weights,
    attention_first,
    attention_second,
    expand_weight,
    expand_first,
    expand_second,
    project_weight,
    project_first,
    project_second,
    vectors,
    vector_first,
    vector_second,
):
    dp = lax.axis_index("dp")
    gy = lax.axis_index("xl")
    me = jnp.stack([dp, gy]).astype(jnp.int32)

    token_own, token_other = own_images(tokens, gy)
    token_got = swap(token_other, "xl")
    grad_own, grad_other = own_images(cotangent, gy)
    grad_got = swap(grad_other, "xl")
    vec_got = swap(vectors, "xl")
    attn_piece, ff_piece = call(
        prepare_kernel,
        [SCALARS, WHOLE, WHOLE, WHOLE],
        [((24, D), bf16, WHOLE), ((24, 2 * D), bf16, WHOLE)],
        (me, attention_weights, expand_weight, project_weight),
        name="prepare",
    )
    ff = lax.all_gather(ff_piece, EVERY).reshape(2, 32, 2, 24, 2 * D)
    at_x, at_y, at_z = place(X), place(Y), place(Z)

    def across_x(p):
        return p % 2, 0, p // 2, 0, 0

    attn = to_all(attn_piece, X)
    attn = assemble(attn, at_x, (2, 1, 2, 24, D), (1, 1, 1, 24, D), across_x)
    attn = to_all(attn.reshape(2, 48, D), Y)
    attn, token_got, vec_got = lax.optimization_barrier((attn, token_got, vec_got))
    attn = assemble(attn, at_y, (2, 4, 48, D), (2, 1, 48, D), lambda p: (0, p, 0, 0))
    vec_first, vec_last = ordered(gy, vectors, vec_got)
    vec = jnp.concatenate([vec_first, vec_last], axis=1)
    bias = vec[8:].T.reshape(1, FF)
    live = (slot_order[0] < image_counts[0]).astype(jnp.int32)
    live = lax.dynamic_slice_in_dim(live, IMAGES * gy, IMAGES)
    attn = to_all(attn.reshape(2, 192, D), Z)
    attn, vec, bias, live, token_own, token_got = lax.optimization_barrier(
        (attn, vec, bias, live, token_own, token_got)
    )
    attn = assemble(attn, at_z, (2, 4, 192, D), (2, 1, 192, D), lambda p: (0, p, 0, 0))
    w_own, w_got = (w.reshape(2, D, D) for w in (attn, swap(attn, "dp")))

    tall = block((ROWS, D), lambda j: (0, 0))
    wide = block((ROWS, D), lambda j: (0, j))
    w1_block = block((1, 32, 1, 24, D), lambda j: (j % 2, 0, j // 2, 0, 0))
    w2_block = block((2, 8, 2, 24, D), lambda j: (0, j, 0, 0, 1))
    pieces2 = block((2, 8, 48, HALF), lambda j: (0, j, 0, 0))
    soft_shape = (6, 2 * IMAGES, PAD, PAD)

    soft, mixed, x, normed, qkv, w_qkv, w_o = call(
        attend_kernel,
        [SCALARS, *(WHOLE,) * 5],
        [
            (soft_shape, bf16, block((1, *soft_shape[1:]), lambda p: (jnp.maximum(p - 1, 0), 0, 0, 0))),
            ((ROWS, D), bf16, block((ROWS, 128), lambda p: (0, jnp.maximum(p - 1, 0)))),
            ((ROWS, D), bf16, LEFT),
            ((ROWS, D), bf16, LEFT),
            ((3, ROWS, D), bf16, LEFT),
            ((3, D, D), bf16, LEFT),
            ((D, D), bf16, LEFT),
        ],
        (me, token_own, token_got, vec, w_own, w_got),
        grid=(7,),
        scratch=[
            pltpu.VMEM((ROWS, D), bf16),
            pltpu.VMEM((ROWS, D), bf16),
            pltpu.VMEM((3, ROWS, D), bf16),
            pltpu.VMEM((4, D, D), bf16),
            pltpu.SemaphoreType.DMA((5,)),
        ],
        name="attend",
    )

    up, middle, second = call(
        second_kernel,
        [SCALARS, SCALARS, *(WHOLE,) * 6],
        [((ROWS, D), bf16, WHOLE), ((ROWS, D), f32, WHOLE), ((ROWS, D), bf16, WHOLE)],
        (me, live, grad_own, grad_got, vec, x, mixed, w_o),
        name="second",
    )
    act, slope, mine2, theirs2, w1 = call(
        expand_kernel,
        [SCALARS, WHOLE, WHOLE, block((1, D), lambda j: (0, j)), w1_block],
        [
            ((ROWS, FF), bf16, wide),
            ((ROWS, FF), bf16, wide),
            ((2, 32, 48, HALF), bf16, pieces2),
            ((2, 32, 48, HALF), bf16, pieces2),
            ((D, FF), bf16, block((D, D), lambda j: (0, j))),
        ],
        (me, up, second, bias, ff),
        grid=(4,),
        scratch=[pltpu.VMEM((D, D), bf16)],
        after=(w_o, soft),
        name="expand",
    )
    inner_grad, hidden_sums, mine1, theirs1 = call(
        contract_kernel,
        [SCALARS, WHOLE, wide, WHOLE, w2_block],
        [
            ((ROWS, FF), bf16, wide),
            ((1, FF), f32, block((1, D), lambda j: (0, j))),
            ((2, D, D), bf16, block((1, D, D), lambda j: (j // 2, 0, 0))),
            ((2, D, D), bf16, block((1, D, D), lambda j: (j // 2, 0, 0))),
        ],
        (me, up, slope, second, ff),
        grid=(4,),
        scratch=[pltpu.VMEM((D, ROWS), bf16), pltpu.VMEM((D, D), bf16)],
        name="contract",
    )
    ring2 = ring_blocks(
        (mine2, swap(theirs2, "dp")),
        place(X),
        (2, 16, 2, 48, HALF),
        (1, 16, 1, 48, HALF),
        lambda p: (p % 2, 0, p // 2, 0, 0),
    )
    got1, _ = lax.optimization_barrier((swap(theirs1, "dp"), ring2[0]))
    ring1 = ring_blocks(
        (mine1, got1), place(Y), (8, 4, 48, D), (8, 1, 48, D), lambda p: (0, p, 0, 0)
    )

    mine0, theirs0, sums_c, grads, gm = call(
        middle_back_kernel,
        [SCALARS, WHOLE, *(LEFT,) * 9],
        [
            ((2, D, D), bf16, LEFT),
            ((2, D, D), bf16, LEFT),
            ((6, D), f32, WHOLE),
            ((3, ROWS, D), bf16, LEFT),
            ((ROWS, D), f32, LEFT),
        ],
        (me, vec, inner_grad, w1, soft, up, middle, w_o, normed, mixed, qkv),
        scratch=[
            pltpu.VMEM((4, ROWS, D), bf16),
            pltpu.VMEM((4, D, D), bf16),
            pltpu.VMEM(soft_shape, bf16),
            pltpu.VMEM((ROWS, D), bf16),
            pltpu.VMEM((ROWS, D), f32),
            pltpu.VMEM((D, D), bf16),
            pltpu.VMEM((ROWS, D), bf16),
            pltpu.VMEM((ROWS, D), bf16),
            pltpu.VMEM((3, ROWS, D), bf16),
            pltpu.VMEM((ROWS, D), f32),
            pltpu.VMEM((ROWS, D), bf16),
            pltpu.VMEM((ROWS, D), bf16),
            pltpu.VMEM((D, ROWS), bf16),
            pltpu.VMEM((D, ROWS), bf16),
            pltpu.VMEM((4, 2, D, HALF), bf16),
            pltpu.VMEM((3, ROWS, D), bf16),
            pltpu.VMEM((ROWS, D), f32),
            pltpu.SemaphoreType.DMA((26,)),
        ],
        after=(ring2[0], ring1[0]),
        cost=0,
        name="middle_back",
    )
    got0 = swap(theirs0, "dp")
    ring2 = ring(ring2, X)
    near1 = hop(ring1[1], Y, 1), hop(ring1[3], Y, 3)
    ring2, mine0 = lax.optimization_barrier((ring2, mine0))
    mine0, near1, far1 = lax.optimization_barrier((mine0, near1, ring1[2]))
    far1 = hop(far1, Y, 2)
    part2 = call(
        sum_kernel, [WHOLE] * 4, [((16, 48, HALF), bf16, WHOLE)], ring2, cost=100, after=(near1[0], near1[1]), name="part"
    )[0]
    tiles2 = lax.all_to_all(part2, Z + Y, 0, 0, tiled=True)
    mine0, got0, _ = lax.optimization_barrier((mine0, got0, part2))
    ring0 = ring_blocks(
        (mine0, got0), place(Z), (2, 4, 192, D), (2, 1, 192, D), lambda p: (0, p, 0, 0)
    )
    tiles2, far1, _ = lax.optimization_barrier((tiles2, far1, ring0[0]))
    own0, near0, back0, far0 = ring(ring0, Z)
    keep_in, send_in, sums_e = call(
        input_back_kernel,
        [
            SCALARS, WHOLE,
            block((1, ROWS, D), lambda k: (k, 0, 0)), block((1, D, D), lambda k: (k, 0, 0)),
            WHOLE, WHOLE,
        ],
        [
            ((PAD, D), bf16, block((PAD, D), lambda k: (0, 0))),
            ((PAD, D), bf16, block((PAD, D), lambda k: (0, 0))),
            ((2, D), f32, block((2, D), lambda k: (0, 0))),
        ],
        (me, vec, grads, w_qkv, x, gm),
        grid=(3,),
        scratch=[pltpu.VMEM((ROWS, D), f32)],
        cost=0,
        after=(ring0[0],),
        name="input_back",
    )
    sums_e, hidden_sums = lax.optimization_barrier((sums_e, hidden_sums))
    vector = jnp.concatenate(
        [sums_e, sums_c, hidden_sums.reshape(D, 4).T, jnp.zeros((4, D), f32)], axis=0
    ).astype(bf16)

    def spread(parts, vector, cost, name):
        return call(
            spread_kernel, [WHOLE] * 5, [((16, 40, D), bf16, WHOLE)], (*parts, vector), cost=cost, name=name
        )[0]

    far1, tiles2, near0, back0, vector = lax.optimization_barrier((far1, tiles2, near0, back0, vector))
    part1 = spread((ring1[0], *near1, far1), vector, 0, "spread")
    tiles1 = lax.all_to_all(part1, ("xl", "z", "xh"), 0, 0, tiled=True)
    keep_out, send_out = call(
        output_kernel,
        [SCALARS, WHOLE, WHOLE, wide, w2_block],
        [((PAD, D), bf16, block((PAD, D), lambda j: (0, 0)))] * 2,
        (me, vec, middle, act, ff),
        grid=(4,),
        scratch=[pltpu.VMEM((D, D), bf16), pltpu.VMEM((ROWS, D), f32)],
        after=(part1,),
        cost=100,
        name="output",
    )
    got_in, got_out = swap(send_in, "xl"), swap(send_out, "xl")
    tiles1, _ = lax.optimization_barrier((tiles1, keep_out))
    sum1 = jnp.sum(tiles1.astype(f32), axis=0)
    sum1, got_in = lax.optimization_barrier((sum1, got_in))
    part0 = spread((own0, near0, back0, far0), sum1[:16], 100, "last_spread")
    tiles0 = lax.all_to_all(part0, ("xl", "y", "xh"), 0, 0, tiled=True)
    tiles2, _ = lax.optimization_barrier((tiles2, part0))
    sum2 = jnp.sum(tiles2.astype(f32), axis=0)
    got2 = swap(sum2, "dp")
    sum1 = sum1[16:]
    got1 = swap(sum1, "dp")
    block_out = stored_rows(keep_out, got_out, gy)
    input_grad = stored_rows(keep_in, got_in, gy)

    def step(body, own, got, shape, state, outs=(), cost=0, name=None):
        state = (me, own, got, *state)
        outs = [(shape, f32, WHOLE)] * 3 + [(o, f32, WHOLE) for o in outs]
        return call(body, [SCALARS, *(WHOLE,) * (len(state) - 1)], outs, state, cost=cost, name=name)

    project = step(
        project_step_kernel, sum2, got2, (HALF, 96),
        (project_weight, project_first, project_second), name="project_step",
    )
    expand = step(
        expand_step_kernel, sum1, got1, (24, 2 * D),
        (expand_weight, expand_first, expand_second), name="expand_step",
    )
    tiles0, project = lax.optimization_barrier((tiles0, project))
    sum0 = call(last_sum_kernel, [WHOLE], [((40, D), f32, WHOLE)], (tiles0,), cost=0, name="last_sum")[0]
    got0 = swap(sum0, "dp")
    *attention, vector_grad, vector_second_new, vector_new = step(
        attention_step_kernel, sum0, got0, (24, 2 * D),
        (attention_weights, attention_first, attention_second, vectors, vector_first, vector_second),
        [(12, HALF)] * 3, name="attention_step",
    )
    return (
        block_out,
        input_grad,
        *attention,
        *expand,
        *project,
        vector_grad,
        vector_second_new,
        vector_new,
    )


def solution(mesh):
    fine = Mesh(mesh.devices.reshape(2, 4, 4, 2, 2), EVERY)
    rows = ("dp", "z", "y", "xh")
    deep = ("z", "y", "xh")
    placed = (
        P(rows, "xl"),
        P("dp"),
        P("dp", deep),
        P(rows, "xl"),
        *(P(deep, "xl"),) * 6,
        *(P("xl", deep),) * 3,
        *(P(None, "xl"),) * 3,
    )
    out = (
        P(rows, "xl"),
        P(rows, "xl"),
        *(P(deep, "xl"),) * 6,
        *(P("xl", deep),) * 3,
        *(P(None, "xl"),) * 3,
    )
    return jax.shard_map(per_device, mesh=fine, in_specs=placed, out_specs=out, check_vma=False)
```

```python
import jax
import jax.numpy as jnp
from jax import lax
from jax.experimental import pallas as pl
from jax.experimental.pallas import tpu as pltpu
from jax.sharding import Mesh
from jax.sharding import PartitionSpec as P

D = 768
HD = 64
FF = 3072
SEQ = 197
STEP = 10
PAD = 208
IMAGES = 2
ROWS = PAD * IMAGES
HALF = D // 2

norm_eps = 1e-06
beta_first = 0.9
beta_second = 0.999
learn_rate = 0.04
vector_rate = 0.25
decay_rate = 0.05
adam_eps = 1e-08

f32 = jnp.float32
bf16 = jnp.bfloat16

DP = ("dp",)
Z = ("z",)
Y = ("y",)
X = ("xh", "xl")
CHIPS = ("xl", "z", "y", "xh")
EVERY = ("dp", "z", "y", "xh", "xl")


def dot(a, b):
    return lax.dot_general(a, b, (((1,), (0,)), ((), ())), preferred_element_type=f32)


def dot_rows(a, b):
    return lax.dot_general(a, b, (((0,), (0,)), ((), ())), preferred_element_type=f32)


def dot_lanes(a, b):
    return lax.dot_general(a, b, (((1,), (1,)), ((), ())), preferred_element_type=f32)


def block(shape, index):
    return pl.BlockSpec(shape, index)


WHOLE = pl.BlockSpec(memory_space=pltpu.VMEM)
SCALARS = pl.BlockSpec(memory_space=pltpu.SMEM)
LEFT = pl.BlockSpec(memory_space=pl.ANY)


def call(body, ins, outs, args, grid=(), scratch=(), after=(), cost=10, prefetch=0, name=None):
    count = len(args)

    def run(*refs):
        body(*refs[:count], *refs[count + len(after) :])

    return pl.pallas_call(
        run if after else body,
        out_shape=[jax.ShapeDtypeStruct(s, t) for s, t, _ in outs],
        grid_spec=pltpu.PrefetchScalarGridSpec(
            num_scalar_prefetch=prefetch,
            grid=grid,
            in_specs=[*ins, *(LEFT for _ in after)],
            out_specs=[spec for _, _, spec in outs],
            scratch_shapes=list(scratch),
        ),
        compiler_params=pltpu.CompilerParams(vmem_limit_bytes=52 * 1024 * 1024),
        cost_estimate=pl.CostEstimate(flops=cost * 10**9 + 1000, bytes_accessed=0, transcendentals=0),
        name=name,
    )(*args, *after)


def iota(shape, dim):
    return lax.broadcasted_iota(jnp.int32, shape, dim)


def row_picks():
    r = iota((ROWS, PAD), 0)
    j = iota((ROWS, PAD), 1)
    second = r >= PAD
    s = jnp.where(second, r - PAD, r)
    t = jnp.where(second, s + SEQ, s)
    live = s < SEQ
    even = jnp.where(live & (t == 2 * j), 1.0, 0.0).astype(bf16)
    odd = jnp.where(live & (t == 2 * j + 1), 1.0, 0.0).astype(bf16)
    return even, odd


def row_picks_back():
    r = iota((PAD, ROWS), 1)
    j = iota((PAD, ROWS), 0)
    second = r >= PAD
    s = jnp.where(second, r - PAD, r)
    t = jnp.where(second, s + SEQ, s)
    live = s < SEQ
    even = jnp.where(live & (t == 2 * j), 1.0, 0.0).astype(bf16)
    odd = jnp.where(live & (t == 2 * j + 1), 1.0, 0.0).astype(bf16)
    return even, odd


def lane_split():
    l = iota((256, 256), 0)
    c = iota((256, 256), 1)
    target = jnp.where(c < 128, 2 * c, 2 * (c - 128) + 1)
    return jnp.where(l == target, 1.0, 0.0).astype(bf16)


def lane_join():
    l = iota((256, 256), 1)
    c = iota((256, 256), 0)
    target = jnp.where(c < 128, 2 * c, 2 * (c - 128) + 1)
    return jnp.where(l == target, 1.0, 0.0).astype(bf16)


def unpack(own_ref, got_ref, gy):
    own, got = own_ref[...], got_ref[...]
    first = jnp.where(gy == 0, own.astype(f32), got.astype(f32)).astype(bf16)
    last = jnp.where(gy == 0, got.astype(f32), own.astype(f32)).astype(bf16)
    split = lane_split()
    evens, odds = [], []
    for half in (first, last):
        for b in range(3):
            both = dot(half[:, 256 * b : 256 * b + 256], split).astype(bf16)
            evens.append(both[:, :128])
            odds.append(both[:, 128:])
    even_rows, odd_rows = row_picks()
    return dot(even_rows, jnp.concatenate(evens, axis=1)) + dot(odd_rows, jnp.concatenate(odds, axis=1))


def pack(rows_low, gy, keep_ref, send_ref):
    even_rows, odd_rows = row_picks_back()
    even = dot(even_rows, rows_low).astype(bf16)
    odd = dot(odd_rows, rows_low).astype(bf16)
    join = lane_join()
    for b in range(3):
        blocks = []
        for half in range(2):
            at = HALF * half + 128 * b
            both = jnp.concatenate([even[:, at : at + 128], odd[:, at : at + 128]], axis=1)
            blocks.append(dot(both, join))
        keep_ref[:, 256 * b : 256 * b + 256] = jnp.where(gy == 0, blocks[0], blocks[1]).astype(bf16)
        send_ref[:, 256 * b : 256 * b + 256] = jnp.where(gy == 0, blocks[1], blocks[0]).astype(bf16)


def norm_parts(v):
    center = jnp.mean(v, axis=1, keepdims=True)
    away = v - center
    scale = lax.rsqrt(jnp.mean(away * away, axis=1, keepdims=True) + norm_eps)
    return away * scale, scale


def norm_back(grad, scaled, scale, gain):
    pushed = grad * gain
    first = jnp.mean(pushed, axis=1, keepdims=True)
    cross = jnp.mean(pushed * scaled, axis=1, keepdims=True)
    return (pushed - first - scaled * cross) * scale


def prepare_kernel(me_ref, attn_ref, expand_ref, project_ref, attn_out, ff_out):
    me = me_ref[0]
    l = iota((512, 256), 0)
    c = iota((512, 256), 1)
    kind = 2 * me + jnp.where(c < 128, 0, 1)
    pick = jnp.where(l == 4 * (c & 127) + kind, 1.0, 0.0).astype(bf16)
    for b in range(3):
        both = dot(attn_ref[:, 512 * b : 512 * b + 512].astype(bf16), pick).astype(bf16)
        attn_out[:, 128 * b : 128 * b + 128] = both[:, :128]
        attn_out[:, HALF + 128 * b : HALF + 128 * b + 128] = both[:, 128:]
    ff_out[:, :D] = jnp.where(me == 0, expand_ref[:, :D], expand_ref[:, D:]).astype(bf16)
    turned = project_ref[...].T
    mine = jnp.where(me == 0, turned[:48], turned[48:])
    ff_out[:, D : D + HALF] = mine[:24].astype(bf16)
    ff_out[:, D + HALF :] = mine[24:].astype(bf16)


def attend_kernel(
    me_ref, own_ref, got_ref, vec_ref, w_own, w_got,
    soft_out, mixed_out, x_out, normed_out, qkv_out, w_out, wo_out,
    x_ref, normed_ref, qkv_ref, w_ref, sems,
):
    step = pl.program_id(0)
    copies = [
        pltpu.make_async_copy(x_ref, x_out, sems.at[0]),
        pltpu.make_async_copy(normed_ref, normed_out, sems.at[1]),
        pltpu.make_async_copy(qkv_ref, qkv_out, sems.at[2]),
        pltpu.make_async_copy(w_ref.at[pl.ds(0, 3)], w_out, sems.at[3]),
        pltpu.make_async_copy(w_ref.at[3], wo_out, sems.at[4]),
    ]

    @pl.when(step == 0)
    def _():
        me, gy = me_ref[0], me_ref[1]
        for ref, place in ((w_own, me), (w_got, 1 - me)):
            for half in range(2):
                for y in range(2):
                    w_ref[pl.ds(2 * place + half, 1), :, HALF * y : HALF * y + HALF] = ref[
                        y, :, HALF * half : HALF * half + HALF
                    ][None]
        copies[3].start()
        copies[4].start()
        x_ref[...] = unpack(own_ref, got_ref, gy).astype(bf16)
        copies[0].start()
        scaled, _ = norm_parts(x_ref[...].astype(f32))
        normed_ref[...] = (scaled * vec_ref[0:1, :] + vec_ref[1:2, :]).astype(bf16)
        copies[1].start()

        def project(i, carry):
            cols = pl.ds(pl.multiple_of(256 * i, 256), 256)
            for kind, row in ((0, 2), (1, None), (2, 3)):
                part = dot(normed_ref[...], w_ref[kind, :, cols])
                if row is not None:
                    part = part + vec_ref[row : row + 1, cols]
                qkv_ref[kind, :, cols] = part.astype(bf16)
            return carry

        lax.fori_loop(0, 3, project, 0)
        copies[2].start()

    @pl.when(step > 0)
    def _():
        cols = pl.ds(pl.multiple_of(128 * (step - 1), 128), 128)
        lane = iota((PAD, 128), 1)
        key_live = iota((PAD, PAD), 0) < SEQ
        for image in range(IMAGES):
            rows = pl.ds(PAD * image, PAD)
            q = qkv_ref[0, rows, cols] * jnp.asarray(0.125, bf16)
            k = qkv_ref[1, rows, cols]
            v = qkv_ref[2, rows, cols]
            total = None
            for n in range(2):
                inside = (lane < HD) == (n == 0)
                scores = dot_lanes(k, jnp.where(inside, q, jnp.zeros_like(q)))
                scores = jnp.where(key_live, scores, -1e30)
                terms = jnp.exp(scores - jnp.max(scores, axis=0, keepdims=True))
                soft = terms * (1.0 / jnp.sum(terms, axis=0, keepdims=True))
                soft = soft.astype(bf16)
                soft_out[0, 2 * image + n] = soft
                part = dot_rows(soft, jnp.where(inside, v, jnp.zeros_like(v)))
                total = part if total is None else total + part
            mixed_out[rows, :] = total.astype(bf16)

    @pl.when(step == 6)
    def _():
        for copy in copies:
            copy.wait()


def gelu_parts(v):
    below = 0.5 + 0.5 * lax.erf(v * 0.7071067811865476)
    return v * below, below + v * jnp.exp(-0.5 * v * v) * 0.3989422804014327


def gather_rows(first, last):
    return jnp.concatenate([first.astype(f32), last.astype(f32)], axis=0).astype(bf16)


def place_rows(w2, ff_ref):
    for d in range(2):
        for g in range(8):
            for y in range(2):
                piece = ff_ref[d, g, y]
                rows = slice(96 * g + 48 * d, 96 * g + 48 * d + 48)
                w2[rows, HALF * y : HALF * y + HALF] = gather_rows(piece[:, :HALF], piece[:, HALF:])


def second_kernel(
    me_ref, live_ref, own_ref, got_ref, vec_ref, x_ref, mixed_ref, wo_ref,
    up_out, middle_out, second_out,
):
    up = unpack(own_ref, got_ref, me_ref[1])
    image = jnp.where(iota((ROWS, 1), 0) < PAD, live_ref[0], live_ref[1])
    up_out[...] = jnp.where(image == 1, up, 0.0).astype(bf16)
    middle = x_ref[...].astype(f32) + dot(mixed_ref[...], wo_ref[...]) + vec_ref[4:5, :]
    middle_out[...] = middle
    scaled, _ = norm_parts(middle)
    second_out[...] = (scaled * vec_ref[5:6, :] + vec_ref[6:7, :]).astype(bf16)


def expand_kernel(
    me_ref, up_ref, second_ref, bias_ref, w1_ref,
    act_out, slope_out, mine_out, theirs_out, w1_out,
    total,
):
    me = me_ref[0]
    for pair in range(16):
        w1_out[48 * pair : 48 * pair + 48, :] = gather_rows(
            w1_ref[0, 2 * pair, 0], w1_ref[0, 2 * pair + 1, 0]
        )

    for i in range(3):
        cols = slice(256 * i, 256 * i + 256)
        inner = dot(second_ref[...], w1_out[:, cols]) + bias_ref[:, cols]
        act, slope = gelu_parts(inner)
        act = act.astype(bf16)
        act_out[:, cols] = act
        slope_out[:, cols] = slope.astype(bf16)
    total[...] = dot_rows(act_out[...], up_ref[...]).astype(bf16)

    for g in range(8):
        for ref, place in ((mine_out, me), (theirs_out, 1 - me)):
            part = total[pl.ds(pl.multiple_of(96 * g + 48 * place, 16), 48), :]
            for y in range(2):
                ref[y, g] = part[:, HALF * y : HALF * y + HALF]


def contract_kernel(
    me_ref, up_ref, slope_ref, second_ref, ff_ref,
    grad_out, hidden_out, mine_out, theirs_out,
    turned, w2,
):
    step = pl.program_id(0)
    me = me_ref[0]

    @pl.when(step == 0)
    def _():
        turned[...] = second_ref[...].T

    place_rows(w2, ff_ref)
    for i in range(3):
        cols = slice(256 * i, 256 * i + 256)
        grad = dot_lanes(up_ref[...], w2[cols, :]) * slope_ref[:, cols].astype(f32)
        grad = grad.astype(bf16)
        grad_out[:, cols] = grad
        hidden_out[:, cols] = jnp.sum(grad.astype(f32), axis=0, keepdims=True)

    def outer(ref):
        for i in range(3):
            cols = slice(256 * i, 256 * i + 256)
            ref[0, :, cols] = dot(turned[...], grad_out[:, cols]).astype(bf16)

    pl.when((step & 1) == me)(lambda: outer(mine_out))
    pl.when((step & 1) != me)(lambda: outer(theirs_out))


def middle_back_kernel(
    me_ref, vec_ref, inner_hbm, w1_hbm, soft_hbm, up_hbm, middle_hbm, wo_hbm, normed_hbm, mixed_hbm, qkv_hbm,
    mine_hbm, theirs_hbm, sums_out, grads_hbm, gm_hbm,
    inner_ref, w1_ref, soft_ref, up_ref, middle_ref, wo_ref, normed_ref, mixed_ref, qkv_ref,
    grad_second, gml, grad_mixed, normed_turned, mixed_turned, pieces, grads_ref, gm_ref, sems,
):
    me = me_ref[0]
    ahead = []
    for j in range(4):
        cols = pl.ds(D * j, D)
        ahead.append((inner_hbm.at[:, cols], inner_ref.at[j]))
        ahead.append((w1_hbm.at[:, cols], w1_ref.at[j]))
    ahead += [
        (middle_hbm, middle_ref), (up_hbm, up_ref), (wo_hbm, wo_ref),
        (normed_hbm, normed_ref), (mixed_hbm, mixed_ref), (qkv_hbm, qkv_ref),
    ]
    reads = [pltpu.make_async_copy(src, dst, sems.at[i]) for i, (src, dst) in enumerate(ahead)]

    def read_soft(i):
        return pltpu.make_async_copy(soft_hbm.at[i], soft_ref.at[i], sems.at[14 + i])

    grads_write = pltpu.make_async_copy(grads_ref, grads_hbm, sems.at[20])
    gm_write = pltpu.make_async_copy(gm_ref, gm_hbm, sems.at[21])

    def write(kind, act):
        cols = pl.ds(HALF * (kind % 2), HALF)
        for to, place in ((mine_hbm, kind // 2), (theirs_hbm, 1 - kind // 2)):
            copy = pltpu.make_async_copy(pieces.at[kind], to.at[:, :, cols], sems.at[22 + kind])
            pl.when(me == place)(lambda copy=copy: act(copy))

    def outer(kind, left, right):
        grad = dot(left[...], right[...]).astype(bf16)
        for y in range(2):
            pieces[kind, y] = grad[:, HALF * y : HALF * y + HALF]
        write(kind, lambda copy: copy.start())

    for read in reads:
        read.start()
    for i in range(6):
        read_soft(i).start()
    for j in range(4):
        reads[2 * j].wait()
        reads[2 * j + 1].wait()
        part = dot_lanes(inner_ref[j], w1_ref[j])
        if j == 0:
            grad_second[...] = part
        else:
            grad_second[...] += part
    for read in reads[8:]:
        read.wait()
    grad = grad_second[...]
    scaled, scale = norm_parts(middle_ref[...])
    up = up_ref[...].astype(f32)
    gm = up + norm_back(grad, scaled, scale, vec_ref[5:6, :])
    gm_ref[...] = gm
    gm_write.start()
    gml[...] = gm.astype(bf16)
    sums_out[2:3, :] = jnp.sum(gml[...].astype(f32), axis=0, keepdims=True)
    sums_out[3:4, :] = jnp.sum(grad * scaled, axis=0, keepdims=True)
    sums_out[4:5, :] = jnp.sum(grad, axis=0, keepdims=True)
    sums_out[5:6, :] = jnp.sum(up, axis=0, keepdims=True)
    grad_mixed[...] = dot_lanes(gml[...], wo_ref[...]).astype(bf16)
    mixed_turned[...] = mixed_ref[...].T
    outer(3, mixed_turned, gml)
    normed_turned[...] = normed_ref[...].T
    lane = iota((PAD, 128), 1)

    def attend(i, carry):
        cols = pl.ds(pl.multiple_of(128 * i, 128), 128)
        read_soft(i).wait()
        for image in range(IMAGES):
            rows = pl.ds(PAD * image, PAD)
            q = qkv_ref[0, rows, cols]
            k = qkv_ref[1, rows, cols]
            v = qkv_ref[2, rows, cols]
            g = grad_mixed[rows, cols]
            dq = dk = dv = jnp.zeros((PAD, 128), f32)
            for n in range(2):
                inside = (lane < HD) == (n == 0)
                zero = jnp.zeros_like(g)
                g_in = jnp.where(inside, g, zero)
                soft_low = soft_ref[i, 2 * image + n]
                soft = soft_low.astype(f32)
                grad_soft = dot_lanes(v, g_in)
                level = jnp.sum(grad_soft * soft, axis=0, keepdims=True)
                scores = (soft * (grad_soft - level)).astype(bf16)
                dv = dv + dot(soft_low, g_in)
                dk = dk + dot(scores, jnp.where(inside, q, zero))
                dq = dq + dot_rows(scores, jnp.where(inside, k, zero))
            grads_ref[0, rows, cols] = (dq * 0.125).astype(bf16)
            grads_ref[1, rows, cols] = (dk * 0.125).astype(bf16)
            grads_ref[2, rows, cols] = dv.astype(bf16)
        return carry

    lax.fori_loop(0, 6, attend, 0)
    grads_write.start()
    for kind in range(3):
        outer(kind, normed_turned, grads_ref.at[kind])
    sums_out[0:1, :] = jnp.sum(grads_ref[0].astype(f32), axis=0, keepdims=True)
    sums_out[1:2, :] = jnp.sum(grads_ref[2].astype(f32), axis=0, keepdims=True)
    grads_write.wait()
    gm_write.wait()
    for kind in range(4):
        write(kind, lambda copy: copy.wait())


def input_back_kernel(
    me_ref, vec_ref, grads_ref, w_ref, x_ref, gm_ref, keep_out, send_out, sums_out, total
):
    step = pl.program_id(0)
    part = dot_lanes(grads_ref[0], w_ref[0])

    @pl.when(step == 0)
    def _():
        total[...] = part

    @pl.when(step > 0)
    def _():
        total[...] += part

    @pl.when(step == 2)
    def _():
        grad = total[...]
        scaled, scale = norm_parts(x_ref[...].astype(f32))
        out = gm_ref[...] + norm_back(grad, scaled, scale, vec_ref[0:1, :])
        pack(out.astype(bf16), me_ref[1], keep_out, send_out)
        sums_out[0:1, :] = jnp.sum(grad * scaled, axis=0, keepdims=True)
        sums_out[1:2, :] = jnp.sum(grad, axis=0, keepdims=True)


def output_kernel(me_ref, vec_ref, middle_ref, act_ref, ff_ref, keep_out, send_out, w2, total):
    step = pl.program_id(0)
    place_rows(w2, ff_ref)
    part = dot(act_ref[...], w2[...])

    @pl.when(step == 0)
    def _():
        total[...] = middle_ref[...] + vec_ref[7:8, :] + part

    @pl.when(step > 0)
    def _():
        total[...] += part

    @pl.when(step == 3)
    def _():
        pack(total[...].astype(bf16), me_ref[1], keep_out, send_out)


def assemble_kernel(at_ref, *refs):
    out = refs[-1]
    step = pl.program_id(0)
    for r in range(4):
        pl.when(step == r)(lambda r=r: out.__setitem__(..., refs[r][...].reshape(out.shape)))


def blocks_sum_kernel(at_ref, *refs):
    ins, outs = refs[:-4], refs[-4:]
    step = pl.program_id(0)
    total = ins[0][...].astype(f32)
    for ref in ins[1:]:
        total = total + ref[...].astype(f32)
    total = total.astype(bf16)
    for r in range(4):
        pl.when(step == r)(lambda r=r: outs[r].__setitem__(..., total.reshape(outs[r].shape)))


def sum_kernel(a_ref, b_ref, c_ref, d_ref, out_ref):
    total = a_ref[...].astype(f32) + b_ref[...].astype(f32) + c_ref[...].astype(f32) + d_ref[...].astype(f32)
    out_ref[...] = total.astype(bf16)


def last_spread_kernel(a_ref, b_ref, c_ref, d_ref, va_ref, vb_ref, vc_ref, vd_ref, out_ref):
    vector = va_ref[...].astype(f32) + vb_ref[...].astype(f32) + vc_ref[...].astype(f32) + vd_ref[...].astype(f32)
    vector = vector.astype(bf16)
    total = a_ref[...].astype(f32) + b_ref[...].astype(f32) + c_ref[...].astype(f32) + d_ref[...].astype(f32)
    total = total.reshape(2 * 192, D)
    for i in range(16):
        out_ref[i, :16, :] = vector
        out_ref[i, 16:, :] = total[24 * i : 24 * i + 24].astype(bf16)


def adamw_step(parameter, gradient, first_moment, second_moment, step_rate, decay_factor):
    first_new = beta_first * first_moment + (1.0 - beta_first) * gradient
    second_new = beta_second * second_moment + (1.0 - beta_second) * gradient * gradient
    first_hat = first_new / (1.0 - beta_first**STEP)
    second_hat = second_new / (1.0 - beta_second**STEP)
    updated = parameter - step_rate * (
        first_hat / (jnp.sqrt(second_hat) + adam_eps) + decay_factor * parameter
    )
    return second_new, updated


def ordered(me, own, got):
    return jnp.where(me == 0, own, got), jnp.where(me == 0, got, own)


def attention_step_kernel(
    me_ref, own_ref, got_ref, w_ref, m_ref, v_ref, vec_ref, vec_m_ref, vec_v_ref,
    grad_out, second_out, new_out, vec_grad_out, vec_second_out, vec_new_out,
):
    pieces = ordered(me_ref[0], own_ref[16:, :], got_ref[16:, :])
    l = iota((512, 512), 0)
    c = iota((512, 512), 1)
    pick = jnp.where(c == 4 * (l & 127) + (l >> 7), 1.0, 0.0)
    for b in range(3):
        kinds = [
            pieces[k // 2][:, HALF * (k % 2) + 128 * b : HALF * (k % 2) + 128 * b + 128]
            for k in range(4)
        ]
        grad_out[:, 512 * b : 512 * b + 512] = jnp.dot(
            jnp.concatenate(kinds, axis=1), pick, precision=lax.Precision.HIGHEST,
            preferred_element_type=f32,
        )
    second_out[...], new_out[...] = adamw_step(
        w_ref[...], grad_out[...], m_ref[...], v_ref[...], learn_rate, decay_rate
    )
    vector = own_ref[:12, :] + got_ref[:12, :]
    vec_grad_out[...] = jnp.where(me_ref[1] == 0, vector[:, :HALF], vector[:, HALF:])
    vec_second_out[...], vec_new_out[...] = adamw_step(
        vec_ref[...], vec_grad_out[...], vec_m_ref[...], vec_v_ref[...], vector_rate, 0.0
    )


def expand_step_kernel(me_ref, own_ref, got_ref, w_ref, m_ref, v_ref, grad_out, second_out, new_out):
    first, last = ordered(me_ref[0], own_ref[...], got_ref[...])
    grad_out[:, :D] = first
    grad_out[:, D:] = last
    second_out[...], new_out[...] = adamw_step(
        w_ref[...], grad_out[...], m_ref[...], v_ref[...], learn_rate, decay_rate
    )


def project_step_kernel(me_ref, own_ref, got_ref, w_ref, m_ref, v_ref, grad_out, second_out, new_out):
    first, last = ordered(me_ref[0], own_ref[...], got_ref[...])
    grad_out[...] = jnp.concatenate([first, last], axis=0).T
    second_out[...], new_out[...] = adamw_step(
        w_ref[...], grad_out[...], m_ref[...], v_ref[...], learn_rate, decay_rate
    )


def place(axes):
    at = 0
    for a in axes:
        at = at * lax.axis_size(a) + lax.axis_index(a)
    return at


def swap(x, axis):
    return lax.ppermute(x, axis, [(0, 1), (1, 0)])


def core_sum(mine, theirs):
    return (mine.astype(f32) + swap(theirs, "dp").astype(f32)).astype(bf16)


def assemble(parts, at, shape, piece, index, after=(), cost=0):
    flat = tuple(n for n in piece if n > 1)
    return pl.pallas_call(
        assemble_kernel,
        out_shape=jax.ShapeDtypeStruct(shape, bf16),
        grid_spec=pltpu.PrefetchScalarGridSpec(
            num_scalar_prefetch=1,
            grid=(4,),
            in_specs=[
                *(pl.BlockSpec(flat, lambda r, at: (0,) * len(flat)) for _ in range(4)),
                *(LEFT for _ in after),
            ],
            out_specs=pl.BlockSpec(piece, lambda r, at: index((at[0] + 3 * r) % 4)),
        ),
        compiler_params=pltpu.CompilerParams(vmem_limit_bytes=32 * 1024 * 1024),
        cost_estimate=pl.CostEstimate(flops=cost * 10**9 + 1000, bytes_accessed=0, transcendentals=0),
        name="assemble",
    )(at.reshape(1).astype(jnp.int32), *(p.reshape(flat) for p in parts), *after)


def ring_blocks(parts, at, shape, piece, index):
    spec = pl.BlockSpec(piece, lambda r, at: index((at[0] + r) % 4))
    flat = tuple(n for n in piece if n > 1)
    return pl.pallas_call(
        blocks_sum_kernel,
        out_shape=[jax.ShapeDtypeStruct(flat, bf16)] * 4,
        grid_spec=pltpu.PrefetchScalarGridSpec(
            num_scalar_prefetch=1,
            grid=(4,),
            in_specs=[spec] * len(parts),
            out_specs=[pl.BlockSpec(flat, lambda r, at: (0,) * len(flat))] * 4,
        ),
        compiler_params=pltpu.CompilerParams(vmem_limit_bytes=32 * 1024 * 1024),
        cost_estimate=pl.CostEstimate(flops=1000, bytes_accessed=0, transcendentals=0),
        name="ring_blocks",
    )(at.reshape(1).astype(jnp.int32), *(p.reshape(shape) for p in parts))


def hop(x, axes, r):
    return lax.ppermute(x, axes, [(i, (i + r) % 4) for i in range(4)])


def ring(blocks, axes):
    return blocks[0], *(hop(blocks[r], axes, r) for r in (1, 3, 2))


def crossed(x, axis, bit):
    return lax.ppermute(x, axis, [(i, i ^ bit) for i in range(lax.axis_size(axis))])


def to_all(x, axes):
    near, back = hop(x, axes, 1), hop(x, axes, 3)
    return x, near, hop(x, axes, 2), back


def sum_of(parts):
    total = parts[0].astype(f32)
    for part in parts[1:]:
        total = total + part.astype(f32)
    return total


def spread_sum(blocks, axes):
    tiles = lax.all_to_all(blocks, axes, 0, 0, tiled=True)
    return jnp.sum(tiles.astype(f32), axis=0)


def own_images(stored, gy):
    rows = stored.shape[0] // 2
    own = lax.dynamic_slice_in_dim(stored, rows * gy, rows, 0)
    other = lax.dynamic_slice_in_dim(stored, rows * (1 - gy), rows, 0)
    pad = ((0, PAD - rows), (0, 0))
    return jnp.pad(own, pad), jnp.pad(other, pad)


def stored_rows(keep, got, gy):
    first = jnp.where(gy == 0, keep, got)[:SEQ]
    last = jnp.where(gy == 0, got, keep)[:SEQ]
    return jnp.concatenate([first, last], axis=0).astype(f32)


def per_device(
    tokens,
    image_counts,
    slot_order,
    cotangent,
    attention_weights,
    attention_first,
    attention_second,
    expand_weight,
    expand_first,
    expand_second,
    project_weight,
    project_first,
    project_second,
    vectors,
    vector_first,
    vector_second,
):
    dp = lax.axis_index("dp")
    gy = lax.axis_index("xl")
    me = jnp.stack([dp, gy]).astype(jnp.int32)

    token_own, token_other = own_images(tokens, gy)
    token_got = swap(token_other, "xl")
    grad_own, grad_other = own_images(cotangent, gy)
    grad_got = swap(grad_other, "xl")
    vec_got = swap(vectors, "xl")
    attn_piece, ff_piece = call(
        prepare_kernel,
        [SCALARS, WHOLE, WHOLE, WHOLE],
        [((24, D), bf16, WHOLE), ((24, 2 * D), bf16, WHOLE)],
        (me, attention_weights, expand_weight, project_weight),
        name="prepare",
    )
    ff = lax.all_gather(ff_piece, EVERY).reshape(2, 32, 2, 24, 2 * D)
    at_x, at_y, at_z = place(X), place(Y), place(Z)

    def across_x(p):
        return p % 2, 0, p // 2, 0, 0

    attn = to_all(attn_piece, X)
    attn = assemble(attn, at_x, (2, 1, 2, 24, D), (1, 1, 1, 24, D), across_x)
    attn = to_all(attn.reshape(2, 48, D), Y)
    attn, token_got, vec_got = lax.optimization_barrier((attn, token_got, vec_got))
    attn = assemble(attn, at_y, (2, 4, 48, D), (2, 1, 48, D), lambda p: (0, p, 0, 0))
    vec_first, vec_last = ordered(gy, vectors, vec_got)
    vec = jnp.concatenate([vec_first, vec_last], axis=1)
    bias = vec[8:].T.reshape(1, FF)
    live = (slot_order[0] < image_counts[0]).astype(jnp.int32)
    live = lax.dynamic_slice_in_dim(live, IMAGES * gy, IMAGES)
    attn = to_all(attn.reshape(2, 192, D), Z)
    attn, vec, bias, live, token_own, token_got = lax.optimization_barrier(
        (attn, vec, bias, live, token_own, token_got)
    )
    attn = assemble(attn, at_z, (2, 4, 192, D), (2, 1, 192, D), lambda p: (0, p, 0, 0))
    w_own, w_got = (w.reshape(2, D, D) for w in (attn, swap(attn, "dp")))

    tall = block((ROWS, D), lambda j: (0, 0))
    wide = block((ROWS, D), lambda j: (0, j))
    w1_block = block((1, 32, 1, 24, D), lambda j: (j % 2, 0, j // 2, 0, 0))
    w2_block = block((2, 8, 2, 24, D), lambda j: (0, j, 0, 0, 1))
    pieces2 = block((2, 8, 48, HALF), lambda j: (0, j, 0, 0))
    soft_shape = (6, 2 * IMAGES, PAD, PAD)

    soft, mixed, x, normed, qkv, w_qkv, w_o = call(
        attend_kernel,
        [SCALARS, *(WHOLE,) * 5],
        [
            (soft_shape, bf16, block((1, *soft_shape[1:]), lambda p: (jnp.maximum(p - 1, 0), 0, 0, 0))),
            ((ROWS, D), bf16, block((ROWS, 128), lambda p: (0, jnp.maximum(p - 1, 0)))),
            ((ROWS, D), bf16, LEFT),
            ((ROWS, D), bf16, LEFT),
            ((3, ROWS, D), bf16, LEFT),
            ((3, D, D), bf16, LEFT),
            ((D, D), bf16, LEFT),
        ],
        (me, token_own, token_got, vec, w_own, w_got),
        grid=(7,),
        scratch=[
            pltpu.VMEM((ROWS, D), bf16),
            pltpu.VMEM((ROWS, D), bf16),
            pltpu.VMEM((3, ROWS, D), bf16),
            pltpu.VMEM((4, D, D), bf16),
            pltpu.SemaphoreType.DMA((5,)),
        ],
        name="attend",
    )

    up, middle, second = call(
        second_kernel,
        [SCALARS, SCALARS, *(WHOLE,) * 6],
        [((ROWS, D), bf16, WHOLE), ((ROWS, D), f32, WHOLE), ((ROWS, D), bf16, WHOLE)],
        (me, live, grad_own, grad_got, vec, x, mixed, w_o),
        name="second",
    )
    act, slope, mine2, theirs2, w1 = call(
        expand_kernel,
        [SCALARS, WHOLE, WHOLE, block((1, D), lambda j: (0, j)), w1_block],
        [
            ((ROWS, FF), bf16, wide),
            ((ROWS, FF), bf16, wide),
            ((2, 32, 48, HALF), bf16, pieces2),
            ((2, 32, 48, HALF), bf16, pieces2),
            ((D, FF), bf16, block((D, D), lambda j: (0, j))),
        ],
        (me, up, second, bias, ff),
        grid=(4,),
        scratch=[pltpu.VMEM((D, D), bf16)],
        after=(w_o, soft),
        name="expand",
    )
    inner_grad, hidden_sums, mine1, theirs1 = call(
        contract_kernel,
        [SCALARS, WHOLE, wide, WHOLE, w2_block],
        [
            ((ROWS, FF), bf16, wide),
            ((1, FF), f32, block((1, D), lambda j: (0, j))),
            ((2, D, D), bf16, block((1, D, D), lambda j: (j // 2, 0, 0))),
            ((2, D, D), bf16, block((1, D, D), lambda j: (j // 2, 0, 0))),
        ],
        (me, up, slope, second, ff),
        grid=(4,),
        scratch=[pltpu.VMEM((D, ROWS), bf16), pltpu.VMEM((D, D), bf16)],
        name="contract",
    )
    ring2 = ring_blocks(
        (mine2, swap(theirs2, "dp")),
        place(X),
        (2, 16, 2, 48, HALF),
        (1, 16, 1, 48, HALF),
        lambda p: (p % 2, 0, p // 2, 0, 0),
    )
    got1, _ = lax.optimization_barrier((swap(theirs1, "dp"), ring2[0]))
    ring1 = ring_blocks(
        (mine1, got1), place(Y), (8, 4, 48, D), (8, 1, 48, D), lambda p: (0, p, 0, 0)
    )

    mine0, theirs0, sums_c, grads, gm = call(
        middle_back_kernel,
        [SCALARS, WHOLE, *(LEFT,) * 9],
        [
            ((2, D, D), bf16, LEFT),
            ((2, D, D), bf16, LEFT),
            ((6, D), f32, WHOLE),
            ((3, ROWS, D), bf16, LEFT),
            ((ROWS, D), f32, LEFT),
        ],
        (me, vec, inner_grad, w1, soft, up, middle, w_o, normed, mixed, qkv),
        scratch=[
            pltpu.VMEM((4, ROWS, D), bf16),
            pltpu.VMEM((4, D, D), bf16),
            pltpu.VMEM(soft_shape, bf16),
            pltpu.VMEM((ROWS, D), bf16),
            pltpu.VMEM((ROWS, D), f32),
            pltpu.VMEM((D, D), bf16),
            pltpu.VMEM((ROWS, D), bf16),
            pltpu.VMEM((ROWS, D), bf16),
            pltpu.VMEM((3, ROWS, D), bf16),
            pltpu.VMEM((ROWS, D), f32),
            pltpu.VMEM((ROWS, D), bf16),
            pltpu.VMEM((ROWS, D), bf16),
            pltpu.VMEM((D, ROWS), bf16),
            pltpu.VMEM((D, ROWS), bf16),
            pltpu.VMEM((4, 2, D, HALF), bf16),
            pltpu.VMEM((3, ROWS, D), bf16),
            pltpu.VMEM((ROWS, D), f32),
            pltpu.SemaphoreType.DMA((26,)),
        ],
        after=(ring2[0], ring1[0]),
        cost=0,
        name="middle_back",
    )
    got0 = swap(theirs0, "dp")
    ring2 = ring(ring2, X)
    near1 = hop(ring1[1], Y, 1), hop(ring1[3], Y, 3)
    ring2, mine0 = lax.optimization_barrier((ring2, mine0))
    mine0, near1, far1 = lax.optimization_barrier((mine0, near1, ring1[2]))
    far1 = hop(far1, Y, 2)
    part2 = call(
        sum_kernel, [WHOLE] * 4, [((16, 48, HALF), bf16, WHOLE)], ring2, cost=100, after=(near1[0], near1[1]), name="part"
    )[0]
    tiles2 = lax.all_to_all(part2, Z + Y, 0, 0, tiled=True)
    mine0, got0, _ = lax.optimization_barrier((mine0, got0, part2))
    ring0 = ring_blocks(
        (mine0, got0), place(Z), (2, 4, 192, D), (2, 1, 192, D), lambda p: (0, p, 0, 0)
    )
    tiles2, far1, _ = lax.optimization_barrier((tiles2, far1, ring0[0]))
    own0, near0, back0, far0 = ring(ring0, Z)
    keep_out, send_out = call(
        output_kernel,
        [SCALARS, WHOLE, WHOLE, wide, w2_block],
        [((PAD, D), bf16, block((PAD, D), lambda j: (0, 0)))] * 2,
        (me, vec, middle, act, ff),
        grid=(4,),
        scratch=[pltpu.VMEM((D, D), bf16), pltpu.VMEM((ROWS, D), f32)],
        after=(ring0[0],),
        cost=0,
        name="output",
    )
    far1, tiles2, keep_out = lax.optimization_barrier((far1, tiles2, keep_out))
    part1 = sum_of((ring1[0], *near1, far1)).astype(bf16).reshape(16, 24, D)
    tiles1 = lax.all_to_all(part1, ("xl", "z", "xh"), 0, 0, tiled=True)
    grads, near0, back0 = lax.optimization_barrier((grads, near0, back0))
    keep_in, send_in, sums_e = call(
        input_back_kernel,
        [
            SCALARS, WHOLE,
            block((1, ROWS, D), lambda k: (k, 0, 0)), block((1, D, D), lambda k: (k, 0, 0)),
            WHOLE, WHOLE,
        ],
        [
            ((PAD, D), bf16, block((PAD, D), lambda k: (0, 0))),
            ((PAD, D), bf16, block((PAD, D), lambda k: (0, 0))),
            ((2, D), f32, block((2, D), lambda k: (0, 0))),
        ],
        (me, vec, grads, w_qkv, x, gm),
        grid=(3,),
        scratch=[pltpu.VMEM((ROWS, D), f32)],
        cost=100,
        after=(part1,),
        name="input_back",
    )
    sums_e, hidden_sums = lax.optimization_barrier((sums_e, hidden_sums))
    vector = jnp.concatenate(
        [sums_e, sums_c, hidden_sums.reshape(D, 4).T, jnp.zeros((4, D), f32)], axis=0
    ).astype(bf16)
    vectors4 = ring((vector,) * 4, Z)
    got_in, got_out = swap(send_in, "xl"), swap(send_out, "xl")
    tiles2, vectors4, got_out = lax.optimization_barrier((tiles2, vectors4, got_out))
    sum2 = jnp.sum(tiles2.astype(f32), axis=0)
    got2 = swap(sum2, "dp")
    part0 = call(
        last_spread_kernel,
        [WHOLE] * 8,
        [((16, 40, D), bf16, WHOLE)],
        (own0, near0, back0, far0, *vectors4),
        cost=0,
        name="last_spread",
    )[0]
    tiles0 = lax.all_to_all(part0, ("xl", "y", "xh"), 0, 0, tiled=True)
    sum1 = jnp.sum(tiles1.astype(f32), axis=0)
    got1 = swap(sum1, "dp")
    block_out = stored_rows(keep_out, got_out, gy)
    input_grad = stored_rows(keep_in, got_in, gy)

    def step(body, own, got, shape, state, outs=(), cost=0, name=None):
        state = (me, own, got, *state)
        outs = [(shape, f32, WHOLE)] * 3 + [(o, f32, WHOLE) for o in outs]
        return call(body, [SCALARS, *(WHOLE,) * (len(state) - 1)], outs, state, cost=cost, name=name)

    project = step(
        project_step_kernel, sum2, got2, (HALF, 96),
        (project_weight, project_first, project_second), name="project_step",
    )
    expand = step(
        expand_step_kernel, sum1, got1, (24, 2 * D),
        (expand_weight, expand_first, expand_second), name="expand_step",
    )
    tiles0, project = lax.optimization_barrier((tiles0, project))
    sum0 = jnp.sum(tiles0.astype(f32), axis=0)
    got0 = swap(sum0, "dp")
    *attention, vector_grad, vector_second_new, vector_new = step(
        attention_step_kernel, sum0, got0, (24, 2 * D),
        (attention_weights, attention_first, attention_second, vectors, vector_first, vector_second),
        [(12, HALF)] * 3, name="attention_step",
    )
    return (
        block_out,
        input_grad,
        *attention,
        *expand,
        *project,
        vector_grad,
        vector_second_new,
        vector_new,
    )


def solution(mesh):
    fine = Mesh(mesh.devices.reshape(2, 4, 4, 2, 2), EVERY)
    rows = ("dp", "z", "y", "xh")
    deep = ("z", "y", "xh")
    placed = (
        P(rows, "xl"),
        P("dp"),
        P("dp", deep),
        P(rows, "xl"),
        *(P(deep, "xl"),) * 6,
        *(P("xl", deep),) * 3,
        *(P(None, "xl"),) * 3,
    )
    out = (
        P(rows, "xl"),
        P(rows, "xl"),
        *(P(deep, "xl"),) * 6,
        *(P("xl", deep),) * 3,
        *(P(None, "xl"),) * 3,
    )
    return jax.shard_map(per_device, mesh=fine, in_specs=placed, out_specs=out, check_vma=False)
```

```python
import jax
import jax.numpy as jnp
from jax import lax
from jax.experimental import pallas as pl
from jax.experimental.pallas import tpu as pltpu
from jax.sharding import Mesh
from jax.sharding import PartitionSpec as P

D = 768
HD = 64
FF = 3072
SEQ = 197
STEP = 10
PAD = 208
IMAGES = 2
ROWS = PAD * IMAGES
HALF = D // 2

norm_eps = 1e-06
beta_first = 0.9
beta_second = 0.999
learn_rate = 0.04
vector_rate = 0.25
decay_rate = 0.05
adam_eps = 1e-08

f32 = jnp.float32
bf16 = jnp.bfloat16

DP = ("dp",)
Z = ("z",)
Y = ("y",)
X = ("xh", "xl")
CHIPS = ("xl", "z", "y", "xh")
EVERY = ("dp", "z", "y", "xh", "xl")


def dot(a, b):
    return lax.dot_general(a, b, (((1,), (0,)), ((), ())), preferred_element_type=f32)


def dot_rows(a, b):
    return lax.dot_general(a, b, (((0,), (0,)), ((), ())), preferred_element_type=f32)


def dot_lanes(a, b):
    return lax.dot_general(a, b, (((1,), (1,)), ((), ())), preferred_element_type=f32)


def block(shape, index):
    return pl.BlockSpec(shape, index)


WHOLE = pl.BlockSpec(memory_space=pltpu.VMEM)
SCALARS = pl.BlockSpec(memory_space=pltpu.SMEM)
LEFT = pl.BlockSpec(memory_space=pl.ANY)


def call(body, ins, outs, args, grid=(), scratch=(), after=(), cost=10, prefetch=0, name=None):
    count = len(args)

    def run(*refs):
        body(*refs[:count], *refs[count + len(after) :])

    return pl.pallas_call(
        run if after else body,
        out_shape=[jax.ShapeDtypeStruct(s, t) for s, t, _ in outs],
        grid_spec=pltpu.PrefetchScalarGridSpec(
            num_scalar_prefetch=prefetch,
            grid=grid,
            in_specs=[*ins, *(LEFT for _ in after)],
            out_specs=[spec for _, _, spec in outs],
            scratch_shapes=list(scratch),
        ),
        compiler_params=pltpu.CompilerParams(vmem_limit_bytes=52 * 1024 * 1024),
        cost_estimate=pl.CostEstimate(flops=cost * 10**9 + 1000, bytes_accessed=0, transcendentals=0),
        name=name,
    )(*args, *after)


def iota(shape, dim):
    return lax.broadcasted_iota(jnp.int32, shape, dim)


def row_picks():
    r = iota((ROWS, PAD), 0)
    j = iota((ROWS, PAD), 1)
    second = r >= PAD
    s = jnp.where(second, r - PAD, r)
    t = jnp.where(second, s + SEQ, s)
    live = s < SEQ
    even = jnp.where(live & (t == 2 * j), 1.0, 0.0).astype(bf16)
    odd = jnp.where(live & (t == 2 * j + 1), 1.0, 0.0).astype(bf16)
    return even, odd


def row_picks_back():
    r = iota((PAD, ROWS), 1)
    j = iota((PAD, ROWS), 0)
    second = r >= PAD
    s = jnp.where(second, r - PAD, r)
    t = jnp.where(second, s + SEQ, s)
    live = s < SEQ
    even = jnp.where(live & (t == 2 * j), 1.0, 0.0).astype(bf16)
    odd = jnp.where(live & (t == 2 * j + 1), 1.0, 0.0).astype(bf16)
    return even, odd


def lane_split():
    l = iota((256, 256), 0)
    c = iota((256, 256), 1)
    target = jnp.where(c < 128, 2 * c, 2 * (c - 128) + 1)
    return jnp.where(l == target, 1.0, 0.0).astype(bf16)


def lane_join():
    l = iota((256, 256), 1)
    c = iota((256, 256), 0)
    target = jnp.where(c < 128, 2 * c, 2 * (c - 128) + 1)
    return jnp.where(l == target, 1.0, 0.0).astype(bf16)


def unpack(own_ref, got_ref, gy):
    own, got = own_ref[...], got_ref[...]
    first = jnp.where(gy == 0, own.astype(f32), got.astype(f32)).astype(bf16)
    last = jnp.where(gy == 0, got.astype(f32), own.astype(f32)).astype(bf16)
    split = lane_split()
    evens, odds = [], []
    for half in (first, last):
        for b in range(3):
            both = dot(half[:, 256 * b : 256 * b + 256], split).astype(bf16)
            evens.append(both[:, :128])
            odds.append(both[:, 128:])
    even_rows, odd_rows = row_picks()
    return dot(even_rows, jnp.concatenate(evens, axis=1)) + dot(odd_rows, jnp.concatenate(odds, axis=1))


def pack(rows_low, gy, keep_ref, send_ref):
    even_rows, odd_rows = row_picks_back()
    even = dot(even_rows, rows_low).astype(bf16)
    odd = dot(odd_rows, rows_low).astype(bf16)
    join = lane_join()
    for b in range(3):
        blocks = []
        for half in range(2):
            at = HALF * half + 128 * b
            both = jnp.concatenate([even[:, at : at + 128], odd[:, at : at + 128]], axis=1)
            blocks.append(dot(both, join))
        keep_ref[:, 256 * b : 256 * b + 256] = jnp.where(gy == 0, blocks[0], blocks[1]).astype(bf16)
        send_ref[:, 256 * b : 256 * b + 256] = jnp.where(gy == 0, blocks[1], blocks[0]).astype(bf16)


def norm_parts(v):
    center = jnp.mean(v, axis=1, keepdims=True)
    away = v - center
    scale = lax.rsqrt(jnp.mean(away * away, axis=1, keepdims=True) + norm_eps)
    return away * scale, scale


def norm_back(grad, scaled, scale, gain):
    pushed = grad * gain
    first = jnp.mean(pushed, axis=1, keepdims=True)
    cross = jnp.mean(pushed * scaled, axis=1, keepdims=True)
    return (pushed - first - scaled * cross) * scale


def prepare_kernel(me_ref, attn_ref, expand_ref, project_ref, attn_out, ff_out):
    me = me_ref[0]
    l = iota((512, 256), 0)
    c = iota((512, 256), 1)
    kind = 2 * me + jnp.where(c < 128, 0, 1)
    pick = jnp.where(l == 4 * (c & 127) + kind, 1.0, 0.0).astype(bf16)
    for b in range(3):
        both = dot(attn_ref[:, 512 * b : 512 * b + 512].astype(bf16), pick).astype(bf16)
        attn_out[:, 128 * b : 128 * b + 128] = both[:, :128]
        attn_out[:, HALF + 128 * b : HALF + 128 * b + 128] = both[:, 128:]
    ff_out[:, :D] = jnp.where(me == 0, expand_ref[:, :D], expand_ref[:, D:]).astype(bf16)
    turned = project_ref[...].T
    mine = jnp.where(me == 0, turned[:48], turned[48:])
    ff_out[:, D : D + HALF] = mine[:24].astype(bf16)
    ff_out[:, D + HALF :] = mine[24:].astype(bf16)


def attend_kernel(
    me_ref, own_ref, got_ref, vec_ref, w_own, w_got,
    soft_out, mixed_out, x_out, normed_out, qkv_out, w_out, wo_out,
    x_ref, normed_ref, qkv_ref, w_ref, sems,
):
    step = pl.program_id(0)
    copies = [
        pltpu.make_async_copy(x_ref, x_out, sems.at[0]),
        pltpu.make_async_copy(normed_ref, normed_out, sems.at[1]),
        pltpu.make_async_copy(qkv_ref, qkv_out, sems.at[2]),
        pltpu.make_async_copy(w_ref.at[pl.ds(0, 3)], w_out, sems.at[3]),
        pltpu.make_async_copy(w_ref.at[3], wo_out, sems.at[4]),
    ]

    @pl.when(step == 0)
    def _():
        me, gy = me_ref[0], me_ref[1]
        for ref, place in ((w_own, me), (w_got, 1 - me)):
            for half in range(2):
                for y in range(2):
                    w_ref[pl.ds(2 * place + half, 1), :, HALF * y : HALF * y + HALF] = ref[
                        y, :, HALF * half : HALF * half + HALF
                    ][None]
        copies[3].start()
        copies[4].start()
        x_ref[...] = unpack(own_ref, got_ref, gy).astype(bf16)
        copies[0].start()
        scaled, _ = norm_parts(x_ref[...].astype(f32))
        normed_ref[...] = (scaled * vec_ref[0:1, :] + vec_ref[1:2, :]).astype(bf16)
        copies[1].start()

        def project(i, carry):
            cols = pl.ds(pl.multiple_of(256 * i, 256), 256)
            for kind, row in ((0, 2), (1, None), (2, 3)):
                part = dot(normed_ref[...], w_ref[kind, :, cols])
                if row is not None:
                    part = part + vec_ref[row : row + 1, cols]
                qkv_ref[kind, :, cols] = part.astype(bf16)
            return carry

        lax.fori_loop(0, 3, project, 0)
        copies[2].start()

    @pl.when(step > 0)
    def _():
        cols = pl.ds(pl.multiple_of(128 * (step - 1), 128), 128)
        lane = iota((PAD, 128), 1)
        key_live = iota((PAD, PAD), 0) < SEQ
        for image in range(IMAGES):
            rows = pl.ds(PAD * image, PAD)
            q = qkv_ref[0, rows, cols] * jnp.asarray(0.125, bf16)
            k = qkv_ref[1, rows, cols]
            v = qkv_ref[2, rows, cols]
            total = None
            for n in range(2):
                inside = (lane < HD) == (n == 0)
                scores = dot_lanes(k, jnp.where(inside, q, jnp.zeros_like(q)))
                scores = jnp.where(key_live, scores, -1e30)
                terms = jnp.exp(scores - jnp.max(scores, axis=0, keepdims=True))
                soft = terms * (1.0 / jnp.sum(terms, axis=0, keepdims=True))
                soft = soft.astype(bf16)
                soft_out[0, 2 * image + n] = soft
                part = dot_rows(soft, jnp.where(inside, v, jnp.zeros_like(v)))
                total = part if total is None else total + part
            mixed_out[rows, :] = total.astype(bf16)

    @pl.when(step == 6)
    def _():
        for copy in copies:
            copy.wait()


def gelu_parts(v):
    below = 0.5 + 0.5 * lax.erf(v * 0.7071067811865476)
    return v * below, below + v * jnp.exp(-0.5 * v * v) * 0.3989422804014327


def gather_rows(first, last):
    return jnp.concatenate([first.astype(f32), last.astype(f32)], axis=0).astype(bf16)


def place_rows(w2, ff_ref):
    for d in range(2):
        for g in range(8):
            for y in range(2):
                piece = ff_ref[d, g, y]
                rows = slice(96 * g + 48 * d, 96 * g + 48 * d + 48)
                w2[rows, HALF * y : HALF * y + HALF] = gather_rows(piece[:, :HALF], piece[:, HALF:])


def second_kernel(
    me_ref, live_ref, own_ref, got_ref, vec_ref, x_ref, mixed_ref, wo_ref,
    up_out, middle_out, second_out,
):
    up = unpack(own_ref, got_ref, me_ref[1])
    image = jnp.where(iota((ROWS, 1), 0) < PAD, live_ref[0], live_ref[1])
    up_out[...] = jnp.where(image == 1, up, 0.0).astype(bf16)
    middle = x_ref[...].astype(f32) + dot(mixed_ref[...], wo_ref[...]) + vec_ref[4:5, :]
    middle_out[...] = middle
    scaled, _ = norm_parts(middle)
    second_out[...] = (scaled * vec_ref[5:6, :] + vec_ref[6:7, :]).astype(bf16)


def expand_kernel(
    me_ref, up_ref, second_ref, bias_ref, w1_ref,
    act_out, slope_out, mine_out, theirs_out, w1_out,
    total,
):
    me = me_ref[0]
    for pair in range(16):
        w1_out[48 * pair : 48 * pair + 48, :] = gather_rows(
            w1_ref[0, 2 * pair, 0], w1_ref[0, 2 * pair + 1, 0]
        )

    for i in range(3):
        cols = slice(256 * i, 256 * i + 256)
        inner = dot(second_ref[...], w1_out[:, cols]) + bias_ref[:, cols]
        act, slope = gelu_parts(inner)
        act = act.astype(bf16)
        act_out[:, cols] = act
        slope_out[:, cols] = slope.astype(bf16)
    total[...] = dot_rows(act_out[...], up_ref[...]).astype(bf16)

    for g in range(8):
        for ref, place in ((mine_out, me), (theirs_out, 1 - me)):
            part = total[pl.ds(pl.multiple_of(96 * g + 48 * place, 16), 48), :]
            for y in range(2):
                ref[y, g] = part[:, HALF * y : HALF * y + HALF]


def contract_kernel(
    me_ref, up_ref, slope_ref, second_ref, ff_ref,
    grad_out, hidden_out, mine_out, theirs_out,
    turned, w2,
):
    step = pl.program_id(0)
    me = me_ref[0]

    @pl.when(step == 0)
    def _():
        turned[...] = second_ref[...].T

    place_rows(w2, ff_ref)
    for i in range(3):
        cols = slice(256 * i, 256 * i + 256)
        grad = dot_lanes(up_ref[...], w2[cols, :]) * slope_ref[:, cols].astype(f32)
        grad = grad.astype(bf16)
        grad_out[:, cols] = grad
        hidden_out[:, cols] = jnp.sum(grad.astype(f32), axis=0, keepdims=True)

    def outer(ref):
        for i in range(3):
            cols = slice(256 * i, 256 * i + 256)
            ref[0, :, cols] = dot(turned[...], grad_out[:, cols]).astype(bf16)

    pl.when((step & 1) == me)(lambda: outer(mine_out))
    pl.when((step & 1) != me)(lambda: outer(theirs_out))


def middle_back_kernel(
    me_ref, vec_ref, inner_hbm, w1_hbm, soft_hbm, up_hbm, middle_hbm, wo_hbm, normed_hbm, mixed_hbm, qkv_hbm,
    mine_hbm, theirs_hbm, sums_out, grads_hbm, gm_hbm,
    inner_ref, w1_ref, soft_ref, up_ref, middle_ref, wo_ref, normed_ref, mixed_ref, qkv_ref,
    grad_second, gml, grad_mixed, normed_turned, mixed_turned, pieces, grads_ref, gm_ref, sems,
):
    me = me_ref[0]
    ahead = []
    for j in range(4):
        cols = pl.ds(D * j, D)
        ahead.append((inner_hbm.at[:, cols], inner_ref.at[j]))
        ahead.append((w1_hbm.at[:, cols], w1_ref.at[j]))
    ahead += [
        (middle_hbm, middle_ref), (up_hbm, up_ref), (wo_hbm, wo_ref),
        (normed_hbm, normed_ref), (mixed_hbm, mixed_ref), (qkv_hbm, qkv_ref),
    ]
    reads = [pltpu.make_async_copy(src, dst, sems.at[i]) for i, (src, dst) in enumerate(ahead)]

    def read_soft(i):
        return pltpu.make_async_copy(soft_hbm.at[i], soft_ref.at[i], sems.at[14 + i])

    grads_write = pltpu.make_async_copy(grads_ref, grads_hbm, sems.at[20])
    gm_write = pltpu.make_async_copy(gm_ref, gm_hbm, sems.at[21])

    def write(kind, act):
        cols = pl.ds(HALF * (kind % 2), HALF)
        for to, place in ((mine_hbm, kind // 2), (theirs_hbm, 1 - kind // 2)):
            copy = pltpu.make_async_copy(pieces.at[kind], to.at[:, :, cols], sems.at[22 + kind])
            pl.when(me == place)(lambda copy=copy: act(copy))

    def outer(kind, left, right):
        grad = dot(left[...], right[...]).astype(bf16)
        for y in range(2):
            pieces[kind, y] = grad[:, HALF * y : HALF * y + HALF]
        write(kind, lambda copy: copy.start())

    for read in reads:
        read.start()
    for i in range(6):
        read_soft(i).start()
    for j in range(4):
        reads[2 * j].wait()
        reads[2 * j + 1].wait()
        part = dot_lanes(inner_ref[j], w1_ref[j])
        if j == 0:
            grad_second[...] = part
        else:
            grad_second[...] += part
    for read in reads[8:]:
        read.wait()
    grad = grad_second[...]
    scaled, scale = norm_parts(middle_ref[...])
    up = up_ref[...].astype(f32)
    gm = up + norm_back(grad, scaled, scale, vec_ref[5:6, :])
    gm_ref[...] = gm
    gm_write.start()
    gml[...] = gm.astype(bf16)
    sums_out[2:3, :] = jnp.sum(gml[...].astype(f32), axis=0, keepdims=True)
    sums_out[3:4, :] = jnp.sum(grad * scaled, axis=0, keepdims=True)
    sums_out[4:5, :] = jnp.sum(grad, axis=0, keepdims=True)
    sums_out[5:6, :] = jnp.sum(up, axis=0, keepdims=True)
    grad_mixed[...] = dot_lanes(gml[...], wo_ref[...]).astype(bf16)
    mixed_turned[...] = mixed_ref[...].T
    outer(3, mixed_turned, gml)
    normed_turned[...] = normed_ref[...].T
    lane = iota((PAD, 128), 1)

    def attend(i, carry):
        cols = pl.ds(pl.multiple_of(128 * i, 128), 128)
        read_soft(i).wait()
        for image in range(IMAGES):
            rows = pl.ds(PAD * image, PAD)
            q = qkv_ref[0, rows, cols]
            k = qkv_ref[1, rows, cols]
            v = qkv_ref[2, rows, cols]
            g = grad_mixed[rows, cols]
            dq = dk = dv = jnp.zeros((PAD, 128), f32)
            for n in range(2):
                inside = (lane < HD) == (n == 0)
                zero = jnp.zeros_like(g)
                g_in = jnp.where(inside, g, zero)
                soft_low = soft_ref[i, 2 * image + n]
                soft = soft_low.astype(f32)
                grad_soft = dot_lanes(v, g_in)
                level = jnp.sum(grad_soft * soft, axis=0, keepdims=True)
                scores = (soft * (grad_soft - level)).astype(bf16)
                dv = dv + dot(soft_low, g_in)
                dk = dk + dot(scores, jnp.where(inside, q, zero))
                dq = dq + dot_rows(scores, jnp.where(inside, k, zero))
            grads_ref[0, rows, cols] = (dq * 0.125).astype(bf16)
            grads_ref[1, rows, cols] = (dk * 0.125).astype(bf16)
            grads_ref[2, rows, cols] = dv.astype(bf16)
        return carry

    lax.fori_loop(0, 6, attend, 0)
    grads_write.start()
    for kind in range(3):
        outer(kind, normed_turned, grads_ref.at[kind])
    sums_out[0:1, :] = jnp.sum(grads_ref[0].astype(f32), axis=0, keepdims=True)
    sums_out[1:2, :] = jnp.sum(grads_ref[2].astype(f32), axis=0, keepdims=True)
    grads_write.wait()
    gm_write.wait()
    for kind in range(4):
        write(kind, lambda copy: copy.wait())


def input_back_kernel(
    me_ref, vec_ref, grads_ref, w_ref, x_ref, gm_ref, keep_out, send_out, sums_out, total
):
    step = pl.program_id(0)
    part = dot_lanes(grads_ref[0], w_ref[0])

    @pl.when(step == 0)
    def _():
        total[...] = part

    @pl.when(step > 0)
    def _():
        total[...] += part

    @pl.when(step == 2)
    def _():
        grad = total[...]
        scaled, scale = norm_parts(x_ref[...].astype(f32))
        out = gm_ref[...] + norm_back(grad, scaled, scale, vec_ref[0:1, :])
        pack(out.astype(bf16), me_ref[1], keep_out, send_out)
        sums_out[0:1, :] = jnp.sum(grad * scaled, axis=0, keepdims=True)
        sums_out[1:2, :] = jnp.sum(grad, axis=0, keepdims=True)


def output_kernel(me_ref, vec_ref, middle_ref, act_ref, ff_ref, keep_out, send_out, w2, total):
    step = pl.program_id(0)
    place_rows(w2, ff_ref)
    part = dot(act_ref[...], w2[...])

    @pl.when(step == 0)
    def _():
        total[...] = middle_ref[...] + vec_ref[7:8, :] + part

    @pl.when(step > 0)
    def _():
        total[...] += part

    @pl.when(step == 3)
    def _():
        pack(total[...].astype(bf16), me_ref[1], keep_out, send_out)


def assemble_kernel(at_ref, *refs):
    out = refs[-1]
    step = pl.program_id(0)
    for r in range(4):
        pl.when(step == r)(lambda r=r: out.__setitem__(..., refs[r][...].reshape(out.shape)))


def blocks_sum_kernel(at_ref, *refs):
    ins, outs = refs[:-4], refs[-4:]
    step = pl.program_id(0)
    total = ins[0][...].astype(f32)
    for ref in ins[1:]:
        total = total + ref[...].astype(f32)
    total = total.astype(bf16)
    for r in range(4):
        pl.when(step == r)(lambda r=r: outs[r].__setitem__(..., total.reshape(outs[r].shape)))


def sum_kernel(a_ref, b_ref, c_ref, d_ref, out_ref):
    total = a_ref[...].astype(f32) + b_ref[...].astype(f32) + c_ref[...].astype(f32) + d_ref[...].astype(f32)
    out_ref[...] = total.astype(bf16)


def last_spread_kernel(a_ref, b_ref, c_ref, d_ref, va_ref, vb_ref, vc_ref, vd_ref, out_ref):
    vector = va_ref[...].astype(f32) + vb_ref[...].astype(f32) + vc_ref[...].astype(f32) + vd_ref[...].astype(f32)
    vector = vector.astype(bf16)
    total = a_ref[...].astype(f32) + b_ref[...].astype(f32) + c_ref[...].astype(f32) + d_ref[...].astype(f32)
    total = total.reshape(2 * 192, D)
    for i in range(16):
        out_ref[i, :16, :] = vector
        out_ref[i, 16:, :] = total[24 * i : 24 * i + 24].astype(bf16)


def adamw_step(parameter, gradient, first_moment, second_moment, step_rate, decay_factor):
    first_new = beta_first * first_moment + (1.0 - beta_first) * gradient
    second_new = beta_second * second_moment + (1.0 - beta_second) * gradient * gradient
    first_hat = first_new / (1.0 - beta_first**STEP)
    second_hat = second_new / (1.0 - beta_second**STEP)
    updated = parameter - step_rate * (
        first_hat / (jnp.sqrt(second_hat) + adam_eps) + decay_factor * parameter
    )
    return second_new, updated


def ordered(me, own, got):
    return jnp.where(me == 0, own, got), jnp.where(me == 0, got, own)


def attention_step_kernel(
    me_ref, own_ref, got_ref, w_ref, m_ref, v_ref, vec_ref, vec_m_ref, vec_v_ref,
    grad_out, second_out, new_out, vec_grad_out, vec_second_out, vec_new_out,
):
    pieces = ordered(me_ref[0], own_ref[16:, :], got_ref[16:, :])
    l = iota((512, 512), 0)
    c = iota((512, 512), 1)
    pick = jnp.where(c == 4 * (l & 127) + (l >> 7), 1.0, 0.0)
    for b in range(3):
        kinds = [
            pieces[k // 2][:, HALF * (k % 2) + 128 * b : HALF * (k % 2) + 128 * b + 128]
            for k in range(4)
        ]
        grad_out[:, 512 * b : 512 * b + 512] = jnp.dot(
            jnp.concatenate(kinds, axis=1), pick, precision=lax.Precision.HIGHEST,
            preferred_element_type=f32,
        )
    second_out[...], new_out[...] = adamw_step(
        w_ref[...], grad_out[...], m_ref[...], v_ref[...], learn_rate, decay_rate
    )
    vector = own_ref[:12, :] + got_ref[:12, :]
    vec_grad_out[...] = jnp.where(me_ref[1] == 0, vector[:, :HALF], vector[:, HALF:])
    vec_second_out[...], vec_new_out[...] = adamw_step(
        vec_ref[...], vec_grad_out[...], vec_m_ref[...], vec_v_ref[...], vector_rate, 0.0
    )


def expand_step_kernel(me_ref, own_ref, got_ref, w_ref, m_ref, v_ref, grad_out, second_out, new_out):
    first, last = ordered(me_ref[0], own_ref[...], got_ref[...])
    grad_out[:, :D] = first
    grad_out[:, D:] = last
    second_out[...], new_out[...] = adamw_step(
        w_ref[...], grad_out[...], m_ref[...], v_ref[...], learn_rate, decay_rate
    )


def project_step_kernel(me_ref, own_ref, got_ref, w_ref, m_ref, v_ref, grad_out, second_out, new_out):
    first, last = ordered(me_ref[0], own_ref[...], got_ref[...])
    grad_out[...] = jnp.concatenate([first, last], axis=0).T
    second_out[...], new_out[...] = adamw_step(
        w_ref[...], grad_out[...], m_ref[...], v_ref[...], learn_rate, decay_rate
    )


def place(axes):
    at = 0
    for a in axes:
        at = at * lax.axis_size(a) + lax.axis_index(a)
    return at


def swap(x, axis):
    return lax.ppermute(x, axis, [(0, 1), (1, 0)])


def core_sum(mine, theirs):
    return (mine.astype(f32) + swap(theirs, "dp").astype(f32)).astype(bf16)


def assemble(parts, at, shape, piece, index, after=(), cost=0):
    flat = tuple(n for n in piece if n > 1)
    return pl.pallas_call(
        assemble_kernel,
        out_shape=jax.ShapeDtypeStruct(shape, bf16),
        grid_spec=pltpu.PrefetchScalarGridSpec(
            num_scalar_prefetch=1,
            grid=(4,),
            in_specs=[
                *(pl.BlockSpec(flat, lambda r, at: (0,) * len(flat)) for _ in range(4)),
                *(LEFT for _ in after),
            ],
            out_specs=pl.BlockSpec(piece, lambda r, at: index((at[0] + 3 * r) % 4)),
        ),
        compiler_params=pltpu.CompilerParams(vmem_limit_bytes=32 * 1024 * 1024),
        cost_estimate=pl.CostEstimate(flops=cost * 10**9 + 1000, bytes_accessed=0, transcendentals=0),
        name="assemble",
    )(at.reshape(1).astype(jnp.int32), *(p.reshape(flat) for p in parts), *after)


def ring_blocks(parts, at, shape, piece, index):
    spec = pl.BlockSpec(piece, lambda r, at: index((at[0] + r) % 4))
    flat = tuple(n for n in piece if n > 1)
    return pl.pallas_call(
        blocks_sum_kernel,
        out_shape=[jax.ShapeDtypeStruct(flat, bf16)] * 4,
        grid_spec=pltpu.PrefetchScalarGridSpec(
            num_scalar_prefetch=1,
            grid=(4,),
            in_specs=[spec] * len(parts),
            out_specs=[pl.BlockSpec(flat, lambda r, at: (0,) * len(flat))] * 4,
        ),
        compiler_params=pltpu.CompilerParams(vmem_limit_bytes=32 * 1024 * 1024),
        cost_estimate=pl.CostEstimate(flops=1000, bytes_accessed=0, transcendentals=0),
        name="ring_blocks",
    )(at.reshape(1).astype(jnp.int32), *(p.reshape(shape) for p in parts))


def hop(x, axes, r):
    return lax.ppermute(x, axes, [(i, (i + r) % 4) for i in range(4)])


def ring(blocks, axes):
    return blocks[0], *(hop(blocks[r], axes, r) for r in (1, 3, 2))


def crossed(x, axis, bit):
    return lax.ppermute(x, axis, [(i, i ^ bit) for i in range(lax.axis_size(axis))])


def to_all(x, axes):
    near, back = hop(x, axes, 1), hop(x, axes, 3)
    return x, near, hop(x, axes, 2), back


def sum_of(parts):
    total = parts[0].astype(f32)
    for part in parts[1:]:
        total = total + part.astype(f32)
    return total


def spread_sum(blocks, axes):
    tiles = lax.all_to_all(blocks, axes, 0, 0, tiled=True)
    return jnp.sum(tiles.astype(f32), axis=0)


def own_images(stored, gy):
    rows = stored.shape[0] // 2
    own = lax.dynamic_slice_in_dim(stored, rows * gy, rows, 0)
    other = lax.dynamic_slice_in_dim(stored, rows * (1 - gy), rows, 0)
    pad = ((0, PAD - rows), (0, 0))
    return jnp.pad(own, pad), jnp.pad(other, pad)


def stored_rows(keep, got, gy):
    first = jnp.where(gy == 0, keep, got)[:SEQ]
    last = jnp.where(gy == 0, got, keep)[:SEQ]
    return jnp.concatenate([first, last], axis=0).astype(f32)


def per_device(
    tokens,
    image_counts,
    slot_order,
    cotangent,
    attention_weights,
    attention_first,
    attention_second,
    expand_weight,
    expand_first,
    expand_second,
    project_weight,
    project_first,
    project_second,
    vectors,
    vector_first,
    vector_second,
):
    dp = lax.axis_index("dp")
    gy = lax.axis_index("xl")
    me = jnp.stack([dp, gy]).astype(jnp.int32)

    token_own, token_other = own_images(tokens, gy)
    token_got = swap(token_other, "xl")
    grad_own, grad_other = own_images(cotangent, gy)
    grad_got = swap(grad_other, "xl")
    vec_got = swap(vectors, "xl")
    attn_piece, ff_piece = call(
        prepare_kernel,
        [SCALARS, WHOLE, WHOLE, WHOLE],
        [((24, D), bf16, WHOLE), ((24, 2 * D), bf16, WHOLE)],
        (me, attention_weights, expand_weight, project_weight),
        name="prepare",
    )
    ff = lax.all_gather(ff_piece, EVERY).reshape(2, 32, 2, 24, 2 * D)
    at_x, at_y, at_z = place(X), place(Y), place(Z)

    def across_x(p):
        return p % 2, 0, p // 2, 0, 0

    attn = to_all(attn_piece, X)
    attn = assemble(attn, at_x, (2, 1, 2, 24, D), (1, 1, 1, 24, D), across_x)
    attn = to_all(attn.reshape(2, 48, D), Y)
    attn, token_got, vec_got = lax.optimization_barrier((attn, token_got, vec_got))
    attn = assemble(attn, at_y, (2, 4, 48, D), (2, 1, 48, D), lambda p: (0, p, 0, 0))
    vec_first, vec_last = ordered(gy, vectors, vec_got)
    vec = jnp.concatenate([vec_first, vec_last], axis=1)
    bias = vec[8:].T.reshape(1, FF)
    live = (slot_order[0] < image_counts[0]).astype(jnp.int32)
    live = lax.dynamic_slice_in_dim(live, IMAGES * gy, IMAGES)
    attn = to_all(attn.reshape(2, 192, D), Z)
    attn, vec, bias, live, token_own, token_got = lax.optimization_barrier(
        (attn, vec, bias, live, token_own, token_got)
    )
    attn = assemble(attn, at_z, (2, 4, 192, D), (2, 1, 192, D), lambda p: (0, p, 0, 0))
    w_own, w_got = (w.reshape(2, D, D) for w in (attn, swap(attn, "dp")))

    tall = block((ROWS, D), lambda j: (0, 0))
    wide = block((ROWS, D), lambda j: (0, j))
    w1_block = block((1, 32, 1, 24, D), lambda j: (j % 2, 0, j // 2, 0, 0))
    w2_block = block((2, 8, 2, 24, D), lambda j: (0, j, 0, 0, 1))
    pieces2 = block((2, 8, 48, HALF), lambda j: (0, j, 0, 0))
    soft_shape = (6, 2 * IMAGES, PAD, PAD)

    soft, mixed, x, normed, qkv, w_qkv, w_o = call(
        attend_kernel,
        [SCALARS, *(WHOLE,) * 5],
        [
            (soft_shape, bf16, block((1, *soft_shape[1:]), lambda p: (jnp.maximum(p - 1, 0), 0, 0, 0))),
            ((ROWS, D), bf16, block((ROWS, 128), lambda p: (0, jnp.maximum(p - 1, 0)))),
            ((ROWS, D), bf16, LEFT),
            ((ROWS, D), bf16, LEFT),
            ((3, ROWS, D), bf16, LEFT),
            ((3, D, D), bf16, LEFT),
            ((D, D), bf16, LEFT),
        ],
        (me, token_own, token_got, vec, w_own, w_got),
        grid=(7,),
        scratch=[
            pltpu.VMEM((ROWS, D), bf16),
            pltpu.VMEM((ROWS, D), bf16),
            pltpu.VMEM((3, ROWS, D), bf16),
            pltpu.VMEM((4, D, D), bf16),
            pltpu.SemaphoreType.DMA((5,)),
        ],
        name="attend",
    )

    up, middle, second = call(
        second_kernel,
        [SCALARS, SCALARS, *(WHOLE,) * 6],
        [((ROWS, D), bf16, WHOLE), ((ROWS, D), f32, WHOLE), ((ROWS, D), bf16, WHOLE)],
        (me, live, grad_own, grad_got, vec, x, mixed, w_o),
        name="second",
    )
    act, slope, mine2, theirs2, w1 = call(
        expand_kernel,
        [SCALARS, WHOLE, WHOLE, block((1, D), lambda j: (0, j)), w1_block],
        [
            ((ROWS, FF), bf16, wide),
            ((ROWS, FF), bf16, wide),
            ((2, 32, 48, HALF), bf16, pieces2),
            ((2, 32, 48, HALF), bf16, pieces2),
            ((D, FF), bf16, block((D, D), lambda j: (0, j))),
        ],
        (me, up, second, bias, ff),
        grid=(4,),
        scratch=[pltpu.VMEM((D, D), bf16)],
        after=(w_o, soft),
        name="expand",
    )
    inner_grad, hidden_sums, mine1, theirs1 = call(
        contract_kernel,
        [SCALARS, WHOLE, wide, WHOLE, w2_block],
        [
            ((ROWS, FF), bf16, wide),
            ((1, FF), f32, block((1, D), lambda j: (0, j))),
            ((2, D, D), bf16, block((1, D, D), lambda j: (j // 2, 0, 0))),
            ((2, D, D), bf16, block((1, D, D), lambda j: (j // 2, 0, 0))),
        ],
        (me, up, slope, second, ff),
        grid=(4,),
        scratch=[pltpu.VMEM((D, ROWS), bf16), pltpu.VMEM((D, D), bf16)],
        name="contract",
    )
    ring2 = ring_blocks(
        (mine2, swap(theirs2, "dp")),
        place(X),
        (2, 16, 2, 48, HALF),
        (1, 16, 1, 48, HALF),
        lambda p: (p % 2, 0, p // 2, 0, 0),
    )
    got1, _ = lax.optimization_barrier((swap(theirs1, "dp"), ring2[0]))
    ring1 = ring_blocks(
        (mine1, got1), place(Y), (8, 4, 48, D), (8, 1, 48, D), lambda p: (0, p, 0, 0)
    )

    mine0, theirs0, sums_c, grads, gm = call(
        middle_back_kernel,
        [SCALARS, WHOLE, *(LEFT,) * 9],
        [
            ((2, D, D), bf16, LEFT),
            ((2, D, D), bf16, LEFT),
            ((6, D), f32, WHOLE),
            ((3, ROWS, D), bf16, LEFT),
            ((ROWS, D), f32, LEFT),
        ],
        (me, vec, inner_grad, w1, soft, up, middle, w_o, normed, mixed, qkv),
        scratch=[
            pltpu.VMEM((4, ROWS, D), bf16),
            pltpu.VMEM((4, D, D), bf16),
            pltpu.VMEM(soft_shape, bf16),
            pltpu.VMEM((ROWS, D), bf16),
            pltpu.VMEM((ROWS, D), f32),
            pltpu.VMEM((D, D), bf16),
            pltpu.VMEM((ROWS, D), bf16),
            pltpu.VMEM((ROWS, D), bf16),
            pltpu.VMEM((3, ROWS, D), bf16),
            pltpu.VMEM((ROWS, D), f32),
            pltpu.VMEM((ROWS, D), bf16),
            pltpu.VMEM((ROWS, D), bf16),
            pltpu.VMEM((D, ROWS), bf16),
            pltpu.VMEM((D, ROWS), bf16),
            pltpu.VMEM((4, 2, D, HALF), bf16),
            pltpu.VMEM((3, ROWS, D), bf16),
            pltpu.VMEM((ROWS, D), f32),
            pltpu.SemaphoreType.DMA((26,)),
        ],
        after=(ring2[0], ring1[0]),
        cost=0,
        name="middle_back",
    )
    got0 = swap(theirs0, "dp")
    ring2 = ring(ring2, X)
    near1 = hop(ring1[1], Y, 1), hop(ring1[3], Y, 3)
    ring2, mine0 = lax.optimization_barrier((ring2, mine0))
    mine0, near1, far1 = lax.optimization_barrier((mine0, near1, ring1[2]))
    far1 = hop(far1, Y, 2)
    part2 = call(
        sum_kernel, [WHOLE] * 4, [((16, 48, HALF), bf16, WHOLE)], ring2, cost=100, after=(near1[0], near1[1]), name="part"
    )[0]
    tiles2 = lax.all_to_all(part2, Z + Y, 0, 0, tiled=True)
    mine0, got0, _ = lax.optimization_barrier((mine0, got0, part2))
    ring0 = ring_blocks(
        (mine0, got0), place(Z), (2, 4, 192, D), (2, 1, 192, D), lambda p: (0, p, 0, 0)
    )
    tiles2, far1, _ = lax.optimization_barrier((tiles2, far1, ring0[0]))
    own0, near0, back0, far0 = ring(ring0, Z)
    keep_out, send_out = call(
        output_kernel,
        [SCALARS, WHOLE, WHOLE, wide, w2_block],
        [((PAD, D), bf16, block((PAD, D), lambda j: (0, 0)))] * 2,
        (me, vec, middle, act, ff),
        grid=(4,),
        scratch=[pltpu.VMEM((D, D), bf16), pltpu.VMEM((ROWS, D), f32)],
        after=(ring0[0],),
        cost=0,
        name="output",
    )
    far1, tiles2, keep_out = lax.optimization_barrier((far1, tiles2, keep_out))
    part1 = sum_of((ring1[0], *near1, far1)).astype(bf16).reshape(16, 24, D)
    tiles1 = lax.all_to_all(part1, ("xl", "z", "xh"), 0, 0, tiled=True)
    grads, near0, back0 = lax.optimization_barrier((grads, near0, back0))
    keep_in, send_in, sums_e = call(
        input_back_kernel,
        [
            SCALARS, WHOLE,
            block((1, ROWS, D), lambda k: (k, 0, 0)), block((1, D, D), lambda k: (k, 0, 0)),
            WHOLE, WHOLE,
        ],
        [
            ((PAD, D), bf16, block((PAD, D), lambda k: (0, 0))),
            ((PAD, D), bf16, block((PAD, D), lambda k: (0, 0))),
            ((2, D), f32, block((2, D), lambda k: (0, 0))),
        ],
        (me, vec, grads, w_qkv, x, gm),
        grid=(3,),
        scratch=[pltpu.VMEM((ROWS, D), f32)],
        cost=100,
        after=(part1,),
        name="input_back",
    )
    sums_e, hidden_sums = lax.optimization_barrier((sums_e, hidden_sums))
    vector = jnp.concatenate(
        [sums_e, sums_c, hidden_sums.reshape(D, 4).T, jnp.zeros((4, D), f32)], axis=0
    ).astype(bf16)
    vectors4 = ring((vector,) * 4, Z)
    got_in, got_out = swap(send_in, "xl"), swap(send_out, "xl")
    tiles2, vectors4, got_out = lax.optimization_barrier((tiles2, vectors4, got_out))
    sum2 = jnp.sum(tiles2.astype(f32), axis=0)
    got2 = swap(sum2, "dp")
    part0 = call(
        last_spread_kernel,
        [WHOLE] * 8,
        [((16, 40, D), bf16, WHOLE)],
        (own0, near0, back0, far0, *vectors4),
        cost=100,
        name="last_spread",
    )[0]
    part0, got_in = lax.optimization_barrier((part0, got_in))
    tiles0 = lax.all_to_all(part0, ("xl", "y", "xh"), 0, 0, tiled=True)
    sum1 = jnp.sum(tiles1.astype(f32), axis=0)
    got1 = swap(sum1, "dp")
    block_out = stored_rows(keep_out, got_out, gy)
    input_grad = stored_rows(keep_in, got_in, gy)

    def step(body, own, got, shape, state, outs=(), cost=0, name=None):
        state = (me, own, got, *state)
        outs = [(shape, f32, WHOLE)] * 3 + [(o, f32, WHOLE) for o in outs]
        return call(body, [SCALARS, *(WHOLE,) * (len(state) - 1)], outs, state, cost=cost, name=name)

    project = step(
        project_step_kernel, sum2, got2, (HALF, 96),
        (project_weight, project_first, project_second), name="project_step",
    )
    expand = step(
        expand_step_kernel, sum1, got1, (24, 2 * D),
        (expand_weight, expand_first, expand_second), name="expand_step",
    )
    tiles0, project = lax.optimization_barrier((tiles0, project))
    sum0 = jnp.sum(tiles0.astype(f32), axis=0)
    got0 = swap(sum0, "dp")
    *attention, vector_grad, vector_second_new, vector_new = step(
        attention_step_kernel, sum0, got0, (24, 2 * D),
        (attention_weights, attention_first, attention_second, vectors, vector_first, vector_second),
        [(12, HALF)] * 3, name="attention_step",
    )
    return (
        block_out,
        input_grad,
        *attention,
        *expand,
        *project,
        vector_grad,
        vector_second_new,
        vector_new,
    )


def solution(mesh):
    fine = Mesh(mesh.devices.reshape(2, 4, 4, 2, 2), EVERY)
    rows = ("dp", "z", "y", "xh")
    deep = ("z", "y", "xh")
    placed = (
        P(rows, "xl"),
        P("dp"),
        P("dp", deep),
        P(rows, "xl"),
        *(P(deep, "xl"),) * 6,
        *(P("xl", deep),) * 3,
        *(P(None, "xl"),) * 3,
    )
    out = (
        P(rows, "xl"),
        P(rows, "xl"),
        *(P(deep, "xl"),) * 6,
        *(P("xl", deep),) * 3,
        *(P(None, "xl"),) * 3,
    )
    return jax.shard_map(per_device, mesh=fine, in_specs=placed, out_specs=out, check_vma=False)
```

```python
import jax
import jax.numpy as jnp
from jax import lax
from jax.experimental import pallas as pl
from jax.experimental.pallas import tpu as pltpu
from jax.sharding import Mesh
from jax.sharding import PartitionSpec as P

D = 768
HD = 64
FF = 3072
SEQ = 197
STEP = 10
PAD = 208
IMAGES = 2
ROWS = PAD * IMAGES
HALF = D // 2

norm_eps = 1e-06
beta_first = 0.9
beta_second = 0.999
learn_rate = 0.04
vector_rate = 0.25
decay_rate = 0.05
adam_eps = 1e-08

f32 = jnp.float32
bf16 = jnp.bfloat16

DP = ("dp",)
Z = ("z",)
Y = ("y",)
X = ("xh", "xl")
CHIPS = ("xl", "z", "y", "xh")
EVERY = ("dp", "z", "y", "xh", "xl")


def dot(a, b):
    return lax.dot_general(a, b, (((1,), (0,)), ((), ())), preferred_element_type=f32)


def dot_rows(a, b):
    return lax.dot_general(a, b, (((0,), (0,)), ((), ())), preferred_element_type=f32)


def dot_lanes(a, b):
    return lax.dot_general(a, b, (((1,), (1,)), ((), ())), preferred_element_type=f32)


def block(shape, index):
    return pl.BlockSpec(shape, index)


WHOLE = pl.BlockSpec(memory_space=pltpu.VMEM)
SCALARS = pl.BlockSpec(memory_space=pltpu.SMEM)
LEFT = pl.BlockSpec(memory_space=pl.ANY)


def call(body, ins, outs, args, grid=(), scratch=(), after=(), cost=10, prefetch=0, name=None):
    count = len(args)

    def run(*refs):
        body(*refs[:count], *refs[count + len(after) :])

    return pl.pallas_call(
        run if after else body,
        out_shape=[jax.ShapeDtypeStruct(s, t) for s, t, _ in outs],
        grid_spec=pltpu.PrefetchScalarGridSpec(
            num_scalar_prefetch=prefetch,
            grid=grid,
            in_specs=[*ins, *(LEFT for _ in after)],
            out_specs=[spec for _, _, spec in outs],
            scratch_shapes=list(scratch),
        ),
        compiler_params=pltpu.CompilerParams(vmem_limit_bytes=52 * 1024 * 1024),
        cost_estimate=pl.CostEstimate(flops=cost * 10**9 + 1000, bytes_accessed=0, transcendentals=0),
        name=name,
    )(*args, *after)


def iota(shape, dim):
    return lax.broadcasted_iota(jnp.int32, shape, dim)


def row_picks():
    r = iota((ROWS, PAD), 0)
    j = iota((ROWS, PAD), 1)
    second = r >= PAD
    s = jnp.where(second, r - PAD, r)
    t = jnp.where(second, s + SEQ, s)
    live = s < SEQ
    even = jnp.where(live & (t == 2 * j), 1.0, 0.0).astype(bf16)
    odd = jnp.where(live & (t == 2 * j + 1), 1.0, 0.0).astype(bf16)
    return even, odd


def row_picks_back():
    r = iota((PAD, ROWS), 1)
    j = iota((PAD, ROWS), 0)
    second = r >= PAD
    s = jnp.where(second, r - PAD, r)
    t = jnp.where(second, s + SEQ, s)
    live = s < SEQ
    even = jnp.where(live & (t == 2 * j), 1.0, 0.0).astype(bf16)
    odd = jnp.where(live & (t == 2 * j + 1), 1.0, 0.0).astype(bf16)
    return even, odd


def lane_split():
    l = iota((256, 256), 0)
    c = iota((256, 256), 1)
    target = jnp.where(c < 128, 2 * c, 2 * (c - 128) + 1)
    return jnp.where(l == target, 1.0, 0.0).astype(bf16)


def lane_join():
    l = iota((256, 256), 1)
    c = iota((256, 256), 0)
    target = jnp.where(c < 128, 2 * c, 2 * (c - 128) + 1)
    return jnp.where(l == target, 1.0, 0.0).astype(bf16)


def unpack(own_ref, got_ref, gy):
    own, got = own_ref[...], got_ref[...]
    first = jnp.where(gy == 0, own.astype(f32), got.astype(f32)).astype(bf16)
    last = jnp.where(gy == 0, got.astype(f32), own.astype(f32)).astype(bf16)
    split = lane_split()
    evens, odds = [], []
    for half in (first, last):
        for b in range(3):
            both = dot(half[:, 256 * b : 256 * b + 256], split).astype(bf16)
            evens.append(both[:, :128])
            odds.append(both[:, 128:])
    even_rows, odd_rows = row_picks()
    return dot(even_rows, jnp.concatenate(evens, axis=1)) + dot(odd_rows, jnp.concatenate(odds, axis=1))


def pack(rows_low, gy, keep_ref, send_ref):
    even_rows, odd_rows = row_picks_back()
    even = dot(even_rows, rows_low).astype(bf16)
    odd = dot(odd_rows, rows_low).astype(bf16)
    join = lane_join()
    for b in range(3):
        blocks = []
        for half in range(2):
            at = HALF * half + 128 * b
            both = jnp.concatenate([even[:, at : at + 128], odd[:, at : at + 128]], axis=1)
            blocks.append(dot(both, join))
        keep_ref[:, 256 * b : 256 * b + 256] = jnp.where(gy == 0, blocks[0], blocks[1]).astype(bf16)
        send_ref[:, 256 * b : 256 * b + 256] = jnp.where(gy == 0, blocks[1], blocks[0]).astype(bf16)


def norm_parts(v):
    center = jnp.mean(v, axis=1, keepdims=True)
    away = v - center
    scale = lax.rsqrt(jnp.mean(away * away, axis=1, keepdims=True) + norm_eps)
    return away * scale, scale


def norm_back(grad, scaled, scale, gain):
    pushed = grad * gain
    first = jnp.mean(pushed, axis=1, keepdims=True)
    cross = jnp.mean(pushed * scaled, axis=1, keepdims=True)
    return (pushed - first - scaled * cross) * scale


def prepare_kernel(me_ref, attn_ref, expand_ref, project_ref, attn_out, ff_out):
    me = me_ref[0]
    l = iota((512, 256), 0)
    c = iota((512, 256), 1)
    kind = 2 * me + jnp.where(c < 128, 0, 1)
    pick = jnp.where(l == 4 * (c & 127) + kind, 1.0, 0.0).astype(bf16)
    for b in range(3):
        both = dot(attn_ref[:, 512 * b : 512 * b + 512].astype(bf16), pick).astype(bf16)
        attn_out[:, 128 * b : 128 * b + 128] = both[:, :128]
        attn_out[:, HALF + 128 * b : HALF + 128 * b + 128] = both[:, 128:]
    ff_out[:, :D] = jnp.where(me == 0, expand_ref[:, :D], expand_ref[:, D:]).astype(bf16)
    mine = jnp.where(me == 0, project_ref[:48, :], project_ref[48:, :])
    ff_out[:, D : D + HALF] = mine[:24].astype(bf16)
    ff_out[:, D + HALF :] = mine[24:].astype(bf16)


def attend_kernel(
    me_ref, own_ref, got_ref, vec_ref, w_own, w_got,
    soft_out, mixed_out, x_out, normed_out, qkv_out, w_out, wo_out,
    x_ref, normed_ref, qkv_ref, w_ref, sems,
):
    step = pl.program_id(0)
    copies = [
        pltpu.make_async_copy(x_ref, x_out, sems.at[0]),
        pltpu.make_async_copy(normed_ref, normed_out, sems.at[1]),
        pltpu.make_async_copy(qkv_ref, qkv_out, sems.at[2]),
        pltpu.make_async_copy(w_ref.at[pl.ds(0, 3)], w_out, sems.at[3]),
        pltpu.make_async_copy(w_ref.at[3], wo_out, sems.at[4]),
    ]

    @pl.when(step == 0)
    def _():
        me, gy = me_ref[0], me_ref[1]
        for ref, place in ((w_own, me), (w_got, 1 - me)):
            for half in range(2):
                for y in range(2):
                    w_ref[pl.ds(2 * place + half, 1), :, HALF * y : HALF * y + HALF] = ref[
                        y, :, HALF * half : HALF * half + HALF
                    ][None]
        copies[3].start()
        copies[4].start()
        x_ref[...] = unpack(own_ref, got_ref, gy).astype(bf16)
        copies[0].start()
        scaled, _ = norm_parts(x_ref[...].astype(f32))
        normed_ref[...] = (scaled * vec_ref[0:1, :] + vec_ref[1:2, :]).astype(bf16)
        copies[1].start()

        def project(i, carry):
            cols = pl.ds(pl.multiple_of(256 * i, 256), 256)
            for kind, row in ((0, 2), (1, None), (2, 3)):
                part = dot(normed_ref[...], w_ref[kind, :, cols])
                if row is not None:
                    part = part + vec_ref[row : row + 1, cols]
                qkv_ref[kind, :, cols] = part.astype(bf16)
            return carry

        lax.fori_loop(0, 3, project, 0)
        copies[2].start()

    @pl.when(step > 0)
    def _():
        cols = pl.ds(pl.multiple_of(128 * (step - 1), 128), 128)
        lane = iota((PAD, 128), 1)
        key_live = iota((PAD, PAD), 0) < SEQ
        for image in range(IMAGES):
            rows = pl.ds(PAD * image, PAD)
            q = qkv_ref[0, rows, cols] * jnp.asarray(0.125, bf16)
            k = qkv_ref[1, rows, cols]
            v = qkv_ref[2, rows, cols]
            total = None
            for n in range(2):
                inside = (lane < HD) == (n == 0)
                scores = dot_lanes(k, jnp.where(inside, q, jnp.zeros_like(q)))
                scores = jnp.where(key_live, scores, -1e30)
                terms = jnp.exp(scores - jnp.max(scores, axis=0, keepdims=True))
                soft = terms * (1.0 / jnp.sum(terms, axis=0, keepdims=True))
                soft = soft.astype(bf16)
                soft_out[0, 2 * image + n] = soft
                part = dot_rows(soft, jnp.where(inside, v, jnp.zeros_like(v)))
                total = part if total is None else total + part
            mixed_out[rows, :] = total.astype(bf16)

    @pl.when(step == 6)
    def _():
        for copy in copies:
            copy.wait()


def gelu_parts(v):
    below = 0.5 + 0.5 * lax.erf(v * 0.7071067811865476)
    return v * below, below + v * jnp.exp(-0.5 * v * v) * 0.3989422804014327


def gather_rows(first, last):
    return jnp.concatenate([first.astype(f32), last.astype(f32)], axis=0).astype(bf16)


def place_rows(w2, ff_ref):
    for d in range(2):
        for g in range(8):
            for y in range(2):
                piece = ff_ref[d, g, y]
                rows = slice(96 * g + 48 * d, 96 * g + 48 * d + 48)
                w2[rows, HALF * y : HALF * y + HALF] = gather_rows(piece[:, :HALF], piece[:, HALF:])


def second_kernel(
    me_ref, live_ref, own_ref, got_ref, vec_ref, x_ref, mixed_ref, wo_ref,
    up_out, middle_out, second_out,
):
    up = unpack(own_ref, got_ref, me_ref[1])
    image = jnp.where(iota((ROWS, 1), 0) < PAD, live_ref[0], live_ref[1])
    up_out[...] = jnp.where(image == 1, up, 0.0).astype(bf16)
    middle = x_ref[...].astype(f32) + dot(mixed_ref[...], wo_ref[...]) + vec_ref[4:5, :]
    middle_out[...] = middle
    scaled, _ = norm_parts(middle)
    second_out[...] = (scaled * vec_ref[5:6, :] + vec_ref[6:7, :]).astype(bf16)


def expand_kernel(
    me_ref, up_ref, second_ref, bias_ref, w1_ref,
    act_out, slope_out, mine_out, theirs_out, w1_out,
    total,
):
    me = me_ref[0]
    for pair in range(16):
        w1_out[48 * pair : 48 * pair + 48, :] = gather_rows(
            w1_ref[0, 2 * pair, 0], w1_ref[0, 2 * pair + 1, 0]
        )

    for i in range(3):
        cols = slice(256 * i, 256 * i + 256)
        inner = dot(second_ref[...], w1_out[:, cols]) + bias_ref[:, cols]
        act, slope = gelu_parts(inner)
        act = act.astype(bf16)
        act_out[:, cols] = act
        slope_out[:, cols] = slope.astype(bf16)
    total[...] = dot_rows(act_out[...], up_ref[...]).astype(bf16)

    for g in range(8):
        for ref, place in ((mine_out, me), (theirs_out, 1 - me)):
            part = total[pl.ds(pl.multiple_of(96 * g + 48 * place, 16), 48), :]
            for y in range(2):
                ref[y, g] = part[:, HALF * y : HALF * y + HALF]


def contract_kernel(
    me_ref, up_ref, slope_ref, second_ref, ff_ref,
    grad_out, hidden_out, mine_out, theirs_out,
    turned, w2,
):
    step = pl.program_id(0)
    me = me_ref[0]

    @pl.when(step == 0)
    def _():
        turned[...] = second_ref[...].T

    place_rows(w2, ff_ref)
    for i in range(3):
        cols = slice(256 * i, 256 * i + 256)
        grad = dot_lanes(up_ref[...], w2[cols, :]) * slope_ref[:, cols].astype(f32)
        grad = grad.astype(bf16)
        grad_out[:, cols] = grad
        hidden_out[:, cols] = jnp.sum(grad.astype(f32), axis=0, keepdims=True)

    def outer(ref):
        for i in range(3):
            cols = slice(256 * i, 256 * i + 256)
            ref[0, :, cols] = dot(turned[...], grad_out[:, cols]).astype(bf16)

    pl.when((step & 1) == me)(lambda: outer(mine_out))
    pl.when((step & 1) != me)(lambda: outer(theirs_out))


def middle_back_kernel(
    me_ref, vec_ref, inner_hbm, w1_hbm, soft_hbm, up_hbm, middle_hbm, wo_hbm, normed_hbm, mixed_hbm, qkv_hbm,
    mine_hbm, theirs_hbm, sums_out, grads_hbm, gm_hbm,
    inner_ref, w1_ref, soft_ref, up_ref, middle_ref, wo_ref, normed_ref, mixed_ref, qkv_ref,
    grad_second, gml, grad_mixed, normed_turned, mixed_turned, pieces, grads_ref, gm_ref, sems,
):
    me = me_ref[0]
    ahead = []
    for j in range(4):
        cols = pl.ds(D * j, D)
        ahead.append((inner_hbm.at[:, cols], inner_ref.at[j]))
        ahead.append((w1_hbm.at[:, cols], w1_ref.at[j]))
    ahead += [
        (middle_hbm, middle_ref), (up_hbm, up_ref), (wo_hbm, wo_ref),
        (normed_hbm, normed_ref), (mixed_hbm, mixed_ref), (qkv_hbm, qkv_ref),
    ]
    reads = [pltpu.make_async_copy(src, dst, sems.at[i]) for i, (src, dst) in enumerate(ahead)]

    def read_soft(i):
        return pltpu.make_async_copy(soft_hbm.at[i], soft_ref.at[i], sems.at[14 + i])

    grads_write = pltpu.make_async_copy(grads_ref, grads_hbm, sems.at[20])
    gm_write = pltpu.make_async_copy(gm_ref, gm_hbm, sems.at[21])

    def write(kind, act):
        cols = pl.ds(HALF * (kind % 2), HALF)
        for to, place in ((mine_hbm, kind // 2), (theirs_hbm, 1 - kind // 2)):
            copy = pltpu.make_async_copy(pieces.at[kind], to.at[:, :, cols], sems.at[22 + kind])
            pl.when(me == place)(lambda copy=copy: act(copy))

    def outer(kind, left, right):
        grad = dot(left[...], right[...]).astype(bf16)
        for y in range(2):
            pieces[kind, y] = grad[:, HALF * y : HALF * y + HALF]
        write(kind, lambda copy: copy.start())

    for read in reads:
        read.start()
    for i in range(6):
        read_soft(i).start()
    for j in range(4):
        reads[2 * j].wait()
        reads[2 * j + 1].wait()
        part = dot_lanes(inner_ref[j], w1_ref[j])
        if j == 0:
            grad_second[...] = part
        else:
            grad_second[...] += part
    for read in reads[8:]:
        read.wait()
    grad = grad_second[...]
    scaled, scale = norm_parts(middle_ref[...])
    up = up_ref[...].astype(f32)
    gm = up + norm_back(grad, scaled, scale, vec_ref[5:6, :])
    gm_ref[...] = gm
    gm_write.start()
    gml[...] = gm.astype(bf16)
    sums_out[2:3, :] = jnp.sum(gml[...].astype(f32), axis=0, keepdims=True)
    sums_out[3:4, :] = jnp.sum(grad * scaled, axis=0, keepdims=True)
    sums_out[4:5, :] = jnp.sum(grad, axis=0, keepdims=True)
    sums_out[5:6, :] = jnp.sum(up, axis=0, keepdims=True)
    grad_mixed[...] = dot_lanes(gml[...], wo_ref[...]).astype(bf16)
    mixed_turned[...] = mixed_ref[...].T
    outer(3, mixed_turned, gml)
    normed_turned[...] = normed_ref[...].T
    lane = iota((PAD, 128), 1)

    def attend(i, carry):
        cols = pl.ds(pl.multiple_of(128 * i, 128), 128)
        read_soft(i).wait()
        for image in range(IMAGES):
            rows = pl.ds(PAD * image, PAD)
            q = qkv_ref[0, rows, cols]
            k = qkv_ref[1, rows, cols]
            v = qkv_ref[2, rows, cols]
            g = grad_mixed[rows, cols]
            dq = dk = dv = jnp.zeros((PAD, 128), f32)
            for n in range(2):
                inside = (lane < HD) == (n == 0)
                zero = jnp.zeros_like(g)
                g_in = jnp.where(inside, g, zero)
                soft_low = soft_ref[i, 2 * image + n]
                soft = soft_low.astype(f32)
                grad_soft = dot_lanes(v, g_in)
                level = jnp.sum(grad_soft * soft, axis=0, keepdims=True)
                scores = (soft * (grad_soft - level)).astype(bf16)
                dv = dv + dot(soft_low, g_in)
                dk = dk + dot(scores, jnp.where(inside, q, zero))
                dq = dq + dot_rows(scores, jnp.where(inside, k, zero))
            grads_ref[0, rows, cols] = (dq * 0.125).astype(bf16)
            grads_ref[1, rows, cols] = (dk * 0.125).astype(bf16)
            grads_ref[2, rows, cols] = dv.astype(bf16)
        return carry

    lax.fori_loop(0, 6, attend, 0)
    grads_write.start()
    for kind in range(3):
        outer(kind, normed_turned, grads_ref.at[kind])
    sums_out[0:1, :] = jnp.sum(grads_ref[0].astype(f32), axis=0, keepdims=True)
    sums_out[1:2, :] = jnp.sum(grads_ref[2].astype(f32), axis=0, keepdims=True)
    grads_write.wait()
    gm_write.wait()
    for kind in range(4):
        write(kind, lambda copy: copy.wait())


def input_back_kernel(
    me_ref, vec_ref, grads_ref, w_ref, x_ref, gm_ref, keep_out, send_out, sums_out, total
):
    step = pl.program_id(0)
    part = dot_lanes(grads_ref[0], w_ref[0])

    @pl.when(step == 0)
    def _():
        total[...] = part

    @pl.when(step > 0)
    def _():
        total[...] += part

    @pl.when(step == 2)
    def _():
        grad = total[...]
        scaled, scale = norm_parts(x_ref[...].astype(f32))
        out = gm_ref[...] + norm_back(grad, scaled, scale, vec_ref[0:1, :])
        pack(out.astype(bf16), me_ref[1], keep_out, send_out)
        sums_out[0:1, :] = jnp.sum(grad * scaled, axis=0, keepdims=True)
        sums_out[1:2, :] = jnp.sum(grad, axis=0, keepdims=True)


def output_kernel(me_ref, vec_ref, middle_ref, act_ref, ff_ref, keep_out, send_out, w2, total):
    step = pl.program_id(0)
    place_rows(w2, ff_ref)
    part = dot(act_ref[...], w2[...])

    @pl.when(step == 0)
    def _():
        total[...] = middle_ref[...] + vec_ref[7:8, :] + part

    @pl.when(step > 0)
    def _():
        total[...] += part

    @pl.when(step == 3)
    def _():
        pack(total[...].astype(bf16), me_ref[1], keep_out, send_out)


def assemble_kernel(at_ref, *refs):
    out = refs[-1]
    step = pl.program_id(0)
    for r in range(4):
        pl.when(step == r)(lambda r=r: out.__setitem__(..., refs[r][...].reshape(out.shape)))


def blocks_sum_kernel(at_ref, *refs):
    ins, outs = refs[:-4], refs[-4:]
    step = pl.program_id(0)
    total = ins[0][...].astype(f32)
    for ref in ins[1:]:
        total = total + ref[...].astype(f32)
    total = total.astype(bf16)
    for r in range(4):
        pl.when(step == r)(lambda r=r: outs[r].__setitem__(..., total.reshape(outs[r].shape)))


def sum_kernel(a_ref, b_ref, c_ref, d_ref, out_ref):
    total = a_ref[...].astype(f32) + b_ref[...].astype(f32) + c_ref[...].astype(f32) + d_ref[...].astype(f32)
    out_ref[...] = total.astype(bf16)


def last_spread_kernel(a_ref, b_ref, c_ref, d_ref, va_ref, vb_ref, vc_ref, vd_ref, out_ref):
    vector = va_ref[...].astype(f32) + vb_ref[...].astype(f32) + vc_ref[...].astype(f32) + vd_ref[...].astype(f32)
    vector = vector.astype(bf16)
    total = a_ref[...].astype(f32) + b_ref[...].astype(f32) + c_ref[...].astype(f32) + d_ref[...].astype(f32)
    total = total.reshape(2 * 192, D)
    for i in range(16):
        out_ref[i, :16, :] = vector
        out_ref[i, 16:, :] = total[24 * i : 24 * i + 24].astype(bf16)


def adamw_step(parameter, gradient, first_moment, second_moment, step_rate, decay_factor):
    first_new = beta_first * first_moment + (1.0 - beta_first) * gradient
    second_new = beta_second * second_moment + (1.0 - beta_second) * gradient * gradient
    first_hat = first_new / (1.0 - beta_first**STEP)
    second_hat = second_new / (1.0 - beta_second**STEP)
    updated = parameter - step_rate * (
        first_hat / (jnp.sqrt(second_hat) + adam_eps) + decay_factor * parameter
    )
    return second_new, updated


def ordered(me, own, got):
    return jnp.where(me == 0, own, got), jnp.where(me == 0, got, own)


def attention_step_kernel(
    me_ref, own_ref, got_ref, w_ref, m_ref, v_ref, vec_ref, vec_m_ref, vec_v_ref,
    grad_out, second_out, new_out, vec_grad_out, vec_second_out, vec_new_out,
):
    pieces = ordered(me_ref[0], own_ref[16:, :], got_ref[16:, :])
    l = iota((512, 512), 0)
    c = iota((512, 512), 1)
    pick = jnp.where(c == 4 * (l & 127) + (l >> 7), 1.0, 0.0)
    for b in range(3):
        kinds = [
            pieces[k // 2][:, HALF * (k % 2) + 128 * b : HALF * (k % 2) + 128 * b + 128]
            for k in range(4)
        ]
        grad_out[:, 512 * b : 512 * b + 512] = jnp.dot(
            jnp.concatenate(kinds, axis=1), pick, precision=lax.Precision.HIGHEST,
            preferred_element_type=f32,
        )
    second_out[...], new_out[...] = adamw_step(
        w_ref[...], grad_out[...], m_ref[...], v_ref[...], learn_rate, decay_rate
    )
    vector = own_ref[:12, :] + got_ref[:12, :]
    vec_grad_out[...] = jnp.where(me_ref[1] == 0, vector[:, :HALF], vector[:, HALF:])
    vec_second_out[...], vec_new_out[...] = adamw_step(
        vec_ref[...], vec_grad_out[...], vec_m_ref[...], vec_v_ref[...], vector_rate, 0.0
    )


def expand_step_kernel(me_ref, own_ref, got_ref, w_ref, m_ref, v_ref, grad_out, second_out, new_out):
    first, last = ordered(me_ref[0], own_ref[...], got_ref[...])
    grad_out[:, :D] = first
    grad_out[:, D:] = last
    second_out[...], new_out[...] = adamw_step(
        w_ref[...], grad_out[...], m_ref[...], v_ref[...], learn_rate, decay_rate
    )


def project_step_kernel(me_ref, own_ref, got_ref, w_ref, m_ref, v_ref, grad_out, second_out, new_out):
    first, last = ordered(me_ref[0], own_ref[...], got_ref[...])
    grad_out[...] = jnp.concatenate([first, last], axis=0)
    second_out[...], new_out[...] = adamw_step(
        w_ref[...], grad_out[...], m_ref[...], v_ref[...], learn_rate, decay_rate
    )


def place(axes):
    at = 0
    for a in axes:
        at = at * lax.axis_size(a) + lax.axis_index(a)
    return at


def swap(x, axis):
    return lax.ppermute(x, axis, [(0, 1), (1, 0)])


def core_sum(mine, theirs):
    return (mine.astype(f32) + swap(theirs, "dp").astype(f32)).astype(bf16)


def assemble(parts, at, shape, piece, index, after=(), cost=0):
    flat = tuple(n for n in piece if n > 1)
    return pl.pallas_call(
        assemble_kernel,
        out_shape=jax.ShapeDtypeStruct(shape, bf16),
        grid_spec=pltpu.PrefetchScalarGridSpec(
            num_scalar_prefetch=1,
            grid=(4,),
            in_specs=[
                *(pl.BlockSpec(flat, lambda r, at: (0,) * len(flat)) for _ in range(4)),
                *(LEFT for _ in after),
            ],
            out_specs=pl.BlockSpec(piece, lambda r, at: index((at[0] + 3 * r) % 4)),
        ),
        compiler_params=pltpu.CompilerParams(vmem_limit_bytes=32 * 1024 * 1024),
        cost_estimate=pl.CostEstimate(flops=cost * 10**9 + 1000, bytes_accessed=0, transcendentals=0),
        name="assemble",
    )(at.reshape(1).astype(jnp.int32), *(p.reshape(flat) for p in parts), *after)


def ring_blocks(parts, at, shape, piece, index):
    spec = pl.BlockSpec(piece, lambda r, at: index((at[0] + r) % 4))
    flat = tuple(n for n in piece if n > 1)
    return pl.pallas_call(
        blocks_sum_kernel,
        out_shape=[jax.ShapeDtypeStruct(flat, bf16)] * 4,
        grid_spec=pltpu.PrefetchScalarGridSpec(
            num_scalar_prefetch=1,
            grid=(4,),
            in_specs=[spec] * len(parts),
            out_specs=[pl.BlockSpec(flat, lambda r, at: (0,) * len(flat))] * 4,
        ),
        compiler_params=pltpu.CompilerParams(vmem_limit_bytes=32 * 1024 * 1024),
        cost_estimate=pl.CostEstimate(flops=1000, bytes_accessed=0, transcendentals=0),
        name="ring_blocks",
    )(at.reshape(1).astype(jnp.int32), *(p.reshape(shape) for p in parts))


def hop(x, axes, r):
    return lax.ppermute(x, axes, [(i, (i + r) % 4) for i in range(4)])


def ring(blocks, axes):
    return blocks[0], *(hop(blocks[r], axes, r) for r in (1, 3, 2))


def crossed(x, axis, bit):
    return lax.ppermute(x, axis, [(i, i ^ bit) for i in range(lax.axis_size(axis))])


def to_all(x, axes):
    near, back = hop(x, axes, 1), hop(x, axes, 3)
    return x, near, hop(x, axes, 2), back


def sum_of(parts):
    total = parts[0].astype(f32)
    for part in parts[1:]:
        total = total + part.astype(f32)
    return total


def spread_sum(blocks, axes):
    tiles = lax.all_to_all(blocks, axes, 0, 0, tiled=True)
    return jnp.sum(tiles.astype(f32), axis=0)


def own_images(stored, gy):
    rows = stored.shape[0] // 2
    own = lax.dynamic_slice_in_dim(stored, rows * gy, rows, 0)
    other = lax.dynamic_slice_in_dim(stored, rows * (1 - gy), rows, 0)
    pad = ((0, PAD - rows), (0, 0))
    return jnp.pad(own, pad), jnp.pad(other, pad)


def stored_rows(keep, got, gy):
    first = jnp.where(gy == 0, keep, got)[:SEQ]
    last = jnp.where(gy == 0, got, keep)[:SEQ]
    return jnp.concatenate([first, last], axis=0).astype(f32)


def per_device(
    tokens,
    image_counts,
    slot_order,
    cotangent,
    attention_weights,
    attention_first,
    attention_second,
    expand_weight,
    expand_first,
    expand_second,
    project_weight,
    project_first,
    project_second,
    vectors,
    vector_first,
    vector_second,
):
    dp = lax.axis_index("dp")
    gy = lax.axis_index("xl")
    me = jnp.stack([dp, gy]).astype(jnp.int32)

    token_own, token_other = own_images(tokens, gy)
    token_got = swap(token_other, "xl")
    grad_own, grad_other = own_images(cotangent, gy)
    grad_got = swap(grad_other, "xl")
    vec_got = swap(vectors, "xl")
    attn_piece, ff_piece = call(
        prepare_kernel,
        [SCALARS, WHOLE, WHOLE, WHOLE],
        [((24, D), bf16, WHOLE), ((24, 2 * D), bf16, WHOLE)],
        (me, attention_weights, expand_weight, project_weight.T),
        name="prepare",
    )
    ff = lax.all_gather(ff_piece, EVERY).reshape(2, 32, 2, 24, 2 * D)
    at_x, at_y, at_z = place(X), place(Y), place(Z)

    def across_x(p):
        return p % 2, 0, p // 2, 0, 0

    attn = to_all(attn_piece, X)
    attn = assemble(attn, at_x, (2, 1, 2, 24, D), (1, 1, 1, 24, D), across_x)
    attn = to_all(attn.reshape(2, 48, D), Y)
    attn, token_got, vec_got = lax.optimization_barrier((attn, token_got, vec_got))
    attn = assemble(attn, at_y, (2, 4, 48, D), (2, 1, 48, D), lambda p: (0, p, 0, 0))
    vec_first, vec_last = ordered(gy, vectors, vec_got)
    vec = jnp.concatenate([vec_first, vec_last], axis=1)
    bias = vec[8:].T.reshape(1, FF)
    live = (slot_order[0] < image_counts[0]).astype(jnp.int32)
    live = lax.dynamic_slice_in_dim(live, IMAGES * gy, IMAGES)
    attn = to_all(attn.reshape(2, 192, D), Z)
    attn, vec, bias, live, token_own, token_got = lax.optimization_barrier(
        (attn, vec, bias, live, token_own, token_got)
    )
    attn = assemble(attn, at_z, (2, 4, 192, D), (2, 1, 192, D), lambda p: (0, p, 0, 0))
    w_own, w_got = (w.reshape(2, D, D) for w in (attn, swap(attn, "dp")))

    tall = block((ROWS, D), lambda j: (0, 0))
    wide = block((ROWS, D), lambda j: (0, j))
    w1_block = block((1, 32, 1, 24, D), lambda j: (j % 2, 0, j // 2, 0, 0))
    w2_block = block((2, 8, 2, 24, D), lambda j: (0, j, 0, 0, 1))
    pieces2 = block((2, 8, 48, HALF), lambda j: (0, j, 0, 0))
    soft_shape = (6, 2 * IMAGES, PAD, PAD)

    soft, mixed, x, normed, qkv, w_qkv, w_o = call(
        attend_kernel,
        [SCALARS, *(WHOLE,) * 5],
        [
            (soft_shape, bf16, block((1, *soft_shape[1:]), lambda p: (jnp.maximum(p - 1, 0), 0, 0, 0))),
            ((ROWS, D), bf16, block((ROWS, 128), lambda p: (0, jnp.maximum(p - 1, 0)))),
            ((ROWS, D), bf16, LEFT),
            ((ROWS, D), bf16, LEFT),
            ((3, ROWS, D), bf16, LEFT),
            ((3, D, D), bf16, LEFT),
            ((D, D), bf16, LEFT),
        ],
        (me, token_own, token_got, vec, w_own, w_got),
        grid=(7,),
        scratch=[
            pltpu.VMEM((ROWS, D), bf16),
            pltpu.VMEM((ROWS, D), bf16),
            pltpu.VMEM((3, ROWS, D), bf16),
            pltpu.VMEM((4, D, D), bf16),
            pltpu.SemaphoreType.DMA((5,)),
        ],
        name="attend",
    )

    up, middle, second = call(
        second_kernel,
        [SCALARS, SCALARS, *(WHOLE,) * 6],
        [((ROWS, D), bf16, WHOLE), ((ROWS, D), f32, WHOLE), ((ROWS, D), bf16, WHOLE)],
        (me, live, grad_own, grad_got, vec, x, mixed, w_o),
        name="second",
    )
    act, slope, mine2, theirs2, w1 = call(
        expand_kernel,
        [SCALARS, WHOLE, WHOLE, block((1, D), lambda j: (0, j)), w1_block],
        [
            ((ROWS, FF), bf16, wide),
            ((ROWS, FF), bf16, wide),
            ((2, 32, 48, HALF), bf16, pieces2),
            ((2, 32, 48, HALF), bf16, pieces2),
            ((D, FF), bf16, block((D, D), lambda j: (0, j))),
        ],
        (me, up, second, bias, ff),
        grid=(4,),
        scratch=[pltpu.VMEM((D, D), bf16)],
        after=(w_o, soft),
        name="expand",
    )
    inner_grad, hidden_sums, mine1, theirs1 = call(
        contract_kernel,
        [SCALARS, WHOLE, wide, WHOLE, w2_block],
        [
            ((ROWS, FF), bf16, wide),
            ((1, FF), f32, block((1, D), lambda j: (0, j))),
            ((2, D, D), bf16, block((1, D, D), lambda j: (j // 2, 0, 0))),
            ((2, D, D), bf16, block((1, D, D), lambda j: (j // 2, 0, 0))),
        ],
        (me, up, slope, second, ff),
        grid=(4,),
        scratch=[pltpu.VMEM((D, ROWS), bf16), pltpu.VMEM((D, D), bf16)],
        name="contract",
    )
    ring2 = ring_blocks(
        (mine2, swap(theirs2, "dp")),
        place(X),
        (2, 16, 2, 48, HALF),
        (1, 16, 1, 48, HALF),
        lambda p: (p % 2, 0, p // 2, 0, 0),
    )
    got1, _ = lax.optimization_barrier((swap(theirs1, "dp"), ring2[0]))
    ring1 = ring_blocks(
        (mine1, got1), place(Y), (8, 4, 48, D), (8, 1, 48, D), lambda p: (0, p, 0, 0)
    )

    mine0, theirs0, sums_c, grads, gm = call(
        middle_back_kernel,
        [SCALARS, WHOLE, *(LEFT,) * 9],
        [
            ((2, D, D), bf16, LEFT),
            ((2, D, D), bf16, LEFT),
            ((6, D), f32, WHOLE),
            ((3, ROWS, D), bf16, LEFT),
            ((ROWS, D), f32, LEFT),
        ],
        (me, vec, inner_grad, w1, soft, up, middle, w_o, normed, mixed, qkv),
        scratch=[
            pltpu.VMEM((4, ROWS, D), bf16),
            pltpu.VMEM((4, D, D), bf16),
            pltpu.VMEM(soft_shape, bf16),
            pltpu.VMEM((ROWS, D), bf16),
            pltpu.VMEM((ROWS, D), f32),
            pltpu.VMEM((D, D), bf16),
            pltpu.VMEM((ROWS, D), bf16),
            pltpu.VMEM((ROWS, D), bf16),
            pltpu.VMEM((3, ROWS, D), bf16),
            pltpu.VMEM((ROWS, D), f32),
            pltpu.VMEM((ROWS, D), bf16),
            pltpu.VMEM((ROWS, D), bf16),
            pltpu.VMEM((D, ROWS), bf16),
            pltpu.VMEM((D, ROWS), bf16),
            pltpu.VMEM((4, 2, D, HALF), bf16),
            pltpu.VMEM((3, ROWS, D), bf16),
            pltpu.VMEM((ROWS, D), f32),
            pltpu.SemaphoreType.DMA((26,)),
        ],
        after=(ring2[0], ring1[0]),
        cost=0,
        name="middle_back",
    )
    got0 = swap(theirs0, "dp")
    ring2 = ring(ring2, X)
    near1 = hop(ring1[1], Y, 1), hop(ring1[3], Y, 3)
    ring2, mine0 = lax.optimization_barrier((ring2, mine0))
    mine0, near1, far1 = lax.optimization_barrier((mine0, near1, ring1[2]))
    far1 = hop(far1, Y, 2)
    part2 = call(
        sum_kernel, [WHOLE] * 4, [((16, 48, HALF), bf16, WHOLE)], ring2, cost=100, after=(near1[0], near1[1]), name="part"
    )[0]
    tiles2 = lax.all_to_all(part2, Z + Y, 0, 0, tiled=True)
    mine0, got0, _ = lax.optimization_barrier((mine0, got0, part2))
    ring0 = ring_blocks(
        (mine0, got0), place(Z), (2, 4, 192, D), (2, 1, 192, D), lambda p: (0, p, 0, 0)
    )
    tiles2, far1, _ = lax.optimization_barrier((tiles2, far1, ring0[0]))
    own0, near0, back0, far0 = ring(ring0, Z)
    keep_out, send_out = call(
        output_kernel,
        [SCALARS, WHOLE, WHOLE, wide, w2_block],
        [((PAD, D), bf16, block((PAD, D), lambda j: (0, 0)))] * 2,
        (me, vec, middle, act, ff),
        grid=(4,),
        scratch=[pltpu.VMEM((D, D), bf16), pltpu.VMEM((ROWS, D), f32)],
        after=(ring0[0],),
        cost=0,
        name="output",
    )
    far1, tiles2, keep_out = lax.optimization_barrier((far1, tiles2, keep_out))
    part1 = sum_of((ring1[0], *near1, far1)).astype(bf16).reshape(16, 24, D)
    tiles1 = lax.all_to_all(part1, ("xl", "z", "xh"), 0, 0, tiled=True)
    grads, near0, back0 = lax.optimization_barrier((grads, near0, back0))
    keep_in, send_in, sums_e = call(
        input_back_kernel,
        [
            SCALARS, WHOLE,
            block((1, ROWS, D), lambda k: (k, 0, 0)), block((1, D, D), lambda k: (k, 0, 0)),
            WHOLE, WHOLE,
        ],
        [
            ((PAD, D), bf16, block((PAD, D), lambda k: (0, 0))),
            ((PAD, D), bf16, block((PAD, D), lambda k: (0, 0))),
            ((2, D), f32, block((2, D), lambda k: (0, 0))),
        ],
        (me, vec, grads, w_qkv, x, gm),
        grid=(3,),
        scratch=[pltpu.VMEM((ROWS, D), f32)],
        cost=100,
        after=(part1,),
        name="input_back",
    )
    sums_e, hidden_sums = lax.optimization_barrier((sums_e, hidden_sums))
    vector = jnp.concatenate(
        [sums_e, sums_c, hidden_sums.reshape(D, 4).T, jnp.zeros((4, D), f32)], axis=0
    ).astype(bf16)
    vectors4 = ring((vector,) * 4, Z)
    got_in, got_out = swap(send_in, "xl"), swap(send_out, "xl")
    tiles2, vectors4, got_in, got_out = lax.optimization_barrier((tiles2, vectors4, got_in, got_out))
    sum2 = jnp.sum(tiles2.astype(f32), axis=0)
    got2 = swap(sum2, "dp")
    part0 = call(
        last_spread_kernel,
        [WHOLE] * 8,
        [((16, 40, D), bf16, WHOLE)],
        (own0, near0, back0, far0, *vectors4),
        cost=0,
        name="last_spread",
    )[0]
    tiles0 = lax.all_to_all(part0, ("xl", "y", "xh"), 0, 0, tiled=True)
    sum1 = jnp.sum(tiles1.astype(f32), axis=0)
    got1 = swap(sum1, "dp")
    block_out = stored_rows(keep_out, got_out, gy)
    input_grad = stored_rows(keep_in, got_in, gy)

    def step(body, own, got, shape, state, outs=(), cost=0, name=None):
        state = (me, own, got, *state)
        outs = [(shape, f32, WHOLE)] * 3 + [(o, f32, WHOLE) for o in outs]
        return call(body, [SCALARS, *(WHOLE,) * (len(state) - 1)], outs, state, cost=cost, name=name)

    project = step(
        project_step_kernel, sum2, got2, (96, HALF),
        (project_weight.T, project_first.T, project_second.T), name="project_step",
    )
    expand = step(
        expand_step_kernel, sum1, got1, (24, 2 * D),
        (expand_weight, expand_first, expand_second), name="expand_step",
    )
    tiles0, project = lax.optimization_barrier((tiles0, project))
    sum0 = jnp.sum(tiles0.astype(f32), axis=0)
    got0 = swap(sum0, "dp")
    *attention, vector_grad, vector_second_new, vector_new = step(
        attention_step_kernel, sum0, got0, (24, 2 * D),
        (attention_weights, attention_first, attention_second, vectors, vector_first, vector_second),
        [(12, HALF)] * 3, name="attention_step",
    )
    return (
        block_out,
        input_grad,
        *attention,
        *expand,
        *(p.T for p in project),
        vector_grad,
        vector_second_new,
        vector_new,
    )


def solution(mesh):
    fine = Mesh(mesh.devices.reshape(2, 4, 4, 2, 2), EVERY)
    rows = ("dp", "z", "y", "xh")
    deep = ("z", "y", "xh")
    placed = (
        P(rows, "xl"),
        P("dp"),
        P("dp", deep),
        P(rows, "xl"),
        *(P(deep, "xl"),) * 6,
        *(P("xl", deep),) * 3,
        *(P(None, "xl"),) * 3,
    )
    out = (
        P(rows, "xl"),
        P(rows, "xl"),
        *(P(deep, "xl"),) * 6,
        *(P("xl", deep),) * 3,
        *(P(None, "xl"),) * 3,
    )
    return jax.shard_map(per_device, mesh=fine, in_specs=placed, out_specs=out, check_vma=False)
```

```python
import jax
import jax.numpy as jnp
from jax import lax
from jax.experimental import pallas as pl
from jax.experimental.pallas import tpu as pltpu
from jax.sharding import Mesh
from jax.sharding import PartitionSpec as P

D = 768
HD = 64
FF = 3072
SEQ = 197
STEP = 10
PAD = 208
IMAGES = 2
ROWS = PAD * IMAGES
HALF = D // 2

norm_eps = 1e-06
beta_first = 0.9
beta_second = 0.999
learn_rate = 0.04
vector_rate = 0.25
decay_rate = 0.05
adam_eps = 1e-08

f32 = jnp.float32
bf16 = jnp.bfloat16

DP = ("dp",)
Z = ("z",)
Y = ("y",)
X = ("xh", "xl")
CHIPS = ("xl", "z", "y", "xh")
EVERY = ("dp", "z", "y", "xh", "xl")


def dot(a, b):
    return lax.dot_general(a, b, (((1,), (0,)), ((), ())), preferred_element_type=f32)


def dot_rows(a, b):
    return lax.dot_general(a, b, (((0,), (0,)), ((), ())), preferred_element_type=f32)


def dot_lanes(a, b):
    return lax.dot_general(a, b, (((1,), (1,)), ((), ())), preferred_element_type=f32)


def block(shape, index):
    return pl.BlockSpec(shape, index)


WHOLE = pl.BlockSpec(memory_space=pltpu.VMEM)
SCALARS = pl.BlockSpec(memory_space=pltpu.SMEM)
LEFT = pl.BlockSpec(memory_space=pl.ANY)


def call(body, ins, outs, args, grid=(), scratch=(), after=(), cost=10, prefetch=0, name=None):
    count = len(args)

    def run(*refs):
        body(*refs[:count], *refs[count + len(after) :])

    return pl.pallas_call(
        run if after else body,
        out_shape=[jax.ShapeDtypeStruct(s, t) for s, t, _ in outs],
        grid_spec=pltpu.PrefetchScalarGridSpec(
            num_scalar_prefetch=prefetch,
            grid=grid,
            in_specs=[*ins, *(LEFT for _ in after)],
            out_specs=[spec for _, _, spec in outs],
            scratch_shapes=list(scratch),
        ),
        compiler_params=pltpu.CompilerParams(vmem_limit_bytes=52 * 1024 * 1024),
        cost_estimate=pl.CostEstimate(flops=cost * 10**9 + 1000, bytes_accessed=0, transcendentals=0),
        name=name,
    )(*args, *after)


def iota(shape, dim):
    return lax.broadcasted_iota(jnp.int32, shape, dim)


def row_picks():
    r = iota((ROWS, PAD), 0)
    j = iota((ROWS, PAD), 1)
    second = r >= PAD
    s = jnp.where(second, r - PAD, r)
    t = jnp.where(second, s + SEQ, s)
    live = s < SEQ
    even = jnp.where(live & (t == 2 * j), 1.0, 0.0).astype(bf16)
    odd = jnp.where(live & (t == 2 * j + 1), 1.0, 0.0).astype(bf16)
    return even, odd


def row_picks_back():
    r = iota((PAD, ROWS), 1)
    j = iota((PAD, ROWS), 0)
    second = r >= PAD
    s = jnp.where(second, r - PAD, r)
    t = jnp.where(second, s + SEQ, s)
    live = s < SEQ
    even = jnp.where(live & (t == 2 * j), 1.0, 0.0).astype(bf16)
    odd = jnp.where(live & (t == 2 * j + 1), 1.0, 0.0).astype(bf16)
    return even, odd


def lane_split():
    l = iota((256, 256), 0)
    c = iota((256, 256), 1)
    target = jnp.where(c < 128, 2 * c, 2 * (c - 128) + 1)
    return jnp.where(l == target, 1.0, 0.0).astype(bf16)


def lane_join():
    l = iota((256, 256), 1)
    c = iota((256, 256), 0)
    target = jnp.where(c < 128, 2 * c, 2 * (c - 128) + 1)
    return jnp.where(l == target, 1.0, 0.0).astype(bf16)


def unpack(own_ref, got_ref, gy):
    own, got = own_ref[...], got_ref[...]
    first = jnp.where(gy == 0, own.astype(f32), got.astype(f32)).astype(bf16)
    last = jnp.where(gy == 0, got.astype(f32), own.astype(f32)).astype(bf16)
    split = lane_split()
    evens, odds = [], []
    for half in (first, last):
        for b in range(3):
            both = dot(half[:, 256 * b : 256 * b + 256], split).astype(bf16)
            evens.append(both[:, :128])
            odds.append(both[:, 128:])
    even_rows, odd_rows = row_picks()
    return dot(even_rows, jnp.concatenate(evens, axis=1)) + dot(odd_rows, jnp.concatenate(odds, axis=1))


def pack(rows_low, gy, keep_ref, send_ref):
    even_rows, odd_rows = row_picks_back()
    even = dot(even_rows, rows_low).astype(bf16)
    odd = dot(odd_rows, rows_low).astype(bf16)
    join = lane_join()
    for b in range(3):
        blocks = []
        for half in range(2):
            at = HALF * half + 128 * b
            both = jnp.concatenate([even[:, at : at + 128], odd[:, at : at + 128]], axis=1)
            blocks.append(dot(both, join))
        keep_ref[:, 256 * b : 256 * b + 256] = jnp.where(gy == 0, blocks[0], blocks[1]).astype(bf16)
        send_ref[:, 256 * b : 256 * b + 256] = jnp.where(gy == 0, blocks[1], blocks[0]).astype(bf16)


def norm_parts(v):
    center = jnp.mean(v, axis=1, keepdims=True)
    away = v - center
    scale = lax.rsqrt(jnp.mean(away * away, axis=1, keepdims=True) + norm_eps)
    return away * scale, scale


def norm_back(grad, scaled, scale, gain):
    pushed = grad * gain
    first = jnp.mean(pushed, axis=1, keepdims=True)
    cross = jnp.mean(pushed * scaled, axis=1, keepdims=True)
    return (pushed - first - scaled * cross) * scale


def prepare_kernel(
    me_ref, attn_hbm, expand_hbm, project_hbm, attn_out, ff_out, attn_ref, expand_ref, project_ref, sems
):
    reads = [
        pltpu.make_async_copy(attn_hbm, attn_ref, sems.at[0]),
        pltpu.make_async_copy(expand_hbm, expand_ref, sems.at[1]),
        pltpu.make_async_copy(project_hbm, project_ref, sems.at[2]),
    ]
    for read in reads:
        read.start()
    me = me_ref[0]
    l = iota((512, 256), 0)
    c = iota((512, 256), 1)
    kind = 2 * me + jnp.where(c < 128, 0, 1)
    pick = jnp.where(l == 4 * (c & 127) + kind, 1.0, 0.0).astype(bf16)
    for read in reads:
        read.wait()
    for b in range(3):
        both = dot(attn_ref[:, 512 * b : 512 * b + 512].astype(bf16), pick).astype(bf16)
        attn_out[:, 128 * b : 128 * b + 128] = both[:, :128]
        attn_out[:, HALF + 128 * b : HALF + 128 * b + 128] = both[:, 128:]
    ff_out[:, :D] = jnp.where(me == 0, expand_ref[:, :D], expand_ref[:, D:]).astype(bf16)
    mine = jnp.where(me == 0, project_ref[:48, :], project_ref[48:, :])
    ff_out[:, D : D + HALF] = mine[:24].astype(bf16)
    ff_out[:, D + HALF :] = mine[24:].astype(bf16)


def attend_kernel(
    me_ref, own_ref, got_ref, vec_ref, w_own, w_got,
    soft_out, mixed_out, x_out, normed_out, qkv_out, w_out, wo_out,
    x_ref, normed_ref, qkv_ref, w_ref, sems,
):
    step = pl.program_id(0)
    copies = [
        pltpu.make_async_copy(x_ref, x_out, sems.at[0]),
        pltpu.make_async_copy(normed_ref, normed_out, sems.at[1]),
        pltpu.make_async_copy(qkv_ref, qkv_out, sems.at[2]),
        pltpu.make_async_copy(w_ref.at[pl.ds(0, 3)], w_out, sems.at[3]),
        pltpu.make_async_copy(w_ref.at[3], wo_out, sems.at[4]),
    ]

    @pl.when(step == 0)
    def _():
        me, gy = me_ref[0], me_ref[1]
        for ref, place in ((w_own, me), (w_got, 1 - me)):
            for half in range(2):
                for y in range(2):
                    w_ref[pl.ds(2 * place + half, 1), :, HALF * y : HALF * y + HALF] = ref[
                        y, :, HALF * half : HALF * half + HALF
                    ][None]
        copies[3].start()
        copies[4].start()
        x_ref[...] = unpack(own_ref, got_ref, gy).astype(bf16)
        copies[0].start()
        scaled, _ = norm_parts(x_ref[...].astype(f32))
        normed_ref[...] = (scaled * vec_ref[0:1, :] + vec_ref[1:2, :]).astype(bf16)
        copies[1].start()

        def project(i, carry):
            cols = pl.ds(pl.multiple_of(256 * i, 256), 256)
            for kind, row in ((0, 2), (1, None), (2, 3)):
                part = dot(normed_ref[...], w_ref[kind, :, cols])
                if row is not None:
                    part = part + vec_ref[row : row + 1, cols]
                qkv_ref[kind, :, cols] = part.astype(bf16)
            return carry

        lax.fori_loop(0, 3, project, 0)
        copies[2].start()

    @pl.when(step > 0)
    def _():
        cols = pl.ds(pl.multiple_of(128 * (step - 1), 128), 128)
        lane = iota((PAD, 128), 1)
        key_live = iota((PAD, PAD), 0) < SEQ
        for image in range(IMAGES):
            rows = pl.ds(PAD * image, PAD)
            q = qkv_ref[0, rows, cols] * jnp.asarray(0.125, bf16)
            k = qkv_ref[1, rows, cols]
            v = qkv_ref[2, rows, cols]
            total = None
            for n in range(2):
                inside = (lane < HD) == (n == 0)
                scores = dot_lanes(k, jnp.where(inside, q, jnp.zeros_like(q)))
                scores = jnp.where(key_live, scores, -1e30)
                terms = jnp.exp(scores - jnp.max(scores, axis=0, keepdims=True))
                soft = terms * (1.0 / jnp.sum(terms, axis=0, keepdims=True))
                soft = soft.astype(bf16)
                soft_out[0, 2 * image + n] = soft
                part = dot_rows(soft, jnp.where(inside, v, jnp.zeros_like(v)))
                total = part if total is None else total + part
            mixed_out[rows, :] = total.astype(bf16)

    @pl.when(step == 6)
    def _():
        for copy in copies:
            copy.wait()


def gelu_parts(v):
    below = 0.5 + 0.5 * lax.erf(v * 0.7071067811865476)
    return v * below, below + v * jnp.exp(-0.5 * v * v) * 0.3989422804014327


def gather_rows(first, last):
    return jnp.concatenate([first.astype(f32), last.astype(f32)], axis=0).astype(bf16)


def place_rows(w2, ff_ref):
    for d in range(2):
        for g in range(8):
            for y in range(2):
                piece = ff_ref[d, g, y]
                rows = slice(96 * g + 48 * d, 96 * g + 48 * d + 48)
                w2[rows, HALF * y : HALF * y + HALF] = gather_rows(piece[:, :HALF], piece[:, HALF:])


def second_kernel(
    me_ref, live_ref, own_ref, got_ref, vec_ref, x_ref, mixed_ref, wo_ref,
    up_out, middle_out, second_out,
):
    up = unpack(own_ref, got_ref, me_ref[1])
    image = jnp.where(iota((ROWS, 1), 0) < PAD, live_ref[0], live_ref[1])
    up_out[...] = jnp.where(image == 1, up, 0.0).astype(bf16)
    middle = x_ref[...].astype(f32) + dot(mixed_ref[...], wo_ref[...]) + vec_ref[4:5, :]
    middle_out[...] = middle
    scaled, _ = norm_parts(middle)
    second_out[...] = (scaled * vec_ref[5:6, :] + vec_ref[6:7, :]).astype(bf16)


def expand_kernel(
    me_ref, up_ref, second_ref, bias_ref, w1_ref,
    act_out, slope_out, mine_out, theirs_out, w1_out,
    total,
):
    me = me_ref[0]
    for pair in range(16):
        w1_out[48 * pair : 48 * pair + 48, :] = gather_rows(
            w1_ref[0, 2 * pair, 0], w1_ref[0, 2 * pair + 1, 0]
        )

    for i in range(3):
        cols = slice(256 * i, 256 * i + 256)
        inner = dot(second_ref[...], w1_out[:, cols]) + bias_ref[:, cols]
        act, slope = gelu_parts(inner)
        act = act.astype(bf16)
        act_out[:, cols] = act
        slope_out[:, cols] = slope.astype(bf16)
    total[...] = dot_rows(act_out[...], up_ref[...]).astype(bf16)

    for g in range(8):
        for ref, place in ((mine_out, me), (theirs_out, 1 - me)):
            part = total[pl.ds(pl.multiple_of(96 * g + 48 * place, 16), 48), :]
            for y in range(2):
                ref[y, g] = part[:, HALF * y : HALF * y + HALF]


def contract_kernel(
    me_ref, up_ref, slope_ref, second_ref, ff_ref,
    grad_out, hidden_out, mine_out, theirs_out,
    turned, w2,
):
    step = pl.program_id(0)
    me = me_ref[0]

    @pl.when(step == 0)
    def _():
        turned[...] = second_ref[...].T

    place_rows(w2, ff_ref)
    for i in range(3):
        cols = slice(256 * i, 256 * i + 256)
        grad = dot_lanes(up_ref[...], w2[cols, :]) * slope_ref[:, cols].astype(f32)
        grad = grad.astype(bf16)
        grad_out[:, cols] = grad
        hidden_out[:, cols] = jnp.sum(grad.astype(f32), axis=0, keepdims=True)

    def outer(ref):
        for i in range(3):
            cols = slice(256 * i, 256 * i + 256)
            ref[0, :, cols] = dot(turned[...], grad_out[:, cols]).astype(bf16)

    pl.when((step & 1) == me)(lambda: outer(mine_out))
    pl.when((step & 1) != me)(lambda: outer(theirs_out))


def middle_back_kernel(
    me_ref, vec_ref, inner_hbm, w1_hbm, soft_hbm, up_hbm, middle_hbm, wo_hbm, normed_hbm, mixed_hbm, qkv_hbm,
    mine_hbm, theirs_hbm, sums_out, grads_hbm, gm_hbm,
    inner_ref, w1_ref, soft_ref, up_ref, middle_ref, wo_ref, normed_ref, mixed_ref, qkv_ref,
    grad_second, gml, grad_mixed, normed_turned, mixed_turned, pieces, grads_ref, gm_ref, sems,
):
    me = me_ref[0]
    ahead = []
    for j in range(4):
        cols = pl.ds(D * j, D)
        ahead.append((inner_hbm.at[:, cols], inner_ref.at[j]))
        ahead.append((w1_hbm.at[:, cols], w1_ref.at[j]))
    ahead += [
        (middle_hbm, middle_ref), (up_hbm, up_ref), (wo_hbm, wo_ref),
        (normed_hbm, normed_ref), (mixed_hbm, mixed_ref), (qkv_hbm, qkv_ref),
    ]
    reads = [pltpu.make_async_copy(src, dst, sems.at[i]) for i, (src, dst) in enumerate(ahead)]

    def read_soft(i):
        return pltpu.make_async_copy(soft_hbm.at[i], soft_ref.at[i], sems.at[14 + i])

    grads_write = pltpu.make_async_copy(grads_ref, grads_hbm, sems.at[20])
    gm_write = pltpu.make_async_copy(gm_ref, gm_hbm, sems.at[21])

    def write(kind, act):
        cols = pl.ds(HALF * (kind % 2), HALF)
        for to, place in ((mine_hbm, kind // 2), (theirs_hbm, 1 - kind // 2)):
            copy = pltpu.make_async_copy(pieces.at[kind], to.at[:, :, cols], sems.at[22 + kind])
            pl.when(me == place)(lambda copy=copy: act(copy))

    def outer(kind, left, right):
        grad = dot(left[...], right[...]).astype(bf16)
        for y in range(2):
            pieces[kind, y] = grad[:, HALF * y : HALF * y + HALF]
        write(kind, lambda copy: copy.start())

    for read in reads:
        read.start()
    for i in range(6):
        read_soft(i).start()
    for j in range(4):
        reads[2 * j].wait()
        reads[2 * j + 1].wait()
        part = dot_lanes(inner_ref[j], w1_ref[j])
        if j == 0:
            grad_second[...] = part
        else:
            grad_second[...] += part
    for read in reads[8:]:
        read.wait()
    grad = grad_second[...]
    scaled, scale = norm_parts(middle_ref[...])
    up = up_ref[...].astype(f32)
    gm = up + norm_back(grad, scaled, scale, vec_ref[5:6, :])
    gm_ref[...] = gm
    gm_write.start()
    gml[...] = gm.astype(bf16)
    sums_out[2:3, :] = jnp.sum(gml[...].astype(f32), axis=0, keepdims=True)
    sums_out[3:4, :] = jnp.sum(grad * scaled, axis=0, keepdims=True)
    sums_out[4:5, :] = jnp.sum(grad, axis=0, keepdims=True)
    sums_out[5:6, :] = jnp.sum(up, axis=0, keepdims=True)
    grad_mixed[...] = dot_lanes(gml[...], wo_ref[...]).astype(bf16)
    mixed_turned[...] = mixed_ref[...].T
    outer(3, mixed_turned, gml)
    normed_turned[...] = normed_ref[...].T
    lane = iota((PAD, 128), 1)

    def attend(i, carry):
        cols = pl.ds(pl.multiple_of(128 * i, 128), 128)
        read_soft(i).wait()
        for image in range(IMAGES):
            rows = pl.ds(PAD * image, PAD)
            q = qkv_ref[0, rows, cols]
            k = qkv_ref[1, rows, cols]
            v = qkv_ref[2, rows, cols]
            g = grad_mixed[rows, cols]
            dq = dk = dv = jnp.zeros((PAD, 128), f32)
            for n in range(2):
                inside = (lane < HD) == (n == 0)
                zero = jnp.zeros_like(g)
                g_in = jnp.where(inside, g, zero)
                soft_low = soft_ref[i, 2 * image + n]
                soft = soft_low.astype(f32)
                grad_soft = dot_lanes(v, g_in)
                level = jnp.sum(grad_soft * soft, axis=0, keepdims=True)
                scores = (soft * (grad_soft - level)).astype(bf16)
                dv = dv + dot(soft_low, g_in)
                dk = dk + dot(scores, jnp.where(inside, q, zero))
                dq = dq + dot_rows(scores, jnp.where(inside, k, zero))
            grads_ref[0, rows, cols] = (dq * 0.125).astype(bf16)
            grads_ref[1, rows, cols] = (dk * 0.125).astype(bf16)
            grads_ref[2, rows, cols] = dv.astype(bf16)
        return carry

    lax.fori_loop(0, 6, attend, 0)
    grads_write.start()
    for kind in range(3):
        outer(kind, normed_turned, grads_ref.at[kind])
    sums_out[0:1, :] = jnp.sum(grads_ref[0].astype(f32), axis=0, keepdims=True)
    sums_out[1:2, :] = jnp.sum(grads_ref[2].astype(f32), axis=0, keepdims=True)
    grads_write.wait()
    gm_write.wait()
    for kind in range(4):
        write(kind, lambda copy: copy.wait())


def input_back_kernel(
    me_ref, vec_ref, grads_ref, w_ref, x_ref, gm_ref, keep_out, send_out, sums_out, total
):
    step = pl.program_id(0)
    part = dot_lanes(grads_ref[0], w_ref[0])

    @pl.when(step == 0)
    def _():
        total[...] = part

    @pl.when(step > 0)
    def _():
        total[...] += part

    @pl.when(step == 2)
    def _():
        grad = total[...]
        scaled, scale = norm_parts(x_ref[...].astype(f32))
        out = gm_ref[...] + norm_back(grad, scaled, scale, vec_ref[0:1, :])
        pack(out.astype(bf16), me_ref[1], keep_out, send_out)
        sums_out[0:1, :] = jnp.sum(grad * scaled, axis=0, keepdims=True)
        sums_out[1:2, :] = jnp.sum(grad, axis=0, keepdims=True)


def output_kernel(me_ref, vec_ref, middle_ref, act_ref, ff_ref, keep_out, send_out, w2, total):
    step = pl.program_id(0)
    place_rows(w2, ff_ref)
    part = dot(act_ref[...], w2[...])

    @pl.when(step == 0)
    def _():
        total[...] = middle_ref[...] + vec_ref[7:8, :] + part

    @pl.when(step > 0)
    def _():
        total[...] += part

    @pl.when(step == 3)
    def _():
        pack(total[...].astype(bf16), me_ref[1], keep_out, send_out)


def assemble_kernel(at_ref, *refs):
    out = refs[-1]
    step = pl.program_id(0)
    for r in range(4):
        pl.when(step == r)(lambda r=r: out.__setitem__(..., refs[r][...].reshape(out.shape)))


def blocks_sum_kernel(at_ref, *refs):
    ins, outs = refs[:-4], refs[-4:]
    step = pl.program_id(0)
    total = ins[0][...].astype(f32)
    for ref in ins[1:]:
        total = total + ref[...].astype(f32)
    total = total.astype(bf16)
    for r in range(4):
        pl.when(step == r)(lambda r=r: outs[r].__setitem__(..., total.reshape(outs[r].shape)))


def sum_kernel(a_ref, b_ref, c_ref, d_ref, out_ref):
    total = a_ref[...].astype(f32) + b_ref[...].astype(f32) + c_ref[...].astype(f32) + d_ref[...].astype(f32)
    out_ref[...] = total.astype(bf16)


def last_spread_kernel(a_ref, b_ref, c_ref, d_ref, va_ref, vb_ref, vc_ref, vd_ref, out_ref):
    vector = va_ref[...].astype(f32) + vb_ref[...].astype(f32) + vc_ref[...].astype(f32) + vd_ref[...].astype(f32)
    vector = vector.astype(bf16)
    total = a_ref[...].astype(f32) + b_ref[...].astype(f32) + c_ref[...].astype(f32) + d_ref[...].astype(f32)
    total = total.reshape(2 * 192, D)
    for i in range(16):
        out_ref[i, :16, :] = vector
        out_ref[i, 16:, :] = total[24 * i : 24 * i + 24].astype(bf16)


def adamw_step(parameter, gradient, first_moment, second_moment, step_rate, decay_factor):
    first_new = beta_first * first_moment + (1.0 - beta_first) * gradient
    second_new = beta_second * second_moment + (1.0 - beta_second) * gradient * gradient
    first_hat = first_new / (1.0 - beta_first**STEP)
    second_hat = second_new / (1.0 - beta_second**STEP)
    updated = parameter - step_rate * (
        first_hat / (jnp.sqrt(second_hat) + adam_eps) + decay_factor * parameter
    )
    return second_new, updated


def ordered(me, own, got):
    return jnp.where(me == 0, own, got), jnp.where(me == 0, got, own)


def attention_step_kernel(
    me_ref, own_ref, got_ref, w_ref, m_ref, v_ref, vec_ref, vec_m_ref, vec_v_ref,
    grad_out, second_out, new_out, vec_grad_out, vec_second_out, vec_new_out,
):
    pieces = ordered(me_ref[0], own_ref[16:, :], got_ref[16:, :])
    l = iota((512, 512), 0)
    c = iota((512, 512), 1)
    pick = jnp.where(c == 4 * (l & 127) + (l >> 7), 1.0, 0.0)
    for b in range(3):
        kinds = [
            pieces[k // 2][:, HALF * (k % 2) + 128 * b : HALF * (k % 2) + 128 * b + 128]
            for k in range(4)
        ]
        grad_out[:, 512 * b : 512 * b + 512] = jnp.dot(
            jnp.concatenate(kinds, axis=1), pick, precision=lax.Precision.HIGHEST,
            preferred_element_type=f32,
        )
    second_out[...], new_out[...] = adamw_step(
        w_ref[...], grad_out[...], m_ref[...], v_ref[...], learn_rate, decay_rate
    )
    vector = own_ref[:12, :] + got_ref[:12, :]
    vec_grad_out[...] = jnp.where(me_ref[1] == 0, vector[:, :HALF], vector[:, HALF:])
    vec_second_out[...], vec_new_out[...] = adamw_step(
        vec_ref[...], vec_grad_out[...], vec_m_ref[...], vec_v_ref[...], vector_rate, 0.0
    )


def expand_step_kernel(me_ref, own_ref, got_ref, w_ref, m_ref, v_ref, grad_out, second_out, new_out):
    first, last = ordered(me_ref[0], own_ref[...], got_ref[...])
    grad_out[:, :D] = first
    grad_out[:, D:] = last
    second_out[...], new_out[...] = adamw_step(
        w_ref[...], grad_out[...], m_ref[...], v_ref[...], learn_rate, decay_rate
    )


def project_step_kernel(me_ref, own_ref, got_ref, w_ref, m_ref, v_ref, grad_out, second_out, new_out):
    first, last = ordered(me_ref[0], own_ref[...], got_ref[...])
    grad_out[...] = jnp.concatenate([first, last], axis=0)
    second_out[...], new_out[...] = adamw_step(
        w_ref[...], grad_out[...], m_ref[...], v_ref[...], learn_rate, decay_rate
    )


def place(axes):
    at = 0
    for a in axes:
        at = at * lax.axis_size(a) + lax.axis_index(a)
    return at


def swap(x, axis):
    return lax.ppermute(x, axis, [(0, 1), (1, 0)])


def core_sum(mine, theirs):
    return (mine.astype(f32) + swap(theirs, "dp").astype(f32)).astype(bf16)


def assemble(parts, at, shape, piece, index, after=(), cost=0):
    flat = tuple(n for n in piece if n > 1)
    return pl.pallas_call(
        assemble_kernel,
        out_shape=jax.ShapeDtypeStruct(shape, bf16),
        grid_spec=pltpu.PrefetchScalarGridSpec(
            num_scalar_prefetch=1,
            grid=(4,),
            in_specs=[
                *(pl.BlockSpec(flat, lambda r, at: (0,) * len(flat)) for _ in range(4)),
                *(LEFT for _ in after),
            ],
            out_specs=pl.BlockSpec(piece, lambda r, at: index((at[0] + 3 * r) % 4)),
        ),
        compiler_params=pltpu.CompilerParams(vmem_limit_bytes=32 * 1024 * 1024),
        cost_estimate=pl.CostEstimate(flops=cost * 10**9 + 1000, bytes_accessed=0, transcendentals=0),
        name="assemble",
    )(at.reshape(1).astype(jnp.int32), *(p.reshape(flat) for p in parts), *after)


def ring_blocks(parts, at, shape, piece, index):
    spec = pl.BlockSpec(piece, lambda r, at: index((at[0] + r) % 4))
    flat = tuple(n for n in piece if n > 1)
    return pl.pallas_call(
        blocks_sum_kernel,
        out_shape=[jax.ShapeDtypeStruct(flat, bf16)] * 4,
        grid_spec=pltpu.PrefetchScalarGridSpec(
            num_scalar_prefetch=1,
            grid=(4,),
            in_specs=[spec] * len(parts),
            out_specs=[pl.BlockSpec(flat, lambda r, at: (0,) * len(flat))] * 4,
        ),
        compiler_params=pltpu.CompilerParams(vmem_limit_bytes=32 * 1024 * 1024),
        cost_estimate=pl.CostEstimate(flops=1000, bytes_accessed=0, transcendentals=0),
        name="ring_blocks",
    )(at.reshape(1).astype(jnp.int32), *(p.reshape(shape) for p in parts))


def hop(x, axes, r):
    return lax.ppermute(x, axes, [(i, (i + r) % 4) for i in range(4)])


def ring(blocks, axes):
    return blocks[0], *(hop(blocks[r], axes, r) for r in (1, 3, 2))


def crossed(x, axis, bit):
    return lax.ppermute(x, axis, [(i, i ^ bit) for i in range(lax.axis_size(axis))])


def to_all(x, axes):
    near, back = hop(x, axes, 1), hop(x, axes, 3)
    return x, near, hop(x, axes, 2), back


def sum_of(parts):
    total = parts[0].astype(f32)
    for part in parts[1:]:
        total = total + part.astype(f32)
    return total


def spread_sum(blocks, axes):
    tiles = lax.all_to_all(blocks, axes, 0, 0, tiled=True)
    return jnp.sum(tiles.astype(f32), axis=0)


def own_images(stored, gy):
    rows = stored.shape[0] // 2
    own = lax.dynamic_slice_in_dim(stored, rows * gy, rows, 0)
    other = lax.dynamic_slice_in_dim(stored, rows * (1 - gy), rows, 0)
    pad = ((0, PAD - rows), (0, 0))
    return jnp.pad(own, pad), jnp.pad(other, pad)


def stored_rows(keep, got, gy):
    first = jnp.where(gy == 0, keep, got)[:SEQ]
    last = jnp.where(gy == 0, got, keep)[:SEQ]
    return jnp.concatenate([first, last], axis=0).astype(f32)


def per_device(
    tokens,
    image_counts,
    slot_order,
    cotangent,
    attention_weights,
    attention_first,
    attention_second,
    expand_weight,
    expand_first,
    expand_second,
    project_weight,
    project_first,
    project_second,
    vectors,
    vector_first,
    vector_second,
):
    dp = lax.axis_index("dp")
    gy = lax.axis_index("xl")
    me = jnp.stack([dp, gy]).astype(jnp.int32)

    token_own, token_other = own_images(tokens, gy)
    token_got = swap(token_other, "xl")
    grad_own, grad_other = own_images(cotangent, gy)
    grad_got = swap(grad_other, "xl")
    vec_got = swap(vectors, "xl")
    attn_piece, ff_piece = call(
        prepare_kernel,
        [SCALARS, LEFT, LEFT, LEFT],
        [((24, D), bf16, WHOLE), ((24, 2 * D), bf16, WHOLE)],
        (me, *(pltpu.with_memory_space_constraint(w, pltpu.HBM) for w in (attention_weights, expand_weight, project_weight.T))),
        scratch=[
            pltpu.VMEM((24, 4 * HALF), f32),
            pltpu.VMEM((24, 4 * HALF), f32),
            pltpu.VMEM((96, HALF), f32),
            pltpu.SemaphoreType.DMA((3,)),
        ],
        name="prepare",
    )
    ff = lax.all_gather(ff_piece, EVERY).reshape(2, 32, 2, 24, 2 * D)
    at_x, at_y, at_z = place(X), place(Y), place(Z)

    def across_x(p):
        return p % 2, 0, p // 2, 0, 0

    attn = to_all(attn_piece, X)
    attn = assemble(attn, at_x, (2, 1, 2, 24, D), (1, 1, 1, 24, D), across_x)
    attn = to_all(attn.reshape(2, 48, D), Y)
    attn, token_got, vec_got = lax.optimization_barrier((attn, token_got, vec_got))
    attn = assemble(attn, at_y, (2, 4, 48, D), (2, 1, 48, D), lambda p: (0, p, 0, 0))
    vec_first, vec_last = ordered(gy, vectors, vec_got)
    vec = jnp.concatenate([vec_first, vec_last], axis=1)
    bias = vec[8:].T.reshape(1, FF)
    live = (slot_order[0] < image_counts[0]).astype(jnp.int32)
    live = lax.dynamic_slice_in_dim(live, IMAGES * gy, IMAGES)
    attn = to_all(attn.reshape(2, 192, D), Z)
    attn, vec, bias, live, token_own, token_got = lax.optimization_barrier(
        (attn, vec, bias, live, token_own, token_got)
    )
    attn = assemble(attn, at_z, (2, 4, 192, D), (2, 1, 192, D), lambda p: (0, p, 0, 0))
    w_own, w_got = (w.reshape(2, D, D) for w in (attn, swap(attn, "dp")))

    tall = block((ROWS, D), lambda j: (0, 0))
    wide = block((ROWS, D), lambda j: (0, j))
    w1_block = block((1, 32, 1, 24, D), lambda j: (j % 2, 0, j // 2, 0, 0))
    w2_block = block((2, 8, 2, 24, D), lambda j: (0, j, 0, 0, 1))
    pieces2 = block((2, 8, 48, HALF), lambda j: (0, j, 0, 0))
    soft_shape = (6, 2 * IMAGES, PAD, PAD)

    soft, mixed, x, normed, qkv, w_qkv, w_o = call(
        attend_kernel,
        [SCALARS, *(WHOLE,) * 5],
        [
            (soft_shape, bf16, block((1, *soft_shape[1:]), lambda p: (jnp.maximum(p - 1, 0), 0, 0, 0))),
            ((ROWS, D), bf16, block((ROWS, 128), lambda p: (0, jnp.maximum(p - 1, 0)))),
            ((ROWS, D), bf16, LEFT),
            ((ROWS, D), bf16, LEFT),
            ((3, ROWS, D), bf16, LEFT),
            ((3, D, D), bf16, LEFT),
            ((D, D), bf16, LEFT),
        ],
        (me, token_own, token_got, vec, w_own, w_got),
        grid=(7,),
        scratch=[
            pltpu.VMEM((ROWS, D), bf16),
            pltpu.VMEM((ROWS, D), bf16),
            pltpu.VMEM((3, ROWS, D), bf16),
            pltpu.VMEM((4, D, D), bf16),
            pltpu.SemaphoreType.DMA((5,)),
        ],
        name="attend",
    )

    up, middle, second = call(
        second_kernel,
        [SCALARS, SCALARS, *(WHOLE,) * 6],
        [((ROWS, D), bf16, WHOLE), ((ROWS, D), f32, WHOLE), ((ROWS, D), bf16, WHOLE)],
        (me, live, grad_own, grad_got, vec, x, mixed, w_o),
        name="second",
    )
    act, slope, mine2, theirs2, w1 = call(
        expand_kernel,
        [SCALARS, WHOLE, WHOLE, block((1, D), lambda j: (0, j)), w1_block],
        [
            ((ROWS, FF), bf16, wide),
            ((ROWS, FF), bf16, wide),
            ((2, 32, 48, HALF), bf16, pieces2),
            ((2, 32, 48, HALF), bf16, pieces2),
            ((D, FF), bf16, block((D, D), lambda j: (0, j))),
        ],
        (me, up, second, bias, ff),
        grid=(4,),
        scratch=[pltpu.VMEM((D, D), bf16)],
        after=(w_o, soft),
        name="expand",
    )
    inner_grad, hidden_sums, mine1, theirs1 = call(
        contract_kernel,
        [SCALARS, WHOLE, wide, WHOLE, w2_block],
        [
            ((ROWS, FF), bf16, wide),
            ((1, FF), f32, block((1, D), lambda j: (0, j))),
            ((2, D, D), bf16, block((1, D, D), lambda j: (j // 2, 0, 0))),
            ((2, D, D), bf16, block((1, D, D), lambda j: (j // 2, 0, 0))),
        ],
        (me, up, slope, second, ff),
        grid=(4,),
        scratch=[pltpu.VMEM((D, ROWS), bf16), pltpu.VMEM((D, D), bf16)],
        name="contract",
    )
    ring2 = ring_blocks(
        (mine2, swap(theirs2, "dp")),
        place(X),
        (2, 16, 2, 48, HALF),
        (1, 16, 1, 48, HALF),
        lambda p: (p % 2, 0, p // 2, 0, 0),
    )
    got1, _ = lax.optimization_barrier((swap(theirs1, "dp"), ring2[0]))
    ring1 = ring_blocks(
        (mine1, got1), place(Y), (8, 4, 48, D), (8, 1, 48, D), lambda p: (0, p, 0, 0)
    )

    mine0, theirs0, sums_c, grads, gm = call(
        middle_back_kernel,
        [SCALARS, WHOLE, *(LEFT,) * 9],
        [
            ((2, D, D), bf16, LEFT),
            ((2, D, D), bf16, LEFT),
            ((6, D), f32, WHOLE),
            ((3, ROWS, D), bf16, LEFT),
            ((ROWS, D), f32, LEFT),
        ],
        (me, vec, inner_grad, w1, soft, up, middle, w_o, normed, mixed, qkv),
        scratch=[
            pltpu.VMEM((4, ROWS, D), bf16),
            pltpu.VMEM((4, D, D), bf16),
            pltpu.VMEM(soft_shape, bf16),
            pltpu.VMEM((ROWS, D), bf16),
            pltpu.VMEM((ROWS, D), f32),
            pltpu.VMEM((D, D), bf16),
            pltpu.VMEM((ROWS, D), bf16),
            pltpu.VMEM((ROWS, D), bf16),
            pltpu.VMEM((3, ROWS, D), bf16),
            pltpu.VMEM((ROWS, D), f32),
            pltpu.VMEM((ROWS, D), bf16),
            pltpu.VMEM((ROWS, D), bf16),
            pltpu.VMEM((D, ROWS), bf16),
            pltpu.VMEM((D, ROWS), bf16),
            pltpu.VMEM((4, 2, D, HALF), bf16),
            pltpu.VMEM((3, ROWS, D), bf16),
            pltpu.VMEM((ROWS, D), f32),
            pltpu.SemaphoreType.DMA((26,)),
        ],
        after=(ring2[0], ring1[0]),
        cost=0,
        name="middle_back",
    )
    got0 = swap(theirs0, "dp")
    ring2 = ring(ring2, X)
    near1 = hop(ring1[1], Y, 1), hop(ring1[3], Y, 3)
    ring2, mine0 = lax.optimization_barrier((ring2, mine0))
    mine0, near1, far1 = lax.optimization_barrier((mine0, near1, ring1[2]))
    far1 = hop(far1, Y, 2)
    part2 = call(
        sum_kernel, [WHOLE] * 4, [((16, 48, HALF), bf16, WHOLE)], ring2, cost=100, after=(near1[0], near1[1]), name="part"
    )[0]
    tiles2 = lax.all_to_all(part2, Z + Y, 0, 0, tiled=True)
    mine0, got0, _ = lax.optimization_barrier((mine0, got0, part2))
    ring0 = ring_blocks(
        (mine0, got0), place(Z), (2, 4, 192, D), (2, 1, 192, D), lambda p: (0, p, 0, 0)
    )
    tiles2, far1, _ = lax.optimization_barrier((tiles2, far1, ring0[0]))
    own0, near0, back0, far0 = ring(ring0, Z)
    keep_out, send_out = call(
        output_kernel,
        [SCALARS, WHOLE, WHOLE, wide, w2_block],
        [((PAD, D), bf16, block((PAD, D), lambda j: (0, 0)))] * 2,
        (me, vec, middle, act, ff),
        grid=(4,),
        scratch=[pltpu.VMEM((D, D), bf16), pltpu.VMEM((ROWS, D), f32)],
        after=(ring0[0],),
        cost=0,
        name="output",
    )
    far1, tiles2, keep_out = lax.optimization_barrier((far1, tiles2, keep_out))
    part1 = sum_of((ring1[0], *near1, far1)).astype(bf16).reshape(16, 24, D)
    tiles1 = lax.all_to_all(part1, ("xl", "z", "xh"), 0, 0, tiled=True)
    grads, near0, back0 = lax.optimization_barrier((grads, near0, back0))
    keep_in, send_in, sums_e = call(
        input_back_kernel,
        [
            SCALARS, WHOLE,
            block((1, ROWS, D), lambda k: (k, 0, 0)), block((1, D, D), lambda k: (k, 0, 0)),
            WHOLE, WHOLE,
        ],
        [
            ((PAD, D), bf16, block((PAD, D), lambda k: (0, 0))),
            ((PAD, D), bf16, block((PAD, D), lambda k: (0, 0))),
            ((2, D), f32, block((2, D), lambda k: (0, 0))),
        ],
        (me, vec, grads, w_qkv, x, gm),
        grid=(3,),
        scratch=[pltpu.VMEM((ROWS, D), f32)],
        cost=100,
        after=(part1,),
        name="input_back",
    )
    sums_e, hidden_sums = lax.optimization_barrier((sums_e, hidden_sums))
    vector = jnp.concatenate(
        [sums_e, sums_c, hidden_sums.reshape(D, 4).T, jnp.zeros((4, D), f32)], axis=0
    ).astype(bf16)
    vectors4 = ring((vector,) * 4, Z)
    got_in, got_out = swap(send_in, "xl"), swap(send_out, "xl")
    tiles2, vectors4, got_in, got_out = lax.optimization_barrier((tiles2, vectors4, got_in, got_out))
    sum2 = jnp.sum(tiles2.astype(f32), axis=0)
    got2 = swap(sum2, "dp")
    part0 = call(
        last_spread_kernel,
        [WHOLE] * 8,
        [((16, 40, D), bf16, WHOLE)],
        (own0, near0, back0, far0, *vectors4),
        cost=0,
        name="last_spread",
    )[0]
    tiles0 = lax.all_to_all(part0, ("xl", "y", "xh"), 0, 0, tiled=True)
    sum1 = jnp.sum(tiles1.astype(f32), axis=0)
    got1 = swap(sum1, "dp")
    block_out = stored_rows(keep_out, got_out, gy)
    input_grad = stored_rows(keep_in, got_in, gy)

    def step(body, own, got, shape, state, outs=(), cost=0, name=None):
        state = (me, own, got, *state)
        outs = [(shape, f32, WHOLE)] * 3 + [(o, f32, WHOLE) for o in outs]
        return call(body, [SCALARS, *(WHOLE,) * (len(state) - 1)], outs, state, cost=cost, name=name)

    project = step(
        project_step_kernel, sum2, got2, (96, HALF),
        (project_weight.T, project_first.T, project_second.T), name="project_step",
    )
    expand = step(
        expand_step_kernel, sum1, got1, (24, 2 * D),
        (expand_weight, expand_first, expand_second), name="expand_step",
    )
    tiles0, project = lax.optimization_barrier((tiles0, project))
    sum0 = jnp.sum(tiles0.astype(f32), axis=0)
    got0 = swap(sum0, "dp")
    *attention, vector_grad, vector_second_new, vector_new = step(
        attention_step_kernel, sum0, got0, (24, 2 * D),
        (attention_weights, attention_first, attention_second, vectors, vector_first, vector_second),
        [(12, HALF)] * 3, name="attention_step",
    )
    return (
        block_out,
        input_grad,
        *attention,
        *expand,
        *(p.T for p in project),
        vector_grad,
        vector_second_new,
        vector_new,
    )


def solution(mesh):
    fine = Mesh(mesh.devices.reshape(2, 4, 4, 2, 2), EVERY)
    rows = ("dp", "z", "y", "xh")
    deep = ("z", "y", "xh")
    placed = (
        P(rows, "xl"),
        P("dp"),
        P("dp", deep),
        P(rows, "xl"),
        *(P(deep, "xl"),) * 6,
        *(P("xl", deep),) * 3,
        *(P(None, "xl"),) * 3,
    )
    out = (
        P(rows, "xl"),
        P(rows, "xl"),
        *(P(deep, "xl"),) * 6,
        *(P("xl", deep),) * 3,
        *(P(None, "xl"),) * 3,
    )
    return jax.shard_map(per_device, mesh=fine, in_specs=placed, out_specs=out, check_vma=False)
```
